32 devices in a mesh: sec: 4 (over y, x), lat: 8 (over z, core).
Axes of the slice: x: 2, y: 2, z: 4, core: 2. Of those that a mesh axis runs over, the one named last changes fastest.
Arguments:
- spectra: float32 [32, 96, 768], P('lat', 'sec'), may hold values from 0.2 to 2
- turning: float32 [32, 96], P('lat', 'sec'), may hold values from -0.45 to 0.45
- currents: float32 [32, 96, 64], P('lat', 'sec'), may hold values from -3 to 3
- drag_rates: float32 [32], replicated, may hold values from 0.02 to 0.3
- land_mask: int32 [32, 96], P('lat', 'sec'), may hold values 0 or 1
- ocean_target: int32 [32, 96], P('lat', 'sec'), may hold values from 0 to 3, as said below
Outputs:
- spectra_out: float32 [32, 96, 768], P('lat', 'sec')
- currents_out: float32 [32, 96, 64], P('lat', 'sec')
The draws below stay inside these ranges and needn't reach their ends.
Inputs may be any that keep to these rules, and one draw needn't show every extreme that they name: `ocean_target`: in each device's block of 4 x 24 columns every target value appears on exactly 24 columns.
All inputs are finite; a program needn't handle non-finite values. No bound on the sum of `land_mask` on one device may be relied on, other than what follows from the above.
Results may differ from the reference program's by a relative error of at most 0.0003.
Values sent between devices are 32-bit elements; how exact they have to be, the bound alone decides.
No kernel may reach another device: no remote copies, remote signals or barrier semaphores. Data moves between devices by JAX's collectives and lax.ppermute only.
A program may use at most 64 MiB of HBM per device.

```python
import math
import jax
import jax.numpy as jnp
from jax import lax

NFREQ = 24
NDIR = 32
NDEPTH = 32
LAT_DEV = 4
LON_DEV = 24
STEPS = 3
NLAT = 32
NLON = 96
N_SEC = 4
N_LAT = 8


def draw_ocean_target(key, part):
    column_count = LAT_DEV * LON_DEV
    band_count = NLAT // LAT_DEV
    sections = NLON // LON_DEV
    labels = jnp.arange(column_count, dtype=jnp.int32) % sections
    scores = jax.random.randint(key, (band_count * sections, column_count), 0, 32768, dtype=jnp.int32) * column_count + jnp.arange(column_count, dtype=jnp.int32)[None, :]
    shuffle = jnp.argsort(scores, axis=1, stable=True)
    values = labels[shuffle]
    return values.reshape(band_count, sections, LAT_DEV, LON_DEV).transpose(0, 2, 1, 3).reshape(NLAT, NLON)


def plant(result, key, least, top_value):
    place = [jax.random.randint(jax.random.fold_in(key, axis), (), 0, length) for axis, length in enumerate(result.shape)]
    main_axis = result.shape.index(max(result.shape))
    beside = place[:main_axis] + [(place[main_axis] + 1) % result.shape[main_axis]] + place[main_axis + 1:]
    return result.at[tuple(place)].set(least).at[tuple(beside)].set(top_value)


def block_levels(rng, dims, cuts, least, high):
    def one(dim, shards_of):
        draws = jax.random.uniform(jax.random.fold_in(jax.random.fold_in(rng, 6), dim), (shards_of,), jnp.float32, least / len(cuts), high / len(cuts))
        return jnp.repeat(jnp.exp(draws), dims[dim] // shards_of).reshape((-1,) + (1,) * (len(dims) - dim - 1))

    factor_of = one(*cuts[0])
    for cut in cuts[1:]:
        factor_of = factor_of * one(*cut)
    return factor_of


def gaussian(own_key, shape, width, bound, cuts=(), held_as=jnp.bfloat16):
    entries = width * jax.random.normal(own_key, shape, jnp.float32)
    if cuts:
        entries = entries * block_levels(own_key, shape, cuts, -0.22, 0.18)
    return jnp.clip(entries, -bound, bound).astype(held_as)


def setup_inputs(seed: int = 0) -> dict:
    seeds = jax.random.split(jax.random.key(seed), 7)
    return {
        "spectra": jnp.clip(jnp.exp(math.log(2.0) - 2.3025851 * jax.random.uniform(seeds[0], (NLAT, NLON, NFREQ * NDIR), jnp.float32) ** block_levels(seeds[0], (NLAT, NLON, NFREQ * NDIR), ((0, 8), (1, 4)), -0.2, 0.2)), 0.2, 2.0),
        "turning": jnp.clip(jax.random.uniform(seeds[1], (NLAT, NLON), jnp.float32, -0.45, 0.45) * block_levels(seeds[1], (NLAT, NLON), ((0, 8), (1, 4)), -0.4, 0.0), -0.45, 0.45),
        "currents": gaussian(seeds[2], (NLAT, NLON, 2 * NDEPTH), 0.5, 3.0, ((0, 8), (1, 4)), jnp.float32),
        "drag_rates": jnp.clip(jnp.exp(jax.random.uniform(seeds[3], (NDEPTH,), jnp.float32, math.log(0.02), math.log(0.3))), 0.02, 0.3),
        "land_mask": plant((jax.random.randint(seeds[4], (NLAT, NLON), 0, 8) < 7).astype(jnp.int32), jax.random.fold_in(seeds[4], 1), 0, 1),
        "ocean_target": draw_ocean_target(jax.random.fold_in(seeds[6], 71), 0),
    }


stokes_scale = 0.1
ocean_dt = 0.3
current_gain = 0.2


def build_tables(nfreq, ndir, ndepth):
    fraction = jnp.arange(nfreq, dtype=jnp.float32) / (nfreq - 1)
    angles = (jnp.arange(ndir, dtype=jnp.float32) + 0.5) * (2.0 * math.pi / ndir)
    east_part = jnp.cos(angles)
    north_part = jnp.sin(angles)
    courant = 0.1 + 0.3 * fraction
    levels = jnp.arange(ndepth, dtype=jnp.float32)
    depth_level = 0.5 + (ndepth - 2) * (1.0 - fraction)
    weights = jnp.maximum(1.0 - jnp.abs(levels[None, :] - depth_level[:, None]), 0.0)
    mean_weights = weights / jnp.sum(weights, axis=1, keepdims=True)
    x_rate = (courant[:, None] * east_part[None, :]).reshape(-1)
    y_rate = (courant[:, None] * north_part[None, :]).reshape(-1)
    compass = jnp.stack([east_part, north_part])
    eye_freq = jnp.eye(nfreq, dtype=jnp.float32)
    eye_two = jnp.eye(2, dtype=jnp.float32)
    stokes_matrix = (stokes_scale * weights[:, None, None, :] * compass.T[None, :, :, None]).reshape(nfreq * ndir, 2 * ndepth)
    moment_matrix = (eye_freq[:, None, None, :] * compass.T[None, :, :, None]).reshape(nfreq * ndir, 2 * nfreq)
    profile_matrix = (stokes_scale * eye_two[:, None, :, None] * weights[None, :, None, :]).reshape(2 * nfreq, 2 * ndepth)
    average_matrix = (eye_two[:, None, :, None] * mean_weights.T[None, :, None, :]).reshape(2 * ndepth, 2 * nfreq)
    turn_gain = 1.0 - 0.5 * fraction
    growth = current_gain * (1.0 + fraction)
    return (east_part, north_part, x_rate, y_rate, stokes_matrix, moment_matrix, profile_matrix,
            average_matrix, turn_gain, growth)


def upwind(center, west, east, south, north, x_rate, y_rate):
    along_x = jnp.maximum(x_rate, 0.0) * (center - west) + jnp.minimum(x_rate, 0.0) * (east - center)
    along_y = jnp.maximum(y_rate, 0.0) * (center - south) + jnp.minimum(y_rate, 0.0) * (north - center)
    return center - along_x - along_y


def turn_grow(advected, turning, current_eff, east_part, north_part, turn_gain, growth, nfreq, ndir):
    layout = advected.shape
    spread = advected.reshape(layout[:-1] + (nfreq, ndir))
    turn_rate = turning[..., None, None] * turn_gain[:, None]
    behind = jnp.roll(spread, 1, axis=-1)
    forward = jnp.roll(spread, -1, axis=-1)
    turned = spread - jnp.maximum(turn_rate, 0.0) * (spread - behind) - jnp.minimum(turn_rate, 0.0) * (forward - spread)
    zonal = current_eff[..., :nfreq]
    meridional = current_eff[..., nfreq:]
    aligned = zonal[..., None] * east_part + meridional[..., None] * north_part
    grown = turned * (1.0 + growth[:, None] * aligned)
    return grown.reshape(layout)


def ocean_step(currents, padded, stokes, coriolis, keep, ndepth):
    zonal = currents[..., :ndepth]
    meridional = currents[..., ndepth:]
    shear = 0.5 * (padded[1:-1, 2:, ndepth:] - padded[1:-1, :-2, ndepth:]) - 0.5 * (padded[2:, 1:-1, :ndepth] - padded[:-2, 1:-1, :ndepth])
    spin = coriolis[:, None, None] + shear
    new_zonal = keep * (zonal + ocean_dt * spin * (meridional + stokes[..., ndepth:]))
    new_merid = keep * (meridional - ocean_dt * spin * (zonal + stokes[..., :ndepth]))
    return jnp.concatenate([new_zonal, new_merid], axis=-1)


def to_blocks(field):
    trailing = field.shape[-1]
    split = field.reshape(N_LAT, LAT_DEV, N_SEC, LON_DEV, trailing)
    return split.transpose(0, 2, 1, 3, 4).reshape(N_LAT, N_SEC, LAT_DEV * LON_DEV, trailing)


def from_blocks(blocks):
    trailing = blocks.shape[-1]
    split = blocks.reshape(N_LAT, N_SEC, LAT_DEV, LON_DEV, trailing)
    return split.transpose(0, 2, 1, 3, 4).reshape(NLAT, NLON, trailing)


def swap_sections(blocks):
    trailing = blocks.shape[-1]
    per_target = LAT_DEV * LON_DEV // N_SEC
    grouped = blocks.reshape(N_LAT, N_SEC, N_SEC, per_target, trailing)
    return jnp.swapaxes(grouped, 1, 2).reshape(N_LAT, N_SEC, LAT_DEV * LON_DEV, trailing)


def reference(spectra, turning, currents, drag_rates, land_mask, ocean_target):
    (east_part, north_part, x_rate, y_rate, stokes_matrix, moment_matrix, profile_matrix,
     average_matrix, turn_gain, growth) = build_tables(NFREQ, NDIR, NDEPTH)
    order = jnp.argsort(to_blocks(ocean_target[..., None])[..., 0], axis=-1, stable=True)
    inverse = jnp.argsort(order, axis=-1, stable=True)
    sea = land_mask.astype(jnp.float32)[..., None]
    keep = 1.0 - drag_rates
    coriolis = 0.2 + 0.6 * jnp.arange(NLAT, dtype=jnp.float32) / NLAT
    for iteration in range(STEPS):
        stokes_wave = jnp.dot(spectra.reshape(-1, NFREQ * NDIR), stokes_matrix,
                              precision=lax.Precision.HIGHEST).reshape(NLAT, NLON, 2 * NDEPTH)
        sorted_stokes = jnp.take_along_axis(to_blocks(stokes_wave), order[..., None], axis=2)
        stokes = from_blocks(swap_sections(sorted_stokes))
        at_waves = jnp.take_along_axis(swap_sections(to_blocks(currents)), inverse[..., None], axis=2)
        current_eff = jnp.dot(from_blocks(at_waves).reshape(-1, 2 * NDEPTH), average_matrix,
                              precision=lax.Precision.HIGHEST).reshape(NLAT, NLON, 2 * NFREQ)
        padded = jnp.pad(spectra, ((1, 1), (1, 1), (0, 0)))
        advected = upwind(spectra, padded[1:-1, :-2], padded[1:-1, 2:], padded[:-2, 1:-1], padded[2:, 1:-1], x_rate, y_rate)
        new_spectra = turn_grow(advected, turning, current_eff, east_part, north_part, turn_gain, growth, NFREQ, NDIR) * sea
        ocean_padded = jnp.pad(currents, ((1, 1), (1, 1), (0, 0)))
        currents = ocean_step(currents, ocean_padded, stokes, coriolis, keep, NDEPTH) * sea
        spectra = new_spectra
    return (spectra, currents)
```

```python
import functools
import math

import jax
import jax.numpy as jnp
import ml_dtypes
import numpy as np
from jax import lax
from jax.experimental import pallas as pl
from jax.experimental.pallas import tpu as pltpu
from jax.sharding import PartitionSpec as P

NFREQ = 24
NDIR = 32
STEPS = 3

stokes_scale = 0.1
ocean_dt = 0.3
current_gain = 0.2

LANES = 128
VMEM = pl.BlockSpec(memory_space=pltpu.VMEM)
F32 = jnp.float32
BF16 = jnp.bfloat16


def split_halves(table):
    high = table.astype(ml_dtypes.bfloat16)
    low = (table - high.astype(np.float64)).astype(ml_dtypes.bfloat16)
    return high, low


def build_tables(nfreq, ndir, ndepth):
    fraction = np.arange(nfreq) / (nfreq - 1)
    angles = (np.arange(ndir) + 0.5) * (2.0 * math.pi / ndir)
    east_part, north_part = np.cos(angles), np.sin(angles)
    courant = 0.1 + 0.3 * fraction
    depth_level = 0.5 + (ndepth - 2) * (1.0 - fraction)
    weights = np.maximum(1.0 - np.abs(np.arange(ndepth)[None, :] - depth_level[:, None]), 0.0)
    mean_weights = weights / weights.sum(axis=1, keepdims=True)
    x_rate = np.abs(courant[:, None] * east_part[None, :]).reshape(-1)
    y_rate = np.abs(courant[:, None] * north_part[None, :]).reshape(-1)
    turn_gain = np.repeat(1.0 - 0.5 * fraction, ndir)
    rates = np.stack([1.0 - x_rate - y_rate, x_rate, y_rate, turn_gain] * 2).astype(np.float32)
    compass = np.stack([east_part, north_part])
    stokes = (stokes_scale * weights[:, None, None, :] * compass.T[None, :, :, None]).reshape(
        nfreq * ndir, 2 * ndepth
    )
    growth = current_gain * (1.0 + fraction)
    grow = (
        growth[None, None, :, None] * mean_weights.T[None, :, :, None] * compass[:, None, None, :]
    ).reshape(2 * ndepth, nfreq * ndir)
    stokes_high, stokes_low = split_halves(stokes)
    grow_high, grow_low = split_halves(grow)
    return (
        rates,
        np.concatenate([stokes_high, stokes_low], axis=1),
        np.concatenate([grow_high, grow_high, grow_low, grow_low], axis=0),
    )


def sec_exchanges(count):
    if count % 4 == 0:
        far = count // 4
        return [
            [((i // 4 + hop) % far) * 4 + ((i % 4) ^ flip) for i in range(count)]
            for hop in range(far)
            for flip in range(4)
            if hop or flip
        ]
    return [[(i + hop) % count for i in range(count)] for hop in range(1, count)]


class Plan:
    def __init__(self, sections, bands, rows, cols, spectral, depth):
        self.sections, self.bands = sections, bands
        self.rows, self.cols, self.spectral, self.depth = rows, cols, spectral, depth
        self.columns = rows * cols
        self.chunk = self.columns // sections
        self.tiles = spectral // LANES
        self.exchanges = sec_exchanges(sections)
        self.edges = [
            any(abs(target - i) == 1 for i, target in enumerate(table)) for table in self.exchanges
        ]
        self.sec_rows = [
            self.chunk + (self.tiles * rows + 8 if edge else 0) for edge in self.edges
        ]

    def partner(self, section, number):
        if self.sections % 4 == 0:
            far = self.sections // 4
            hop, flip = divmod(number + 1, 4)
            high, low = lax.div(section, 4), lax.rem(section, 4)
            flipped = low
            if flip & 1:
                flipped = flipped + 1 - 2 * lax.rem(flipped, 2)
            if flip & 2:
                flipped = flipped + 2 - 4 * lax.div(flipped, 2)
            return (
                lax.rem(high + hop, far) * 4 + flipped,
                lax.rem(high + far - hop, far) * 4 + flipped,
            )
        hop = number + 1
        return (
            lax.rem(section + hop, self.sections),
            lax.rem(section + self.sections - hop, self.sections),
        )


def lane_of(shape):
    return lax.broadcasted_iota(jnp.int32, shape, len(shape) - 1)


def dot(a, b):
    return jnp.dot(a, b, preferred_element_type=F32)


def send_parts(plan, section, even, waves, ocean, permute_t, coupling, sec_out, lat_out):
    chunk, tiles, rows, cols = plan.chunk, plan.tiles, plan.rows, plan.cols
    shape = (plan.columns, LANES)
    lane = lane_of(shape)
    total = None
    for start in range(0, plan.spectral, 256):
        part = waves[:, :, start : start + 256].reshape(plan.columns, 256)
        high = part.astype(BF16)
        low = (part - high.astype(F32)).astype(BF16)
        product = dot(jnp.concatenate([high, low], axis=0), coupling["stokes"][start : start + 256, :])
        total = product if total is None else total + product
    moments = total[: plan.columns] + total[plan.columns :]
    moments = moments + pltpu.roll(moments, LANES // 2, 1)
    high = moments.astype(BF16).astype(F32)
    halves = jnp.where(lane < LANES // 2, high, moments - high).astype(BF16)
    ordered = dot(permute_t, halves)
    ordered = ordered + pltpu.roll(ordered, LANES // 2, 1)
    packed = jnp.where(lane < LANES // 2, ocean, ordered)
    coupling["packed"][...] = packed
    ocean = ocean.reshape(rows, cols, LANES)
    for number, out in enumerate(sec_out):
        target, _ = plan.partner(section, number)
        out[0:chunk, :] = coupling["packed"][pl.ds(pl.multiple_of(target * chunk, 8), chunk), :]
        if not plan.edges[number]:
            continue
        eastward = target == section + 1
        for row in range(rows):
            edge = jnp.where(
                eastward, waves[row, cols - 1 : cols, :], waves[row, 0:1, :]
            )
            for tile in range(tiles):
                place = chunk + tile * rows + row
                out[place : place + 1, :] = edge[:, tile * LANES : (tile + 1) * LANES]
            place = chunk + tiles * rows + row
            out[place : place + 1, :] = jnp.where(
                eastward, ocean[row, cols - 1 : cols, :], ocean[row, 0:1, :]
            )
    near, far = lat_out
    for out, northward in ((near, even), (far, jnp.logical_not(even))):
        out[:, 0 : plan.spectral] = jnp.where(northward, waves[rows - 1], waves[0])
        out[:, plan.spectral :] = jnp.where(northward, ocean[rows - 1], ocean[0])


def first_kernel(plan, axes, *refs):
    waves, turning, currents, drag, mask, target, stokes_table = refs[:7]
    refs = refs[7:]
    permute_out, permute_t_out, turn_out, sea_out, keep_out, ocean_out, packed_out = refs[:7]
    refs = refs[7:]
    sec_out, lat_out = refs[: len(plan.exchanges)], refs[len(plan.exchanges) :]
    section, band = lax.axis_index(axes[1]), lax.axis_index(axes[0])
    even = lax.rem(band, 2) == 0
    columns, rows = plan.columns, plan.rows

    across = lane_of((columns, columns))
    down = lax.broadcasted_iota(jnp.int32, (columns, columns), 0)
    here = across == down

    def row_of(ref):
        return jnp.concatenate([ref[row : row + 1, :] for row in range(rows)], axis=1)

    def column_of(row):
        spread = jnp.broadcast_to(row, (columns, columns))
        return jnp.sum(jnp.where(here, spread, jnp.zeros_like(spread)), axis=1, keepdims=True)

    target_row = row_of(target).astype(F32)
    target_col = column_of(target_row)
    same = target_col == target_row
    rank_col = jnp.sum(jnp.where(same & (across < down), 1.0, 0.0), axis=1, keepdims=True)
    rank_row = jnp.sum(jnp.where(same & (down < across), 1.0, 0.0), axis=0, keepdims=True)
    slot_col = target_col * float(plan.chunk) + rank_col
    slot_row = target_row * float(plan.chunk) + rank_row
    permute = jnp.where(slot_col == across.astype(F32), 1.0, 0.0)
    permute_t = jnp.where(slot_row == down.astype(F32), 1.0, 0.0)
    permute_out[...] = permute.astype(BF16)
    permute_t = permute_t.astype(BF16)
    permute_t_out[...] = permute_t
    turn_out[...] = jnp.broadcast_to(column_of(row_of(turning)), (columns, LANES))
    sea_out[...] = jnp.broadcast_to(column_of(row_of(mask).astype(F32)), (columns, LANES))
    keep = 1.0 - drag[...].reshape(1, plan.depth)
    blank = jnp.zeros((1, LANES - 2 * plan.depth), F32)
    keep_out[...] = jnp.broadcast_to(jnp.concatenate([keep, keep, blank], axis=1), (8, LANES))
    flat = currents[...].reshape(columns, 2 * plan.depth)
    ocean = jnp.concatenate([flat, jnp.zeros((columns, LANES - 2 * plan.depth), F32)], axis=1)
    ocean_out[...] = ocean
    coupling = {"stokes": stokes_table, "packed": packed_out}
    send_parts(plan, section, even, waves, ocean, permute_t, coupling, sec_out, lat_out)


def step_kernel(plan, axes, last, *refs):
    waves, ocean_in, packed_in, permute, permute_t, turn, sea, keep, rates, stokes, grow = refs[:11]
    refs = refs[11:]
    count = len(plan.exchanges)
    sec_in, lat_in = refs[:count], refs[count : count + 2]
    refs = refs[count + 2 :]
    waves_out, ocean_out = refs[:2]
    refs = refs[2:]
    if not last:
        packed_out, sec_out, lat_out = refs[0], refs[1 : count + 1], refs[count + 1 : count + 3]
        refs = refs[count + 3 :]
    coupled, factor, west_edge, east_edge = refs
    section, band = lax.axis_index(axes[1]), lax.axis_index(axes[0])
    even = lax.rem(band, 2) == 0
    rows, cols, tiles, chunk = plan.rows, plan.cols, plan.tiles, plan.chunk
    columns = plan.columns

    own = pl.ds(pl.multiple_of(section * chunk, 8), chunk)
    coupled[own, :] = packed_in[own, :]
    west_edge[...] = jnp.zeros_like(west_edge)
    east_edge[...] = jnp.zeros_like(east_edge)
    for number, message in enumerate(sec_in):
        _, source = plan.partner(section, number)
        coupled[pl.ds(pl.multiple_of(source * chunk, 8), chunk), :] = message[0:chunk, :]
        if plan.edges[number]:

            @pl.when(source == section + 1)
            def _():
                east_edge[...] = message[chunk:, :]

            @pl.when(source == section - 1)
            def _():
                west_edge[...] = message[chunk:, :]

    arrived = coupled[...]
    lane = lane_of((columns, LANES))
    high = arrived.astype(BF16).astype(F32)
    halves = jnp.where(lane < LANES // 2, high, pltpu.roll(arrived - high, LANES // 2, 1))
    at_waves = dot(permute[...], halves.astype(BF16)).astype(BF16)
    factor[...] = dot(jnp.concatenate([at_waves, at_waves], axis=1), grow[...])

    near, far = lat_in
    block = (cols, LANES)
    direction = lax.rem(lane_of(block), NDIR)
    eastward = (direction < NDIR // 4) | (direction >= 3 * NDIR // 4)
    northward = direction < NDIR // 2
    first, final = direction == 0, direction == NDIR - 1
    place = lax.broadcasted_iota(jnp.int32, block, 0)
    at_west, at_east = place == 0, place == cols - 1
    for tile in range(tiles):
        lanes = slice(tile * LANES, (tile + 1) * LANES)
        stay, along_x, along_y, gain = (rates[k : k + 1, lanes] for k in range(4))
        south_edge = jnp.where(even, far[:, lanes], near[:, lanes])
        north_edge = jnp.where(even, near[:, lanes], far[:, lanes])
        for row in range(rows):
            flat = slice(row * cols, (row + 1) * cols)
            edge = slice(tile * rows + row, tile * rows + row + 1)
            center = waves[row, :, lanes]
            west = jnp.where(at_west, west_edge[edge, :], pltpu.roll(center, 1, 0))
            east = jnp.where(at_east, east_edge[edge, :], pltpu.roll(center, cols - 1, 0))
            south = waves[row - 1, :, lanes] if row else south_edge
            north = waves[row + 1, :, lanes] if row < rows - 1 else north_edge
            moved = (
                stay * center
                + along_x * jnp.where(eastward, west, east)
                + along_y * jnp.where(northward, south, north)
            )
            behind = jnp.where(
                first, pltpu.roll(moved, LANES - (NDIR - 1), 1), pltpu.roll(moved, 1, 1)
            )
            forward = jnp.where(
                final, pltpu.roll(moved, NDIR - 1, 1), pltpu.roll(moved, LANES - 1, 1)
            )
            rate = turn[flat, :]
            turned = moved - jnp.abs(rate) * gain * (moved - jnp.where(rate > 0.0, behind, forward))
            waves_out[row, :, lanes] = turned * (1.0 + factor[flat, lanes]) * sea[flat, :]

    half = plan.depth
    span = 2 * half
    side = lane_of(block)
    zonal = side < half

    def swapped(value):
        return jnp.where(zonal, pltpu.roll(value, LANES - half, 1), pltpu.roll(value, half, 1))

    wave_lanes = slice(plan.spectral, plan.spectral + LANES)
    south_edge = jnp.where(even, far[:, wave_lanes], near[:, wave_lanes])
    north_edge = jnp.where(even, near[:, wave_lanes], far[:, wave_lanes])
    new_ocean = []
    for row in range(rows):
        flat = slice(row * cols, (row + 1) * cols)
        edge = slice(tiles * rows + row, tiles * rows + row + 1)
        center = ocean_in[flat, :]
        west = jnp.where(at_west, west_edge[edge, :], pltpu.roll(center, 1, 0))
        east = jnp.where(at_east, east_edge[edge, :], pltpu.roll(center, cols - 1, 0))
        south = ocean_in[(row - 1) * cols : row * cols, :] if row else south_edge
        north = (
            ocean_in[(row + 1) * cols : (row + 2) * cols, :] if row < rows - 1 else north_edge
        )
        shear = 0.5 * jnp.where(zonal, south - north, east - west)
        shear = shear + swapped(shear)
        y = (band * rows + row).astype(F32)
        spin = 0.2 + 0.6 * y / float(plan.bands * rows) + shear
        pushed = swapped(center + pltpu.roll(coupled[flat, :], LANES // 2, 1))
        turn_by = ocean_dt * spin * pushed
        new = keep[0:1, :] * (center + jnp.where(zonal, turn_by, -turn_by)) * sea[flat, :]
        if last:
            ocean_out[row] = new[:, :span]
        else:
            ocean_out[flat, :] = new
            new_ocean.append(new)
    if not last:
        coupling = {"stokes": stokes, "packed": packed_out}
        send_parts(
            plan,
            section,
            even,
            waves_out,
            jnp.concatenate(new_ocean, axis=0),
            permute_t[...],
            coupling,
            sec_out,
            lat_out,
        )


def per_device(plan, axes, spectra, turning, currents, drag_rates, land_mask, ocean_target):
    rates, stokes, grow = (
        jnp.asarray(table) for table in build_tables(NFREQ, NDIR, drag_rates.shape[0])
    )
    columns = plan.columns
    shape = jax.ShapeDtypeStruct
    params = pltpu.CompilerParams(vmem_limit_bytes=32 * 1024 * 1024)
    messages = [shape((rows, LANES), F32) for rows in plan.sec_rows] + [
        shape((plan.cols, plan.spectral + LANES), F32)
    ] * 2
    state = shape((columns, LANES), F32)

    def call(kernel, outs, scratch, *args):
        return pl.pallas_call(
            kernel,
            out_shape=outs,
            in_specs=[VMEM] * len(args),
            out_specs=[VMEM] * len(outs),
            scratch_shapes=scratch,
            compiler_params=params,
        )(*args)

    def exchange(sent):
        count = plan.sections
        near = [(i, i ^ 1) for i in range(plan.bands) if i ^ 1 < plan.bands]
        far = [(i, ((i + 1) ^ 1) - 1) for i in range(1, plan.bands) if ((i + 1) ^ 1) - 1 < plan.bands]
        got = [
            lax.ppermute(message, axes[1], [(i, table[i]) for i in range(count)])
            for message, table in zip(sent, plan.exchanges)
        ]
        got.append(lax.ppermute(sent[-2], axes[0], near))
        got.append(lax.ppermute(sent[-1], axes[0], far))
        return got

    square = shape((columns, columns), BF16)
    permute, permute_t, turn, sea, keep, ocean, packed, *sent = call(
        functools.partial(first_kernel, plan, axes),
        [square, square, state, state, shape((8, LANES), F32), state, state] + messages,
        [],
        spectra,
        turning,
        currents,
        drag_rates,
        land_mask,
        ocean_target,
        stokes,
    )
    waves = spectra
    edge = pltpu.VMEM((plan.tiles * plan.rows + 8, LANES), F32)
    scratch = [pltpu.VMEM((columns, LANES), F32), pltpu.VMEM((columns, plan.spectral), F32), edge, edge]
    for step in range(STEPS):
        last = step == STEPS - 1
        got = exchange(sent)
        outs = [
            shape(spectra.shape, F32),
            shape(currents.shape, F32) if last else state,
        ] + ([] if last else [state] + messages)
        result = call(
            functools.partial(step_kernel, plan, axes, last),
            outs,
            scratch,
            waves,
            ocean,
            packed,
            permute,
            permute_t,
            turn,
            sea,
            keep,
            rates,
            stokes,
            grow,
            *got,
        )
        waves, ocean = result[:2]
        if not last:
            packed, *sent = result[2:]
    return waves, ocean


def solution(mesh):
    sections, bands = mesh.shape["sec"], mesh.shape["lat"]

    def local(spectra, turning, currents, drag_rates, land_mask, ocean_target):
        rows, cols, spectral = spectra.shape
        plan = Plan(sections, bands, rows, cols, spectral, drag_rates.shape[0])
        return per_device(
            plan, ("lat", "sec"), spectra, turning, currents, drag_rates, land_mask, ocean_target
        )

    return jax.shard_map(
        local,
        mesh=mesh,
        in_specs=(
            P("lat", "sec", None),
            P("lat", "sec"),
            P("lat", "sec", None),
            P(),
            P("lat", "sec"),
            P("lat", "sec"),
        ),
        out_specs=(P("lat", "sec", None), P("lat", "sec", None)),
        check_vma=False,
    )
```

```python
import functools
import math

import jax
import jax.numpy as jnp
import ml_dtypes
import numpy as np
from jax import lax
from jax.experimental import pallas as pl
from jax.experimental.pallas import tpu as pltpu
from jax.sharding import PartitionSpec as P

NFREQ = 24
NDIR = 32
STEPS = 3

stokes_scale = 0.1
ocean_dt = 0.3
current_gain = 0.2

LANES = 128
F32 = jnp.float32
BF16 = jnp.bfloat16


def split_halves(table):
    high = table.astype(ml_dtypes.bfloat16)
    low = (table - high.astype(np.float64)).astype(ml_dtypes.bfloat16)
    return high, low


def build_tables(nfreq, ndir, ndepth):
    fraction = np.arange(nfreq) / (nfreq - 1)
    angles = (np.arange(ndir) + 0.5) * (2.0 * math.pi / ndir)
    east_part, north_part = np.cos(angles), np.sin(angles)
    courant = 0.1 + 0.3 * fraction
    depth_level = 0.5 + (ndepth - 2) * (1.0 - fraction)
    weights = np.maximum(1.0 - np.abs(np.arange(ndepth)[None, :] - depth_level[:, None]), 0.0)
    mean_weights = weights / weights.sum(axis=1, keepdims=True)
    x_rate = np.abs(courant[:, None] * east_part[None, :]).reshape(-1)
    y_rate = np.abs(courant[:, None] * north_part[None, :]).reshape(-1)
    turn_gain = np.repeat(1.0 - 0.5 * fraction, ndir)
    rates = np.stack([1.0 - x_rate - y_rate, x_rate, y_rate, turn_gain] * 2).astype(np.float32)
    compass = np.stack([east_part, north_part])
    stokes = (stokes_scale * weights[:, None, None, :] * compass.T[None, :, :, None]).reshape(
        nfreq * ndir, 2 * ndepth
    )
    growth = current_gain * (1.0 + fraction)
    grow = (
        growth[None, None, :, None] * mean_weights.T[None, :, :, None] * compass[:, None, None, :]
    ).reshape(2 * ndepth, nfreq * ndir)
    stokes_high, stokes_low = split_halves(stokes)
    grow_high, grow_low = split_halves(grow)
    return (
        np.concatenate([stokes_high, stokes_low], axis=1),
        rates,
        np.concatenate([grow_high, grow_high, grow_low, grow_low], axis=0)
        .reshape(8 * ndepth, -1, LANES)
        .transpose(1, 0, 2)
        .reshape(-1, LANES),
    )


def sec_exchanges(count):
    if count % 4 == 0:
        far = count // 4
        return [
            [((i // 4 + hop) % far) * 4 + ((i % 4) ^ flip) for i in range(count)]
            for hop in range(far)
            for flip in range(4)
            if hop or flip
        ]
    return [[(i + hop) % count for i in range(count)] for hop in range(1, count)]


class Plan:
    def __init__(self, sections, bands, rows, cols, spectral, depth):
        self.sections, self.bands = sections, bands
        self.rows, self.cols, self.spectral, self.depth = rows, cols, spectral, depth
        self.columns = rows * cols
        self.chunk = self.columns // sections
        self.tiles = spectral // LANES
        self.exchanges = sec_exchanges(sections)
        self.edges = [
            any(abs(target - i) == 1 for i, target in enumerate(table)) for table in self.exchanges
        ]
        self.sec_rows = [
            self.chunk + (self.tiles * rows + 8 if edge else 0) for edge in self.edges
        ]

    def partner(self, section, number):
        if self.sections % 4 == 0:
            far = self.sections // 4
            hop, flip = divmod(number + 1, 4)
            high, low = lax.div(section, 4), lax.rem(section, 4)
            flipped = low
            if flip & 1:
                flipped = flipped + 1 - 2 * lax.rem(flipped, 2)
            if flip & 2:
                flipped = flipped + 2 - 4 * lax.div(flipped, 2)
            return (
                lax.rem(high + hop, far) * 4 + flipped,
                lax.rem(high + far - hop, far) * 4 + flipped,
            )
        hop = number + 1
        return (
            lax.rem(section + hop, self.sections),
            lax.rem(section + self.sections - hop, self.sections),
        )


def lane_of(shape):
    return lax.broadcasted_iota(jnp.int32, shape, len(shape) - 1)


def dot(a, b):
    return jnp.dot(a, b, preferred_element_type=F32)


def split_value(value):
    high = value.astype(BF16).astype(F32)
    return jnp.where(lane_of(value.shape) < LANES // 2, high, value - high).astype(BF16)


def stokes_product(part, table):
    high = part.astype(BF16)
    low = (part - high.astype(F32)).astype(BF16)
    return dot(jnp.concatenate([high, low], axis=0), table)


def send_parts(plan, section, even, waves, ocean, total, permute_t, packed_out, sec_out, lat_out):
    chunk, tiles, rows, cols = plan.chunk, plan.tiles, plan.rows, plan.cols
    lane = lane_of((plan.columns, LANES))
    near, far = lat_out
    sea_rows = ocean.reshape(rows, cols, LANES)
    low_half = lax.rem(lane_of((cols, LANES)), NDIR) < NDIR // 2
    for out, northward in ((far, jnp.logical_not(even)), (near, even)):
        edge = jnp.where(northward, waves[rows - 1], waves[0])
        for tile in range(tiles // 2):
            first = edge[:, tile * LANES : (tile + 1) * LANES]
            second = edge[:, (tile + tiles // 2) * LANES : (tile + tiles // 2 + 1) * LANES]
            up = jnp.where(low_half, first, pltpu.roll(second, NDIR // 2, 1))
            down = jnp.where(low_half, pltpu.roll(second, LANES - NDIR // 2, 1), first)
            out[:, tile * LANES : (tile + 1) * LANES] = jnp.where(northward, up, down)
        out[:, plan.spectral // 2 :] = jnp.where(northward, sea_rows[rows - 1], sea_rows[0])
    moments = total[: plan.columns] + total[plan.columns :]
    moments = moments + pltpu.roll(moments, LANES // 2, 1)
    ordered = dot(permute_t, split_value(moments))
    ordered = ordered + pltpu.roll(ordered, LANES // 2, 1)
    packed_out[...] = jnp.where(lane < LANES // 2, ocean, ordered)
    for number, out in enumerate(sec_out):
        target, _ = plan.partner(section, number)
        out[0:chunk, :] = packed_out[pl.ds(pl.multiple_of(target * chunk, 8), chunk), :]
        if not plan.edges[number]:
            continue
        eastward = target == section + 1
        for row in range(rows):
            edge = jnp.where(eastward, waves[row, cols - 1 : cols, :], waves[row, 0:1, :])
            for tile in range(tiles):
                place = chunk + tile * rows + row
                out[place : place + 1, :] = edge[:, tile * LANES : (tile + 1) * LANES]
            place = chunk + tiles * rows + row
            out[place : place + 1, :] = jnp.where(
                eastward, sea_rows[row, cols - 1 : cols, :], sea_rows[row, 0:1, :]
            )


def first_kernel(plan, axes, *refs):
    waves_in, turning_in, currents_in, drag_in, mask_in, target_in = refs[:6]
    tables_in, refs = refs[6:9], refs[9:]
    waves, ocean_out, permute_out, permute_t_out, turn_out, sea_out, keep_out = refs[:7]
    tables_out, packed_out, refs = refs[7:10], refs[10], refs[11:]
    count = len(plan.exchanges)
    sec_out, lat_out, refs = refs[:count], refs[count : count + 2], refs[count + 2 :]
    turning, currents, drag, mask, target, done = refs
    pairs = [
        (target_in, target),
        (turning_in, turning),
        (mask_in, mask),
        (drag_in, drag),
        (waves_in, waves),
        (tables_in[0], tables_out[0]),
        (currents_in, currents),
        (tables_in[1], tables_out[1]),
        (tables_in[2], tables_out[2]),
    ]
    copies = [pltpu.make_async_copy(a, b, done.at[k]) for k, (a, b) in enumerate(pairs)]
    for copy in copies:
        copy.start()
    section, band = lax.axis_index(axes[1]), lax.axis_index(axes[0])
    even = lax.rem(band, 2) == 0
    columns, rows = plan.columns, plan.rows
    across = lane_of((columns, columns))
    down = lax.broadcasted_iota(jnp.int32, (columns, columns), 0)
    here = across == down

    def row_of(ref):
        return jnp.concatenate([ref[row : row + 1, :] for row in range(rows)], axis=1)

    def column_of(row):
        spread = jnp.broadcast_to(row, (columns, columns))
        return jnp.sum(jnp.where(here, spread, jnp.zeros_like(spread)), axis=1, keepdims=True)

    for copy in copies[:4]:
        copy.wait()
    sea = column_of(row_of(mask).astype(F32))
    target_row = row_of(target).astype(F32)
    target_col = column_of(target_row)
    same = target_col == target_row
    rank_col = jnp.sum(jnp.where(same & (across < down), 1.0, 0.0), axis=1, keepdims=True)
    rank_row = jnp.sum(jnp.where(same & (down < across), 1.0, 0.0), axis=0, keepdims=True)
    slot_col = target_col * float(plan.chunk) + rank_col
    slot_row = target_row * float(plan.chunk) + rank_row
    permute_out[...] = jnp.where(slot_col == across.astype(F32), sea, 0.0).astype(BF16)
    permute_t = jnp.where(slot_row == down.astype(F32), 1.0, 0.0).astype(BF16)
    permute_t_out[...] = permute_t
    turn_out[...] = jnp.broadcast_to(column_of(row_of(turning)), (columns, LANES))
    sea_out[...] = jnp.broadcast_to(sea, (columns, LANES))
    keep = 1.0 - drag[...].reshape(1, plan.depth)
    blank = jnp.zeros((1, LANES - 2 * plan.depth), F32)
    keep_out[...] = jnp.broadcast_to(jnp.concatenate([keep, keep, blank], axis=1), (8, LANES))
    for copy in copies[4:7]:
        copy.wait()
    flat = currents[...].reshape(columns, 2 * plan.depth)
    ocean = jnp.concatenate([flat, jnp.zeros((columns, LANES - 2 * plan.depth), F32)], axis=1)
    ocean_out[...] = ocean
    total = None
    for start in range(0, plan.spectral, 256):
        part = waves[:, :, start : start + 256].reshape(columns, 256)
        product = stokes_product(part, tables_out[0][start : start + 256, :])
        total = product if total is None else total + product
    send_parts(
        plan, section, even, waves, ocean, total, permute_t, packed_out, sec_out, lat_out
    )
    for copy in copies[7:]:
        copy.wait()


def move_kernel(plan, axes, *refs):
    waves, ocean, turn, rates = refs[:4]
    edge_numbers = [number for number, edge in enumerate(plan.edges) if edge]
    sec_in, refs = refs[4 : 4 + len(edge_numbers)], refs[4 + len(edge_numbers) :]
    near, far, turned_out, spin_out, west_edge, east_edge = refs
    section, band = lax.axis_index(axes[1]), lax.axis_index(axes[0])
    even = lax.rem(band, 2) == 0
    rows, cols, tiles, chunk = plan.rows, plan.cols, plan.tiles, plan.chunk

    west_edge[...] = jnp.zeros_like(west_edge)
    east_edge[...] = jnp.zeros_like(east_edge)
    for number, message in zip(edge_numbers, sec_in):
        _, source = plan.partner(section, number)

        @pl.when(source == section + 1)
        def _():
            east_edge[...] = message[chunk:, :]

        @pl.when(source == section - 1)
        def _():
            west_edge[...] = message[chunk:, :]

    block = (cols, LANES)
    direction = lax.rem(lane_of(block), NDIR)
    eastward = (direction < NDIR // 4) | (direction >= 3 * NDIR // 4)
    northward = direction < NDIR // 2
    first, final = direction == 0, direction == NDIR - 1
    place = lax.broadcasted_iota(jnp.int32, block, 0)
    at_west, at_east = place == 0, place == cols - 1
    for tile in range(tiles):
        lanes = slice(tile * LANES, (tile + 1) * LANES)
        stay, along_x, along_y, gain = (rates[k : k + 1, lanes] for k in range(4))
        half = tile % (tiles // 2)
        half = slice(half * LANES, (half + 1) * LANES)
        south_edge = jnp.where(even, far[:, half], near[:, half])
        north_edge = jnp.where(even, near[:, half], far[:, half])
        if tile >= tiles // 2:
            south_edge = pltpu.roll(south_edge, LANES - NDIR // 2, 1)
            north_edge = pltpu.roll(north_edge, NDIR // 2, 1)
        for row in range(rows):
            edge = slice(tile * rows + row, tile * rows + row + 1)
            center = waves[row, :, lanes]
            west = jnp.where(at_west, west_edge[edge, :], pltpu.roll(center, 1, 0))
            east = jnp.where(at_east, east_edge[edge, :], pltpu.roll(center, cols - 1, 0))
            south = waves[row - 1, :, lanes] if row else south_edge
            north = waves[row + 1, :, lanes] if row < rows - 1 else north_edge
            moved = (
                stay * center
                + along_x * jnp.where(eastward, west, east)
                + along_y * jnp.where(northward, south, north)
            )
            behind = jnp.where(
                first, pltpu.roll(moved, LANES - (NDIR - 1), 1), pltpu.roll(moved, 1, 1)
            )
            forward = jnp.where(
                final, pltpu.roll(moved, NDIR - 1, 1), pltpu.roll(moved, LANES - 1, 1)
            )
            rate = turn[row * cols : (row + 1) * cols, :]
            turned_out[row, :, lanes] = moved - jnp.abs(rate) * gain * (
                moved - jnp.where(rate > 0.0, behind, forward)
            )

    zonal = lane_of(block) < plan.depth
    half = slice(plan.spectral // 2, plan.spectral // 2 + LANES)
    south_edge = jnp.where(even, far[:, half], near[:, half])
    north_edge = jnp.where(even, near[:, half], far[:, half])
    for row in range(rows):
        flat = slice(row * cols, (row + 1) * cols)
        edge = slice(tiles * rows + row, tiles * rows + row + 1)
        center = ocean[flat, :]
        west = jnp.where(at_west, west_edge[edge, :], pltpu.roll(center, 1, 0))
        east = jnp.where(at_east, east_edge[edge, :], pltpu.roll(center, cols - 1, 0))
        south = ocean[(row - 1) * cols : row * cols, :] if row else south_edge
        north = ocean[(row + 1) * cols : (row + 2) * cols, :] if row < rows - 1 else north_edge
        shear = 0.5 * jnp.where(zonal, south - north, east - west)
        shear = shear + swapped(plan, shear)
        y = (band * rows + row).astype(F32)
        spin_out[flat, :] = 0.2 + 0.6 * y / float(plan.bands * rows) + shear


def swapped(plan, value):
    half = plan.depth
    zonal = lane_of(value.shape) < half
    return jnp.where(zonal, pltpu.roll(value, LANES - half, 1), pltpu.roll(value, half, 1))


def couple_kernel(plan, axes, last, *refs):
    turned, spin, ocean_in, packed_in, permute, permute_t, sea, keep, stokes, grow = refs[:10]
    refs = refs[10:]
    count = len(plan.exchanges)
    sec_in, refs = refs[:count], refs[count:]
    if last:
        waves_far, ocean_far, coupled, waves_out, ocean_out, done = refs
    else:
        waves_out, ocean_out, packed_out = refs[:3]
        sec_out, lat_out, coupled = refs[3 : count + 3], refs[count + 3 : count + 5], refs[-1]
    section, band = lax.axis_index(axes[1]), lax.axis_index(axes[0])
    even = lax.rem(band, 2) == 0
    rows, cols, chunk, columns = plan.rows, plan.cols, plan.chunk, plan.columns

    own = pl.ds(pl.multiple_of(section * chunk, 8), chunk)
    coupled[own, :] = packed_in[own, :]
    for number, message in enumerate(sec_in):
        _, source = plan.partner(section, number)
        coupled[pl.ds(pl.multiple_of(source * chunk, 8), chunk), :] = message[0:chunk, :]
    arrived = coupled[...]
    other = pltpu.roll(arrived, LANES // 2, 1)
    lane = lane_of((columns, LANES))
    both = jnp.where(lane < LANES // 2, arrived, other)
    at_waves = dot(permute[...], split_value(both)).astype(BF16)
    at_waves = jnp.concatenate([at_waves, at_waves], axis=1)

    pushed = swapped(plan, ocean_in[...] + other)
    turn_by = ocean_dt * spin[...] * pushed
    new = keep[0:1, :] * (ocean_in[...] + jnp.where(lane < plan.depth, turn_by, -turn_by)) * sea[...]
    if last:
        ocean_out[...] = new[:, : 2 * plan.depth].reshape(rows, cols, 2 * plan.depth)
        copies = [pltpu.make_async_copy(ocean_out, ocean_far, done.at[0])]
        copies[0].start()
    else:
        ocean_out[...] = new

    total = None
    wet = jnp.concatenate([sea[...], sea[...]], axis=1)
    for number, start in enumerate(range(0, plan.spectral, 256)):
        lanes = slice(start, start + 256)
        table = jnp.concatenate(
            [grow[(2 * number + k) * 256 : (2 * number + k + 1) * 256, :] for k in range(2)], axis=1
        )
        grown = turned[:, :, lanes].reshape(columns, 256) * (wet + dot(at_waves, table))
        waves_out[:, :, lanes] = grown.reshape(rows, cols, 256)
        if last:
            copy = pltpu.make_async_copy(
                waves_out.at[:, :, lanes], waves_far.at[:, :, lanes], done.at[number + 1]
            )
            copy.start()
            copies.append(copy)
        else:
            product = stokes_product(grown, stokes[lanes, :])
            total = product if total is None else total + product
    if last:
        for copy in copies:
            copy.wait()
        return
    send_parts(
        plan, section, even, waves_out, new, total, permute_t[...], packed_out, sec_out, lat_out
    )


def per_device(plan, axes, spectra, turning, currents, drag_rates, land_mask, ocean_target):
    tables = [jnp.asarray(table) for table in build_tables(NFREQ, NDIR, drag_rates.shape[0])]
    columns, rows, cols, spectral = plan.columns, plan.rows, plan.cols, plan.spectral
    shape = jax.ShapeDtypeStruct
    params = pltpu.CompilerParams(vmem_limit_bytes=32 * 1024 * 1024)
    messages = [shape((size, LANES), F32) for size in plan.sec_rows] + [
        shape((cols, spectral // 2 + LANES), F32)
    ] * 2
    state = shape((columns, LANES), F32)
    field = shape(spectra.shape, F32)
    square = shape((columns, columns), BF16)
    edge = pltpu.VMEM((plan.tiles * rows + 8, LANES), F32)
    coupled = pltpu.VMEM((columns, LANES), F32)
    spans = spectral // 256

    def call(kernel, outs, scratch, *args, space_in=pltpu.VMEM, space_out=pltpu.VMEM):
        return pl.pallas_call(
            kernel,
            out_shape=outs,
            in_specs=[pl.BlockSpec(memory_space=space_in)] * len(args),
            out_specs=[pl.BlockSpec(memory_space=space_out)] * len(outs),
            scratch_shapes=scratch,
            compiler_params=params,
        )(*args)

    def exchange(sent):
        near = [(i, i ^ 1) for i in range(plan.bands) if i ^ 1 < plan.bands]
        far = [(i, ((i + 1) ^ 1) - 1) for i in range(1, plan.bands) if ((i + 1) ^ 1) - 1 < plan.bands]
        got = [
            lax.ppermute(message, axes[1], list(enumerate(table)))
            for message, table in zip(sent, plan.exchanges)
        ]
        return got, lax.ppermute(sent[-2], axes[0], near), lax.ppermute(sent[-1], axes[0], far)

    waves, ocean, permute, permute_t, turn, sea, keep, stokes, rates, grow, packed, *sent = call(
        functools.partial(first_kernel, plan, axes),
        [field, state, square, square, state, state, shape((8, LANES), F32)]
        + [shape(table.shape, table.dtype) for table in tables]
        + [state]
        + messages,
        [
            pltpu.VMEM(turning.shape, F32),
            pltpu.VMEM(currents.shape, F32),
            pltpu.VMEM(drag_rates.shape, F32),
            pltpu.VMEM(land_mask.shape, jnp.int32),
            pltpu.VMEM(ocean_target.shape, jnp.int32),
            pltpu.SemaphoreType.DMA((9,)),
        ],
        spectra,
        turning,
        currents,
        drag_rates,
        land_mask,
        ocean_target,
        *tables,
        space_in=pltpu.HBM,
    )
    for step in range(STEPS):
        last = step == STEPS - 1
        got, near, far = exchange(sent)
        turned, spin = call(
            functools.partial(move_kernel, plan, axes),
            [field, state],
            [edge, edge],
            waves,
            ocean,
            turn,
            rates,
            *[message for message, edged in zip(got, plan.edges) if edged],
            near,
            far,
        )
        result = call(
            functools.partial(couple_kernel, plan, axes, last),
            [field, shape(currents.shape, F32)] if last else [field, state, state] + messages,
            [
                coupled,
                pltpu.VMEM(spectra.shape, F32),
                pltpu.VMEM(currents.shape, F32),
                pltpu.SemaphoreType.DMA((1 + spans,)),
            ]
            if last
            else [coupled],
            turned,
            spin,
            ocean,
            packed,
            permute,
            permute_t,
            sea,
            keep,
            stokes,
            grow,
            *got,
            space_out=pltpu.HBM if last else pltpu.VMEM,
        )
        waves, ocean = result[:2]
        if not last:
            packed, *sent = result[2:]
    return waves, ocean


def solution(mesh):
    sections, bands = mesh.shape["sec"], mesh.shape["lat"]

    def local(spectra, turning, currents, drag_rates, land_mask, ocean_target):
        rows, cols, spectral = spectra.shape
        plan = Plan(sections, bands, rows, cols, spectral, drag_rates.shape[0])
        return per_device(
            plan, ("lat", "sec"), spectra, turning, currents, drag_rates, land_mask, ocean_target
        )

    return jax.shard_map(
        local,
        mesh=mesh,
        in_specs=(
            P("lat", "sec", None),
            P("lat", "sec"),
            P("lat", "sec", None),
            P(),
            P("lat", "sec"),
            P("lat", "sec"),
        ),
        out_specs=(P("lat", "sec", None), P("lat", "sec", None)),
        check_vma=False,
    )
```

```python
import functools
import math

import jax
import jax.numpy as jnp
import ml_dtypes
import numpy as np
from jax import lax
from jax.experimental import pallas as pl
from jax.experimental.pallas import tpu as pltpu
from jax.sharding import PartitionSpec as P

NFREQ = 24
NDIR = 32
STEPS = 3

stokes_scale = 0.1
ocean_dt = 0.3
current_gain = 0.2

LANES = 128
F32 = jnp.float32
BF16 = jnp.bfloat16


def split_halves(table):
    high = table.astype(ml_dtypes.bfloat16)
    low = (table - high.astype(np.float64)).astype(ml_dtypes.bfloat16)
    return high, low


def build_tables(nfreq, ndir, ndepth):
    fraction = np.arange(nfreq) / (nfreq - 1)
    angles = (np.arange(ndir) + 0.5) * (2.0 * math.pi / ndir)
    east_part, north_part = np.cos(angles), np.sin(angles)
    courant = 0.1 + 0.3 * fraction
    depth_level = 0.5 + (ndepth - 2) * (1.0 - fraction)
    weights = np.maximum(1.0 - np.abs(np.arange(ndepth)[None, :] - depth_level[:, None]), 0.0)
    mean_weights = weights / weights.sum(axis=1, keepdims=True)
    x_rate = np.abs(courant[:, None] * east_part[None, :]).reshape(-1)
    y_rate = np.abs(courant[:, None] * north_part[None, :]).reshape(-1)
    turn_gain = np.repeat(1.0 - 0.5 * fraction, ndir)
    rates = np.stack([1.0 - x_rate - y_rate, x_rate, y_rate, turn_gain] * 2).astype(np.float32)
    compass = np.stack([east_part, north_part])
    stokes = (stokes_scale * weights[:, None, None, :] * compass.T[None, :, :, None]).reshape(
        nfreq * ndir, 2 * ndepth
    )
    growth = current_gain * (1.0 + fraction)
    grow = (
        growth[None, None, :, None] * mean_weights.T[None, :, :, None] * compass[:, None, None, :]
    ).reshape(2 * ndepth, nfreq * ndir)
    stokes_high, stokes_low = split_halves(stokes)
    grow_high, grow_low = split_halves(grow)
    return (
        np.concatenate([stokes_high, stokes_low], axis=1),
        rates,
        np.concatenate([grow_high, grow_high, grow_low, grow_low], axis=0)
        .reshape(8 * ndepth, -1, LANES)
        .transpose(1, 0, 2)
        .reshape(-1, LANES),
    )


def sec_exchanges(count):
    if count % 4 == 0:
        far = count // 4
        return [
            [((i // 4 + hop) % far) * 4 + ((i % 4) ^ flip) for i in range(count)]
            for hop in range(far)
            for flip in range(4)
            if hop or flip
        ]
    return [[(i + hop) % count for i in range(count)] for hop in range(1, count)]


class Plan:
    def __init__(self, sections, bands, rows, cols, spectral, depth):
        self.sections, self.bands = sections, bands
        self.rows, self.cols, self.spectral, self.depth = rows, cols, spectral, depth
        self.columns = rows * cols
        self.chunk = self.columns // sections
        self.tiles = spectral // LANES
        self.exchanges = sec_exchanges(sections)
        self.edges = [
            any(abs(target - i) == 1 for i, target in enumerate(table)) for table in self.exchanges
        ]
        self.sec_rows = [
            self.chunk + (self.tiles * rows + 8 if edge else 0) for edge in self.edges
        ]

    def partner(self, section, number):
        if self.sections % 4 == 0:
            far = self.sections // 4
            hop, flip = divmod(number + 1, 4)
            high, low = lax.div(section, 4), lax.rem(section, 4)
            flipped = low
            if flip & 1:
                flipped = flipped + 1 - 2 * lax.rem(flipped, 2)
            if flip & 2:
                flipped = flipped + 2 - 4 * lax.div(flipped, 2)
            return (
                lax.rem(high + hop, far) * 4 + flipped,
                lax.rem(high + far - hop, far) * 4 + flipped,
            )
        hop = number + 1
        return (
            lax.rem(section + hop, self.sections),
            lax.rem(section + self.sections - hop, self.sections),
        )


def lane_of(shape):
    return lax.broadcasted_iota(jnp.int32, shape, len(shape) - 1)


def dot(a, b):
    return jnp.dot(a, b, preferred_element_type=F32)


def split_value(value):
    high = value.astype(BF16).astype(F32)
    return jnp.where(lane_of(value.shape) < LANES // 2, high, value - high).astype(BF16)


def stokes_product(part, table):
    high = part.astype(BF16)
    low = (part - high.astype(F32)).astype(BF16)
    return dot(jnp.concatenate([high, low], axis=0), table)


def send_parts(plan, section, even, waves, ocean, total, permute_t, packed_out, sec_out, lat_out):
    chunk, tiles, rows, cols = plan.chunk, plan.tiles, plan.rows, plan.cols
    lane = lane_of((plan.columns, LANES))
    near, far = lat_out
    sea_rows = ocean.reshape(rows, cols, LANES)
    low_half = lax.rem(lane_of((cols, LANES)), NDIR) < NDIR // 2
    for out, northward in ((far, jnp.logical_not(even)), (near, even)):
        edge = jnp.where(northward, waves[rows - 1], waves[0])
        for tile in range(tiles // 2):
            first = edge[:, tile * LANES : (tile + 1) * LANES]
            second = edge[:, (tile + tiles // 2) * LANES : (tile + tiles // 2 + 1) * LANES]
            up = jnp.where(low_half, first, pltpu.roll(second, NDIR // 2, 1))
            down = jnp.where(low_half, pltpu.roll(second, LANES - NDIR // 2, 1), first)
            out[:, tile * LANES : (tile + 1) * LANES] = jnp.where(northward, up, down)
        out[:, plan.spectral // 2 :] = jnp.where(northward, sea_rows[rows - 1], sea_rows[0])
    moments = total[: plan.columns] + total[plan.columns :]
    moments = moments + pltpu.roll(moments, LANES // 2, 1)
    ordered = dot(permute_t, split_value(moments))
    ordered = ordered + pltpu.roll(ordered, LANES // 2, 1)
    packed_out[...] = jnp.where(lane < LANES // 2, ocean, ordered)
    for number, out in enumerate(sec_out):
        target, _ = plan.partner(section, number)
        out[0:chunk, :] = packed_out[pl.ds(pl.multiple_of(target * chunk, 8), chunk), :]
        if not plan.edges[number]:
            continue
        eastward = target == section + 1
        for row in range(rows):
            edge = jnp.where(eastward, waves[row, cols - 1 : cols, :], waves[row, 0:1, :])
            for tile in range(tiles):
                place = chunk + tile * rows + row
                out[place : place + 1, :] = edge[:, tile * LANES : (tile + 1) * LANES]
            place = chunk + tiles * rows + row
            out[place : place + 1, :] = jnp.where(
                eastward, sea_rows[row, cols - 1 : cols, :], sea_rows[row, 0:1, :]
            )


def first_kernel(plan, axes, *refs):
    waves_in, turning_in, currents_in, drag_in, mask_in, target_in = refs[:6]
    tables_in, refs = refs[6:9], refs[9:]
    waves, ocean_out, permute_out, permute_t_out, turn_out, sea_out, keep_out = refs[:7]
    tables_out, packed_out, refs = refs[7:10], refs[10], refs[11:]
    count = len(plan.exchanges)
    sec_out, lat_out, refs = refs[:count], refs[count : count + 2], refs[count + 2 :]
    turning, currents, drag, mask, target, done = refs
    pairs = [
        (target_in, target),
        (turning_in, turning),
        (mask_in, mask),
        (drag_in, drag),
        (waves_in, waves),
        (tables_in[0], tables_out[0]),
        (currents_in, currents),
        (tables_in[1], tables_out[1]),
        (tables_in[2], tables_out[2]),
    ]
    copies = [pltpu.make_async_copy(a, b, done.at[k]) for k, (a, b) in enumerate(pairs)]
    for copy in copies:
        copy.start()
    section, band = lax.axis_index(axes[1]), lax.axis_index(axes[0])
    even = lax.rem(band, 2) == 0
    columns, rows = plan.columns, plan.rows
    across = lane_of((columns, columns))
    down = lax.broadcasted_iota(jnp.int32, (columns, columns), 0)
    here = across == down

    def row_of(ref):
        return jnp.concatenate([ref[row : row + 1, :] for row in range(rows)], axis=1)

    def column_of(row):
        spread = jnp.broadcast_to(row, (columns, columns))
        return jnp.sum(jnp.where(here, spread, jnp.zeros_like(spread)), axis=1, keepdims=True)

    for copy in copies[:4]:
        copy.wait()
    sea = column_of(row_of(mask).astype(F32))
    target_row = row_of(target).astype(F32)
    target_col = column_of(target_row)
    same = target_col == target_row
    rank_col = jnp.sum(jnp.where(same & (across < down), 1.0, 0.0), axis=1, keepdims=True)
    rank_row = jnp.sum(jnp.where(same & (down < across), 1.0, 0.0), axis=0, keepdims=True)
    slot_col = target_col * float(plan.chunk) + rank_col
    slot_row = target_row * float(plan.chunk) + rank_row
    permute_out[...] = jnp.where(slot_col == across.astype(F32), sea, 0.0).astype(BF16)
    permute_t = jnp.where(slot_row == down.astype(F32), 1.0, 0.0).astype(BF16)
    permute_t_out[...] = permute_t
    turn_out[...] = jnp.broadcast_to(column_of(row_of(turning)), (columns, LANES))
    sea_out[...] = jnp.broadcast_to(sea, (columns, LANES))
    keep = 1.0 - drag[...].reshape(1, plan.depth)
    blank = jnp.zeros((1, LANES - 2 * plan.depth), F32)
    keep_out[...] = jnp.broadcast_to(jnp.concatenate([keep, keep, blank], axis=1), (8, LANES))
    for copy in copies[4:7]:
        copy.wait()
    flat = currents[...].reshape(columns, 2 * plan.depth)
    ocean = jnp.concatenate([flat, jnp.zeros((columns, LANES - 2 * plan.depth), F32)], axis=1)
    ocean_out[...] = ocean
    total = None
    for start in range(0, plan.spectral, 256):
        part = waves[:, :, start : start + 256].reshape(columns, 256)
        product = stokes_product(part, tables_out[0][start : start + 256, :])
        total = product if total is None else total + product
    send_parts(
        plan, section, even, waves, ocean, total, permute_t, packed_out, sec_out, lat_out
    )
    for copy in copies[7:]:
        copy.wait()


def move_kernel(plan, axes, *refs):
    waves, ocean, turn, rates = refs[:4]
    edge_numbers = [number for number, edge in enumerate(plan.edges) if edge]
    sec_in, refs = refs[4 : 4 + len(edge_numbers)], refs[4 + len(edge_numbers) :]
    near, far, turned_out, spin_out, west_edge, east_edge = refs
    section, band = lax.axis_index(axes[1]), lax.axis_index(axes[0])
    even = lax.rem(band, 2) == 0
    rows, cols, tiles, chunk = plan.rows, plan.cols, plan.tiles, plan.chunk

    west_edge[...] = jnp.zeros_like(west_edge)
    east_edge[...] = jnp.zeros_like(east_edge)
    for number, message in zip(edge_numbers, sec_in):
        _, source = plan.partner(section, number)

        @pl.when(source == section + 1)
        def _():
            east_edge[...] = message[chunk:, :]

        @pl.when(source == section - 1)
        def _():
            west_edge[...] = message[chunk:, :]

    block = (cols, LANES)
    direction = lax.rem(lane_of(block), NDIR)
    eastward = (direction < NDIR // 4) | (direction >= 3 * NDIR // 4)
    northward = direction < NDIR // 2
    first, final = direction == 0, direction == NDIR - 1
    place = lax.broadcasted_iota(jnp.int32, block, 0)
    at_west, at_east = place == 0, place == cols - 1
    for tile in range(tiles):
        lanes = slice(tile * LANES, (tile + 1) * LANES)
        stay, along_x, along_y, gain = (rates[k : k + 1, lanes] for k in range(4))
        half = tile % (tiles // 2)
        half = slice(half * LANES, (half + 1) * LANES)
        south_edge = jnp.where(even, far[:, half], near[:, half])
        north_edge = jnp.where(even, near[:, half], far[:, half])
        if tile >= tiles // 2:
            south_edge = pltpu.roll(south_edge, LANES - NDIR // 2, 1)
            north_edge = pltpu.roll(north_edge, NDIR // 2, 1)
        for row in range(rows):
            edge = slice(tile * rows + row, tile * rows + row + 1)
            center = waves[row, :, lanes]
            west = jnp.where(at_west, west_edge[edge, :], pltpu.roll(center, 1, 0))
            east = jnp.where(at_east, east_edge[edge, :], pltpu.roll(center, cols - 1, 0))
            south = waves[row - 1, :, lanes] if row else south_edge
            north = waves[row + 1, :, lanes] if row < rows - 1 else north_edge
            moved = (
                stay * center
                + along_x * jnp.where(eastward, west, east)
                + along_y * jnp.where(northward, south, north)
            )
            behind = jnp.where(
                first, pltpu.roll(moved, LANES - (NDIR - 1), 1), pltpu.roll(moved, 1, 1)
            )
            forward = jnp.where(
                final, pltpu.roll(moved, NDIR - 1, 1), pltpu.roll(moved, LANES - 1, 1)
            )
            rate = turn[row * cols : (row + 1) * cols, :]
            turned_out[row, :, lanes] = moved - jnp.abs(rate) * gain * (
                moved - jnp.where(rate > 0.0, behind, forward)
            )

    zonal = lane_of(block) < plan.depth
    half = slice(plan.spectral // 2, plan.spectral // 2 + LANES)
    south_edge = jnp.where(even, far[:, half], near[:, half])
    north_edge = jnp.where(even, near[:, half], far[:, half])
    for row in range(rows):
        flat = slice(row * cols, (row + 1) * cols)
        edge = slice(tiles * rows + row, tiles * rows + row + 1)
        center = ocean[flat, :]
        west = jnp.where(at_west, west_edge[edge, :], pltpu.roll(center, 1, 0))
        east = jnp.where(at_east, east_edge[edge, :], pltpu.roll(center, cols - 1, 0))
        south = ocean[(row - 1) * cols : row * cols, :] if row else south_edge
        north = ocean[(row + 1) * cols : (row + 2) * cols, :] if row < rows - 1 else north_edge
        shear = 0.5 * jnp.where(zonal, south - north, east - west)
        shear = shear + swapped(plan, shear)
        y = (band * rows + row).astype(F32)
        spin_out[flat, :] = 0.2 + 0.6 * y / float(plan.bands * rows) + shear


def swapped(plan, value):
    half = plan.depth
    zonal = lane_of(value.shape) < half
    return jnp.where(zonal, pltpu.roll(value, LANES - half, 1), pltpu.roll(value, half, 1))


def couple_kernel(plan, axes, last, *refs):
    turned, spin, ocean_in, packed_in, permute, permute_t, sea, keep, stokes, grow = refs[:10]
    refs = refs[10:]
    count = len(plan.exchanges)
    sec_in, refs = refs[:count], refs[count:]
    if last:
        waves_far, ocean_far, coupled, waves_out, ocean_out, done = refs
    else:
        waves_out, ocean_out, packed_out = refs[:3]
        sec_out, lat_out, coupled = refs[3 : count + 3], refs[count + 3 : count + 5], refs[-1]
    section, band = lax.axis_index(axes[1]), lax.axis_index(axes[0])
    even = lax.rem(band, 2) == 0
    rows, cols, chunk, columns = plan.rows, plan.cols, plan.chunk, plan.columns

    own = pl.ds(pl.multiple_of(section * chunk, 8), chunk)
    coupled[own, :] = packed_in[own, :]
    for number, message in enumerate(sec_in):
        _, source = plan.partner(section, number)
        coupled[pl.ds(pl.multiple_of(source * chunk, 8), chunk), :] = message[0:chunk, :]
    arrived = coupled[...]
    other = pltpu.roll(arrived, LANES // 2, 1)
    lane = lane_of((columns, LANES))
    both = jnp.where(lane < LANES // 2, arrived, other)
    at_waves = dot(permute[...], split_value(both)).astype(BF16)
    at_waves = jnp.concatenate([at_waves, at_waves], axis=1)

    pushed = swapped(plan, ocean_in[...] + other)
    turn_by = ocean_dt * spin[...] * pushed
    new = keep[0:1, :] * (ocean_in[...] + jnp.where(lane < plan.depth, turn_by, -turn_by)) * sea[...]
    if last:
        ocean_out[...] = new[:, : 2 * plan.depth].reshape(rows, cols, 2 * plan.depth)
        copies = [pltpu.make_async_copy(ocean_out, ocean_far, done.at[0])]
        copies[0].start()
    else:
        ocean_out[...] = new

    total = None
    wet = jnp.concatenate([sea[...], sea[...]], axis=1)
    for number, start in enumerate(range(0, plan.spectral, 256)):
        lanes = slice(start, start + 256)
        table = jnp.concatenate(
            [grow[(2 * number + k) * 256 : (2 * number + k + 1) * 256, :] for k in range(2)], axis=1
        )
        grown = turned[:, :, lanes].reshape(columns, 256) * (wet + dot(at_waves, table))
        waves_out[:, :, lanes] = grown.reshape(rows, cols, 256)
        if last:
            copy = pltpu.make_async_copy(
                waves_out.at[:, :, lanes], waves_far.at[:, :, lanes], done.at[number + 1]
            )
            copy.start()
            copies.append(copy)
        else:
            product = stokes_product(grown, stokes[lanes, :])
            total = product if total is None else total + product
    if last:
        for copy in copies:
            copy.wait()
        return
    send_parts(
        plan, section, even, waves_out, new, total, permute_t[...], packed_out, sec_out, lat_out
    )


def per_device(plan, axes, spectra, turning, currents, drag_rates, land_mask, ocean_target):
    tables = [jnp.asarray(table) for table in build_tables(NFREQ, NDIR, drag_rates.shape[0])]
    columns, rows, cols, spectral = plan.columns, plan.rows, plan.cols, plan.spectral
    shape = jax.ShapeDtypeStruct
    params = pltpu.CompilerParams(vmem_limit_bytes=32 * 1024 * 1024)
    messages = [shape((size, LANES), F32) for size in plan.sec_rows] + [
        shape((cols, spectral // 2 + LANES), F32)
    ] * 2
    state = shape((columns, LANES), F32)
    field = shape(spectra.shape, F32)
    square = shape((columns, columns), BF16)
    edge = pltpu.VMEM((plan.tiles * rows + 8, LANES), F32)
    coupled = pltpu.VMEM((columns, LANES), F32)
    spans = spectral // 256

    def call(kernel, outs, scratch, *args, space_in=pltpu.VMEM, space_out=pltpu.VMEM):
        return pl.pallas_call(
            kernel,
            out_shape=outs,
            in_specs=[pl.BlockSpec(memory_space=space_in)] * len(args),
            out_specs=[pl.BlockSpec(memory_space=space_out)] * len(outs),
            scratch_shapes=scratch,
            compiler_params=params,
        )(*args)

    def exchange(sent):
        near = [(i, i ^ 1) for i in range(plan.bands) if i ^ 1 < plan.bands]
        far = [(i, ((i + 1) ^ 1) - 1) for i in range(1, plan.bands) if ((i + 1) ^ 1) - 1 < plan.bands]
        got = [
            lax.ppermute(message, axes[1], list(enumerate(table)))
            for message, table in zip(sent, plan.exchanges)
        ]
        return got, lax.ppermute(sent[-2], axes[0], near), lax.ppermute(sent[-1], axes[0], far)

    waves, ocean, permute, permute_t, turn, sea, keep, stokes, rates, grow, packed, *sent = call(
        functools.partial(first_kernel, plan, axes),
        [field, state, square, square, state, state, shape((8, LANES), F32)]
        + [shape(table.shape, table.dtype) for table in tables]
        + [state]
        + messages,
        [
            pltpu.VMEM(turning.shape, F32),
            pltpu.VMEM(currents.shape, F32),
            pltpu.VMEM(drag_rates.shape, F32),
            pltpu.VMEM(land_mask.shape, jnp.int32),
            pltpu.VMEM(ocean_target.shape, jnp.int32),
            pltpu.SemaphoreType.DMA((9,)),
        ],
        *[
            pltpu.with_memory_space_constraint(array, pltpu.HBM)
            for array in (
                spectra,
                turning,
                currents,
                drag_rates,
                land_mask,
                ocean_target,
                *tables,
            )
        ],
        space_in=pltpu.HBM,
    )
    for step in range(STEPS):
        last = step == STEPS - 1
        got, near, far = exchange(sent)
        turned, spin = call(
            functools.partial(move_kernel, plan, axes),
            [field, state],
            [edge, edge],
            waves,
            ocean,
            turn,
            rates,
            *[message for message, edged in zip(got, plan.edges) if edged],
            near,
            far,
        )
        result = call(
            functools.partial(couple_kernel, plan, axes, last),
            [field, shape(currents.shape, F32)] if last else [field, state, state] + messages,
            [
                coupled,
                pltpu.VMEM(spectra.shape, F32),
                pltpu.VMEM(currents.shape, F32),
                pltpu.SemaphoreType.DMA((1 + spans,)),
            ]
            if last
            else [coupled],
            turned,
            spin,
            ocean,
            packed,
            permute,
            permute_t,
            sea,
            keep,
            stokes,
            grow,
            *got,
            space_out=pltpu.HBM if last else pltpu.VMEM,
        )
        waves, ocean = result[:2]
        if not last:
            packed, *sent = result[2:]
    return waves, ocean


def solution(mesh):
    sections, bands = mesh.shape["sec"], mesh.shape["lat"]

    def local(spectra, turning, currents, drag_rates, land_mask, ocean_target):
        rows, cols, spectral = spectra.shape
        plan = Plan(sections, bands, rows, cols, spectral, drag_rates.shape[0])
        return per_device(
            plan, ("lat", "sec"), spectra, turning, currents, drag_rates, land_mask, ocean_target
        )

    return jax.shard_map(
        local,
        mesh=mesh,
        in_specs=(
            P("lat", "sec", None),
            P("lat", "sec"),
            P("lat", "sec", None),
            P(),
            P("lat", "sec"),
            P("lat", "sec"),
        ),
        out_specs=(P("lat", "sec", None), P("lat", "sec", None)),
        check_vma=False,
    )
```

```python
import functools
import math

import jax
import jax.numpy as jnp
import ml_dtypes
import numpy as np
from jax import lax
from jax.experimental import pallas as pl
from jax.experimental.pallas import tpu as pltpu
from jax.sharding import PartitionSpec as P

NFREQ = 24
NDIR = 32
STEPS = 3

stokes_scale = 0.1
ocean_dt = 0.3
current_gain = 0.2

LANES = 128
F32 = jnp.float32
BF16 = jnp.bfloat16


def split_halves(table):
    high = table.astype(ml_dtypes.bfloat16)
    low = (table - high.astype(np.float64)).astype(ml_dtypes.bfloat16)
    return high, low


def build_tables(nfreq, ndir, ndepth):
    fraction = np.arange(nfreq) / (nfreq - 1)
    angles = (np.arange(ndir) + 0.5) * (2.0 * math.pi / ndir)
    east_part, north_part = np.cos(angles), np.sin(angles)
    courant = 0.1 + 0.3 * fraction
    depth_level = 0.5 + (ndepth - 2) * (1.0 - fraction)
    weights = np.maximum(1.0 - np.abs(np.arange(ndepth)[None, :] - depth_level[:, None]), 0.0)
    mean_weights = weights / weights.sum(axis=1, keepdims=True)
    x_rate = np.abs(courant[:, None] * east_part[None, :]).reshape(-1)
    y_rate = np.abs(courant[:, None] * north_part[None, :]).reshape(-1)
    turn_gain = np.repeat(1.0 - 0.5 * fraction, ndir)
    rates = np.stack([1.0 - x_rate - y_rate, x_rate, y_rate, turn_gain] * 2).astype(np.float32)
    compass = np.stack([east_part, north_part])
    stokes = (stokes_scale * weights[:, None, None, :] * compass.T[None, :, :, None]).reshape(
        nfreq * ndir, 2 * ndepth
    )
    growth = current_gain * (1.0 + fraction)
    grow = (
        growth[None, None, :, None] * mean_weights.T[None, :, :, None] * compass[:, None, None, :]
    ).reshape(2 * ndepth, nfreq * ndir)
    stokes_high, stokes_low = split_halves(stokes)
    grow_high, grow_low = split_halves(grow)
    return (
        np.concatenate([stokes_high, stokes_low], axis=1),
        rates,
        np.concatenate([grow_high, grow_high, grow_low, grow_low], axis=0)
        .reshape(8 * ndepth, -1, LANES)
        .transpose(1, 0, 2)
        .reshape(-1, LANES),
    )


def sec_exchanges(count):
    if count % 4 == 0:
        return [(hop, flip) for hop in range(count // 4) for flip in (3, 1, 2, 0) if hop or flip]
    return [(hop, 0) for hop in range(1, count)]


class Plan:
    def __init__(self, sections, bands, rows, cols, spectral, depth):
        self.sections, self.bands = sections, bands
        self.rows, self.cols, self.spectral, self.depth = rows, cols, spectral, depth
        self.columns = rows * cols
        self.chunk = self.columns // sections
        self.tiles = spectral // LANES
        self.quad = 4 if sections % 4 == 0 else 1
        self.hops = sec_exchanges(sections)
        self.exchanges = [
            [self.partner(i, number, divmod)[0] for i in range(sections)]
            for number in range(len(self.hops))
        ]
        self.edges = [
            any(abs(target - i) == 1 for i, target in enumerate(table)) for table in self.exchanges
        ]
        self.sec_rows = [
            self.chunk + (self.tiles * rows + 8 if edge else 0) for edge in self.edges
        ]

    def partner(self, section, number, divide=lambda a, b: (lax.div(a, b), lax.rem(a, b))):
        hop, flip = self.hops[number]
        groups = self.sections // self.quad
        high, low = divide(section, self.quad)
        if flip & 1:
            low = low + 1 - 2 * divide(low, 2)[1]
        if flip & 2:
            low = low + 2 - 4 * divide(low, 2)[0]
        return tuple(
            divide(high + shift, groups)[1] * self.quad + low for shift in (hop, groups - hop)
        )


def lane_of(shape):
    return lax.broadcasted_iota(jnp.int32, shape, len(shape) - 1)


def dot(a, b):
    return jnp.dot(a, b, preferred_element_type=F32)


def split_value(value):
    high = value.astype(BF16).astype(F32)
    return jnp.where(lane_of(value.shape) < LANES // 2, high, value - high).astype(BF16)


def stokes_product(part, table):
    high = part.astype(BF16)
    low = (part - high.astype(F32)).astype(BF16)
    return dot(jnp.concatenate([high, low], axis=0), table)


def send_parts(plan, section, even, waves, ocean, total, permute_t, packed_out, sec_out, lat_out):
    chunk, tiles, rows, cols = plan.chunk, plan.tiles, plan.rows, plan.cols
    lane = lane_of((plan.columns, LANES))
    near, far = lat_out
    sea_rows = ocean.reshape(rows, cols, LANES)
    low_half = lax.rem(lane_of((cols, LANES)), NDIR) < NDIR // 2
    for out, northward in ((far, jnp.logical_not(even)), (near, even)):
        edge = jnp.where(northward, waves[rows - 1], waves[0])
        for tile in range(tiles // 2):
            first = edge[:, tile * LANES : (tile + 1) * LANES]
            second = edge[:, (tile + tiles // 2) * LANES : (tile + tiles // 2 + 1) * LANES]
            up = jnp.where(low_half, first, pltpu.roll(second, NDIR // 2, 1))
            down = jnp.where(low_half, pltpu.roll(second, LANES - NDIR // 2, 1), first)
            out[:, tile * LANES : (tile + 1) * LANES] = jnp.where(northward, up, down)
        out[:, plan.spectral // 2 :] = jnp.where(northward, sea_rows[rows - 1], sea_rows[0])
    moments = total[: plan.columns] + total[plan.columns :]
    moments = moments + pltpu.roll(moments, LANES // 2, 1)
    ordered = dot(permute_t, split_value(moments))
    ordered = ordered + pltpu.roll(ordered, LANES // 2, 1)
    packed_out[...] = jnp.where(lane < LANES // 2, ocean, ordered)
    for number, out in enumerate(sec_out):
        target, _ = plan.partner(section, number)
        out[0:chunk, :] = packed_out[pl.ds(pl.multiple_of(target * chunk, 8), chunk), :]
        if not plan.edges[number]:
            continue
        eastward = target == section + 1
        for row in range(rows):
            edge = jnp.where(eastward, waves[row, cols - 1 : cols, :], waves[row, 0:1, :])
            for tile in range(tiles):
                place = chunk + tile * rows + row
                out[place : place + 1, :] = edge[:, tile * LANES : (tile + 1) * LANES]
            place = chunk + tiles * rows + row
            out[place : place + 1, :] = jnp.where(
                eastward, sea_rows[row, cols - 1 : cols, :], sea_rows[row, 0:1, :]
            )


def first_kernel(plan, axes, *refs):
    waves_in, turning_in, currents_in, drag_in, mask_in, target_in = refs[:6]
    tables_in, refs = refs[6:9], refs[9:]
    waves, ocean_out, permute_out, permute_t_out, turn_out, sea_out, keep_out = refs[:7]
    tables_out, packed_out, refs = refs[7:10], refs[10], refs[11:]
    count = len(plan.exchanges)
    sec_out, lat_out, refs = refs[:count], refs[count : count + 2], refs[count + 2 :]
    turning, currents, drag, mask, target, done = refs
    pairs = [
        (target_in, target),
        (turning_in, turning),
        (mask_in, mask),
        (drag_in, drag),
        (waves_in, waves),
        (tables_in[0], tables_out[0]),
        (currents_in, currents),
        (tables_in[1], tables_out[1]),
        (tables_in[2], tables_out[2]),
    ]
    copies = [pltpu.make_async_copy(a, b, done.at[k]) for k, (a, b) in enumerate(pairs)]
    for copy in copies:
        copy.start()
    section, band = lax.axis_index(axes[1]), lax.axis_index(axes[0])
    even = lax.rem(band, 2) == 0
    columns, rows = plan.columns, plan.rows
    across = lane_of((columns, columns))
    down = lax.broadcasted_iota(jnp.int32, (columns, columns), 0)
    here = across == down

    def row_of(ref):
        return jnp.concatenate([ref[row : row + 1, :] for row in range(rows)], axis=1)

    def column_of(row):
        spread = jnp.broadcast_to(row, (columns, columns))
        return jnp.sum(jnp.where(here, spread, jnp.zeros_like(spread)), axis=1, keepdims=True)

    for copy in copies[:4]:
        copy.wait()
    sea = column_of(row_of(mask).astype(F32))
    target_row = row_of(target).astype(F32)
    target_col = column_of(target_row)
    same = target_col == target_row
    rank_col = jnp.sum(jnp.where(same & (across < down), 1.0, 0.0), axis=1, keepdims=True)
    rank_row = jnp.sum(jnp.where(same & (down < across), 1.0, 0.0), axis=0, keepdims=True)
    slot_col = target_col * float(plan.chunk) + rank_col
    slot_row = target_row * float(plan.chunk) + rank_row
    permute_out[...] = jnp.where(slot_col == across.astype(F32), sea, 0.0).astype(BF16)
    permute_t = jnp.where(slot_row == down.astype(F32), 1.0, 0.0).astype(BF16)
    permute_t_out[...] = permute_t
    turn_out[...] = jnp.broadcast_to(column_of(row_of(turning)), (columns, LANES))
    sea_out[...] = jnp.broadcast_to(sea, (columns, LANES))
    keep = 1.0 - drag[...].reshape(1, plan.depth)
    blank = jnp.zeros((1, LANES - 2 * plan.depth), F32)
    keep_out[...] = jnp.broadcast_to(jnp.concatenate([keep, keep, blank], axis=1), (8, LANES))
    for copy in copies[4:7]:
        copy.wait()
    flat = currents[...].reshape(columns, 2 * plan.depth)
    ocean = jnp.concatenate([flat, jnp.zeros((columns, LANES - 2 * plan.depth), F32)], axis=1)
    ocean_out[...] = ocean
    total = None
    for start in range(0, plan.spectral, 256):
        part = waves[:, :, start : start + 256].reshape(columns, 256)
        product = stokes_product(part, tables_out[0][start : start + 256, :])
        total = product if total is None else total + product
    send_parts(
        plan, section, even, waves, ocean, total, permute_t, packed_out, sec_out, lat_out
    )
    for copy in copies[7:]:
        copy.wait()


def move_kernel(plan, axes, *refs):
    waves, ocean, turn, rates = refs[:4]
    edge_numbers = [number for number, edge in enumerate(plan.edges) if edge]
    sec_in, refs = refs[4 : 4 + len(edge_numbers)], refs[4 + len(edge_numbers) :]
    near, far, turned_out, spin_out, west_edge, east_edge = refs
    section, band = lax.axis_index(axes[1]), lax.axis_index(axes[0])
    even = lax.rem(band, 2) == 0
    rows, cols, tiles, chunk = plan.rows, plan.cols, plan.tiles, plan.chunk

    west_edge[...] = jnp.zeros_like(west_edge)
    east_edge[...] = jnp.zeros_like(east_edge)
    for number, message in zip(edge_numbers, sec_in):
        _, source = plan.partner(section, number)

        @pl.when(source == section + 1)
        def _():
            east_edge[...] = message[chunk:, :]

        @pl.when(source == section - 1)
        def _():
            west_edge[...] = message[chunk:, :]

    block = (cols, LANES)
    direction = lax.rem(lane_of(block), NDIR)
    eastward = (direction < NDIR // 4) | (direction >= 3 * NDIR // 4)
    northward = direction < NDIR // 2
    first, final = direction == 0, direction == NDIR - 1
    place = lax.broadcasted_iota(jnp.int32, block, 0)
    at_west, at_east = place == 0, place == cols - 1
    for tile in range(tiles):
        lanes = slice(tile * LANES, (tile + 1) * LANES)
        stay, along_x, along_y, gain = (rates[k : k + 1, lanes] for k in range(4))
        half = tile % (tiles // 2)
        half = slice(half * LANES, (half + 1) * LANES)
        south_edge = jnp.where(even, far[:, half], near[:, half])
        north_edge = jnp.where(even, near[:, half], far[:, half])
        if tile >= tiles // 2:
            south_edge = pltpu.roll(south_edge, LANES - NDIR // 2, 1)
            north_edge = pltpu.roll(north_edge, NDIR // 2, 1)
        for row in range(rows):
            edge = slice(tile * rows + row, tile * rows + row + 1)
            center = waves[row, :, lanes]
            west = jnp.where(at_west, west_edge[edge, :], pltpu.roll(center, 1, 0))
            east = jnp.where(at_east, east_edge[edge, :], pltpu.roll(center, cols - 1, 0))
            south = waves[row - 1, :, lanes] if row else south_edge
            north = waves[row + 1, :, lanes] if row < rows - 1 else north_edge
            moved = (
                stay * center
                + along_x * jnp.where(eastward, west, east)
                + along_y * jnp.where(northward, south, north)
            )
            behind = jnp.where(
                first, pltpu.roll(moved, LANES - (NDIR - 1), 1), pltpu.roll(moved, 1, 1)
            )
            forward = jnp.where(
                final, pltpu.roll(moved, NDIR - 1, 1), pltpu.roll(moved, LANES - 1, 1)
            )
            rate = turn[row * cols : (row + 1) * cols, :]
            turned_out[row, :, lanes] = moved - jnp.abs(rate) * gain * (
                moved - jnp.where(rate > 0.0, behind, forward)
            )

    zonal = lane_of(block) < plan.depth
    half = slice(plan.spectral // 2, plan.spectral // 2 + LANES)
    south_edge = jnp.where(even, far[:, half], near[:, half])
    north_edge = jnp.where(even, near[:, half], far[:, half])
    for row in range(rows):
        flat = slice(row * cols, (row + 1) * cols)
        edge = slice(tiles * rows + row, tiles * rows + row + 1)
        center = ocean[flat, :]
        west = jnp.where(at_west, west_edge[edge, :], pltpu.roll(center, 1, 0))
        east = jnp.where(at_east, east_edge[edge, :], pltpu.roll(center, cols - 1, 0))
        south = ocean[(row - 1) * cols : row * cols, :] if row else south_edge
        north = ocean[(row + 1) * cols : (row + 2) * cols, :] if row < rows - 1 else north_edge
        shear = 0.5 * jnp.where(zonal, south - north, east - west)
        shear = shear + swapped(plan, shear)
        y = (band * rows + row).astype(F32)
        spin_out[flat, :] = 0.2 + 0.6 * y / float(plan.bands * rows) + shear


def swapped(plan, value):
    half = plan.depth
    zonal = lane_of(value.shape) < half
    return jnp.where(zonal, pltpu.roll(value, LANES - half, 1), pltpu.roll(value, half, 1))


def couple_kernel(plan, axes, last, *refs):
    turned, spin, ocean_in, packed_in, permute, permute_t, sea, keep, stokes, grow = refs[:10]
    refs = refs[10:]
    count = len(plan.exchanges)
    sec_in, refs = refs[:count], refs[count:]
    if last:
        waves_far, ocean_far, coupled, waves_out, ocean_out, done = refs
    else:
        waves_out, ocean_out, packed_out = refs[:3]
        sec_out, lat_out, coupled = refs[3 : count + 3], refs[count + 3 : count + 5], refs[-1]
    section, band = lax.axis_index(axes[1]), lax.axis_index(axes[0])
    even = lax.rem(band, 2) == 0
    rows, cols, chunk, columns = plan.rows, plan.cols, plan.chunk, plan.columns

    own = pl.ds(pl.multiple_of(section * chunk, 8), chunk)
    coupled[own, :] = packed_in[own, :]
    for number, message in enumerate(sec_in):
        _, source = plan.partner(section, number)
        coupled[pl.ds(pl.multiple_of(source * chunk, 8), chunk), :] = message[0:chunk, :]
    arrived = coupled[...]
    other = pltpu.roll(arrived, LANES // 2, 1)
    lane = lane_of((columns, LANES))
    both = jnp.where(lane < LANES // 2, arrived, other)
    at_waves = dot(permute[...], split_value(both)).astype(BF16)
    at_waves = jnp.concatenate([at_waves, at_waves], axis=1)

    pushed = swapped(plan, ocean_in[...] + other)
    turn_by = ocean_dt * spin[...] * pushed
    new = keep[0:1, :] * (ocean_in[...] + jnp.where(lane < plan.depth, turn_by, -turn_by)) * sea[...]
    if last:
        ocean_out[...] = new[:, : 2 * plan.depth].reshape(rows, cols, 2 * plan.depth)
        copies = [pltpu.make_async_copy(ocean_out, ocean_far, done.at[0])]
        copies[0].start()
    else:
        ocean_out[...] = new

    total = None
    wet = jnp.concatenate([sea[...], sea[...]], axis=1)
    for number, start in enumerate(range(0, plan.spectral, 256)):
        lanes = slice(start, start + 256)
        table = jnp.concatenate(
            [grow[(2 * number + k) * 256 : (2 * number + k + 1) * 256, :] for k in range(2)], axis=1
        )
        grown = turned[:, :, lanes].reshape(columns, 256) * (wet + dot(at_waves, table))
        waves_out[:, :, lanes] = grown.reshape(rows, cols, 256)
        if last:
            copy = pltpu.make_async_copy(
                waves_out.at[:, :, lanes], waves_far.at[:, :, lanes], done.at[number + 1]
            )
            copy.start()
            copies.append(copy)
        else:
            product = stokes_product(grown, stokes[lanes, :])
            total = product if total is None else total + product
    if last:
        for copy in copies:
            copy.wait()
        return
    send_parts(
        plan, section, even, waves_out, new, total, permute_t[...], packed_out, sec_out, lat_out
    )


def per_device(plan, axes, spectra, turning, currents, drag_rates, land_mask, ocean_target):
    tables = [jnp.asarray(table) for table in build_tables(NFREQ, NDIR, drag_rates.shape[0])]
    columns, rows, cols, spectral = plan.columns, plan.rows, plan.cols, plan.spectral
    shape = jax.ShapeDtypeStruct
    params = pltpu.CompilerParams(vmem_limit_bytes=32 * 1024 * 1024)
    messages = [shape((size, LANES), F32) for size in plan.sec_rows] + [
        shape((cols, spectral // 2 + LANES), F32)
    ] * 2
    state = shape((columns, LANES), F32)
    field = shape(spectra.shape, F32)
    square = shape((columns, columns), BF16)
    edge = pltpu.VMEM((plan.tiles * rows + 8, LANES), F32)
    coupled = pltpu.VMEM((columns, LANES), F32)
    spans = spectral // 256

    def call(kernel, outs, scratch, *args, space_in=pltpu.VMEM, space_out=pltpu.VMEM):
        return pl.pallas_call(
            kernel,
            out_shape=outs,
            in_specs=[pl.BlockSpec(memory_space=space_in)] * len(args),
            out_specs=[pl.BlockSpec(memory_space=space_out)] * len(outs),
            scratch_shapes=scratch,
            compiler_params=params,
        )(*args)

    def exchange(sent):
        near = [(i, i ^ 1) for i in range(plan.bands) if i ^ 1 < plan.bands]
        far = [(i, ((i + 1) ^ 1) - 1) for i in range(1, plan.bands) if ((i + 1) ^ 1) - 1 < plan.bands]
        got = [
            lax.ppermute(message, axes[1], list(enumerate(table)))
            for message, table in zip(sent, plan.exchanges)
        ]
        return got, lax.ppermute(sent[-2], axes[0], near), lax.ppermute(sent[-1], axes[0], far)

    waves, ocean, permute, permute_t, turn, sea, keep, stokes, rates, grow, packed, *sent = call(
        functools.partial(first_kernel, plan, axes),
        [field, state, square, square, state, state, shape((8, LANES), F32)]
        + [shape(table.shape, table.dtype) for table in tables]
        + [state]
        + messages,
        [
            pltpu.VMEM(turning.shape, F32),
            pltpu.VMEM(currents.shape, F32),
            pltpu.VMEM(drag_rates.shape, F32),
            pltpu.VMEM(land_mask.shape, jnp.int32),
            pltpu.VMEM(ocean_target.shape, jnp.int32),
            pltpu.SemaphoreType.DMA((9,)),
        ],
        *[
            pltpu.with_memory_space_constraint(array, pltpu.HBM)
            for array in (
                spectra,
                turning,
                currents,
                drag_rates,
                land_mask,
                ocean_target,
                *tables,
            )
        ],
        space_in=pltpu.HBM,
    )
    for step in range(STEPS):
        last = step == STEPS - 1
        got, near, far = exchange(sent)
        turned, spin = call(
            functools.partial(move_kernel, plan, axes),
            [field, state],
            [edge, edge],
            waves,
            ocean,
            turn,
            rates,
            *[message for message, edged in zip(got, plan.edges) if edged],
            near,
            far,
        )
        result = call(
            functools.partial(couple_kernel, plan, axes, last),
            [field, shape(currents.shape, F32)] if last else [field, state, state] + messages,
            [
                coupled,
                pltpu.VMEM(spectra.shape, F32),
                pltpu.VMEM(currents.shape, F32),
                pltpu.SemaphoreType.DMA((1 + spans,)),
            ]
            if last
            else [coupled],
            turned,
            spin,
            ocean,
            packed,
            permute,
            permute_t,
            sea,
            keep,
            stokes,
            grow,
            *got,
            space_out=pltpu.HBM if last else pltpu.VMEM,
        )
        waves, ocean = result[:2]
        if not last:
            packed, *sent = result[2:]
    return waves, ocean


def solution(mesh):
    sections, bands = mesh.shape["sec"], mesh.shape["lat"]

    def local(spectra, turning, currents, drag_rates, land_mask, ocean_target):
        rows, cols, spectral = spectra.shape
        plan = Plan(sections, bands, rows, cols, spectral, drag_rates.shape[0])
        return per_device(
            plan, ("lat", "sec"), spectra, turning, currents, drag_rates, land_mask, ocean_target
        )

    return jax.shard_map(
        local,
        mesh=mesh,
        in_specs=(
            P("lat", "sec", None),
            P("lat", "sec"),
            P("lat", "sec", None),
            P(),
            P("lat", "sec"),
            P("lat", "sec"),
        ),
        out_specs=(P("lat", "sec", None), P("lat", "sec", None)),
        check_vma=False,
    )
```

```python
import functools
import math

import jax
import jax.numpy as jnp
import ml_dtypes
import numpy as np
from jax import lax
from jax.experimental import pallas as pl
from jax.experimental.pallas import tpu as pltpu
from jax.sharding import PartitionSpec as P

NFREQ = 24
NDIR = 32
STEPS = 3

stokes_scale = 0.1
ocean_dt = 0.3
current_gain = 0.2

LANES = 128
F32 = jnp.float32
BF16 = jnp.bfloat16


def split_halves(table):
    high = table.astype(ml_dtypes.bfloat16)
    low = (table - high.astype(np.float64)).astype(ml_dtypes.bfloat16)
    return high, low


def build_tables(nfreq, ndir, ndepth):
    fraction = np.arange(nfreq) / (nfreq - 1)
    angles = (np.arange(ndir) + 0.5) * (2.0 * math.pi / ndir)
    east_part, north_part = np.cos(angles), np.sin(angles)
    courant = 0.1 + 0.3 * fraction
    depth_level = 0.5 + (ndepth - 2) * (1.0 - fraction)
    weights = np.maximum(1.0 - np.abs(np.arange(ndepth)[None, :] - depth_level[:, None]), 0.0)
    mean_weights = weights / weights.sum(axis=1, keepdims=True)
    x_rate = np.abs(courant[:, None] * east_part[None, :]).reshape(-1)
    y_rate = np.abs(courant[:, None] * north_part[None, :]).reshape(-1)
    turn_gain = np.repeat(1.0 - 0.5 * fraction, ndir)
    rates = np.stack([1.0 - x_rate - y_rate, x_rate, y_rate, turn_gain] * 2).astype(np.float32)
    compass = np.stack([east_part, north_part])
    stokes = (stokes_scale * weights[:, None, None, :] * compass.T[None, :, :, None]).reshape(
        nfreq * ndir, 2 * ndepth
    )
    growth = current_gain * (1.0 + fraction)
    grow = (
        growth[None, None, :, None] * mean_weights.T[None, :, :, None] * compass[:, None, None, :]
    ).reshape(2 * ndepth, nfreq * ndir)
    stokes_high, stokes_low = split_halves(stokes)
    grow_high, grow_low = split_halves(grow)
    return (
        np.concatenate([stokes_high, stokes_low], axis=1),
        rates,
        np.concatenate([grow_high, grow_high, grow_low, grow_low], axis=0)
        .reshape(8 * ndepth, -1, LANES)
        .transpose(1, 0, 2)
        .reshape(-1, LANES),
    )


def sec_exchanges(count):
    if count % 4 == 0:
        return [(hop, flip) for hop in range(count // 4) for flip in (3, 1, 2, 0) if hop or flip]
    return [(hop, 0) for hop in range(1, count)]


class Plan:
    def __init__(self, sections, bands, rows, cols, spectral, depth):
        self.sections, self.bands = sections, bands
        self.rows, self.cols, self.spectral, self.depth = rows, cols, spectral, depth
        self.columns = rows * cols
        self.chunk = self.columns // sections
        self.tiles = spectral // LANES
        self.quad = 4 if sections % 4 == 0 else 1
        self.hops = sec_exchanges(sections)
        self.exchanges = [
            [self.partner(i, number, divmod)[0] for i in range(sections)]
            for number in range(len(self.hops))
        ]
        self.edges = [
            any(abs(target - i) == 1 for i, target in enumerate(table)) for table in self.exchanges
        ]
        self.sec_rows = [
            self.chunk + (self.tiles * rows + 8 if edge else 0) for edge in self.edges
        ]

    def partner(self, section, number, divide=lambda a, b: (lax.div(a, b), lax.rem(a, b))):
        hop, flip = self.hops[number]
        groups = self.sections // self.quad
        high, low = divide(section, self.quad)
        if flip & 1:
            low = low + 1 - 2 * divide(low, 2)[1]
        if flip & 2:
            low = low + 2 - 4 * divide(low, 2)[0]
        return tuple(
            divide(high + shift, groups)[1] * self.quad + low for shift in (hop, groups - hop)
        )


def lane_of(shape):
    return lax.broadcasted_iota(jnp.int32, shape, len(shape) - 1)


def dot(a, b):
    return jnp.dot(a, b, preferred_element_type=F32)


def split_value(value):
    high = value.astype(BF16).astype(F32)
    return jnp.where(lane_of(value.shape) < LANES // 2, high, value - high).astype(BF16)


def stokes_product(part, table):
    high = part.astype(BF16)
    low = (part - high.astype(F32)).astype(BF16)
    return dot(jnp.concatenate([high, low], axis=0), table)


def send_parts(plan, section, even, waves, ocean, total, permute_t, packed_out, sec_out, lat_out):
    chunk, tiles, rows, cols = plan.chunk, plan.tiles, plan.rows, plan.cols
    lane = lane_of((plan.columns, LANES))
    near, far = lat_out
    sea_rows = ocean.reshape(rows, cols, LANES)
    low_half = lax.rem(lane_of((cols, LANES)), NDIR) < NDIR // 2
    for out, northward in ((far, jnp.logical_not(even)), (near, even)):
        edge = jnp.where(northward, waves[rows - 1], waves[0])
        for tile in range(tiles // 2):
            first = edge[:, tile * LANES : (tile + 1) * LANES]
            second = edge[:, (tile + tiles // 2) * LANES : (tile + tiles // 2 + 1) * LANES]
            up = jnp.where(low_half, first, pltpu.roll(second, NDIR // 2, 1))
            down = jnp.where(low_half, pltpu.roll(second, LANES - NDIR // 2, 1), first)
            out[:, tile * LANES : (tile + 1) * LANES] = jnp.where(northward, up, down)
        out[:, plan.spectral // 2 :] = jnp.where(northward, sea_rows[rows - 1], sea_rows[0])
    moments = total[: plan.columns] + total[plan.columns :]
    moments = moments + pltpu.roll(moments, LANES // 2, 1)
    ordered = dot(permute_t, split_value(moments))
    ordered = ordered + pltpu.roll(ordered, LANES // 2, 1)
    packed_out[...] = jnp.where(lane < LANES // 2, ocean, ordered)
    for number, out in enumerate(sec_out):
        target, _ = plan.partner(section, number)
        out[0:chunk, :] = packed_out[pl.ds(pl.multiple_of(target * chunk, 8), chunk), :]
        if not plan.edges[number]:
            continue
        eastward = target == section + 1
        for row in range(rows):
            edge = jnp.where(eastward, waves[row, cols - 1 : cols, :], waves[row, 0:1, :])
            for tile in range(tiles):
                place = chunk + tile * rows + row
                out[place : place + 1, :] = edge[:, tile * LANES : (tile + 1) * LANES]
            place = chunk + tiles * rows + row
            out[place : place + 1, :] = jnp.where(
                eastward, sea_rows[row, cols - 1 : cols, :], sea_rows[row, 0:1, :]
            )


def first_kernel(plan, axes, *refs):
    waves_in, turning_in, currents_in, drag_in, mask_in, target_in = refs[:6]
    tables_in, refs = refs[6:9], refs[9:]
    waves, ocean_out, permute_out, permute_t_out, turn_out, turn_edge_out = refs[:6]
    sea_out, keep_out, tables_out, packed_out, refs = refs[6], refs[7], refs[8:11], refs[11], refs[12:]
    count = len(plan.exchanges)
    sec_out, lat_out, refs = refs[:count], refs[count : count + 2], refs[count + 2 :]
    turning, currents, drag, mask, target, done = refs
    pairs = [
        (target_in, target),
        (turning_in, turning),
        (mask_in, mask),
        (drag_in, drag),
        (waves_in, waves),
        (tables_in[0], tables_out[0]),
        (currents_in, currents),
        (tables_in[1], tables_out[1]),
        (tables_in[2], tables_out[2]),
    ]
    copies = [pltpu.make_async_copy(a, b, done.at[k]) for k, (a, b) in enumerate(pairs)]
    for copy in copies:
        copy.start()
    section, band = lax.axis_index(axes[1]), lax.axis_index(axes[0])
    even = lax.rem(band, 2) == 0
    columns, rows = plan.columns, plan.rows
    across = lane_of((columns, columns))
    down = lax.broadcasted_iota(jnp.int32, (columns, columns), 0)
    here = across == down

    def row_of(ref):
        return jnp.concatenate([ref[row : row + 1, :] for row in range(rows)], axis=1)

    def column_of(row):
        spread = jnp.broadcast_to(row, (columns, columns))
        return jnp.sum(jnp.where(here, spread, jnp.zeros_like(spread)), axis=1, keepdims=True)

    for copy in copies[:4]:
        copy.wait()
    sea = column_of(row_of(mask).astype(F32))
    target_row = row_of(target).astype(F32)
    target_col = column_of(target_row)
    same = target_col == target_row
    rank_col = jnp.sum(jnp.where(same & (across < down), 1.0, 0.0), axis=1, keepdims=True)
    rank_row = jnp.sum(jnp.where(same & (down < across), 1.0, 0.0), axis=0, keepdims=True)
    slot_col = target_col * float(plan.chunk) + rank_col
    slot_row = target_row * float(plan.chunk) + rank_row
    permute_out[...] = jnp.where(slot_col == across.astype(F32), sea, 0.0).astype(BF16)
    permute_t = jnp.where(slot_row == down.astype(F32), 1.0, 0.0).astype(BF16)
    permute_t_out[...] = permute_t
    turn = jnp.broadcast_to(column_of(row_of(turning)), (columns, LANES))
    turn_out[...] = turn
    cols = plan.cols
    for row in range(rows):
        turn_edge_out[row : row + 1, :] = turn[row * cols : row * cols + 1, :]
        turn_edge_out[rows + row : rows + row + 1, :] = turn[(row + 1) * cols - 1 : (row + 1) * cols, :]
    sea_out[...] = jnp.broadcast_to(sea, (columns, LANES))
    keep = 1.0 - drag[...].reshape(1, plan.depth)
    blank = jnp.zeros((1, LANES - 2 * plan.depth), F32)
    keep_out[...] = jnp.broadcast_to(jnp.concatenate([keep, keep, blank], axis=1), (8, LANES))
    for copy in copies[4:7]:
        copy.wait()
    flat = currents[...].reshape(columns, 2 * plan.depth)
    ocean = jnp.concatenate([flat, jnp.zeros((columns, LANES - 2 * plan.depth), F32)], axis=1)
    ocean_out[...] = ocean
    total = None
    for start in range(0, plan.spectral, 256):
        part = waves[:, :, start : start + 256].reshape(columns, 256)
        product = stokes_product(part, tables_out[0][start : start + 256, :])
        total = product if total is None else total + product
    send_parts(
        plan, section, even, waves, ocean, total, permute_t, packed_out, sec_out, lat_out
    )
    for copy in copies[7:]:
        copy.wait()


class Directions:
    def __init__(self, shape):
        direction = lax.rem(lane_of(shape), NDIR)
        self.eastward = (direction < NDIR // 4) | (direction >= 3 * NDIR // 4)
        self.northward = direction < NDIR // 2
        self.first, self.final = direction == 0, direction == NDIR - 1

    def turned(self, moved, rate, gain):
        behind = jnp.where(
            self.first, pltpu.roll(moved, LANES - (NDIR - 1), 1), pltpu.roll(moved, 1, 1)
        )
        forward = jnp.where(
            self.final, pltpu.roll(moved, NDIR - 1, 1), pltpu.roll(moved, LANES - 1, 1)
        )
        return moved - jnp.abs(rate) * gain * (moved - jnp.where(rate > 0.0, behind, forward))


def move_kernel(plan, axes, *refs):
    waves, turn, rates, near, far, turned_out = refs
    even = lax.rem(lax.axis_index(axes[0]), 2) == 0
    rows, cols, tiles = plan.rows, plan.cols, plan.tiles
    block = (cols, LANES)
    masks = Directions(block)
    place = lax.broadcasted_iota(jnp.int32, block, 0)
    outside = place == jnp.where(masks.eastward, 0, cols - 1)
    for tile in range(tiles):
        lanes = slice(tile * LANES, (tile + 1) * LANES)
        stay, along_x, along_y, gain = (rates[k : k + 1, lanes] for k in range(4))
        along_x = jnp.where(outside, 0.0, along_x)
        half = tile % (tiles // 2)
        half = slice(half * LANES, (half + 1) * LANES)
        south_edge = jnp.where(even, far[:, half], near[:, half])
        north_edge = jnp.where(even, near[:, half], far[:, half])
        if tile >= tiles // 2:
            south_edge = pltpu.roll(south_edge, LANES - NDIR // 2, 1)
            north_edge = pltpu.roll(north_edge, NDIR // 2, 1)
        for row in range(rows):
            center = waves[row, :, lanes]
            south = waves[row - 1, :, lanes] if row else south_edge
            north = waves[row + 1, :, lanes] if row < rows - 1 else north_edge
            moved = (
                stay * center
                + along_x
                * jnp.where(
                    masks.eastward, pltpu.roll(center, 1, 0), pltpu.roll(center, cols - 1, 0)
                )
                + along_y * jnp.where(masks.northward, south, north)
            )
            rate = turn[row * cols : (row + 1) * cols, :]
            turned_out[row, :, lanes] = masks.turned(moved, rate, gain)


def swapped(plan, value):
    half = plan.depth
    zonal = lane_of(value.shape) < half
    return jnp.where(zonal, pltpu.roll(value, LANES - half, 1), pltpu.roll(value, half, 1))


def couple_kernel(plan, axes, last, *refs):
    turned, ocean_in, packed_in, permute, permute_t, turn_edge, sea, keep = refs[:8]
    stokes, rates, grow, refs = refs[8], refs[9], refs[10], refs[11:]
    count = len(plan.exchanges)
    sec_in, near, far, refs = refs[:count], refs[count], refs[count + 1], refs[count + 2 :]
    if last:
        waves_far, ocean_far, coupled, west_edge, east_edge, waves_out, ocean_out, done = refs
    else:
        waves_out, ocean_out, packed_out = refs[:3]
        sec_out, lat_out = refs[3 : count + 3], refs[count + 3 : count + 5]
        coupled, west_edge, east_edge = refs[count + 5 :]
    section, band = lax.axis_index(axes[1]), lax.axis_index(axes[0])
    even = lax.rem(band, 2) == 0
    rows, cols, chunk, columns, tiles = plan.rows, plan.cols, plan.chunk, plan.columns, plan.tiles

    own = pl.ds(pl.multiple_of(section * chunk, 8), chunk)
    coupled[own, :] = packed_in[own, :]
    west_edge[...] = jnp.zeros_like(west_edge)
    east_edge[...] = jnp.zeros_like(east_edge)
    for number, message in enumerate(sec_in):
        _, source = plan.partner(section, number)
        coupled[pl.ds(pl.multiple_of(source * chunk, 8), chunk), :] = message[0:chunk, :]
        if plan.edges[number]:

            @pl.when(source == section + 1)
            def _():
                east_edge[...] = message[chunk:, :]

            @pl.when(source == section - 1)
            def _():
                west_edge[...] = message[chunk:, :]

    arrived = coupled[...]
    other = pltpu.roll(arrived, LANES // 2, 1)
    lane = lane_of((columns, LANES))
    both = jnp.where(lane < LANES // 2, arrived, other)
    at_waves = dot(permute[...], split_value(both)).astype(BF16)
    at_waves = jnp.concatenate([at_waves, at_waves], axis=1)

    masks = Directions((2 * rows, LANES))
    westmost = lax.broadcasted_iota(jnp.int32, (2 * rows, LANES), 0) < rows
    reached = jnp.where(masks.eastward, 1, 0) == jnp.where(westmost, 1, 0)
    extra = []
    for tile in range(tiles):
        lanes = slice(tile * LANES, (tile + 1) * LANES)
        edge = slice(tile * rows, (tile + 1) * rows)
        came = jnp.concatenate([west_edge[edge, :], east_edge[edge, :]], axis=0)
        moved = rates[1:2, lanes] * jnp.where(reached, came, 0.0)
        extra.append(masks.turned(moved, turn_edge[...], rates[3:4, lanes]))

    block = (cols, LANES)
    zonal = lane_of(block) < plan.depth
    place = lax.broadcasted_iota(jnp.int32, block, 0)
    at_west, at_east = place == 0, place == cols - 1
    half = slice(plan.spectral // 2, plan.spectral // 2 + LANES)
    south_edge = jnp.where(even, far[:, half], near[:, half])
    north_edge = jnp.where(even, near[:, half], far[:, half])
    new = []
    for row in range(rows):
        flat = slice(row * cols, (row + 1) * cols)
        edge = slice(tiles * rows + row, tiles * rows + row + 1)
        center = ocean_in[flat, :]
        west = jnp.where(at_west, west_edge[edge, :], pltpu.roll(center, 1, 0))
        east = jnp.where(at_east, east_edge[edge, :], pltpu.roll(center, cols - 1, 0))
        south = ocean_in[(row - 1) * cols : row * cols, :] if row else south_edge
        north = ocean_in[(row + 1) * cols : (row + 2) * cols, :] if row < rows - 1 else north_edge
        shear = 0.5 * jnp.where(zonal, south - north, east - west)
        y = (band * rows + row).astype(F32)
        spin = 0.2 + 0.6 * y / float(plan.bands * rows) + (shear + swapped(plan, shear))
        turn_by = ocean_dt * spin * swapped(plan, center + other[flat, :])
        value = keep[0:1, :] * (center + jnp.where(zonal, turn_by, -turn_by)) * sea[flat, :]
        if last:
            ocean_out[row] = value[:, : 2 * plan.depth]
        else:
            ocean_out[flat, :] = value
        new.append(value)
    if last:
        copies = [pltpu.make_async_copy(ocean_out, ocean_far, done.at[0])]
        copies[0].start()

    total = None
    wet = jnp.concatenate([sea[...], sea[...]], axis=1)
    place = lax.broadcasted_iota(jnp.int32, (8, 256), 0)
    at_first, at_last = place == 0, place == 7
    for number, start in enumerate(range(0, plan.spectral, 256)):
        lanes = slice(start, start + 256)
        table = jnp.concatenate(
            [grow[(2 * number + k) * 256 : (2 * number + k + 1) * 256, :] for k in range(2)], axis=1
        )
        from_edges = jnp.concatenate(extra[2 * number : 2 * number + 2], axis=1)
        parts = []
        for row in range(rows):
            west = jnp.where(at_first, from_edges[row : row + 1, :], 0.0)
            east = jnp.where(at_last, from_edges[rows + row : rows + row + 1, :], 0.0)
            parts += [
                turned[row, 0:8, lanes] + west,
                turned[row, 8 : cols - 8, lanes],
                turned[row, cols - 8 :, lanes] + east,
            ]
        grown = jnp.concatenate(parts, axis=0) * (wet + dot(at_waves, table))
        waves_out[:, :, lanes] = grown.reshape(rows, cols, 256)
        if last:
            copy = pltpu.make_async_copy(
                waves_out.at[:, :, lanes], waves_far.at[:, :, lanes], done.at[number + 1]
            )
            copy.start()
            copies.append(copy)
        else:
            product = stokes_product(grown, stokes[lanes, :])
            total = product if total is None else total + product
    if last:
        for copy in copies:
            copy.wait()
        return
    ocean = jnp.concatenate(new, axis=0)
    send_parts(
        plan, section, even, waves_out, ocean, total, permute_t[...], packed_out, sec_out, lat_out
    )


def per_device(plan, axes, spectra, turning, currents, drag_rates, land_mask, ocean_target):
    tables = [jnp.asarray(table) for table in build_tables(NFREQ, NDIR, drag_rates.shape[0])]
    columns, rows, cols, spectral = plan.columns, plan.rows, plan.cols, plan.spectral
    shape = jax.ShapeDtypeStruct
    params = pltpu.CompilerParams(vmem_limit_bytes=32 * 1024 * 1024)
    messages = [shape((size, LANES), F32) for size in plan.sec_rows] + [
        shape((cols, spectral // 2 + LANES), F32)
    ] * 2
    state = shape((columns, LANES), F32)
    field = shape(spectra.shape, F32)
    square = shape((columns, columns), BF16)
    edge = pltpu.VMEM((plan.tiles * rows + 8, LANES), F32)
    coupled = pltpu.VMEM((columns, LANES), F32)
    spans = spectral // 256

    def call(kernel, outs, scratch, *args, space_in=pltpu.VMEM, space_out=pltpu.VMEM):
        return pl.pallas_call(
            kernel,
            out_shape=outs,
            in_specs=[pl.BlockSpec(memory_space=space_in)] * len(args),
            out_specs=[pl.BlockSpec(memory_space=space_out)] * len(outs),
            scratch_shapes=scratch,
            compiler_params=params,
        )(*args)

    def exchange(sent):
        near = [(i, i ^ 1) for i in range(plan.bands) if i ^ 1 < plan.bands]
        far = [(i, ((i + 1) ^ 1) - 1) for i in range(1, plan.bands) if ((i + 1) ^ 1) - 1 < plan.bands]
        got = [
            lax.ppermute(message, axes[1], list(enumerate(table)))
            for message, table in zip(sent, plan.exchanges)
        ]
        return got, lax.ppermute(sent[-2], axes[0], near), lax.ppermute(sent[-1], axes[0], far)

    waves, ocean, permute, permute_t, turn, turn_edge, sea, keep, stokes, rates, grow, packed, *sent = call(
        functools.partial(first_kernel, plan, axes),
        [field, state, square, square, state, shape((2 * rows, LANES), F32), state]
        + [shape((8, LANES), F32)]
        + [shape(table.shape, table.dtype) for table in tables]
        + [state]
        + messages,
        [
            pltpu.VMEM(turning.shape, F32),
            pltpu.VMEM(currents.shape, F32),
            pltpu.VMEM(drag_rates.shape, F32),
            pltpu.VMEM(land_mask.shape, jnp.int32),
            pltpu.VMEM(ocean_target.shape, jnp.int32),
            pltpu.SemaphoreType.DMA((9,)),
        ],
        *[
            pltpu.with_memory_space_constraint(array, pltpu.HBM)
            for array in (
                spectra,
                turning,
                currents,
                drag_rates,
                land_mask,
                ocean_target,
                *tables,
            )
        ],
        space_in=pltpu.HBM,
    )
    for step in range(STEPS):
        last = step == STEPS - 1
        got, near, far = exchange(sent)
        (turned,) = call(
            functools.partial(move_kernel, plan, axes), [field], [], waves, turn, rates, near, far
        )
        result = call(
            functools.partial(couple_kernel, plan, axes, last),
            [field, shape(currents.shape, F32)] if last else [field, state, state] + messages,
            [coupled, edge, edge]
            + (
                [
                    pltpu.VMEM(spectra.shape, F32),
                    pltpu.VMEM(currents.shape, F32),
                    pltpu.SemaphoreType.DMA((1 + spans,)),
                ]
                if last
                else []
            ),
            turned,
            ocean,
            packed,
            permute,
            permute_t,
            turn_edge,
            sea,
            keep,
            stokes,
            rates,
            grow,
            *got,
            near,
            far,
            space_out=pltpu.HBM if last else pltpu.VMEM,
        )
        waves, ocean = result[:2]
        if not last:
            packed, *sent = result[2:]
    return waves, ocean


def solution(mesh):
    sections, bands = mesh.shape["sec"], mesh.shape["lat"]

    def local(spectra, turning, currents, drag_rates, land_mask, ocean_target):
        rows, cols, spectral = spectra.shape
        plan = Plan(sections, bands, rows, cols, spectral, drag_rates.shape[0])
        return per_device(
            plan, ("lat", "sec"), spectra, turning, currents, drag_rates, land_mask, ocean_target
        )

    return jax.shard_map(
        local,
        mesh=mesh,
        in_specs=(
            P("lat", "sec", None),
            P("lat", "sec"),
            P("lat", "sec", None),
            P(),
            P("lat", "sec"),
            P("lat", "sec"),
        ),
        out_specs=(P("lat", "sec", None), P("lat", "sec", None)),
        check_vma=False,
    )
```

```python
import functools
import math

import jax
import jax.numpy as jnp
import ml_dtypes
import numpy as np
from jax import lax
from jax.experimental import pallas as pl
from jax.experimental.pallas import tpu as pltpu
from jax.sharding import PartitionSpec as P

NFREQ = 24
NDIR = 32
STEPS = 3

stokes_scale = 0.1
ocean_dt = 0.3
current_gain = 0.2

LANES = 128
F32 = jnp.float32
BF16 = jnp.bfloat16


def split_halves(table):
    high = table.astype(ml_dtypes.bfloat16)
    low = (table - high.astype(np.float64)).astype(ml_dtypes.bfloat16)
    return high, low


def build_tables(nfreq, ndir, ndepth):
    fraction = np.arange(nfreq) / (nfreq - 1)
    angles = (np.arange(ndir) + 0.5) * (2.0 * math.pi / ndir)
    east_part, north_part = np.cos(angles), np.sin(angles)
    courant = 0.1 + 0.3 * fraction
    depth_level = 0.5 + (ndepth - 2) * (1.0 - fraction)
    weights = np.maximum(1.0 - np.abs(np.arange(ndepth)[None, :] - depth_level[:, None]), 0.0)
    mean_weights = weights / weights.sum(axis=1, keepdims=True)
    x_rate = np.abs(courant[:, None] * east_part[None, :]).reshape(-1)
    y_rate = np.abs(courant[:, None] * north_part[None, :]).reshape(-1)
    turn_gain = np.repeat(1.0 - 0.5 * fraction, ndir)
    rates = np.stack([1.0 - x_rate - y_rate, x_rate, y_rate, turn_gain] * 2).astype(np.float32)
    compass = np.stack([east_part, north_part])
    stokes = (stokes_scale * weights[:, None, None, :] * compass.T[None, :, :, None]).reshape(
        nfreq * ndir, 2 * ndepth
    )
    growth = current_gain * (1.0 + fraction)
    grow = (
        growth[None, None, :, None] * mean_weights.T[None, :, :, None] * compass[:, None, None, :]
    ).reshape(2 * ndepth, nfreq * ndir)
    stokes_high, stokes_low = split_halves(stokes)
    grow_high, grow_low = split_halves(grow)
    return (
        np.concatenate([stokes_high, stokes_low], axis=1),
        rates,
        np.concatenate([grow_high, grow_high, grow_low, grow_low], axis=0)
        .reshape(8 * ndepth, -1, LANES)
        .transpose(1, 0, 2)
        .reshape(-1, LANES),
    )


class Plan:
    def __init__(self, sections, bands, rows, cols, spectral, depth):
        self.sections, self.bands = sections, bands
        self.rows, self.cols, self.spectral, self.depth = rows, cols, spectral, depth
        self.columns = rows * cols
        self.chunk = self.columns // sections
        self.tiles = spectral // LANES
        self.edge = ((self.tiles // 2 + 1) * rows + 7) // 8 * 8
        self.relay = sections % 4 == 0
        self.quad = 4 if self.relay else 1
        self.hops = [
            (hop, flip)
            for hop in range(1, sections // self.quad)
            for flip in ((3, 1, 2, 0) if self.relay else (0,))
        ]
        self.direct = [self.table(*hop) for hop in self.hops]
        self.edges = [
            any(abs(target - i) == 1 for i, target in table) for table in self.direct
        ]
        self.sizes = [self.chunk + (self.edge if edge else 0) for edge in self.edges]
        if self.relay:
            self.sizes = [2 * (self.chunk + self.edge), self.chunk] + self.sizes

    def table(self, hop, flip):
        return [(i, self.partner(i, hop, flip, divmod)[0]) for i in range(self.sections)]

    def partner(self, section, hop, flip, divide=lambda a, b: (lax.div(a, b), lax.rem(a, b))):
        groups = self.sections // self.quad
        high, low = divide(section, self.quad)
        if flip & 1:
            low = low + 1 - 2 * divide(low, 2)[1]
        if flip & 2:
            low = low + 2 - 4 * divide(low, 2)[0]
        return tuple(
            divide(high + shift, groups)[1] * self.quad + low for shift in (hop, groups - hop)
        )

    def received(self, section, messages):
        parts = []
        if self.relay:
            from_x, from_y = messages[:2]
            parts = [
                (self.partner(section, 0, 1)[1], from_x, 0, self.chunk),
                (self.partner(section, 0, 2)[1], from_y, 0, None),
                (self.partner(section, 0, 3)[1], from_y, self.chunk, 2 * self.chunk),
            ]
            messages = messages[2:]
        for message, hop, edge in zip(messages, self.hops, self.edges):
            parts.append((self.partner(section, *hop)[1], message, 0, self.chunk if edge else None))
        return parts

    def sent(self, section, messages):
        parts = []
        if self.relay:
            to_x, to_y = messages[:2]
            parts = [
                (self.partner(section, 0, 1)[0], to_x, 0, self.chunk),
                (self.partner(section, 0, 2)[0], to_y, 0, None),
                (
                    self.partner(section, 0, 3)[0],
                    to_x,
                    self.chunk + self.edge,
                    2 * self.chunk + self.edge,
                ),
            ]
            messages = messages[2:]
        for message, hop, edge in zip(messages, self.hops, self.edges):
            parts.append((self.partner(section, *hop)[0], message, 0, self.chunk if edge else None))
        return parts


def lane_of(shape):
    return lax.broadcasted_iota(jnp.int32, shape, len(shape) - 1)


def dot(a, b):
    return jnp.dot(a, b, preferred_element_type=F32)


def split_value(value):
    high = value.astype(BF16).astype(F32)
    return jnp.where(lane_of(value.shape) < LANES // 2, high, value - high).astype(BF16)


def stokes_product(part, table):
    high = part.astype(BF16)
    low = (part - high.astype(F32)).astype(BF16)
    return dot(jnp.concatenate([high, low], axis=0), table)


def packed_half(edge, tile, half, ahead, forward):
    first = edge[:, tile * LANES : (tile + 1) * LANES]
    second = edge[:, (tile + half) * LANES : (tile + half + 1) * LANES]
    keep = jnp.where(ahead, 1, 0) == jnp.where(forward, 1, 0)
    return jnp.where(keep, first, pltpu.roll(second, NDIR // 2, 1))


def send_parts(plan, section, even, waves, ocean, total, permute_t, packed_out, sec_out, lat_out):
    chunk, tiles, rows, cols = plan.chunk, plan.tiles, plan.rows, plan.cols
    lane = lane_of((plan.columns, LANES))
    near, far = lat_out
    sea_rows = ocean.reshape(rows, cols, LANES)
    half = tiles // 2
    masks = Directions((cols, LANES))
    for out, northward in ((far, jnp.logical_not(even)), (near, even)):
        edge = jnp.where(northward, waves[rows - 1], waves[0])
        for tile in range(half):
            out[:, tile * LANES : (tile + 1) * LANES] = packed_half(
                edge, tile, half, masks.northward, northward
            )
        out[:, plan.spectral // 2 :] = jnp.where(northward, sea_rows[rows - 1], sea_rows[0])
    moments = total[: plan.columns] + total[plan.columns :]
    moments = moments + pltpu.roll(moments, LANES // 2, 1)
    ordered = dot(permute_t, split_value(moments))
    ordered = ordered + pltpu.roll(ordered, LANES // 2, 1)
    packed_out[...] = jnp.where(lane < LANES // 2, ocean, ordered)
    for target, out, at, edge_at in plan.sent(section, sec_out):
        out[at : at + chunk, :] = packed_out[pl.ds(pl.multiple_of(target * chunk, 8), chunk), :]
        if edge_at is None:
            continue
        eastward = target == section + 1
        for row in range(rows):
            edge = jnp.where(eastward, waves[row, cols - 1 : cols, :], waves[row, 0:1, :])
            for tile in range(half):
                place = edge_at + tile * rows + row
                out[place : place + 1, :] = packed_half(
                    edge, tile, half, masks.eastward[0:1, :], eastward
                )
            place = edge_at + half * rows + row
            out[place : place + 1, :] = jnp.where(
                eastward, sea_rows[row, cols - 1 : cols, :], sea_rows[row, 0:1, :]
            )


def relay_kernel(plan, from_x, to_y, out):
    out[0 : plan.chunk, :] = to_y[...]
    out[plan.chunk :, :] = from_x[plan.chunk + plan.edge :, :]


def first_kernel(plan, axes, *refs):
    waves_in, turning_in, currents_in, drag_in, mask_in, target_in = refs[:6]
    tables_in, refs = refs[6:9], refs[9:]
    waves, ocean_out, permute_out, permute_t_out, turn_out, turn_edge_out = refs[:6]
    sea_out, keep_out, tables_out, packed_out, refs = refs[6], refs[7], refs[8:11], refs[11], refs[12:]
    count = len(plan.sizes)
    sec_out, lat_out, refs = refs[:count], refs[count : count + 2], refs[count + 2 :]
    turning, currents, drag, mask, target, done = refs
    pairs = [
        (target_in, target),
        (turning_in, turning),
        (mask_in, mask),
        (drag_in, drag),
        (waves_in, waves),
        (tables_in[0], tables_out[0]),
        (currents_in, currents),
        (tables_in[1], tables_out[1]),
        (tables_in[2], tables_out[2]),
    ]
    copies = [pltpu.make_async_copy(a, b, done.at[k]) for k, (a, b) in enumerate(pairs)]
    for copy in copies:
        copy.start()
    section, band = lax.axis_index(axes[1]), lax.axis_index(axes[0])
    even = lax.rem(band, 2) == 0
    columns, rows = plan.columns, plan.rows
    across = lane_of((columns, columns))
    down = lax.broadcasted_iota(jnp.int32, (columns, columns), 0)
    here = across == down

    def row_of(ref):
        return jnp.concatenate([ref[row : row + 1, :] for row in range(rows)], axis=1)

    def column_of(row):
        spread = jnp.broadcast_to(row, (columns, columns))
        return jnp.sum(jnp.where(here, spread, jnp.zeros_like(spread)), axis=1, keepdims=True)

    for copy in copies[:4]:
        copy.wait()
    sea = column_of(row_of(mask).astype(F32))
    target_row = row_of(target).astype(F32)
    target_col = column_of(target_row)
    same = target_col == target_row
    rank_col = jnp.sum(jnp.where(same & (across < down), 1.0, 0.0), axis=1, keepdims=True)
    rank_row = jnp.sum(jnp.where(same & (down < across), 1.0, 0.0), axis=0, keepdims=True)
    slot_col = target_col * float(plan.chunk) + rank_col
    slot_row = target_row * float(plan.chunk) + rank_row
    permute_out[...] = jnp.where(slot_col == across.astype(F32), sea, 0.0).astype(BF16)
    permute_t = jnp.where(slot_row == down.astype(F32), 1.0, 0.0).astype(BF16)
    permute_t_out[...] = permute_t
    turn = jnp.broadcast_to(column_of(row_of(turning)), (columns, LANES))
    turn_out[...] = turn
    cols = plan.cols
    for row in range(rows):
        turn_edge_out[row : row + 1, :] = turn[row * cols : row * cols + 1, :]
        turn_edge_out[rows + row : rows + row + 1, :] = turn[(row + 1) * cols - 1 : (row + 1) * cols, :]
    sea_out[...] = jnp.broadcast_to(sea, (columns, LANES))
    keep = 1.0 - drag[...].reshape(1, plan.depth)
    blank = jnp.zeros((1, LANES - 2 * plan.depth), F32)
    keep_out[...] = jnp.broadcast_to(jnp.concatenate([keep, keep, blank], axis=1), (8, LANES))
    for copy in copies[4:7]:
        copy.wait()
    flat = currents[...].reshape(columns, 2 * plan.depth)
    ocean = jnp.concatenate([flat, jnp.zeros((columns, LANES - 2 * plan.depth), F32)], axis=1)
    ocean_out[...] = ocean
    total = None
    for start in range(0, plan.spectral, 256):
        part = waves[:, :, start : start + 256].reshape(columns, 256)
        product = stokes_product(part, tables_out[0][start : start + 256, :])
        total = product if total is None else total + product
    send_parts(
        plan, section, even, waves, ocean, total, permute_t, packed_out, sec_out, lat_out
    )
    for copy in copies[7:]:
        copy.wait()


class Directions:
    def __init__(self, shape):
        direction = lax.rem(lane_of(shape), NDIR)
        self.eastward = (direction < NDIR // 4) | (direction >= 3 * NDIR // 4)
        self.northward = direction < NDIR // 2
        self.first, self.final = direction == 0, direction == NDIR - 1

    def turned(self, moved, rate, gain):
        behind = jnp.where(
            self.first, pltpu.roll(moved, LANES - (NDIR - 1), 1), pltpu.roll(moved, 1, 1)
        )
        forward = jnp.where(
            self.final, pltpu.roll(moved, NDIR - 1, 1), pltpu.roll(moved, LANES - 1, 1)
        )
        return moved - jnp.abs(rate) * gain * (moved - jnp.where(rate > 0.0, behind, forward))


def move_kernel(plan, axes, *refs):
    waves, turn, rates, near, far, turned_out = refs
    even = lax.rem(lax.axis_index(axes[0]), 2) == 0
    rows, cols, tiles = plan.rows, plan.cols, plan.tiles
    block = (cols, LANES)
    masks = Directions(block)
    place = lax.broadcasted_iota(jnp.int32, block, 0)
    outside = place == jnp.where(masks.eastward, 0, cols - 1)
    for tile in range(tiles):
        lanes = slice(tile * LANES, (tile + 1) * LANES)
        stay, along_x, along_y, gain = (rates[k : k + 1, lanes] for k in range(4))
        along_x = jnp.where(outside, 0.0, along_x)
        half = tile % (tiles // 2)
        half = slice(half * LANES, (half + 1) * LANES)
        south_edge = jnp.where(even, far[:, half], near[:, half])
        north_edge = jnp.where(even, near[:, half], far[:, half])
        if tile >= tiles // 2:
            south_edge = pltpu.roll(south_edge, LANES - NDIR // 2, 1)
            north_edge = pltpu.roll(north_edge, LANES - NDIR // 2, 1)
        for row in range(rows):
            center = waves[row, :, lanes]
            south = waves[row - 1, :, lanes] if row else south_edge
            north = waves[row + 1, :, lanes] if row < rows - 1 else north_edge
            moved = (
                stay * center
                + along_x
                * jnp.where(
                    masks.eastward, pltpu.roll(center, 1, 0), pltpu.roll(center, cols - 1, 0)
                )
                + along_y * jnp.where(masks.northward, south, north)
            )
            rate = turn[row * cols : (row + 1) * cols, :]
            turned_out[row, :, lanes] = masks.turned(moved, rate, gain)


def swapped(plan, value):
    half = plan.depth
    zonal = lane_of(value.shape) < half
    return jnp.where(zonal, pltpu.roll(value, LANES - half, 1), pltpu.roll(value, half, 1))


def couple_kernel(plan, axes, last, *refs):
    turned, ocean_in, packed_in, permute, permute_t, turn_edge, sea, keep = refs[:8]
    stokes, rates, grow, refs = refs[8], refs[9], refs[10], refs[11:]
    count = len(plan.sizes)
    sec_in, near, far, refs = refs[:count], refs[count], refs[count + 1], refs[count + 2 :]
    if last:
        waves_far, ocean_far, coupled, west_edge, east_edge, waves_out, ocean_out, done = refs
    else:
        waves_out, ocean_out, packed_out = refs[:3]
        sec_out, lat_out = refs[3 : count + 3], refs[count + 3 : count + 5]
        coupled, west_edge, east_edge = refs[count + 5 :]
    section, band = lax.axis_index(axes[1]), lax.axis_index(axes[0])
    even = lax.rem(band, 2) == 0
    rows, cols, chunk, columns, tiles = plan.rows, plan.cols, plan.chunk, plan.columns, plan.tiles

    own = pl.ds(pl.multiple_of(section * chunk, 8), chunk)
    coupled[own, :] = packed_in[own, :]
    west_edge[...] = jnp.zeros_like(west_edge)
    east_edge[...] = jnp.zeros_like(east_edge)
    for source, message, at, edge_at in plan.received(section, sec_in):
        coupled[pl.ds(pl.multiple_of(source * chunk, 8), chunk), :] = message[at : at + chunk, :]
        if edge_at is None:
            continue

        @pl.when(source == section + 1)
        def _():
            east_edge[...] = message[edge_at : edge_at + plan.edge, :]

        @pl.when(source == section - 1)
        def _():
            west_edge[...] = message[edge_at : edge_at + plan.edge, :]

    arrived = coupled[...]
    other = pltpu.roll(arrived, LANES // 2, 1)
    lane = lane_of((columns, LANES))
    both = jnp.where(lane < LANES // 2, arrived, other)
    at_waves = dot(permute[...], split_value(both)).astype(BF16)
    at_waves = jnp.concatenate([at_waves, at_waves], axis=1)

    masks = Directions((2 * rows, LANES))
    westmost = lax.broadcasted_iota(jnp.int32, (2 * rows, LANES), 0) < rows
    reached = jnp.where(masks.eastward, 1, 0) == jnp.where(westmost, 1, 0)
    extra = []
    for tile in range(tiles):
        lanes = slice(tile * LANES, (tile + 1) * LANES)
        edge = tile % (tiles // 2)
        edge = slice(edge * rows, (edge + 1) * rows)
        came = jnp.concatenate([west_edge[edge, :], east_edge[edge, :]], axis=0)
        if tile >= tiles // 2:
            came = pltpu.roll(came, LANES - NDIR // 2, 1)
        moved = rates[1:2, lanes] * jnp.where(reached, came, 0.0)
        extra.append(masks.turned(moved, turn_edge[...], rates[3:4, lanes]))

    block = (cols, LANES)
    zonal = lane_of(block) < plan.depth
    place = lax.broadcasted_iota(jnp.int32, block, 0)
    at_west, at_east = place == 0, place == cols - 1
    half = slice(plan.spectral // 2, plan.spectral // 2 + LANES)
    south_edge = jnp.where(even, far[:, half], near[:, half])
    north_edge = jnp.where(even, near[:, half], far[:, half])
    new = []
    for row in range(rows):
        flat = slice(row * cols, (row + 1) * cols)
        edge = slice(tiles // 2 * rows + row, tiles // 2 * rows + row + 1)
        center = ocean_in[flat, :]
        west = jnp.where(at_west, west_edge[edge, :], pltpu.roll(center, 1, 0))
        east = jnp.where(at_east, east_edge[edge, :], pltpu.roll(center, cols - 1, 0))
        south = ocean_in[(row - 1) * cols : row * cols, :] if row else south_edge
        north = ocean_in[(row + 1) * cols : (row + 2) * cols, :] if row < rows - 1 else north_edge
        shear = 0.5 * jnp.where(zonal, south - north, east - west)
        y = (band * rows + row).astype(F32)
        spin = 0.2 + 0.6 * y / float(plan.bands * rows) + (shear + swapped(plan, shear))
        turn_by = ocean_dt * spin * swapped(plan, center + other[flat, :])
        value = keep[0:1, :] * (center + jnp.where(zonal, turn_by, -turn_by)) * sea[flat, :]
        if last:
            ocean_out[row] = value[:, : 2 * plan.depth]
        else:
            ocean_out[flat, :] = value
        new.append(value)
    if last:
        copies = [pltpu.make_async_copy(ocean_out, ocean_far, done.at[0])]
        copies[0].start()

    total = None
    wet = jnp.concatenate([sea[...], sea[...]], axis=1)
    place = lax.broadcasted_iota(jnp.int32, (8, 256), 0)
    at_first, at_last = place == 0, place == 7
    for number, start in enumerate(range(0, plan.spectral, 256)):
        lanes = slice(start, start + 256)
        table = jnp.concatenate(
            [grow[(2 * number + k) * 256 : (2 * number + k + 1) * 256, :] for k in range(2)], axis=1
        )
        from_edges = jnp.concatenate(extra[2 * number : 2 * number + 2], axis=1)
        parts = []
        for row in range(rows):
            west = jnp.where(at_first, from_edges[row : row + 1, :], 0.0)
            east = jnp.where(at_last, from_edges[rows + row : rows + row + 1, :], 0.0)
            parts += [
                turned[row, 0:8, lanes] + west,
                turned[row, 8 : cols - 8, lanes],
                turned[row, cols - 8 :, lanes] + east,
            ]
        grown = jnp.concatenate(parts, axis=0) * (wet + dot(at_waves, table))
        waves_out[:, :, lanes] = grown.reshape(rows, cols, 256)
        if last:
            copy = pltpu.make_async_copy(
                waves_out.at[:, :, lanes], waves_far.at[:, :, lanes], done.at[number + 1]
            )
            copy.start()
            copies.append(copy)
        else:
            product = stokes_product(grown, stokes[lanes, :])
            total = product if total is None else total + product
    if last:
        for copy in copies:
            copy.wait()
        return
    ocean = jnp.concatenate(new, axis=0)
    send_parts(
        plan, section, even, waves_out, ocean, total, permute_t[...], packed_out, sec_out, lat_out
    )


def per_device(plan, axes, spectra, turning, currents, drag_rates, land_mask, ocean_target):
    tables = [jnp.asarray(table) for table in build_tables(NFREQ, NDIR, drag_rates.shape[0])]
    columns, rows, cols, spectral = plan.columns, plan.rows, plan.cols, plan.spectral
    shape = jax.ShapeDtypeStruct
    params = pltpu.CompilerParams(vmem_limit_bytes=32 * 1024 * 1024)
    messages = [shape((size, LANES), F32) for size in plan.sizes] + [
        shape((cols, spectral // 2 + LANES), F32)
    ] * 2
    state = shape((columns, LANES), F32)
    field = shape(spectra.shape, F32)
    square = shape((columns, columns), BF16)
    edge = pltpu.VMEM((plan.edge, LANES), F32)
    coupled = pltpu.VMEM((columns, LANES), F32)
    spans = spectral // 256

    def call(kernel, outs, scratch, *args, space_in=pltpu.VMEM, space_out=pltpu.VMEM):
        return pl.pallas_call(
            kernel,
            out_shape=outs,
            in_specs=[pl.BlockSpec(memory_space=space_in)] * len(args),
            out_specs=[pl.BlockSpec(memory_space=space_out)] * len(outs),
            scratch_shapes=scratch,
            compiler_params=params,
        )(*args)

    def exchange(sent):
        near = [(i, i ^ 1) for i in range(plan.bands) if i ^ 1 < plan.bands]
        far = [(i, ((i + 1) ^ 1) - 1) for i in range(1, plan.bands) if ((i + 1) ^ 1) - 1 < plan.bands]
        sent, near_out, far_out = sent[:-2], sent[-2], sent[-1]
        got = []
        if plan.relay:
            to_x, to_y, *sent = sent
            got.append(lax.ppermute(to_x, axes[1], plan.table(0, 1)))
        far_in = lax.ppermute(far_out, axes[0], far)
        near_in = lax.ppermute(near_out, axes[0], near)
        if plan.relay:
            (to_y,) = call(
                functools.partial(relay_kernel, plan),
                [shape((2 * plan.chunk + plan.edge, LANES), F32)],
                [],
                got[0],
                to_y,
            )
            got.append(lax.ppermute(to_y, axes[1], plan.table(0, 2)))
        got += [
            lax.ppermute(message, axes[1], table) for message, table in zip(sent, plan.direct)
        ]
        return got, near_in, far_in

    waves, ocean, permute, permute_t, turn, turn_edge, sea, keep, stokes, rates, grow, packed, *sent = call(
        functools.partial(first_kernel, plan, axes),
        [field, state, square, square, state, shape((2 * rows, LANES), F32), state]
        + [shape((8, LANES), F32)]
        + [shape(table.shape, table.dtype) for table in tables]
        + [state]
        + messages,
        [
            pltpu.VMEM(turning.shape, F32),
            pltpu.VMEM(currents.shape, F32),
            pltpu.VMEM(drag_rates.shape, F32),
            pltpu.VMEM(land_mask.shape, jnp.int32),
            pltpu.VMEM(ocean_target.shape, jnp.int32),
            pltpu.SemaphoreType.DMA((9,)),
        ],
        *[
            pltpu.with_memory_space_constraint(array, pltpu.HBM)
            for array in (
                spectra,
                turning,
                currents,
                drag_rates,
                land_mask,
                ocean_target,
                *tables,
            )
        ],
        space_in=pltpu.HBM,
    )
    for step in range(STEPS):
        last = step == STEPS - 1
        got, near, far = exchange(sent)
        (turned,) = call(
            functools.partial(move_kernel, plan, axes), [field], [], waves, turn, rates, near, far
        )
        result = call(
            functools.partial(couple_kernel, plan, axes, last),
            [field, shape(currents.shape, F32)] if last else [field, state, state] + messages,
            [coupled, edge, edge]
            + (
                [
                    pltpu.VMEM(spectra.shape, F32),
                    pltpu.VMEM(currents.shape, F32),
                    pltpu.SemaphoreType.DMA((1 + spans,)),
                ]
                if last
                else []
            ),
            turned,
            ocean,
            packed,
            permute,
            permute_t,
            turn_edge,
            sea,
            keep,
            stokes,
            rates,
            grow,
            *got,
            near,
            far,
            space_out=pltpu.HBM if last else pltpu.VMEM,
        )
        waves, ocean = result[:2]
        if not last:
            packed, *sent = result[2:]
    return waves, ocean


def solution(mesh):
    sections, bands = mesh.shape["sec"], mesh.shape["lat"]

    def local(spectra, turning, currents, drag_rates, land_mask, ocean_target):
        rows, cols, spectral = spectra.shape
        plan = Plan(sections, bands, rows, cols, spectral, drag_rates.shape[0])
        return per_device(
            plan, ("lat", "sec"), spectra, turning, currents, drag_rates, land_mask, ocean_target
        )

    return jax.shard_map(
        local,
        mesh=mesh,
        in_specs=(
            P("lat", "sec", None),
            P("lat", "sec"),
            P("lat", "sec", None),
            P(),
            P("lat", "sec"),
            P("lat", "sec"),
        ),
        out_specs=(P("lat", "sec", None), P("lat", "sec", None)),
        check_vma=False,
    )
```

```python
import functools
import math

import jax
import jax.numpy as jnp
import ml_dtypes
import numpy as np
from jax import lax
from jax.experimental import pallas as pl
from jax.experimental.pallas import tpu as pltpu
from jax.sharding import PartitionSpec as P

NFREQ = 24
NDIR = 32
STEPS = 3

stokes_scale = 0.1
ocean_dt = 0.3
current_gain = 0.2

LANES = 128
F32 = jnp.float32
BF16 = jnp.bfloat16


def split_halves(table):
    high = table.astype(ml_dtypes.bfloat16)
    low = (table - high.astype(np.float64)).astype(ml_dtypes.bfloat16)
    return high, low


def build_tables(nfreq, ndir, ndepth):
    fraction = np.arange(nfreq) / (nfreq - 1)
    angles = (np.arange(ndir) + 0.5) * (2.0 * math.pi / ndir)
    east_part, north_part = np.cos(angles), np.sin(angles)
    courant = 0.1 + 0.3 * fraction
    depth_level = 0.5 + (ndepth - 2) * (1.0 - fraction)
    weights = np.maximum(1.0 - np.abs(np.arange(ndepth)[None, :] - depth_level[:, None]), 0.0)
    mean_weights = weights / weights.sum(axis=1, keepdims=True)
    x_rate = np.abs(courant[:, None] * east_part[None, :]).reshape(-1)
    y_rate = np.abs(courant[:, None] * north_part[None, :]).reshape(-1)
    turn_gain = np.repeat(1.0 - 0.5 * fraction, ndir)
    rates = np.stack([1.0 - x_rate - y_rate, x_rate, y_rate, turn_gain] * 2).astype(np.float32)
    compass = np.stack([east_part, north_part])
    stokes = (stokes_scale * weights[:, None, None, :] * compass.T[None, :, :, None]).reshape(
        nfreq * ndir, 2 * ndepth
    )
    growth = current_gain * (1.0 + fraction)
    grow = (
        growth[None, None, :, None] * mean_weights.T[None, :, :, None] * compass[:, None, None, :]
    ).reshape(2 * ndepth, nfreq * ndir)
    stokes_high, stokes_low = split_halves(stokes)
    grow_high, grow_low = split_halves(grow)
    return (
        np.concatenate([stokes_high, stokes_low], axis=1),
        rates,
        np.concatenate([grow_high, grow_high, grow_low, grow_low], axis=0)
        .reshape(8 * ndepth, -1, LANES)
        .transpose(1, 0, 2)
        .reshape(-1, LANES),
    )


class Plan:
    def __init__(self, sections, bands, rows, cols, spectral, depth):
        self.sections, self.bands = sections, bands
        self.rows, self.cols, self.spectral, self.depth = rows, cols, spectral, depth
        self.columns = rows * cols
        self.chunk = self.columns // sections
        self.tiles = spectral // LANES
        self.edge = ((self.tiles // 2 + 1) * rows + 7) // 8 * 8
        self.relay = sections % 4 == 0
        self.quad = 4 if self.relay else 1
        self.hops = [
            (hop, flip)
            for hop in range(1, sections // self.quad)
            for flip in ((3, 1, 2, 0) if self.relay else (0,))
        ]
        self.direct = [self.table(*hop) for hop in self.hops]
        self.edges = [
            any(abs(target - i) == 1 for i, target in table) for table in self.direct
        ]
        self.sizes = [self.chunk + (self.edge if edge else 0) for edge in self.edges]
        if self.relay:
            self.sizes = [2 * (self.chunk + self.edge), self.chunk] + self.sizes

    def table(self, hop, flip):
        return [(i, self.partner(i, hop, flip, divmod)[0]) for i in range(self.sections)]

    def partner(self, section, hop, flip, divide=lambda a, b: (lax.div(a, b), lax.rem(a, b))):
        groups = self.sections // self.quad
        high, low = divide(section, self.quad)
        if flip & 1:
            low = low + 1 - 2 * divide(low, 2)[1]
        if flip & 2:
            low = low + 2 - 4 * divide(low, 2)[0]
        return tuple(
            divide(high + shift, groups)[1] * self.quad + low for shift in (hop, groups - hop)
        )

    def received(self, section, messages):
        parts = []
        if self.relay:
            from_x, from_y = messages[:2]
            parts = [
                (self.partner(section, 0, 1)[1], from_x, 0, self.chunk),
                (self.partner(section, 0, 2)[1], from_y, 0, None),
                (self.partner(section, 0, 3)[1], from_y, self.chunk, 2 * self.chunk),
            ]
            messages = messages[2:]
        for message, hop, edge in zip(messages, self.hops, self.edges):
            parts.append((self.partner(section, *hop)[1], message, 0, self.chunk if edge else None))
        return parts

    def sent(self, section, messages):
        parts = []
        if self.relay:
            to_x, to_y = messages[:2]
            parts = [
                (self.partner(section, 0, 1)[0], to_x, 0, self.chunk),
                (self.partner(section, 0, 2)[0], to_y, 0, None),
                (
                    self.partner(section, 0, 3)[0],
                    to_x,
                    self.chunk + self.edge,
                    2 * self.chunk + self.edge,
                ),
            ]
            messages = messages[2:]
        for message, hop, edge in zip(messages, self.hops, self.edges):
            parts.append((self.partner(section, *hop)[0], message, 0, self.chunk if edge else None))
        return parts


def lane_of(shape):
    return lax.broadcasted_iota(jnp.int32, shape, len(shape) - 1)


def dot(a, b):
    return jnp.dot(a, b, preferred_element_type=F32)


def split_value(value):
    high = value.astype(BF16).astype(F32)
    return jnp.where(lane_of(value.shape) < LANES // 2, high, value - high).astype(BF16)


def stokes_product(part, table):
    high = part.astype(BF16)
    low = (part - high.astype(F32)).astype(BF16)
    return dot(jnp.concatenate([high, low], axis=0), table)


def packed_half(edge, tile, half, ahead, forward):
    first = edge[:, tile * LANES : (tile + 1) * LANES]
    second = edge[:, (tile + half) * LANES : (tile + half + 1) * LANES]
    keep = jnp.where(ahead, 1, 0) == jnp.where(forward, 1, 0)
    return jnp.where(keep, first, pltpu.roll(second, NDIR // 2, 1))


def fill_lat(plan, even, waves, sea_rows, lat_out):
    half = plan.tiles // 2
    masks = Directions((plan.cols, LANES))
    near, far = lat_out
    for out, northward in ((far, jnp.logical_not(even)), (near, even)):
        edge = jnp.where(northward, waves[plan.rows - 1], waves[0])
        for tile in range(half):
            out[:, tile * LANES : (tile + 1) * LANES] = packed_half(
                edge, tile, half, masks.northward, northward
            )
        out[:, plan.spectral // 2 :] = jnp.where(northward, sea_rows[plan.rows - 1], sea_rows[0])


def fill_sections(plan, section, edges, ocean, ordered, packed_out, sec_out):
    chunk, rows, cols, half = plan.chunk, plan.rows, plan.cols, plan.tiles // 2
    lane = lane_of((plan.columns, LANES))
    packed_out[...] = jnp.where(lane < LANES // 2, ocean, ordered)
    sea_rows = ocean.reshape(rows, cols, LANES)
    masks = Directions((rows, LANES))
    for target, out, at, edge_at in plan.sent(section, sec_out):
        out[at : at + chunk, :] = packed_out[pl.ds(pl.multiple_of(target * chunk, 8), chunk), :]
        if edge_at is None:
            continue
        eastward = target == section + 1
        edge = jnp.where(eastward, edges[rows:, :], edges[:rows, :])
        for tile in range(half):
            place = edge_at + tile * rows
            out[place : place + rows, :] = packed_half(edge, tile, half, masks.eastward, eastward)
        for row in range(rows):
            place = edge_at + half * rows + row
            out[place : place + 1, :] = jnp.where(
                eastward, sea_rows[row, cols - 1 : cols, :], sea_rows[row, 0:1, :]
            )


def take_sections(plan, section, packed_in, sec_in, coupled, west_edge, east_edge):
    chunk = plan.chunk
    own = pl.ds(pl.multiple_of(section * chunk, 8), chunk)
    coupled[own, :] = packed_in[own, :]
    west_edge[...] = jnp.zeros_like(west_edge)
    east_edge[...] = jnp.zeros_like(east_edge)
    for source, message, at, edge_at in plan.received(section, sec_in):
        coupled[pl.ds(pl.multiple_of(source * chunk, 8), chunk), :] = message[at : at + chunk, :]
        if edge_at is None:
            continue

        @pl.when(source == section + 1)
        def _():
            east_edge[...] = message[edge_at : edge_at + plan.edge, :]

        @pl.when(source == section - 1)
        def _():
            west_edge[...] = message[edge_at : edge_at + plan.edge, :]


def edge_part(plan, rates, turn_edge, west_edge, east_edge):
    rows, half = plan.rows, plan.tiles // 2
    shape = (2 * rows, LANES)
    masks = Directions(shape)
    westmost = lax.broadcasted_iota(jnp.int32, shape, 0) < rows
    reached = jnp.where(masks.eastward, 1, 0) == jnp.where(westmost, 1, 0)
    parts = []
    for tile in range(plan.tiles):
        lanes = slice(tile * LANES, (tile + 1) * LANES)
        edge = slice(tile % half * rows, (tile % half + 1) * rows)
        came = jnp.concatenate([west_edge[edge, :], east_edge[edge, :]], axis=0)
        if tile >= half:
            came = pltpu.roll(came, LANES - NDIR // 2, 1)
        moved = rates[1:2, lanes] * jnp.where(reached, came, 0.0)
        parts.append(masks.turned(moved, turn_edge[...], rates[3:4, lanes]))
    return parts


def ocean_step(plan, band, even, ocean_in, stokes, near, far, west_edge, east_edge, keep, sea):
    rows, cols, half = plan.rows, plan.cols, plan.tiles // 2
    block = (cols, LANES)
    zonal = lane_of(block) < plan.depth
    place = lax.broadcasted_iota(jnp.int32, block, 0)
    at_west, at_east = place == 0, place == cols - 1
    lanes = slice(plan.spectral // 2, plan.spectral // 2 + LANES)
    south_edge = jnp.where(even, far[:, lanes], near[:, lanes])
    north_edge = jnp.where(even, near[:, lanes], far[:, lanes])
    new = []
    for row in range(rows):
        flat = slice(row * cols, (row + 1) * cols)
        edge = slice(half * rows + row, half * rows + row + 1)
        center = ocean_in[flat, :]
        west = jnp.where(at_west, west_edge[edge, :], pltpu.roll(center, 1, 0))
        east = jnp.where(at_east, east_edge[edge, :], pltpu.roll(center, cols - 1, 0))
        south = ocean_in[(row - 1) * cols : row * cols, :] if row else south_edge
        north = ocean_in[(row + 1) * cols : (row + 2) * cols, :] if row < rows - 1 else north_edge
        shear = 0.5 * jnp.where(zonal, south - north, east - west)
        y = (band * rows + row).astype(F32)
        spin = 0.2 + 0.6 * y / float(plan.bands * rows) + (shear + swapped(plan, shear))
        turn_by = ocean_dt * spin * swapped(plan, center + stokes[flat, :])
        new.append(keep[0:1, :] * (center + jnp.where(zonal, turn_by, -turn_by)) * sea[flat, :])
    return new


def twice(value, axis=1):
    return jnp.concatenate([value, value], axis=axis)


def growth_table(grow, number):
    return jnp.concatenate(
        [grow[(2 * number + k) * 256 : (2 * number + k + 1) * 256, :] for k in range(2)], axis=1
    )


def currents_twice(arrived):
    other = pltpu.roll(arrived, LANES // 2, 1)
    return jnp.where(lane_of(arrived.shape) < LANES // 2, arrived, other), other


def grown_part(plan, turned, from_edges, factor, lanes):
    rows, cols = plan.rows, plan.cols
    place = lax.broadcasted_iota(jnp.int32, (8, 256), 0)
    at_first, at_last = place == 0, place == 7
    parts = []
    for row in range(rows):
        west = jnp.where(at_first, from_edges[row : row + 1, :], 0.0)
        east = jnp.where(at_last, from_edges[rows + row : rows + row + 1, :], 0.0)
        parts += [
            turned[row, 0:8, lanes] + west,
            turned[row, 8 : cols - 8, lanes],
            turned[row, cols - 8 :, lanes] + east,
        ]
    return jnp.concatenate(parts, axis=0) * factor


def relay_kernel(plan, axes, from_x, to_y, out):
    out[0 : plan.chunk, :] = to_y[...]
    out[plan.chunk :, :] = from_x[plan.chunk + plan.edge :, :]


def first_kernel(plan, axes, *refs):
    waves_in, turning_in, currents_in, drag_in, mask_in, target_in = refs[:6]
    tables_in, refs = refs[6:9], refs[9:]
    waves, ocean_out, packed_out, permute_out, order_out, permute_edge_out, order_edge_out = refs[:7]
    turn_out, turn_edge_out, sea_out, sea_order_out, sea_edge_out, keep_out = refs[7:13]
    tables_out, refs = refs[13:16], refs[16:]
    count = len(plan.sizes)
    sec_out, lat_out, refs = refs[:count], refs[count : count + 2], refs[count + 2 :]
    turning, currents, drag, mask, target, done = refs
    pairs = [
        (target_in, target),
        (turning_in, turning),
        (mask_in, mask),
        (drag_in, drag),
        (waves_in, waves),
        (tables_in[0], tables_out[0]),
        (currents_in, currents),
        (tables_in[1], tables_out[1]),
        (tables_in[2], tables_out[2]),
    ]
    copies = [pltpu.make_async_copy(a, b, done.at[k]) for k, (a, b) in enumerate(pairs)]
    for copy in copies:
        copy.start()
    section, band = lax.axis_index(axes[1]), lax.axis_index(axes[0])
    even = lax.rem(band, 2) == 0
    columns, rows, cols = plan.columns, plan.rows, plan.cols
    across = lane_of((columns, columns))
    down = lax.broadcasted_iota(jnp.int32, (columns, columns), 0)
    here = across == down

    def row_of(ref):
        return jnp.concatenate([ref[row : row + 1, :] for row in range(rows)], axis=1)

    def column_of(row):
        spread = jnp.broadcast_to(row, (columns, columns))
        return jnp.sum(jnp.where(here, spread, jnp.zeros_like(spread)), axis=1, keepdims=True)

    def edges_of(value):
        west = [value[row * cols : row * cols + 1, :] for row in range(rows)]
        east = [value[(row + 1) * cols - 1 : (row + 1) * cols, :] for row in range(rows)]
        return jnp.concatenate(west + east, axis=0)

    for copy in copies[:4]:
        copy.wait()
    sea_row = row_of(mask).astype(F32)
    sea = column_of(sea_row)
    target_row = row_of(target).astype(F32)
    target_col = column_of(target_row)
    same = target_col == target_row
    rank_col = jnp.sum(jnp.where(same & (across < down), 1.0, 0.0), axis=1, keepdims=True)
    rank_row = jnp.sum(jnp.where(same & (down < across), 1.0, 0.0), axis=0, keepdims=True)
    slot_col = target_col * float(plan.chunk) + rank_col
    slot_row = target_row * float(plan.chunk) + rank_row
    permute = jnp.where(slot_col == across.astype(F32), sea, 0.0)
    order = jnp.where(slot_row == down.astype(F32), 1.0, 0.0)
    permute_out[...] = permute.astype(BF16)
    order_out[...] = twice(order).astype(BF16)
    sea_order = jnp.sum(order * sea_row, axis=1, keepdims=True)
    sea_order_out[...] = jnp.broadcast_to(sea_order, (columns, LANES))
    edge_count = 4 * rows
    number = lax.rem(lane_of((columns, edge_count)), 2 * rows)
    wanted = lax.rem(number, rows) * cols + lax.div(number, rows) * (cols - 1)
    chosen = lax.broadcasted_iota(jnp.int32, (columns, edge_count), 0) == wanted
    order_edge_out[...] = dot(
        order.astype(BF16), jnp.where(chosen, 1.0, 0.0).astype(BF16)
    ).astype(BF16)
    number = lax.rem(lax.broadcasted_iota(jnp.int32, (edge_count, columns), 0), 2 * rows)
    wanted = lax.rem(number, rows) * cols + lax.div(number, rows) * (cols - 1)
    chosen = lane_of((edge_count, columns)) == wanted
    permute_edge_out[...] = dot(
        jnp.where(chosen, 1.0, 0.0).astype(BF16), permute.astype(BF16)
    ).astype(BF16)
    sea_out[...] = jnp.broadcast_to(sea, (columns, LANES))
    sea_edge_out[...] = edges_of(jnp.broadcast_to(sea, (columns, LANES)))
    turn = jnp.broadcast_to(column_of(row_of(turning)), (columns, LANES))
    turn_out[...] = turn
    turn_edge_out[...] = edges_of(turn)
    keep = 1.0 - drag[...].reshape(1, plan.depth)
    blank = jnp.zeros((1, LANES - 2 * plan.depth), F32)
    keep_out[...] = jnp.broadcast_to(jnp.concatenate([keep, keep, blank], axis=1), (8, LANES))
    for copy in copies[4:7]:
        copy.wait()
    flat = currents[...].reshape(columns, 2 * plan.depth)
    ocean = jnp.concatenate([flat, jnp.zeros((columns, LANES - 2 * plan.depth), F32)], axis=1)
    ocean_out[...] = ocean
    total = None
    for start in range(0, plan.spectral, 256):
        part = waves[:, :, start : start + 256].reshape(columns, 256)
        product = stokes_product(part, tables_out[0][start : start + 256, :])
        total = product if total is None else total + product
    moments = total[:columns] + total[columns:]
    moments = moments + pltpu.roll(moments, LANES // 2, 1)
    ordered = dot(order.astype(BF16), split_value(moments))
    ordered = ordered + pltpu.roll(ordered, LANES // 2, 1)
    west = [waves[row, 0:1, :] for row in range(rows)]
    east = [waves[row, cols - 1 : cols, :] for row in range(rows)]
    edges = jnp.concatenate(west + east, axis=0)
    fill_sections(plan, section, edges, ocean, ordered, packed_out, sec_out)
    fill_lat(plan, even, waves, ocean.reshape(rows, cols, LANES), lat_out)
    for copy in copies[7:]:
        copy.wait()


class Directions:
    def __init__(self, shape):
        direction = lax.rem(lane_of(shape), NDIR)
        self.eastward = (direction < NDIR // 4) | (direction >= 3 * NDIR // 4)
        self.northward = direction < NDIR // 2
        self.first, self.final = direction == 0, direction == NDIR - 1

    def turned(self, moved, rate, gain):
        behind = jnp.where(
            self.first, pltpu.roll(moved, LANES - (NDIR - 1), 1), pltpu.roll(moved, 1, 1)
        )
        forward = jnp.where(
            self.final, pltpu.roll(moved, NDIR - 1, 1), pltpu.roll(moved, LANES - 1, 1)
        )
        return moved - jnp.abs(rate) * gain * (moved - jnp.where(rate > 0.0, behind, forward))


def move_kernel(plan, axes, *refs):
    waves, turn, rates, near, far, refs = *refs[:5], refs[5:]
    if len(refs) > 1:
        order, turned_out, edge_out, sorted_out = refs
    else:
        (turned_out,) = refs
    even = lax.rem(lax.axis_index(axes[0]), 2) == 0
    rows, cols, tiles = plan.rows, plan.cols, plan.tiles
    block = (cols, LANES)
    masks = Directions(block)
    place = lax.broadcasted_iota(jnp.int32, block, 0)
    outside = place == jnp.where(masks.eastward, 0, cols - 1)
    for tile in range(tiles):
        lanes = slice(tile * LANES, (tile + 1) * LANES)
        stay, along_x, along_y, gain = (rates[k : k + 1, lanes] for k in range(4))
        along_x = jnp.where(outside, 0.0, along_x)
        half = tile % (tiles // 2)
        half = slice(half * LANES, (half + 1) * LANES)
        south_edge = jnp.where(even, far[:, half], near[:, half])
        north_edge = jnp.where(even, near[:, half], far[:, half])
        if tile >= tiles // 2:
            south_edge = pltpu.roll(south_edge, LANES - NDIR // 2, 1)
            north_edge = pltpu.roll(north_edge, LANES - NDIR // 2, 1)
        for row in range(rows):
            center = waves[row, :, lanes]
            south = waves[row - 1, :, lanes] if row else south_edge
            north = waves[row + 1, :, lanes] if row < rows - 1 else north_edge
            moved = (
                stay * center
                + along_x
                * jnp.where(
                    masks.eastward, pltpu.roll(center, 1, 0), pltpu.roll(center, cols - 1, 0)
                )
                + along_y * jnp.where(masks.northward, south, north)
            )
            rate = turn[row * cols : (row + 1) * cols, :]
            turned = masks.turned(moved, rate, gain)
            turned_out[row, :, lanes] = turned
            if len(refs) > 1:
                edge_out[row : row + 1, lanes] = turned[0:1, :]
                edge_out[rows + row : rows + row + 1, lanes] = turned[cols - 1 : cols, :]
    if len(refs) > 1:
        for start in range(0, plan.spectral, 256):
            part = turned_out[:, :, start : start + 256].reshape(plan.columns, 256)
            high = part.astype(BF16)
            low = (part - high.astype(F32)).astype(BF16)
            sorted_out[:, start : start + 256] = dot(
                order[...], jnp.concatenate([high, low], axis=0)
            )


def swapped(plan, value):
    half = plan.depth
    zonal = lane_of(value.shape) < half
    return jnp.where(zonal, pltpu.roll(value, LANES - half, 1), pltpu.roll(value, half, 1))


def send_kernel(plan, axes, *refs):
    turned_order, turned_edge, ocean_in, packed_in, permute_edge, order_edge, turn_edge = refs[:7]
    sea, sea_order, sea_edge, keep, stokes, rates, grow = refs[7:14]
    count = len(plan.sizes)
    near, far, sec_in, refs = refs[14], refs[15], refs[16 : 16 + count], refs[16 + count :]
    ocean_out, packed_out, coupled, extra_out, sec_out = *refs[:4], refs[4 : 4 + count]
    west_edge, east_edge = refs[4 + count :]
    section, band = lax.axis_index(axes[1]), lax.axis_index(axes[0])
    even = lax.rem(band, 2) == 0
    columns, rows = plan.columns, plan.rows

    take_sections(plan, section, packed_in, sec_in, coupled, west_edge, east_edge)
    both, drift = currents_twice(coupled[...])
    in_order = twice(split_value(both * sea_order[...]))
    at_edge = twice(dot(permute_edge[...], split_value(both)).astype(BF16))
    extra = edge_part(plan, rates, turn_edge, west_edge, east_edge)
    total = None
    edges = []
    wet, wet_edge = twice(sea_order[...]), twice(sea_edge[...])
    for number, start in enumerate(range(0, plan.spectral, 256)):
        lanes = slice(start, start + 256)
        table = growth_table(grow, number)
        from_edges = jnp.concatenate(extra[2 * number : 2 * number + 2], axis=1)
        extra_out[:, lanes] = from_edges
        high = from_edges.astype(BF16).astype(F32)
        halves = jnp.concatenate([high, from_edges - high], axis=0).astype(BF16)
        turned = turned_order[:, lanes] + dot(order_edge[...], halves)
        grown = turned * (wet + dot(in_order, table))
        product = stokes_product(grown, stokes[lanes, :])
        total = product if total is None else total + product
        edges.append(
            (turned_edge[:, lanes] + from_edges)
            * (wet_edge + dot(at_edge, table)[: 2 * rows, :])
        )
    new = ocean_step(
        plan, band, even, ocean_in, drift, near, far, west_edge, east_edge, keep, sea
    )
    ocean = jnp.concatenate(new, axis=0)
    ocean_out[...] = ocean
    moments = total[:columns] + total[columns:]
    moments = moments + pltpu.roll(moments, LANES // 2, 1)
    fill_sections(
        plan, section, jnp.concatenate(edges, axis=1), ocean, moments, packed_out, sec_out
    )


def grow_kernel(plan, axes, *refs):
    turned, extra, coupled, permute, sea, grow, ocean, waves_out, *lat_out = refs
    even = lax.rem(lax.axis_index(axes[0]), 2) == 0
    both, _ = currents_twice(coupled[...])
    at_waves = twice(dot(permute[...], split_value(both)).astype(BF16))
    wet = twice(sea[...])
    for number, start in enumerate(range(0, plan.spectral, 256)):
        lanes = slice(start, start + 256)
        factor = wet + dot(at_waves, growth_table(grow, number))
        grown = grown_part(plan, turned, extra[:, lanes], factor, lanes)
        waves_out[:, :, lanes] = grown.reshape(plan.rows, plan.cols, 256)
    sea_rows = ocean[...].reshape(plan.rows, plan.cols, LANES)
    fill_lat(plan, even, waves_out, sea_rows, lat_out)


def last_kernel(plan, axes, *refs):
    turned, ocean_in, packed_in, permute, turn_edge, sea, keep, rates, grow = refs[:9]
    count = len(plan.sizes)
    near, far, sec_in, refs = refs[9], refs[10], refs[11 : 11 + count], refs[11 + count :]
    waves_far, ocean_far, coupled, west_edge, east_edge, waves_out, ocean_out, done = refs
    section, band = lax.axis_index(axes[1]), lax.axis_index(axes[0])
    even = lax.rem(band, 2) == 0

    take_sections(plan, section, packed_in, sec_in, coupled, west_edge, east_edge)
    both, drift = currents_twice(coupled[...])
    at_waves = twice(dot(permute[...], split_value(both)).astype(BF16))
    extra = edge_part(plan, rates, turn_edge, west_edge, east_edge)
    new = ocean_step(
        plan, band, even, ocean_in, drift, near, far, west_edge, east_edge, keep, sea
    )
    for row, value in enumerate(new):
        ocean_out[row] = value[:, : 2 * plan.depth]
    copies = [pltpu.make_async_copy(ocean_out, ocean_far, done.at[0])]
    copies[0].start()
    wet = twice(sea[...])
    for number, start in enumerate(range(0, plan.spectral, 256)):
        lanes = slice(start, start + 256)
        factor = wet + dot(at_waves, growth_table(grow, number))
        from_edges = jnp.concatenate(extra[2 * number : 2 * number + 2], axis=1)
        grown = grown_part(plan, turned, from_edges, factor, lanes)
        waves_out[:, :, lanes] = grown.reshape(plan.rows, plan.cols, 256)
        copy = pltpu.make_async_copy(
            waves_out.at[:, :, lanes], waves_far.at[:, :, lanes], done.at[number + 1]
        )
        copy.start()
        copies.append(copy)
    for copy in copies:
        copy.wait()


def per_device(plan, axes, spectra, turning, currents, drag_rates, land_mask, ocean_target):
    tables = [jnp.asarray(table) for table in build_tables(NFREQ, NDIR, drag_rates.shape[0])]
    columns, rows, cols, spectral = plan.columns, plan.rows, plan.cols, plan.spectral
    shape = jax.ShapeDtypeStruct
    params = pltpu.CompilerParams(vmem_limit_bytes=32 * 1024 * 1024)
    to_sections = [shape((size, LANES), F32) for size in plan.sizes]
    to_bands = [shape((cols, spectral // 2 + LANES), F32)] * 2
    state = shape((columns, LANES), F32)
    field = shape(spectra.shape, F32)
    at_edges = shape((2 * rows, LANES), F32)
    edge_field = shape((2 * rows, spectral), F32)
    edge = pltpu.VMEM((plan.edge, LANES), F32)
    spans = spectral // 256

    def call(kernel, outs, scratch, *args, space_in=pltpu.VMEM, space_out=pltpu.VMEM):
        return pl.pallas_call(
            functools.partial(kernel, plan, axes),
            out_shape=outs,
            in_specs=[pl.BlockSpec(memory_space=space_in)] * len(args),
            out_specs=[pl.BlockSpec(memory_space=space_out)] * len(outs),
            scratch_shapes=scratch,
            compiler_params=params,
        )(*args)

    pairs = [(i, i ^ 1) for i in range(plan.bands) if i ^ 1 < plan.bands]
    others = [(i, ((i + 1) ^ 1) - 1) for i in range(1, plan.bands)]
    others = [(i, j) for i, j in others if j < plan.bands]

    def exchange(to_sections, make_to_bands):
        got = []
        if plan.relay:
            to_x, to_y, *to_sections = to_sections
            got.append(lax.ppermute(to_x, axes[1], plan.table(0, 1)))
        kept, near_out, far_out = make_to_bands()
        far_in = lax.ppermute(far_out, axes[0], others)
        near_in = lax.ppermute(near_out, axes[0], pairs)
        if plan.relay:
            (to_y,) = call(
                relay_kernel,
                [shape((2 * plan.chunk + plan.edge, LANES), F32)],
                [],
                got[0],
                to_y,
            )
            got.append(lax.ppermute(to_y, axes[1], plan.table(0, 2)))
        got += [
            lax.ppermute(message, axes[1], table)
            for message, table in zip(to_sections, plan.direct)
        ]
        return kept, [near_in, far_in, *got]

    started = call(
        first_kernel,
        [
            field,
            state,
            state,
            shape((columns, columns), BF16),
            shape((columns, 2 * columns), BF16),
            shape((4 * rows, columns), BF16),
            shape((columns, 4 * rows), BF16),
            state,
            at_edges,
            state,
            state,
            at_edges,
            shape((8, LANES), F32),
        ]
        + [shape(table.shape, table.dtype) for table in tables]
        + to_sections
        + to_bands,
        [
            pltpu.VMEM(turning.shape, F32),
            pltpu.VMEM(currents.shape, F32),
            pltpu.VMEM(drag_rates.shape, F32),
            pltpu.VMEM(land_mask.shape, jnp.int32),
            pltpu.VMEM(ocean_target.shape, jnp.int32),
            pltpu.SemaphoreType.DMA((9,)),
        ],
        *[
            pltpu.with_memory_space_constraint(array, pltpu.HBM)
            for array in (
                spectra,
                turning,
                currents,
                drag_rates,
                land_mask,
                ocean_target,
                *tables,
            )
        ],
        space_in=pltpu.HBM,
    )
    waves, ocean, packed, permute, order, permute_edge, order_edge = started[:7]
    turn, turn_edge, sea, sea_order, sea_edge, keep, stokes, rates, grow = started[7:16]
    sent, lat = started[16:-2], started[-2:]
    waves, came = exchange(sent, lambda: (waves, *lat))
    for step in range(STEPS - 1):
        turned, turned_edge, turned_order = call(
            move_kernel,
            [field, edge_field, shape((columns, spectral), F32)],
            [],
            waves,
            turn,
            rates,
            *came[:2],
            order,
        )
        ocean, packed, coupled, extra, *sent = call(
            send_kernel,
            [state, state, state, edge_field] + to_sections,
            [edge, edge],
            turned_order,
            turned_edge,
            ocean,
            packed,
            permute_edge,
            order_edge,
            turn_edge,
            sea,
            sea_order,
            sea_edge,
            keep,
            stokes,
            rates,
            grow,
            *came,
        )

        def grown():
            return call(
                grow_kernel,
                [field] + to_bands,
                [],
                turned,
                extra,
                coupled,
                permute,
                sea,
                grow,
                ocean,
            )

        waves, came = exchange(sent, grown)
    (turned,) = call(move_kernel, [field], [], waves, turn, rates, *came[:2])
    return call(
        last_kernel,
        [field, shape(currents.shape, F32)],
        [
            pltpu.VMEM((columns, LANES), F32),
            edge,
            edge,
            pltpu.VMEM(spectra.shape, F32),
            pltpu.VMEM(currents.shape, F32),
            pltpu.SemaphoreType.DMA((1 + spans,)),
        ],
        turned,
        ocean,
        packed,
        permute,
        turn_edge,
        sea,
        keep,
        rates,
        grow,
        *came,
        space_out=pltpu.HBM,
    )


def solution(mesh):
    sections, bands = mesh.shape["sec"], mesh.shape["lat"]

    def local(spectra, turning, currents, drag_rates, land_mask, ocean_target):
        rows, cols, spectral = spectra.shape
        plan = Plan(sections, bands, rows, cols, spectral, drag_rates.shape[0])
        return per_device(
            plan, ("lat", "sec"), spectra, turning, currents, drag_rates, land_mask, ocean_target
        )

    return jax.shard_map(
        local,
        mesh=mesh,
        in_specs=(
            P("lat", "sec", None),
            P("lat", "sec"),
            P("lat", "sec", None),
            P(),
            P("lat", "sec"),
            P("lat", "sec"),
        ),
        out_specs=(P("lat", "sec", None), P("lat", "sec", None)),
        check_vma=False,
    )
```

```python
import functools
import math

import jax
import jax.numpy as jnp
import ml_dtypes
import numpy as np
from jax import lax
from jax.experimental import pallas as pl
from jax.experimental.pallas import tpu as pltpu
from jax.sharding import PartitionSpec as P

NFREQ = 24
NDIR = 32
STEPS = 3

stokes_scale = 0.1
ocean_dt = 0.3
current_gain = 0.2

LANES = 128
F32 = jnp.float32
BF16 = jnp.bfloat16


def split_halves(table):
    high = table.astype(ml_dtypes.bfloat16)
    low = (table - high.astype(np.float64)).astype(ml_dtypes.bfloat16)
    return high, low


def build_tables(nfreq, ndir, ndepth):
    fraction = np.arange(nfreq) / (nfreq - 1)
    angles = (np.arange(ndir) + 0.5) * (2.0 * math.pi / ndir)
    east_part, north_part = np.cos(angles), np.sin(angles)
    courant = 0.1 + 0.3 * fraction
    depth_level = 0.5 + (ndepth - 2) * (1.0 - fraction)
    weights = np.maximum(1.0 - np.abs(np.arange(ndepth)[None, :] - depth_level[:, None]), 0.0)
    mean_weights = weights / weights.sum(axis=1, keepdims=True)
    x_rate = np.abs(courant[:, None] * east_part[None, :]).reshape(-1)
    y_rate = np.abs(courant[:, None] * north_part[None, :]).reshape(-1)
    turn_gain = np.repeat(1.0 - 0.5 * fraction, ndir)
    rates = np.stack([1.0 - x_rate - y_rate, x_rate, y_rate, turn_gain] * 2).astype(np.float32)
    compass = np.stack([east_part, north_part])
    stokes = (stokes_scale * weights[:, None, None, :] * compass.T[None, :, :, None]).reshape(
        nfreq * ndir, 2 * ndepth
    )
    growth = current_gain * (1.0 + fraction)
    grow = (
        growth[None, None, :, None] * mean_weights.T[None, :, :, None] * compass[:, None, None, :]
    ).reshape(2 * ndepth, nfreq * ndir)
    stokes_high, stokes_low = split_halves(stokes)
    grow_high, grow_low = split_halves(grow)
    return (
        np.concatenate([stokes_high, stokes_low], axis=1),
        rates,
        np.concatenate([grow_high, grow_high, grow_low, grow_low], axis=0)
        .reshape(8 * ndepth, -1, LANES)
        .transpose(1, 0, 2)
        .reshape(-1, LANES),
    )


class Plan:
    def __init__(self, sections, bands, rows, cols, spectral, depth):
        self.sections, self.bands = sections, bands
        self.rows, self.cols, self.spectral, self.depth = rows, cols, spectral, depth
        self.columns = rows * cols
        self.chunk = self.columns // sections
        self.tiles = spectral // LANES
        self.edge = ((self.tiles // 2 + 1) * rows + 7) // 8 * 8
        self.relay = sections % 4 == 0
        self.quad = 4 if self.relay else 1
        self.hops = [
            (hop, flip)
            for hop in range(1, sections // self.quad)
            for flip in ((3, 1, 2, 0) if self.relay else (0,))
        ]
        self.direct = [self.table(*hop) for hop in self.hops]
        self.edges = [
            any(abs(target - i) == 1 for i, target in table) for table in self.direct
        ]
        self.sizes = [self.chunk + (self.edge if edge else 0) for edge in self.edges]
        if self.relay:
            self.sizes = [2 * (self.chunk + self.edge), self.chunk] + self.sizes

    def table(self, hop, flip):
        return [(i, self.partner(i, hop, flip, divmod)[0]) for i in range(self.sections)]

    def partner(self, section, hop, flip, divide=lambda a, b: (lax.div(a, b), lax.rem(a, b))):
        groups = self.sections // self.quad
        high, low = divide(section, self.quad)
        if flip & 1:
            low = low + 1 - 2 * divide(low, 2)[1]
        if flip & 2:
            low = low + 2 - 4 * divide(low, 2)[0]
        return tuple(
            divide(high + shift, groups)[1] * self.quad + low for shift in (hop, groups - hop)
        )

    def received(self, section, messages):
        parts = []
        if self.relay:
            from_x, from_y = messages[:2]
            parts = [
                (self.partner(section, 0, 1)[1], from_x, 0, self.chunk),
                (self.partner(section, 0, 2)[1], from_y, 0, None),
                (self.partner(section, 0, 3)[1], from_y, self.chunk, 2 * self.chunk),
            ]
            messages = messages[2:]
        for message, hop, edge in zip(messages, self.hops, self.edges):
            parts.append((self.partner(section, *hop)[1], message, 0, self.chunk if edge else None))
        return parts

    def sent(self, section, messages):
        parts = []
        if self.relay:
            to_x, to_y = messages[:2]
            parts = [
                (self.partner(section, 0, 1)[0], to_x, 0, self.chunk),
                (self.partner(section, 0, 2)[0], to_y, 0, None),
                (
                    self.partner(section, 0, 3)[0],
                    to_x,
                    self.chunk + self.edge,
                    2 * self.chunk + self.edge,
                ),
            ]
            messages = messages[2:]
        for message, hop, edge in zip(messages, self.hops, self.edges):
            parts.append((self.partner(section, *hop)[0], message, 0, self.chunk if edge else None))
        return parts


def lane_of(shape):
    return lax.broadcasted_iota(jnp.int32, shape, len(shape) - 1)


def dot(a, b):
    return jnp.dot(a, b, preferred_element_type=F32)


def split_value(value):
    high = value.astype(BF16).astype(F32)
    return jnp.where(lane_of(value.shape) < LANES // 2, high, value - high).astype(BF16)


def stokes_product(part, table):
    high = part.astype(BF16)
    low = (part - high.astype(F32)).astype(BF16)
    return dot(jnp.concatenate([high, low], axis=0), table)


def packed_half(edge, tile, half, ahead, forward):
    first = edge[:, tile * LANES : (tile + 1) * LANES]
    second = edge[:, (tile + half) * LANES : (tile + half + 1) * LANES]
    keep = jnp.where(ahead, 1, 0) == jnp.where(forward, 1, 0)
    return jnp.where(keep, first, pltpu.roll(second, NDIR // 2, 1))


def fill_band(plan, northward, edge, sea_row, out):
    half = plan.tiles // 2
    masks = Directions((plan.cols, LANES))
    for tile in range(half):
        out[:, tile * LANES : (tile + 1) * LANES] = packed_half(
            edge, tile, half, masks.northward, northward
        )
    out[:, plan.spectral // 2 :] = sea_row


def fill_bands(plan, even, edges, sea_rows, far, near):
    for out, northward in ((far, jnp.logical_not(even)), (near, even)):
        edge = jnp.where(northward, edges[1], edges[0])
        fill_band(plan, northward, edge, jnp.where(northward, sea_rows[1], sea_rows[0]), out)


def fill_sections(plan, section, edges, ocean, ordered, packed_out, sec_out):
    chunk, rows, cols, half = plan.chunk, plan.rows, plan.cols, plan.tiles // 2
    lane = lane_of((plan.columns, LANES))
    packed_out[...] = jnp.where(lane < LANES // 2, ocean, ordered)
    sea_rows = ocean.reshape(rows, cols, LANES)
    masks = Directions((rows, LANES))
    for target, out, at, edge_at in plan.sent(section, sec_out):
        out[at : at + chunk, :] = packed_out[pl.ds(pl.multiple_of(target * chunk, 8), chunk), :]
        if edge_at is None:
            continue
        eastward = target == section + 1
        edge = jnp.where(eastward, edges[rows:, :], edges[:rows, :])
        for tile in range(half):
            place = edge_at + tile * rows
            out[place : place + rows, :] = packed_half(edge, tile, half, masks.eastward, eastward)
        for row in range(rows):
            place = edge_at + half * rows + row
            out[place : place + 1, :] = jnp.where(
                eastward, sea_rows[row, cols - 1 : cols, :], sea_rows[row, 0:1, :]
            )


def take_sections(plan, section, packed_in, sec_in, coupled, west_edge, east_edge):
    chunk = plan.chunk
    own = pl.ds(pl.multiple_of(section * chunk, 8), chunk)
    coupled[own, :] = packed_in[own, :]
    west_edge[...] = jnp.zeros_like(west_edge)
    east_edge[...] = jnp.zeros_like(east_edge)
    for source, message, at, edge_at in plan.received(section, sec_in):
        coupled[pl.ds(pl.multiple_of(source * chunk, 8), chunk), :] = message[at : at + chunk, :]
        if edge_at is None:
            continue

        @pl.when(source == section + 1)
        def _():
            east_edge[...] = message[edge_at : edge_at + plan.edge, :]

        @pl.when(source == section - 1)
        def _():
            west_edge[...] = message[edge_at : edge_at + plan.edge, :]


def edge_part(plan, rates, turn_edge, west_edge, east_edge):
    rows, half = plan.rows, plan.tiles // 2
    shape = (2 * rows, LANES)
    masks = Directions(shape)
    westmost = lax.broadcasted_iota(jnp.int32, shape, 0) < rows
    reached = jnp.where(masks.eastward, 1, 0) == jnp.where(westmost, 1, 0)
    parts = []
    for tile in range(plan.tiles):
        lanes = slice(tile * LANES, (tile + 1) * LANES)
        edge = slice(tile % half * rows, (tile % half + 1) * rows)
        came = jnp.concatenate([west_edge[edge, :], east_edge[edge, :]], axis=0)
        if tile >= half:
            came = pltpu.roll(came, LANES - NDIR // 2, 1)
        moved = rates[1:2, lanes] * jnp.where(reached, came, 0.0)
        parts.append(masks.turned(moved, turn_edge[...], rates[3:4, lanes]))
    return parts


def ocean_step(plan, band, even, ocean_in, stokes, near, far, west_edge, east_edge, keep, sea):
    rows, cols, half = plan.rows, plan.cols, plan.tiles // 2
    block = (cols, LANES)
    zonal = lane_of(block) < plan.depth
    place = lax.broadcasted_iota(jnp.int32, block, 0)
    at_west, at_east = place == 0, place == cols - 1
    lanes = slice(plan.spectral // 2, plan.spectral // 2 + LANES)
    south_edge = jnp.where(even, far[:, lanes], near[:, lanes])
    north_edge = jnp.where(even, near[:, lanes], far[:, lanes])
    new = []
    for row in range(rows):
        flat = slice(row * cols, (row + 1) * cols)
        edge = slice(half * rows + row, half * rows + row + 1)
        center = ocean_in[flat, :]
        west = jnp.where(at_west, west_edge[edge, :], pltpu.roll(center, 1, 0))
        east = jnp.where(at_east, east_edge[edge, :], pltpu.roll(center, cols - 1, 0))
        south = ocean_in[(row - 1) * cols : row * cols, :] if row else south_edge
        north = ocean_in[(row + 1) * cols : (row + 2) * cols, :] if row < rows - 1 else north_edge
        shear = 0.5 * jnp.where(zonal, south - north, east - west)
        y = (band * rows + row).astype(F32)
        spin = 0.2 + 0.6 * y / float(plan.bands * rows) + (shear + swapped(plan, shear))
        turn_by = ocean_dt * spin * swapped(plan, center + stokes[flat, :])
        new.append(keep[0:1, :] * (center + jnp.where(zonal, turn_by, -turn_by)) * sea[flat, :])
    return new


def twice(value, axis=1):
    return jnp.concatenate([value, value], axis=axis)


def growth_table(grow, number):
    return jnp.concatenate(
        [grow[(2 * number + k) * 256 : (2 * number + k + 1) * 256, :] for k in range(2)], axis=1
    )


def currents_twice(arrived):
    other = pltpu.roll(arrived, LANES // 2, 1)
    return jnp.where(lane_of(arrived.shape) < LANES // 2, arrived, other), other


def with_edges(plan, turned, west, east):
    place = lax.broadcasted_iota(jnp.int32, (8, 256), 0)
    return [
        turned[0:8, :] + jnp.where(place == 0, west, 0.0),
        turned[8 : plan.cols - 8, :],
        turned[plan.cols - 8 :, :] + jnp.where(place == 7, east, 0.0),
    ]


def grown_part(plan, turned, from_edges, factor, lanes):
    rows = plan.rows
    parts = []
    for row in range(rows):
        west, east = from_edges[row : row + 1, :], from_edges[rows + row : rows + row + 1, :]
        parts += with_edges(plan, turned[row, :, lanes], west, east)
    return jnp.concatenate(parts, axis=0) * factor


def relay_kernel(plan, axes, from_x, to_y, out):
    out[0 : plan.chunk, :] = to_y[...]
    out[plan.chunk :, :] = from_x[plan.chunk + plan.edge :, :]


def first_kernel(plan, axes, *refs):
    waves_in, turning_in, currents_in, drag_in, mask_in, target_in = refs[:6]
    tables_in, refs = refs[6:9], refs[9:]
    waves, ocean_out, packed_out, permute_out, order_out, permute_some_out, order_edge_out = refs[:7]
    turn_out, turn_edge_out, sea_out, sea_order_out, sea_some_out, keep_out = refs[7:13]
    tables_out, refs = refs[13:16], refs[16:]
    count = len(plan.sizes)
    sec_out, lat_out, refs = refs[:count], refs[count : count + 2], refs[count + 2 :]
    turning, currents, drag, mask, target, done = refs
    pairs = [
        (target_in, target),
        (turning_in, turning),
        (mask_in, mask),
        (drag_in, drag),
        (waves_in, waves),
        (tables_in[0], tables_out[0]),
        (currents_in, currents),
        (tables_in[1], tables_out[1]),
        (tables_in[2], tables_out[2]),
    ]
    copies = [pltpu.make_async_copy(a, b, done.at[k]) for k, (a, b) in enumerate(pairs)]
    for copy in copies:
        copy.start()
    section, band = lax.axis_index(axes[1]), lax.axis_index(axes[0])
    even = lax.rem(band, 2) == 0
    columns, rows, cols = plan.columns, plan.rows, plan.cols
    across = lane_of((columns, columns))
    down = lax.broadcasted_iota(jnp.int32, (columns, columns), 0)
    here = across == down

    def row_of(ref):
        return jnp.concatenate([ref[row : row + 1, :] for row in range(rows)], axis=1)

    def column_of(row):
        spread = jnp.broadcast_to(row, (columns, columns))
        return jnp.sum(jnp.where(here, spread, jnp.zeros_like(spread)), axis=1, keepdims=True)

    def edges_of(value):
        west = [value[row * cols : row * cols + 1, :] for row in range(rows)]
        east = [value[(row + 1) * cols - 1 : (row + 1) * cols, :] for row in range(rows)]
        return jnp.concatenate(west + east, axis=0)

    for copy in copies[:7]:
        copy.wait()
    total = None
    for start in range(0, plan.spectral, 256):
        part = waves[:, :, start : start + 256].reshape(columns, 256)
        product = stokes_product(part, tables_out[0][start : start + 256, :])
        total = product if total is None else total + product
    moments = total[:columns] + total[columns:]
    moments = moments + pltpu.roll(moments, LANES // 2, 1)
    sea_row = row_of(mask).astype(F32)
    sea = column_of(sea_row)
    target_row = row_of(target).astype(F32)
    target_col = column_of(target_row)
    same = target_col == target_row
    rank_col = jnp.sum(jnp.where(same & (across < down), 1.0, 0.0), axis=1, keepdims=True)
    rank_row = jnp.sum(jnp.where(same & (down < across), 1.0, 0.0), axis=0, keepdims=True)
    slot_col = target_col * float(plan.chunk) + rank_col
    slot_row = target_row * float(plan.chunk) + rank_row
    permute = jnp.where(slot_col == across.astype(F32), sea, 0.0)
    order = jnp.where(slot_row == down.astype(F32), 1.0, 0.0)
    permute_out[...] = permute.astype(BF16)
    order_out[...] = twice(order).astype(BF16)
    sea_order = jnp.sum(order * sea_row, axis=1, keepdims=True)
    sea_order_out[...] = jnp.broadcast_to(sea_order, (columns, LANES))
    edge_count = 4 * rows
    number = lax.rem(lane_of((columns, edge_count)), 2 * rows)
    wanted = lax.rem(number, rows) * cols + lax.div(number, rows) * (cols - 1)
    chosen = lax.broadcasted_iota(jnp.int32, (columns, edge_count), 0) == wanted
    order_edge_out[...] = dot(
        order.astype(BF16), jnp.where(chosen, 1.0, 0.0).astype(BF16)
    ).astype(BF16)
    shape = (2 * cols + 2 * rows, columns)
    place = lax.broadcasted_iota(jnp.int32, shape, 0)
    number = place - 2 * cols
    wanted = jnp.where(
        place < 2 * cols,
        place + jnp.where(place < cols, 0, (rows - 2) * cols),
        lax.rem(number, rows) * cols + lax.div(number, rows) * (cols - 1),
    )
    chosen = jnp.where(lane_of(shape) == wanted, 1.0, 0.0).astype(BF16)
    permute_some_out[...] = dot(chosen, permute.astype(BF16)).astype(BF16)
    sea_wide = jnp.broadcast_to(sea, (columns, LANES))
    sea_some_out[...] = dot(chosen, sea_wide.astype(BF16))
    sea_out[...] = sea_wide
    turn = jnp.broadcast_to(column_of(row_of(turning)), (columns, LANES))
    turn_out[...] = turn
    turn_edge_out[...] = edges_of(turn)
    keep = 1.0 - drag[...].reshape(1, plan.depth)
    blank = jnp.zeros((1, LANES - 2 * plan.depth), F32)
    keep_out[...] = jnp.broadcast_to(jnp.concatenate([keep, keep, blank], axis=1), (8, LANES))
    flat = currents[...].reshape(columns, 2 * plan.depth)
    ocean = jnp.concatenate([flat, jnp.zeros((columns, LANES - 2 * plan.depth), F32)], axis=1)
    ocean_out[...] = ocean
    ordered = dot(order.astype(BF16), split_value(moments))
    ordered = ordered + pltpu.roll(ordered, LANES // 2, 1)
    west = [waves[row, 0:1, :] for row in range(rows)]
    east = [waves[row, cols - 1 : cols, :] for row in range(rows)]
    edges = jnp.concatenate(west + east, axis=0)
    fill_sections(plan, section, edges, ocean, ordered, packed_out, sec_out)
    sea_rows = ocean.reshape(rows, cols, LANES)
    ends = (waves[0], waves[rows - 1]), (sea_rows[0], sea_rows[rows - 1])
    fill_bands(plan, even, *ends, *lat_out)
    for copy in copies[7:]:
        copy.wait()


class Directions:
    def __init__(self, shape):
        direction = lax.rem(lane_of(shape), NDIR)
        self.eastward = (direction < NDIR // 4) | (direction >= 3 * NDIR // 4)
        self.northward = direction < NDIR // 2
        self.first, self.final = direction == 0, direction == NDIR - 1

    def turned(self, moved, rate, gain):
        behind = jnp.where(
            self.first, pltpu.roll(moved, LANES - (NDIR - 1), 1), pltpu.roll(moved, 1, 1)
        )
        forward = jnp.where(
            self.final, pltpu.roll(moved, NDIR - 1, 1), pltpu.roll(moved, LANES - 1, 1)
        )
        return moved - jnp.abs(rate) * gain * (moved - jnp.where(rate > 0.0, behind, forward))


def move_kernel(plan, axes, *refs):
    waves, turn, rates, near, far, refs = *refs[:5], refs[5:]
    if len(refs) > 1:
        order, turned_out, edge_out, sorted_out = refs
    else:
        (turned_out,) = refs
    even = lax.rem(lax.axis_index(axes[0]), 2) == 0
    rows, cols, tiles = plan.rows, plan.cols, plan.tiles
    block = (cols, LANES)
    masks = Directions(block)
    place = lax.broadcasted_iota(jnp.int32, block, 0)
    outside = place == jnp.where(masks.eastward, 0, cols - 1)
    for tile in range(tiles):
        lanes = slice(tile * LANES, (tile + 1) * LANES)
        stay, along_x, along_y, gain = (rates[k : k + 1, lanes] for k in range(4))
        along_x = jnp.where(outside, 0.0, along_x)
        half = tile % (tiles // 2)
        half = slice(half * LANES, (half + 1) * LANES)
        south_edge = jnp.where(even, far[:, half], near[:, half])
        north_edge = jnp.where(even, near[:, half], far[:, half])
        if tile >= tiles // 2:
            south_edge = pltpu.roll(south_edge, LANES - NDIR // 2, 1)
            north_edge = pltpu.roll(north_edge, LANES - NDIR // 2, 1)
        for row in range(rows):
            center = waves[row, :, lanes]
            south = waves[row - 1, :, lanes] if row else south_edge
            north = waves[row + 1, :, lanes] if row < rows - 1 else north_edge
            moved = (
                stay * center
                + along_x
                * jnp.where(
                    masks.eastward, pltpu.roll(center, 1, 0), pltpu.roll(center, cols - 1, 0)
                )
                + along_y * jnp.where(masks.northward, south, north)
            )
            rate = turn[row * cols : (row + 1) * cols, :]
            turned = masks.turned(moved, rate, gain)
            turned_out[row, :, lanes] = turned
            if len(refs) > 1:
                edge_out[row : row + 1, lanes] = turned[0:1, :]
                edge_out[rows + row : rows + row + 1, lanes] = turned[cols - 1 :, :]
    if len(refs) > 1:
        for start in range(0, plan.spectral, 256):
            part = turned_out[:, :, start : start + 256].reshape(plan.columns, 256)
            high = part.astype(BF16)
            low = (part - high.astype(F32)).astype(BF16)
            sorted_out[:, start : start + 256] = dot(
                order[...], jnp.concatenate([high, low], axis=0)
            )


def swapped(plan, value):
    half = plan.depth
    zonal = lane_of(value.shape) < half
    return jnp.where(zonal, pltpu.roll(value, LANES - half, 1), pltpu.roll(value, half, 1))


def send_kernel(plan, axes, *refs):
    turned, turned_edge, turned_order, ocean_in, packed_in, permute_some, order_edge = refs[:7]
    turn_edge, sea, sea_order, sea_some, keep, stokes, rates, grow, refs = *refs[7:15], refs[15:]
    count = len(plan.sizes)
    near, far, sec_in, refs = refs[0], refs[1], refs[2 : 2 + count], refs[2 + count :]
    ocean_out, packed_out, coupled, extra_out, far_out, near_out = refs[:6]
    sec_out, (west_edge, east_edge) = refs[6 : 6 + count], refs[6 + count :]
    section, band = lax.axis_index(axes[1]), lax.axis_index(axes[0])
    even = lax.rem(band, 2) == 0
    columns, rows, cols = plan.columns, plan.rows, plan.cols

    take_sections(plan, section, packed_in, sec_in, coupled, west_edge, east_edge)
    both, drift = currents_twice(coupled[...])
    in_order = twice(split_value(both * sea_order[...]))
    at_some = twice(dot(permute_some[...], split_value(both)).astype(BF16))
    extra = edge_part(plan, rates, turn_edge, west_edge, east_edge)
    total = None
    some = []
    wet, wet_some = twice(sea_order[...]), twice(sea_some[...])
    for number, start in enumerate(range(0, plan.spectral, 256)):
        lanes = slice(start, start + 256)
        table = growth_table(grow, number)
        from_edges = jnp.concatenate(extra[2 * number : 2 * number + 2], axis=1)
        extra_out[:, lanes] = from_edges
        high = from_edges.astype(BF16).astype(F32)
        halves = jnp.concatenate([high, from_edges - high], axis=0).astype(BF16)
        grown = turned_order[:, lanes] + dot(order_edge[...], halves)
        grown = grown * (wet + dot(in_order, table))
        product = stokes_product(grown, stokes[lanes, :])
        total = product if total is None else total + product
        parts = []
        for row in (0, rows - 1):
            west, east = from_edges[row : row + 1, :], from_edges[rows + row : rows + row + 1, :]
            parts += with_edges(plan, turned[row, :, lanes], west, east)
        parts.append(turned_edge[:, lanes] + from_edges)
        some.append(jnp.concatenate(parts, axis=0) * (wet_some + dot(at_some, table)))
    new = ocean_step(
        plan, band, even, ocean_in, drift, near, far, west_edge, east_edge, keep, sea
    )
    ocean = jnp.concatenate(new, axis=0)
    ocean_out[...] = ocean
    moments = total[:columns] + total[columns:]
    moments = moments + pltpu.roll(moments, LANES // 2, 1)
    some = jnp.concatenate(some, axis=1)
    fill_sections(plan, section, some[2 * cols :, :], ocean, moments, packed_out, sec_out)
    ends = (some[:cols, :], some[cols : 2 * cols, :]), (new[0], new[rows - 1])
    fill_bands(plan, even, *ends, far_out, near_out)


def grow_kernel(plan, axes, *refs):
    turned, extra, coupled, permute, sea, grow, _, waves_out = refs
    both, _ = currents_twice(coupled[...])
    at_waves = twice(dot(permute[...], split_value(both)).astype(BF16))
    wet = twice(sea[...])
    for number, start in enumerate(range(0, plan.spectral, 256)):
        lanes = slice(start, start + 256)
        factor = wet + dot(at_waves, growth_table(grow, number))
        grown = grown_part(plan, turned, extra[:, lanes], factor, lanes)
        waves_out[:, :, lanes] = grown.reshape(plan.rows, plan.cols, 256)


def last_kernel(plan, axes, *refs):
    turned, ocean_in, packed_in, permute, turn_edge, sea, keep, rates, grow = refs[:9]
    count = len(plan.sizes)
    near, far, sec_in, refs = refs[9], refs[10], refs[11 : 11 + count], refs[11 + count :]
    waves_far, ocean_far, coupled, west_edge, east_edge, waves_out, ocean_out, done = refs
    section, band = lax.axis_index(axes[1]), lax.axis_index(axes[0])
    even = lax.rem(band, 2) == 0

    take_sections(plan, section, packed_in, sec_in, coupled, west_edge, east_edge)
    both, drift = currents_twice(coupled[...])
    at_waves = twice(dot(permute[...], split_value(both)).astype(BF16))
    extra = edge_part(plan, rates, turn_edge, west_edge, east_edge)
    new = ocean_step(
        plan, band, even, ocean_in, drift, near, far, west_edge, east_edge, keep, sea
    )
    for row, value in enumerate(new):
        ocean_out[row] = value[:, : 2 * plan.depth]
    copies = [pltpu.make_async_copy(ocean_out, ocean_far, done.at[0])]
    copies[0].start()
    wet = twice(sea[...])
    for number, start in enumerate(range(0, plan.spectral, 256)):
        lanes = slice(start, start + 256)
        factor = wet + dot(at_waves, growth_table(grow, number))
        from_edges = jnp.concatenate(extra[2 * number : 2 * number + 2], axis=1)
        grown = grown_part(plan, turned, from_edges, factor, lanes)
        waves_out[:, :, lanes] = grown.reshape(plan.rows, plan.cols, 256)
        copy = pltpu.make_async_copy(
            waves_out.at[:, :, lanes], waves_far.at[:, :, lanes], done.at[number + 1]
        )
        copy.start()
        copies.append(copy)
    for copy in copies:
        copy.wait()


def per_device(plan, axes, spectra, turning, currents, drag_rates, land_mask, ocean_target):
    tables = [jnp.asarray(table) for table in build_tables(NFREQ, NDIR, drag_rates.shape[0])]
    columns, rows, cols, spectral = plan.columns, plan.rows, plan.cols, plan.spectral
    shape = jax.ShapeDtypeStruct
    params = pltpu.CompilerParams(vmem_limit_bytes=32 * 1024 * 1024)
    to_sections = [shape((size, LANES), F32) for size in plan.sizes]
    to_band = shape((cols, spectral // 2 + LANES), F32)
    state = shape((columns, LANES), F32)
    field = shape(spectra.shape, F32)
    at_edges = shape((2 * rows, LANES), F32)
    edge_field = shape((2 * rows, spectral), F32)
    some = 2 * cols + 2 * rows
    edge = pltpu.VMEM((plan.edge, LANES), F32)
    spans = spectral // 256

    def call(kernel, outs, scratch, *args, space_in=pltpu.VMEM, space_out=pltpu.VMEM):
        return pl.pallas_call(
            functools.partial(kernel, plan, axes),
            out_shape=outs,
            in_specs=[pl.BlockSpec(memory_space=space_in)] * len(args),
            out_specs=[pl.BlockSpec(memory_space=space_out)] * len(outs),
            scratch_shapes=scratch,
            compiler_params=params,
        )(*args)

    pairs = [(i, i ^ 1) for i in range(plan.bands) if i ^ 1 < plan.bands]
    others = [(i, ((i + 1) ^ 1) - 1) for i in range(1, plan.bands)]
    others = [(i, j) for i, j in others if j < plan.bands]

    def exchange(to_far, to_near, to_sections, waves):
        got = []
        if plan.relay:
            to_x, to_y, *to_sections = to_sections
            got.append(lax.ppermute(to_x, axes[1], plan.table(0, 1)))
        far_in = lax.ppermute(to_far, axes[0], others)
        near_in = lax.ppermute(to_near, axes[0], pairs)
        first = to_far
        if plan.relay:
            (first,) = call(
                relay_kernel,
                [shape((2 * plan.chunk + plan.edge, LANES), F32)],
                [],
                got[0],
                to_y,
            )
            got.append(lax.ppermute(first, axes[1], plan.table(0, 2)))
        got += [
            lax.ppermute(message, axes[1], table)
            for message, table in zip(to_sections, plan.direct)
        ]
        return waves(first), [near_in, far_in, *got]

    started = call(
        first_kernel,
        [
            field,
            state,
            state,
            shape((columns, columns), BF16),
            shape((columns, 2 * columns), BF16),
            shape((some, columns), BF16),
            shape((columns, 4 * rows), BF16),
            state,
            at_edges,
            state,
            state,
            shape((some, LANES), F32),
            shape((8, LANES), F32),
        ]
        + [shape(table.shape, table.dtype) for table in tables]
        + to_sections
        + [to_band] * 2,
        [
            pltpu.VMEM(turning.shape, F32),
            pltpu.VMEM(currents.shape, F32),
            pltpu.VMEM(drag_rates.shape, F32),
            pltpu.VMEM(land_mask.shape, jnp.int32),
            pltpu.VMEM(ocean_target.shape, jnp.int32),
            pltpu.SemaphoreType.DMA((9,)),
        ],
        *[
            pltpu.with_memory_space_constraint(array, pltpu.HBM)
            for array in (
                spectra,
                turning,
                currents,
                drag_rates,
                land_mask,
                ocean_target,
                *tables,
            )
        ],
        space_in=pltpu.HBM,
    )
    waves, ocean, packed, permute, order, permute_some, order_edge = started[:7]
    turn, turn_edge, sea, sea_order, sea_some, keep, stokes, rates, grow = started[7:16]
    waves, came = exchange(*started[-2:], started[16:-2], lambda _: waves)
    for step in range(STEPS - 1):
        turned, turned_edge, turned_order = call(
            move_kernel,
            [field, edge_field, shape((columns, spectral), F32)],
            [],
            waves,
            turn,
            rates,
            *came[:2],
            order,
        )
        ocean, packed, coupled, extra, to_far, to_near, *sent = call(
            send_kernel,
            [state, state, state, edge_field, to_band, to_band] + to_sections,
            [edge, edge],
            turned,
            turned_edge,
            turned_order,
            ocean,
            packed,
            permute_some,
            order_edge,
            turn_edge,
            sea,
            sea_order,
            sea_some,
            keep,
            stokes,
            rates,
            grow,
            *came,
        )

        def grown(first):
            (waves,) = call(
                grow_kernel, [field], [], turned, extra, coupled, permute, sea, grow, first
            )
            return waves

        waves, came = exchange(to_far, to_near, sent, grown)
    (turned,) = call(move_kernel, [field], [], waves, turn, rates, *came[:2])
    return call(
        last_kernel,
        [field, shape(currents.shape, F32)],
        [
            pltpu.VMEM((columns, LANES), F32),
            edge,
            edge,
            pltpu.VMEM(spectra.shape, F32),
            pltpu.VMEM(currents.shape, F32),
            pltpu.SemaphoreType.DMA((1 + spans,)),
        ],
        turned,
        ocean,
        packed,
        permute,
        turn_edge,
        sea,
        keep,
        rates,
        grow,
        *came,
        space_out=pltpu.HBM,
    )


def solution(mesh):
    sections, bands = mesh.shape["sec"], mesh.shape["lat"]

    def local(spectra, turning, currents, drag_rates, land_mask, ocean_target):
        rows, cols, spectral = spectra.shape
        plan = Plan(sections, bands, rows, cols, spectral, drag_rates.shape[0])
        return per_device(
            plan, ("lat", "sec"), spectra, turning, currents, drag_rates, land_mask, ocean_target
        )

    return jax.shard_map(
        local,
        mesh=mesh,
        in_specs=(
            P("lat", "sec", None),
            P("lat", "sec"),
            P("lat", "sec", None),
            P(),
            P("lat", "sec"),
            P("lat", "sec"),
        ),
        out_specs=(P("lat", "sec", None), P("lat", "sec", None)),
        check_vma=False,
    )
```

```python
import functools
import math

import jax
import jax.numpy as jnp
import ml_dtypes
import numpy as np
from jax import lax
from jax.experimental import pallas as pl
from jax.experimental.pallas import tpu as pltpu
from jax.sharding import PartitionSpec as P

NFREQ = 24
NDIR = 32
STEPS = 3

stokes_scale = 0.1
ocean_dt = 0.3
current_gain = 0.2

LANES = 128
F32 = jnp.float32
BF16 = jnp.bfloat16


def split_halves(table):
    high = table.astype(ml_dtypes.bfloat16)
    low = (table - high.astype(np.float64)).astype(ml_dtypes.bfloat16)
    return high, low


def build_tables(nfreq, ndir, ndepth):
    fraction = np.arange(nfreq) / (nfreq - 1)
    angles = (np.arange(ndir) + 0.5) * (2.0 * math.pi / ndir)
    east_part, north_part = np.cos(angles), np.sin(angles)
    courant = 0.1 + 0.3 * fraction
    depth_level = 0.5 + (ndepth - 2) * (1.0 - fraction)
    weights = np.maximum(1.0 - np.abs(np.arange(ndepth)[None, :] - depth_level[:, None]), 0.0)
    mean_weights = weights / weights.sum(axis=1, keepdims=True)
    x_rate = np.abs(courant[:, None] * east_part[None, :]).reshape(-1)
    y_rate = np.abs(courant[:, None] * north_part[None, :]).reshape(-1)
    turn_gain = np.repeat(1.0 - 0.5 * fraction, ndir)
    rates = np.stack([1.0 - x_rate - y_rate, x_rate, y_rate, turn_gain] * 2).astype(np.float32)
    compass = np.stack([east_part, north_part])
    stokes = (stokes_scale * weights[:, None, None, :] * compass.T[None, :, :, None]).reshape(
        nfreq * ndir, 2 * ndepth
    )
    growth = current_gain * (1.0 + fraction)
    grow = (
        growth[None, None, :, None] * mean_weights.T[None, :, :, None] * compass[:, None, None, :]
    ).reshape(2 * ndepth, nfreq * ndir)
    stokes_high, stokes_low = split_halves(stokes)
    grow_high, grow_low = split_halves(grow)
    return (
        np.concatenate([stokes_high, stokes_low], axis=1),
        rates,
        np.concatenate([grow_high, grow_high, grow_low, grow_low], axis=0)
        .reshape(8 * ndepth, -1, LANES)
        .transpose(1, 0, 2)
        .reshape(-1, LANES),
    )


class Plan:
    def __init__(self, sections, bands, rows, cols, spectral, depth):
        self.sections, self.bands = sections, bands
        self.rows, self.cols, self.spectral, self.depth = rows, cols, spectral, depth
        self.columns = rows * cols
        self.chunk = self.columns // sections
        self.tiles = spectral // LANES
        self.edge = ((self.tiles // 2 + 1) * rows + 7) // 8 * 8
        self.relay = sections % 4 == 0
        self.quad = 4 if self.relay else 1
        self.hops = [
            (hop, flip)
            for hop in range(1, sections // self.quad)
            for flip in ((3, 1, 2, 0) if self.relay else (0,))
        ]
        self.direct = [self.table(*hop) for hop in self.hops]
        self.edges = [
            any(abs(target - i) == 1 for i, target in table) for table in self.direct
        ]
        self.sizes = [self.chunk + (self.edge if edge else 0) for edge in self.edges]
        if self.relay:
            self.sizes = [2 * (self.chunk + self.edge), self.chunk] + self.sizes

    def table(self, hop, flip):
        return [(i, self.partner(i, hop, flip, divmod)[0]) for i in range(self.sections)]

    def partner(self, section, hop, flip, divide=lambda a, b: (lax.div(a, b), lax.rem(a, b))):
        groups = self.sections // self.quad
        high, low = divide(section, self.quad)
        if flip & 1:
            low = low + 1 - 2 * divide(low, 2)[1]
        if flip & 2:
            low = low + 2 - 4 * divide(low, 2)[0]
        return tuple(
            divide(high + shift, groups)[1] * self.quad + low for shift in (hop, groups - hop)
        )

    def received(self, section, messages):
        parts = []
        if self.relay:
            from_x, from_y = messages[:2]
            parts = [
                (self.partner(section, 0, 1)[1], from_x, 0, self.chunk),
                (self.partner(section, 0, 2)[1], from_y, 0, None),
                (self.partner(section, 0, 3)[1], from_y, self.chunk, 2 * self.chunk),
            ]
            messages = messages[2:]
        for message, hop, edge in zip(messages, self.hops, self.edges):
            parts.append((self.partner(section, *hop)[1], message, 0, self.chunk if edge else None))
        return parts

    def sent(self, section, messages):
        parts = []
        if self.relay:
            to_x, to_y = messages[:2]
            parts = [
                (self.partner(section, 0, 1)[0], to_x, 0, self.chunk),
                (self.partner(section, 0, 2)[0], to_y, 0, None),
                (
                    self.partner(section, 0, 3)[0],
                    to_x,
                    self.chunk + self.edge,
                    2 * self.chunk + self.edge,
                ),
            ]
            messages = messages[2:]
        for message, hop, edge in zip(messages, self.hops, self.edges):
            parts.append((self.partner(section, *hop)[0], message, 0, self.chunk if edge else None))
        return parts


def lane_of(shape):
    return lax.broadcasted_iota(jnp.int32, shape, len(shape) - 1)


def dot(a, b):
    return jnp.dot(a, b, preferred_element_type=F32)


def split_value(value):
    high = value.astype(BF16).astype(F32)
    return jnp.where(lane_of(value.shape) < LANES // 2, high, value - high).astype(BF16)


def stokes_product(part, table):
    high = part.astype(BF16)
    low = (part - high.astype(F32)).astype(BF16)
    return dot(jnp.concatenate([high, low], axis=0), table)


def packed_half(edge, tile, half, ahead, forward):
    first = edge[:, tile * LANES : (tile + 1) * LANES]
    second = edge[:, (tile + half) * LANES : (tile + half + 1) * LANES]
    keep = jnp.where(ahead, 1, 0) == jnp.where(forward, 1, 0)
    return jnp.where(keep, first, pltpu.roll(second, NDIR // 2, 1))


def fill_band(plan, northward, edge, sea_row, out):
    half = plan.tiles // 2
    masks = Directions((plan.cols, LANES))
    for tile in range(half):
        out[:, tile * LANES : (tile + 1) * LANES] = packed_half(
            edge, tile, half, masks.northward, northward
        )
    out[:, plan.spectral // 2 :] = sea_row


def fill_bands(plan, even, edges, sea_rows, far, near):
    for out, northward in ((far, jnp.logical_not(even)), (near, even)):
        edge = jnp.where(northward, edges[1], edges[0])
        fill_band(plan, northward, edge, jnp.where(northward, sea_rows[1], sea_rows[0]), out)


def fill_sections(plan, section, edges, ocean, ordered, packed_out, sec_out):
    chunk, rows, cols, half = plan.chunk, plan.rows, plan.cols, plan.tiles // 2
    lane = lane_of((plan.columns, LANES))
    packed_out[...] = jnp.where(lane < LANES // 2, ocean, ordered)
    sea_rows = ocean.reshape(rows, cols, LANES)
    masks = Directions((rows, LANES))
    for target, out, at, edge_at in plan.sent(section, sec_out):
        out[at : at + chunk, :] = packed_out[pl.ds(pl.multiple_of(target * chunk, 8), chunk), :]
        if edge_at is None:
            continue
        eastward = target == section + 1
        edge = jnp.where(eastward, edges[rows:, :], edges[:rows, :])
        for tile in range(half):
            place = edge_at + tile * rows
            out[place : place + rows, :] = packed_half(edge, tile, half, masks.eastward, eastward)
        for row in range(rows):
            place = edge_at + half * rows + row
            out[place : place + 1, :] = jnp.where(
                eastward, sea_rows[row, cols - 1 : cols, :], sea_rows[row, 0:1, :]
            )


def take_sections(plan, section, packed_in, sec_in, coupled):
    chunk = plan.chunk
    own = pl.ds(pl.multiple_of(section * chunk, 8), chunk)
    coupled[own, :] = packed_in[own, :]
    west = east = jnp.zeros((plan.edge, LANES), F32)
    for source, message, at, edge_at in plan.received(section, sec_in):
        coupled[pl.ds(pl.multiple_of(source * chunk, 8), chunk), :] = message[at : at + chunk, :]
        if edge_at is not None:
            edge = message[edge_at : edge_at + plan.edge, :]
            west = jnp.where(source == section - 1, edge, west)
            east = jnp.where(source == section + 1, edge, east)
    return west, east


def edge_part(plan, rates, turn_edge, west_edge, east_edge):
    rows, half = plan.rows, plan.tiles // 2
    shape = (2 * rows, LANES)
    masks = Directions(shape)
    westmost = lax.broadcasted_iota(jnp.int32, shape, 0) < rows
    reached = jnp.where(masks.eastward, 1, 0) == jnp.where(westmost, 1, 0)
    parts = []
    for tile in range(plan.tiles):
        lanes = slice(tile * LANES, (tile + 1) * LANES)
        edge = slice(tile % half * rows, (tile % half + 1) * rows)
        came = jnp.concatenate([west_edge[edge, :], east_edge[edge, :]], axis=0)
        if tile >= half:
            came = pltpu.roll(came, LANES - NDIR // 2, 1)
        moved = rates[1:2, lanes] * jnp.where(reached, came, 0.0)
        parts.append(masks.turned(moved, turn_edge[...], rates[3:4, lanes]))
    return parts


def ocean_step(plan, band, even, ocean_in, stokes, near, far, west_edge, east_edge, keep, sea):
    rows, cols, half = plan.rows, plan.cols, plan.tiles // 2
    block = (cols, LANES)
    zonal = lane_of(block) < plan.depth
    place = lax.broadcasted_iota(jnp.int32, block, 0)
    at_west, at_east = place == 0, place == cols - 1
    lanes = slice(plan.spectral // 2, plan.spectral // 2 + LANES)
    south_edge = jnp.where(even, far[:, lanes], near[:, lanes])
    north_edge = jnp.where(even, near[:, lanes], far[:, lanes])
    new = []
    for row in range(rows):
        flat = slice(row * cols, (row + 1) * cols)
        edge = slice(half * rows + row, half * rows + row + 1)
        center = ocean_in[flat, :]
        west = jnp.where(at_west, west_edge[edge, :], pltpu.roll(center, 1, 0))
        east = jnp.where(at_east, east_edge[edge, :], pltpu.roll(center, cols - 1, 0))
        south = ocean_in[(row - 1) * cols : row * cols, :] if row else south_edge
        north = ocean_in[(row + 1) * cols : (row + 2) * cols, :] if row < rows - 1 else north_edge
        shear = 0.5 * jnp.where(zonal, south - north, east - west)
        y = (band * rows + row).astype(F32)
        spin = 0.2 + 0.6 * y / float(plan.bands * rows) + (shear + swapped(plan, shear))
        turn_by = ocean_dt * spin * swapped(plan, center + stokes[flat, :])
        new.append(keep[0:1, :] * (center + jnp.where(zonal, turn_by, -turn_by)) * sea[flat, :])
    return new


def twice(value, axis=1):
    return jnp.concatenate([value, value], axis=axis)


def growth_table(grow, number):
    return jnp.concatenate(
        [grow[(2 * number + k) * 256 : (2 * number + k + 1) * 256, :] for k in range(2)], axis=1
    )


def currents_twice(arrived):
    other = pltpu.roll(arrived, LANES // 2, 1)
    return jnp.where(lane_of(arrived.shape) < LANES // 2, arrived, other), other


def with_edges(plan, turned, west, east):
    place = lax.broadcasted_iota(jnp.int32, (8, 256), 0)
    return [
        turned[0:8, :] + jnp.where(place == 0, west, 0.0),
        turned[8 : plan.cols - 8, :],
        turned[plan.cols - 8 :, :] + jnp.where(place == 7, east, 0.0),
    ]


def grown_part(plan, turned, from_edges, factor, lanes):
    rows = plan.rows
    parts = []
    for row in range(rows):
        west, east = from_edges[row : row + 1, :], from_edges[rows + row : rows + row + 1, :]
        parts += with_edges(plan, turned[row, :, lanes], west, east)
    return jnp.concatenate(parts, axis=0) * factor


def relay_kernel(plan, axes, from_x, to_y, out):
    out[0 : plan.chunk, :] = to_y[...]
    out[plan.chunk :, :] = from_x[plan.chunk + plan.edge :, :]


def square_places(plan):
    shape = (plan.columns, plan.columns)
    return lax.broadcasted_iota(jnp.int32, shape, 0), lax.broadcasted_iota(jnp.int32, shape, 1)


def row_of(plan, ref):
    return jnp.concatenate([ref[row : row + 1, :] for row in range(plan.rows)], axis=1)


def column_of(plan, row):
    down, across = square_places(plan)
    spread = jnp.broadcast_to(row, down.shape)
    return jnp.sum(jnp.where(down == across, spread, 0.0), axis=1, keepdims=True)


def first_kernel(plan, axes, *refs):
    waves_in, currents_in, target_in, stokes_in, refs = *refs[:4], refs[4:]
    waves, ocean_out, packed_out, order_out, stokes, refs = *refs[:5], refs[5:]
    count = len(plan.sizes)
    sec_out, lat_out, refs = refs[:count], refs[count : count + 2], refs[count + 2 :]
    currents, target, done = refs
    pairs = [(target_in, target), (waves_in, waves), (stokes_in, stokes), (currents_in, currents)]
    copies = [pltpu.make_async_copy(a, b, done.at[k]) for k, (a, b) in enumerate(pairs)]
    for copy in copies:
        copy.start()
    section, band = lax.axis_index(axes[1]), lax.axis_index(axes[0])
    even = lax.rem(band, 2) == 0
    columns, rows, cols = plan.columns, plan.rows, plan.cols
    copies[0].wait()
    down, across = square_places(plan)
    target_row = row_of(plan, target).astype(F32)
    same = column_of(plan, target_row) == target_row
    rank = jnp.sum(jnp.where(same & (down < across), 1.0, 0.0), axis=0, keepdims=True)
    slot = target_row * float(plan.chunk) + rank
    order = jnp.where(slot == down.astype(F32), 1.0, 0.0).astype(BF16)
    order_out[...] = twice(order)
    for copy in copies[1:]:
        copy.wait()
    total = None
    for start in range(0, plan.spectral, 256):
        part = waves[:, :, start : start + 256].reshape(columns, 256)
        product = stokes_product(part, stokes[start : start + 256, :])
        total = product if total is None else total + product
    moments = total[:columns] + total[columns:]
    moments = moments + pltpu.roll(moments, LANES // 2, 1)
    flat = currents[...].reshape(columns, 2 * plan.depth)
    ocean = jnp.concatenate([flat, jnp.zeros((columns, LANES - 2 * plan.depth), F32)], axis=1)
    ocean_out[...] = ocean
    ordered = dot(order, split_value(moments))
    ordered = ordered + pltpu.roll(ordered, LANES // 2, 1)
    west = [waves[row, 0:1, :] for row in range(rows)]
    east = [waves[row, cols - 1 : cols, :] for row in range(rows)]
    edges = jnp.concatenate(west + east, axis=0)
    fill_sections(plan, section, edges, ocean, ordered, packed_out, sec_out)
    sea_rows = ocean.reshape(rows, cols, LANES)
    ends = (waves[0], waves[rows - 1]), (sea_rows[0], sea_rows[rows - 1])
    fill_bands(plan, even, *ends, *lat_out)


def map_kernel(plan, axes, *refs):
    turning, drag, mask, order_twice, _, refs = *refs[:5], refs[5:]
    permute_out, permute_some_out, order_edge_out, turn_out, turn_edge_out = refs[:5]
    sea_out, sea_order_out, sea_some_out, keep_out = refs[5:]
    columns, rows, cols = plan.columns, plan.rows, plan.cols
    order = order_twice[:, :columns]
    sea = jnp.broadcast_to(column_of(plan, row_of(plan, mask).astype(F32)), (columns, LANES))
    turn = jnp.broadcast_to(column_of(plan, row_of(plan, turning)), (columns, LANES))
    sea_out[...] = sea
    turn_out[...] = turn
    west = [turn[row * cols : row * cols + 1, :] for row in range(rows)]
    east = [turn[(row + 1) * cols - 1 : (row + 1) * cols, :] for row in range(rows)]
    turn_edge_out[...] = jnp.concatenate(west + east, axis=0)
    sea_order_out[...] = dot(order, sea.astype(BF16))
    down, across = square_places(plan)
    same = jnp.where(down == across, 1.0, 0.0).astype(BF16)
    back = lax.dot_general(
        order, same, (((0,), (0,)), ((), ())), preferred_element_type=F32
    )
    permute = (back * sea[:, :columns]).astype(BF16)
    permute_out[...] = permute
    shape = (columns, 4 * rows)
    number = lax.rem(lane_of(shape), 2 * rows)
    wanted = lax.rem(number, rows) * cols + lax.div(number, rows) * (cols - 1)
    chosen = lax.broadcasted_iota(jnp.int32, shape, 0) == wanted
    order_edge_out[...] = dot(order, jnp.where(chosen, 1.0, 0.0).astype(BF16)).astype(BF16)
    shape = (2 * cols + 2 * rows, columns)
    place = lax.broadcasted_iota(jnp.int32, shape, 0)
    number = place - 2 * cols
    wanted = jnp.where(
        place < 2 * cols,
        place + jnp.where(place < cols, 0, (rows - 2) * cols),
        lax.rem(number, rows) * cols + lax.div(number, rows) * (cols - 1),
    )
    chosen = jnp.where(lane_of(shape) == wanted, 1.0, 0.0).astype(BF16)
    permute_some_out[...] = dot(chosen, permute).astype(BF16)
    sea_some_out[...] = dot(chosen, sea.astype(BF16))
    keep = 1.0 - drag[...].reshape(1, plan.depth)
    blank = jnp.zeros((1, LANES - 2 * plan.depth), F32)
    keep_out[...] = jnp.broadcast_to(jnp.concatenate([keep, keep, blank], axis=1), (8, LANES))


class Directions:
    def __init__(self, shape):
        direction = lax.rem(lane_of(shape), NDIR)
        self.eastward = (direction < NDIR // 4) | (direction >= 3 * NDIR // 4)
        self.northward = direction < NDIR // 2
        self.first, self.final = direction == 0, direction == NDIR - 1

    def turned(self, moved, rate, gain):
        behind = jnp.where(
            self.first, pltpu.roll(moved, LANES - (NDIR - 1), 1), pltpu.roll(moved, 1, 1)
        )
        forward = jnp.where(
            self.final, pltpu.roll(moved, NDIR - 1, 1), pltpu.roll(moved, LANES - 1, 1)
        )
        return moved - jnp.abs(rate) * gain * (moved - jnp.where(rate > 0.0, behind, forward))


def move_kernel(plan, axes, *refs):
    waves, turn, rates, near, far, refs = *refs[:5], refs[5:]
    if len(refs) > 1:
        order, turned_out, edge_out, sorted_out = refs
    else:
        (turned_out,) = refs
    even = lax.rem(lax.axis_index(axes[0]), 2) == 0
    rows, cols, tiles = plan.rows, plan.cols, plan.tiles
    block = (cols, LANES)
    masks = Directions(block)
    place = lax.broadcasted_iota(jnp.int32, block, 0)
    outside = place == jnp.where(masks.eastward, 0, cols - 1)
    for tile in range(tiles):
        lanes = slice(tile * LANES, (tile + 1) * LANES)
        stay, along_x, along_y, gain = (rates[k : k + 1, lanes] for k in range(4))
        along_x = jnp.where(outside, 0.0, along_x)
        half = tile % (tiles // 2)
        half = slice(half * LANES, (half + 1) * LANES)
        south_edge = jnp.where(even, far[:, half], near[:, half])
        north_edge = jnp.where(even, near[:, half], far[:, half])
        if tile >= tiles // 2:
            south_edge = pltpu.roll(south_edge, LANES - NDIR // 2, 1)
            north_edge = pltpu.roll(north_edge, LANES - NDIR // 2, 1)
        for row in range(rows):
            center = waves[row, :, lanes]
            south = waves[row - 1, :, lanes] if row else south_edge
            north = waves[row + 1, :, lanes] if row < rows - 1 else north_edge
            moved = (
                stay * center
                + along_x
                * jnp.where(
                    masks.eastward, pltpu.roll(center, 1, 0), pltpu.roll(center, cols - 1, 0)
                )
                + along_y * jnp.where(masks.northward, south, north)
            )
            rate = turn[row * cols : (row + 1) * cols, :]
            turned = masks.turned(moved, rate, gain)
            turned_out[row, :, lanes] = turned
            if len(refs) > 1:
                edge_out[row : row + 1, lanes] = turned[0:1, :]
                edge_out[rows + row : rows + row + 1, lanes] = turned[cols - 1 :, :]
    if len(refs) > 1:
        for start in range(0, plan.spectral, 256):
            part = turned_out[:, :, start : start + 256].reshape(plan.columns, 256)
            high = part.astype(BF16)
            low = (part - high.astype(F32)).astype(BF16)
            sorted_out[:, start : start + 256] = dot(
                order[...], jnp.concatenate([high, low], axis=0)
            )


def swapped(plan, value):
    half = plan.depth
    zonal = lane_of(value.shape) < half
    return jnp.where(zonal, pltpu.roll(value, LANES - half, 1), pltpu.roll(value, half, 1))


def send_kernel(plan, axes, *refs):
    turned, turned_edge, turned_order, ocean_in, packed_in, permute_some, order_edge = refs[:7]
    turn_edge, sea, sea_order, sea_some, keep, stokes, rates, grow, refs = *refs[7:15], refs[15:]
    count = len(plan.sizes)
    near, far, sec_in, refs = refs[0], refs[1], refs[2 : 2 + count], refs[2 + count :]
    ocean_out, packed_out, coupled, extra_out, far_out, near_out = refs[:6]
    sec_out = refs[6:]
    section, band = lax.axis_index(axes[1]), lax.axis_index(axes[0])
    even = lax.rem(band, 2) == 0
    columns, rows, cols = plan.columns, plan.rows, plan.cols

    west_edge, east_edge = take_sections(plan, section, packed_in, sec_in, coupled)
    both, drift = currents_twice(coupled[...])
    in_order = twice(split_value(both * sea_order[...]))
    at_some = twice(dot(permute_some[...], split_value(both)).astype(BF16))
    extra = edge_part(plan, rates, turn_edge, west_edge, east_edge)
    total = None
    some = []
    wet, wet_some = twice(sea_order[...]), twice(sea_some[...])
    for number, start in enumerate(range(0, plan.spectral, 256)):
        lanes = slice(start, start + 256)
        table = growth_table(grow, number)
        from_edges = jnp.concatenate(extra[2 * number : 2 * number + 2], axis=1)
        extra_out[:, lanes] = from_edges
        high = from_edges.astype(BF16).astype(F32)
        halves = jnp.concatenate([high, from_edges - high], axis=0).astype(BF16)
        grown = turned_order[:, lanes] + dot(order_edge[...], halves)
        grown = grown * (wet + dot(in_order, table))
        product = stokes_product(grown, stokes[lanes, :])
        total = product if total is None else total + product
        parts = []
        for row in (0, rows - 1):
            west, east = from_edges[row : row + 1, :], from_edges[rows + row : rows + row + 1, :]
            parts += with_edges(plan, turned[row, :, lanes], west, east)
        parts.append(turned_edge[:, lanes] + from_edges)
        some.append(jnp.concatenate(parts, axis=0) * (wet_some + dot(at_some, table)))
    new = ocean_step(
        plan, band, even, ocean_in, drift, near, far, west_edge, east_edge, keep, sea
    )
    ocean = jnp.concatenate(new, axis=0)
    ocean_out[...] = ocean
    moments = total[:columns] + total[columns:]
    moments = moments + pltpu.roll(moments, LANES // 2, 1)
    some = jnp.concatenate(some, axis=1)
    fill_sections(plan, section, some[2 * cols :, :], ocean, moments, packed_out, sec_out)
    ends = (some[:cols, :], some[cols : 2 * cols, :]), (new[0], new[rows - 1])
    fill_bands(plan, even, *ends, far_out, near_out)


def grow_kernel(plan, axes, *refs):
    turned, extra, coupled, permute, sea, grow, _, waves_out = refs
    both, _ = currents_twice(coupled[...])
    at_waves = twice(dot(permute[...], split_value(both)).astype(BF16))
    wet = twice(sea[...])
    for number, start in enumerate(range(0, plan.spectral, 256)):
        lanes = slice(start, start + 256)
        factor = wet + dot(at_waves, growth_table(grow, number))
        grown = grown_part(plan, turned, extra[:, lanes], factor, lanes)
        waves_out[:, :, lanes] = grown.reshape(plan.rows, plan.cols, 256)


def last_kernel(plan, axes, *refs):
    turned, ocean_in, packed_in, permute, turn_edge, sea, keep, rates, grow = refs[:9]
    count = len(plan.sizes)
    near, far, sec_in, refs = refs[9], refs[10], refs[11 : 11 + count], refs[11 + count :]
    waves_far, ocean_far, coupled, waves_out, ocean_out, done = refs
    section, band = lax.axis_index(axes[1]), lax.axis_index(axes[0])
    even = lax.rem(band, 2) == 0

    west_edge, east_edge = take_sections(plan, section, packed_in, sec_in, coupled)
    both, drift = currents_twice(coupled[...])
    at_waves = twice(dot(permute[...], split_value(both)).astype(BF16))
    extra = edge_part(plan, rates, turn_edge, west_edge, east_edge)
    new = ocean_step(
        plan, band, even, ocean_in, drift, near, far, west_edge, east_edge, keep, sea
    )
    for row, value in enumerate(new):
        ocean_out[row] = value[:, : 2 * plan.depth]
    copies = [pltpu.make_async_copy(ocean_out, ocean_far, done.at[0])]
    copies[0].start()
    wet = twice(sea[...])
    for number, start in enumerate(range(0, plan.spectral, 256)):
        lanes = slice(start, start + 256)
        factor = wet + dot(at_waves, growth_table(grow, number))
        from_edges = jnp.concatenate(extra[2 * number : 2 * number + 2], axis=1)
        grown = grown_part(plan, turned, from_edges, factor, lanes)
        waves_out[:, :, lanes] = grown.reshape(plan.rows, plan.cols, 256)
        copy = pltpu.make_async_copy(
            waves_out.at[:, :, lanes], waves_far.at[:, :, lanes], done.at[number + 1]
        )
        copy.start()
        copies.append(copy)
    for copy in copies:
        copy.wait()


def per_device(plan, axes, spectra, turning, currents, drag_rates, land_mask, ocean_target):
    stokes, rates, grow = (
        jnp.asarray(table) for table in build_tables(NFREQ, NDIR, drag_rates.shape[0])
    )
    columns, rows, cols, spectral = plan.columns, plan.rows, plan.cols, plan.spectral
    shape = jax.ShapeDtypeStruct
    params = pltpu.CompilerParams(vmem_limit_bytes=32 * 1024 * 1024)
    to_sections = [shape((size, LANES), F32) for size in plan.sizes]
    to_band = shape((cols, spectral // 2 + LANES), F32)
    state = shape((columns, LANES), F32)
    field = shape(spectra.shape, F32)
    at_edges = shape((2 * rows, LANES), F32)
    edge_field = shape((2 * rows, spectral), F32)
    some = 2 * cols + 2 * rows
    spans = spectral // 256

    def call(kernel, outs, scratch, *args, space_in=pltpu.VMEM, space_out=pltpu.VMEM):
        return pl.pallas_call(
            functools.partial(kernel, plan, axes),
            out_shape=outs,
            in_specs=[pl.BlockSpec(memory_space=space_in)] * len(args),
            out_specs=[pl.BlockSpec(memory_space=space_out)] * len(outs),
            scratch_shapes=scratch,
            compiler_params=params,
        )(*args)

    pairs = [(i, i ^ 1) for i in range(plan.bands) if i ^ 1 < plan.bands]
    others = [(i, ((i + 1) ^ 1) - 1) for i in range(1, plan.bands)]
    others = [(i, j) for i, j in others if j < plan.bands]

    def exchange(to_far, to_near, to_sections, meanwhile):
        got = []
        if plan.relay:
            to_x, to_y, *to_sections = to_sections
            got.append(lax.ppermute(to_x, axes[1], plan.table(0, 1)))
        far_in = lax.ppermute(to_far, axes[0], others)
        near_in = lax.ppermute(to_near, axes[0], pairs)
        first = to_far
        if plan.relay:
            (first,) = call(
                relay_kernel,
                [shape((2 * plan.chunk + plan.edge, LANES), F32)],
                [],
                got[0],
                to_y,
            )
            got.append(lax.ppermute(first, axes[1], plan.table(0, 2)))
        got += [
            lax.ppermute(message, axes[1], table)
            for message, table in zip(to_sections, plan.direct)
        ]
        return meanwhile(first), [near_in, far_in, *got]

    waves, ocean, packed, order, stokes, *sent = call(
        first_kernel,
        [
            field,
            state,
            state,
            shape((columns, 2 * columns), BF16),
            shape(stokes.shape, stokes.dtype),
            *to_sections,
            to_band,
            to_band,
        ],
        [
            pltpu.VMEM(currents.shape, F32),
            pltpu.VMEM(ocean_target.shape, jnp.int32),
            pltpu.SemaphoreType.DMA((4,)),
        ],
        *[
            pltpu.with_memory_space_constraint(array, pltpu.HBM)
            for array in (spectra, currents, ocean_target, stokes)
        ],
        space_in=pltpu.HBM,
    )

    def maps(first):
        return call(
            map_kernel,
            [
                shape((columns, columns), BF16),
                shape((some, columns), BF16),
                shape((columns, 4 * rows), BF16),
                state,
                at_edges,
                state,
                state,
                shape((some, LANES), F32),
                shape((8, LANES), F32),
            ],
            [],
            turning,
            drag_rates,
            land_mask,
            order,
            first,
        )

    made, came = exchange(*sent[-2:], sent[:-2], maps)
    permute, permute_some, order_edge, turn, turn_edge, sea, sea_order, sea_some, keep = made
    for step in range(STEPS - 1):
        turned, turned_edge, turned_order = call(
            move_kernel,
            [field, edge_field, shape((columns, spectral), F32)],
            [],
            waves,
            turn,
            rates,
            *came[:2],
            order,
        )
        ocean, packed, coupled, extra, to_far, to_near, *sent = call(
            send_kernel,
            [state, state, state, edge_field, to_band, to_band] + to_sections,
            [],
            turned,
            turned_edge,
            turned_order,
            ocean,
            packed,
            permute_some,
            order_edge,
            turn_edge,
            sea,
            sea_order,
            sea_some,
            keep,
            stokes,
            rates,
            grow,
            *came,
        )

        def grown(first):
            (waves,) = call(
                grow_kernel, [field], [], turned, extra, coupled, permute, sea, grow, first
            )
            return waves

        waves, came = exchange(to_far, to_near, sent, grown)
    (turned,) = call(move_kernel, [field], [], waves, turn, rates, *came[:2])
    return call(
        last_kernel,
        [field, shape(currents.shape, F32)],
        [
            pltpu.VMEM((columns, LANES), F32),
            pltpu.VMEM(spectra.shape, F32),
            pltpu.VMEM(currents.shape, F32),
            pltpu.SemaphoreType.DMA((1 + spans,)),
        ],
        turned,
        ocean,
        packed,
        permute,
        turn_edge,
        sea,
        keep,
        rates,
        grow,
        *came,
        space_out=pltpu.HBM,
    )


def solution(mesh):
    sections, bands = mesh.shape["sec"], mesh.shape["lat"]

    def local(spectra, turning, currents, drag_rates, land_mask, ocean_target):
        rows, cols, spectral = spectra.shape
        plan = Plan(sections, bands, rows, cols, spectral, drag_rates.shape[0])
        return per_device(
            plan, ("lat", "sec"), spectra, turning, currents, drag_rates, land_mask, ocean_target
        )

    return jax.shard_map(
        local,
        mesh=mesh,
        in_specs=(
            P("lat", "sec", None),
            P("lat", "sec"),
            P("lat", "sec", None),
            P(),
            P("lat", "sec"),
            P("lat", "sec"),
        ),
        out_specs=(P("lat", "sec", None), P("lat", "sec", None)),
        check_vma=False,
    )
```

```python
import functools
import math

import jax
import jax.numpy as jnp
import ml_dtypes
import numpy as np
from jax import lax
from jax.experimental import pallas as pl
from jax.experimental.pallas import tpu as pltpu
from jax.sharding import PartitionSpec as P

NFREQ = 24
NDIR = 32
STEPS = 3

stokes_scale = 0.1
ocean_dt = 0.3
current_gain = 0.2

LANES = 128
F32 = jnp.float32
BF16 = jnp.bfloat16


def split_halves(table):
    high = table.astype(ml_dtypes.bfloat16)
    low = (table - high.astype(np.float64)).astype(ml_dtypes.bfloat16)
    return high, low


def build_tables(nfreq, ndir, ndepth):
    fraction = np.arange(nfreq) / (nfreq - 1)
    angles = (np.arange(ndir) + 0.5) * (2.0 * math.pi / ndir)
    east_part, north_part = np.cos(angles), np.sin(angles)
    courant = 0.1 + 0.3 * fraction
    depth_level = 0.5 + (ndepth - 2) * (1.0 - fraction)
    weights = np.maximum(1.0 - np.abs(np.arange(ndepth)[None, :] - depth_level[:, None]), 0.0)
    mean_weights = weights / weights.sum(axis=1, keepdims=True)
    x_rate = np.abs(courant[:, None] * east_part[None, :]).reshape(-1)
    y_rate = np.abs(courant[:, None] * north_part[None, :]).reshape(-1)
    turn_gain = np.repeat(1.0 - 0.5 * fraction, ndir)
    rates = np.stack([1.0 - x_rate - y_rate, x_rate, y_rate, turn_gain] * 2).astype(np.float32)
    compass = np.stack([east_part, north_part])
    stokes = (stokes_scale * weights[:, None, None, :] * compass.T[None, :, :, None]).reshape(
        nfreq * ndir, 2 * ndepth
    )
    growth = current_gain * (1.0 + fraction)
    grow = (
        growth[None, None, :, None] * mean_weights.T[None, :, :, None] * compass[:, None, None, :]
    ).reshape(2 * ndepth, nfreq * ndir)
    high, low = split_halves(stokes)
    blank = np.zeros_like(high)
    stokes_once = np.concatenate([high, low], axis=1)
    stokes_upper = np.concatenate([blank, high, blank, low], axis=1)
    high, low = split_halves(grow)
    grow = np.concatenate([high, high, low, low], axis=0)
    return (
        stokes_once,
        stokes_upper,
        rates,
        grow.reshape(2 * LANES, -1, LANES).transpose(1, 0, 2).reshape(-1, LANES),
    )


class Plan:
    def __init__(self, sections, bands, rows, cols, spectral, depth):
        self.sections, self.bands = sections, bands
        self.rows, self.cols, self.spectral, self.depth = rows, cols, spectral, depth
        self.columns = rows * cols
        self.chunk = self.columns // sections
        self.tiles = spectral // LANES
        self.some = -(-(2 * cols + 2 * rows) // 16) * 16
        self.edge = ((self.tiles // 2 + 1) * rows + 7) // 8 * 8
        self.relay = sections % 4 == 0
        self.quad = 4 if self.relay else 1
        self.hops = [
            (hop, flip)
            for hop in range(1, sections // self.quad)
            for flip in ((3, 1, 2, 0) if self.relay else (0,))
        ]
        self.direct = [self.table(*hop) for hop in self.hops]
        self.edges = [
            any(abs(target - i) == 1 for i, target in table) for table in self.direct
        ]
        self.sizes = [self.chunk + (self.edge if edge else 0) for edge in self.edges]
        if self.relay:
            self.sizes = [2 * (self.chunk + self.edge), self.chunk] + self.sizes

    def table(self, hop, flip):
        return [(i, self.partner(i, hop, flip, divmod)[0]) for i in range(self.sections)]

    def partner(self, section, hop, flip, divide=lambda a, b: (lax.div(a, b), lax.rem(a, b))):
        groups = self.sections // self.quad
        high, low = divide(section, self.quad)
        if flip & 1:
            low = low + 1 - 2 * divide(low, 2)[1]
        if flip & 2:
            low = low + 2 - 4 * divide(low, 2)[0]
        return tuple(
            divide(high + shift, groups)[1] * self.quad + low for shift in (hop, groups - hop)
        )

    def received(self, section, messages):
        parts = []
        if self.relay:
            from_x, from_y = messages[:2]
            parts = [
                (self.partner(section, 0, 1)[1], from_x, 0, self.chunk),
                (self.partner(section, 0, 2)[1], from_y, 0, None),
                (self.partner(section, 0, 3)[1], from_y, self.chunk, 2 * self.chunk),
            ]
            messages = messages[2:]
        for message, hop, edge in zip(messages, self.hops, self.edges):
            parts.append((self.partner(section, *hop)[1], message, 0, self.chunk if edge else None))
        return parts

    def sent(self, section, messages):
        parts = []
        if self.relay:
            to_x, to_y = messages[:2]
            parts = [
                (self.partner(section, 0, 1)[0], to_x, 0, self.chunk),
                (self.partner(section, 0, 2)[0], to_y, 0, None),
                (
                    self.partner(section, 0, 3)[0],
                    to_x,
                    self.chunk + self.edge,
                    2 * self.chunk + self.edge,
                ),
            ]
            messages = messages[2:]
        for message, hop, edge in zip(messages, self.hops, self.edges):
            parts.append((self.partner(section, *hop)[0], message, 0, self.chunk if edge else None))
        return parts


def lane_of(shape):
    return lax.broadcasted_iota(jnp.int32, shape, len(shape) - 1)


def dot(a, b):
    return jnp.dot(a, b, preferred_element_type=F32)


def split_value(value):
    high = value.astype(BF16)
    return high, (value - high.astype(F32)).astype(BF16)


def stokes_product(part, table):
    return dot(jnp.concatenate(split_value(part), axis=0), table)


def packed_half(edge, tile, half, ahead, forward):
    first = edge[:, tile * LANES : (tile + 1) * LANES]
    second = edge[:, (tile + half) * LANES : (tile + half + 1) * LANES]
    keep = jnp.where(ahead, 1, 0) == jnp.where(forward, 1, 0)
    return jnp.where(keep, first, pltpu.roll(second, NDIR // 2, 1))


def fill_band(plan, northward, edge, sea_row, out):
    half = plan.tiles // 2
    masks = Directions((plan.cols, LANES))
    for tile in range(half):
        out[:, tile * LANES : (tile + 1) * LANES] = packed_half(
            edge, tile, half, masks.northward, northward
        )
    out[:, plan.spectral // 2 :] = sea_row


def fill_bands(plan, even, edges, sea_rows, far, near):
    for out, northward in ((far, jnp.logical_not(even)), (near, even)):
        edge = jnp.where(northward, edges[1], edges[0])
        fill_band(plan, northward, edge, jnp.where(northward, sea_rows[1], sea_rows[0]), out)


def fill_sections(plan, section, edges, ocean, ordered, packed_out, sec_out):
    chunk, rows, cols, half = plan.chunk, plan.rows, plan.cols, plan.tiles // 2
    lane = lane_of((plan.columns, LANES))
    packed_out[...] = jnp.where(lane < LANES // 2, ocean, ordered)
    sea_rows = ocean.reshape(rows, cols, LANES)
    masks = Directions((rows, LANES))
    for target, out, at, edge_at in plan.sent(section, sec_out):
        out[at : at + chunk, :] = packed_out[pl.ds(pl.multiple_of(target * chunk, 8), chunk), :]
        if edge_at is None:
            continue
        eastward = target == section + 1
        edge = jnp.where(eastward, edges[rows:, :], edges[:rows, :])
        for tile in range(half):
            place = edge_at + tile * rows
            out[place : place + rows, :] = packed_half(edge, tile, half, masks.eastward, eastward)
        for row in range(rows):
            place = edge_at + half * rows + row
            out[place : place + 1, :] = jnp.where(
                eastward, sea_rows[row, cols - 1 : cols, :], sea_rows[row, 0:1, :]
            )


def take_sections(plan, section, packed_in, sec_in, coupled):
    chunk = plan.chunk
    own = pl.ds(pl.multiple_of(section * chunk, 8), chunk)
    coupled[own, :] = packed_in[own, :]
    west = east = jnp.zeros((plan.edge, LANES), F32)
    for source, message, at, edge_at in plan.received(section, sec_in):
        coupled[pl.ds(pl.multiple_of(source * chunk, 8), chunk), :] = message[at : at + chunk, :]
        if edge_at is not None:
            edge = message[edge_at : edge_at + plan.edge, :]
            west = jnp.where(source == section - 1, edge, west)
            east = jnp.where(source == section + 1, edge, east)
    return west, east


def edge_part(plan, rates, turn_edge, west_edge, east_edge):
    rows, half = plan.rows, plan.tiles // 2
    shape = (2 * rows, LANES)
    masks = Directions(shape)
    westmost = lax.broadcasted_iota(jnp.int32, shape, 0) < rows
    reached = jnp.where(masks.eastward, 1, 0) == jnp.where(westmost, 1, 0)
    parts = []
    for tile in range(plan.tiles):
        lanes = slice(tile * LANES, (tile + 1) * LANES)
        edge = slice(tile % half * rows, (tile % half + 1) * rows)
        came = jnp.concatenate([west_edge[edge, :], east_edge[edge, :]], axis=0)
        if tile >= half:
            came = pltpu.roll(came, LANES - NDIR // 2, 1)
        moved = rates[1:2, lanes] * jnp.where(reached, came, 0.0)
        parts.append(masks.turned(moved, turn_edge[...], rates[3:4, lanes]))
    return parts


def ocean_step(plan, band, even, ocean_in, stokes, near, far, west_edge, east_edge, keep, sea):
    rows, cols, half = plan.rows, plan.cols, plan.tiles // 2
    block = (cols, LANES)
    zonal = lane_of(block) < plan.depth
    place = lax.broadcasted_iota(jnp.int32, block, 0)
    at_west, at_east = place == 0, place == cols - 1
    lanes = slice(plan.spectral // 2, plan.spectral // 2 + LANES)
    south_edge = jnp.where(even, far[:, lanes], near[:, lanes])
    north_edge = jnp.where(even, near[:, lanes], far[:, lanes])
    new = []
    for row in range(rows):
        flat = slice(row * cols, (row + 1) * cols)
        edge = slice(half * rows + row, half * rows + row + 1)
        center = ocean_in[flat, :]
        west = jnp.where(at_west, west_edge[edge, :], pltpu.roll(center, 1, 0))
        east = jnp.where(at_east, east_edge[edge, :], pltpu.roll(center, cols - 1, 0))
        south = ocean_in[(row - 1) * cols : row * cols, :] if row else south_edge
        north = ocean_in[(row + 1) * cols : (row + 2) * cols, :] if row < rows - 1 else north_edge
        shear = 0.5 * jnp.where(zonal, south - north, east - west)
        y = (band * rows + row).astype(F32)
        spin = 0.2 + 0.6 * y / float(plan.bands * rows) + (shear + swapped(plan, shear))
        turn_by = ocean_dt * spin * swapped(plan, center + stokes[flat, :])
        new.append(keep[0:1, :] * (center + jnp.where(zonal, turn_by, -turn_by)) * sea[flat, :])
    return new


def twice(value, axis=1):
    return jnp.concatenate([value, value], axis=axis)


def growth_table(grow, number):
    size = 2 * LANES
    return jnp.concatenate(
        [grow[(2 * number + k) * size : (2 * number + k + 1) * size, :] for k in range(2)], axis=1
    )


def growth_halves(arrived):
    high = arrived.astype(BF16).astype(F32)
    lower = lane_of(arrived.shape) < LANES // 2
    return jnp.where(lower, high, pltpu.roll(arrived - high, LANES // 2, 1)).astype(BF16)


def with_edges(plan, turned, west, east):
    place = lax.broadcasted_iota(jnp.int32, (8, 256), 0)
    return [
        turned[0:8, :] + jnp.where(place == 0, west, 0.0),
        turned[8 : plan.cols - 8, :],
        turned[plan.cols - 8 :, :] + jnp.where(place == 7, east, 0.0),
    ]


def grown_part(plan, turned, from_edges, factor, lanes):
    rows = plan.rows
    parts = []
    for row in range(rows):
        west, east = from_edges[row : row + 1, :], from_edges[rows + row : rows + row + 1, :]
        parts += with_edges(plan, turned[row, :, lanes], west, east)
    return jnp.concatenate(parts, axis=0) * factor


def relay_kernel(plan, axes, from_x, to_y, out):
    out[0 : plan.chunk, :] = to_y[...]
    out[plan.chunk :, :] = from_x[plan.chunk + plan.edge :, :]


def square_places(plan):
    shape = (plan.columns, plan.columns)
    return lax.broadcasted_iota(jnp.int32, shape, 0), lax.broadcasted_iota(jnp.int32, shape, 1)


def row_of(plan, ref):
    return jnp.concatenate([ref[row : row + 1, :] for row in range(plan.rows)], axis=1)


def column_of(plan, row):
    down, across = square_places(plan)
    spread = jnp.broadcast_to(row, down.shape)
    return jnp.sum(jnp.where(down == across, spread, 0.0), axis=1, keepdims=True)


def first_kernel(plan, axes, *refs):
    waves_in, currents_in, target_in, stokes_in, refs = *refs[:4], refs[4:]
    waves, ocean_out, packed_out, order_out, refs = *refs[:4], refs[4:]
    count = len(plan.sizes)
    sec_out, lat_out, refs = refs[:count], refs[count : count + 2], refs[count + 2 :]
    currents, target, stokes, done = refs
    pairs = [(target_in, target), (waves_in, waves), (stokes_in, stokes), (currents_in, currents)]
    copies = [pltpu.make_async_copy(a, b, done.at[k]) for k, (a, b) in enumerate(pairs)]
    for copy in copies:
        copy.start()
    section, band = lax.axis_index(axes[1]), lax.axis_index(axes[0])
    even = lax.rem(band, 2) == 0
    columns, rows, cols = plan.columns, plan.rows, plan.cols
    copies[0].wait()
    down, across = square_places(plan)
    target_row = row_of(plan, target).astype(F32)
    same = column_of(plan, target_row) == target_row
    rank = jnp.sum(jnp.where(same & (down < across), 1.0, 0.0), axis=0, keepdims=True)
    slot = target_row * float(plan.chunk) + rank
    order = twice(jnp.where(slot == down.astype(F32), 1.0, 0.0)).astype(BF16)
    order_out[...] = order
    for copy in copies[1:]:
        copy.wait()
    total = None
    for start in range(0, plan.spectral, 256):
        part = waves[:, :, start : start + 256].reshape(columns, 256)
        product = stokes_product(part, stokes[start : start + 256, :])
        total = product if total is None else total + product
    moments = total[:columns] + total[columns:]
    flat = currents[...].reshape(columns, 2 * plan.depth)
    ocean = jnp.concatenate([flat, jnp.zeros((columns, LANES - 2 * plan.depth), F32)], axis=1)
    ocean_out[...] = ocean
    ordered = dot(order, jnp.concatenate(split_value(moments), axis=0))
    ordered = ordered + pltpu.roll(ordered, LANES // 2, 1)
    west = [waves[row, 0:1, :] for row in range(rows)]
    east = [waves[row, cols - 1 : cols, :] for row in range(rows)]
    edges = jnp.concatenate(west + east, axis=0)
    fill_sections(plan, section, edges, ocean, ordered, packed_out, sec_out)
    sea_rows = ocean.reshape(rows, cols, LANES)
    ends = (waves[0], waves[rows - 1]), (sea_rows[0], sea_rows[rows - 1])
    fill_bands(plan, even, *ends, *lat_out)


def map_kernel(plan, axes, *refs):
    turning, drag, mask, order_twice, _, refs = *refs[:5], refs[5:]
    permute_out, permute_some_out, slots_out, turn_out, turn_edge_out = refs[:5]
    sea_out, sea_order_out, sea_some_out, keep_out = refs[5:]
    columns, rows, cols = plan.columns, plan.rows, plan.cols
    order = order_twice[:, :columns]
    sea = jnp.broadcast_to(column_of(plan, row_of(plan, mask).astype(F32)), (columns, LANES))
    turn = jnp.broadcast_to(column_of(plan, row_of(plan, turning)), (columns, LANES))
    sea_out[...] = sea
    turn_out[...] = turn
    west = [turn[row * cols : row * cols + 1, :] for row in range(rows)]
    east = [turn[(row + 1) * cols - 1 : (row + 1) * cols, :] for row in range(rows)]
    turn_edge_out[...] = jnp.concatenate(west + east, axis=0)
    sea_order_out[...] = dot(order, sea.astype(BF16))
    down, across = square_places(plan)
    same = jnp.where(down == across, 1.0, 0.0).astype(BF16)
    back = lax.dot_general(
        order, same, (((0,), (0,)), ((), ())), preferred_element_type=F32
    )
    permute = (back * sea[:, :columns]).astype(BF16)
    permute_out[...] = permute
    shape = (plan.some, columns)
    place = lax.broadcasted_iota(jnp.int32, shape, 0)
    number = place - 2 * cols
    wanted = jnp.where(
        place < 2 * cols,
        place + jnp.where(place < cols, 0, (rows - 2) * cols),
        lax.rem(number, rows) * cols + lax.div(number, rows) * (cols - 1),
    )
    wanted = jnp.where(number < 2 * rows, wanted, -1)
    chosen = jnp.where(lane_of(shape) == wanted, 1.0, 0.0).astype(BF16)
    permute_some_out[...] = dot(chosen, permute).astype(BF16)
    sea_some_out[...] = dot(chosen, sea.astype(BF16))
    slot = jnp.sum(order.astype(F32) * down.astype(F32), axis=0, keepdims=True)
    slot = jnp.broadcast_to(column_of(plan, slot), (columns, LANES)).astype(BF16)
    slots_out[...] = dot(chosen, slot)[2 * cols : 2 * cols + 2 * rows, :].astype(jnp.int32)
    keep = 1.0 - drag[...].reshape(1, plan.depth)
    blank = jnp.zeros((1, LANES - 2 * plan.depth), F32)
    keep_out[...] = jnp.broadcast_to(jnp.concatenate([keep, keep, blank], axis=1), (8, LANES))


class Directions:
    def __init__(self, shape):
        direction = lax.rem(lane_of(shape), NDIR)
        self.eastward = (direction < NDIR // 4) | (direction >= 3 * NDIR // 4)
        self.northward = direction < NDIR // 2
        self.first, self.final = direction == 0, direction == NDIR - 1

    def turned(self, moved, rate, gain):
        behind = jnp.where(
            self.first, pltpu.roll(moved, LANES - (NDIR - 1), 1), pltpu.roll(moved, 1, 1)
        )
        forward = jnp.where(
            self.final, pltpu.roll(moved, NDIR - 1, 1), pltpu.roll(moved, LANES - 1, 1)
        )
        return moved - jnp.abs(rate) * gain * (moved - jnp.where(rate > 0.0, behind, forward))


def move_kernel(plan, axes, *refs):
    waves, turn, rates, near, far, refs = *refs[:5], refs[5:]
    if len(refs) > 1:
        order, turned_out, edge_out, sorted_out = refs
    else:
        (turned_out,) = refs
    even = lax.rem(lax.axis_index(axes[0]), 2) == 0
    rows, cols, tiles = plan.rows, plan.cols, plan.tiles
    block = (cols, LANES)
    masks = Directions(block)
    place = lax.broadcasted_iota(jnp.int32, block, 0)
    outside = place == jnp.where(masks.eastward, 0, cols - 1)
    for tile in range(tiles):
        lanes = slice(tile * LANES, (tile + 1) * LANES)
        stay, along_x, along_y, gain = (rates[k : k + 1, lanes] for k in range(4))
        along_x = jnp.where(outside, 0.0, along_x)
        half = tile % (tiles // 2)
        half = slice(half * LANES, (half + 1) * LANES)
        south_edge = jnp.where(even, far[:, half], near[:, half])
        north_edge = jnp.where(even, near[:, half], far[:, half])
        if tile >= tiles // 2:
            south_edge = pltpu.roll(south_edge, LANES - NDIR // 2, 1)
            north_edge = pltpu.roll(north_edge, LANES - NDIR // 2, 1)
        for row in range(rows):
            center = waves[row, :, lanes]
            south = waves[row - 1, :, lanes] if row else south_edge
            north = waves[row + 1, :, lanes] if row < rows - 1 else north_edge
            moved = (
                stay * center
                + along_x
                * jnp.where(
                    masks.eastward, pltpu.roll(center, 1, 0), pltpu.roll(center, cols - 1, 0)
                )
                + along_y * jnp.where(masks.northward, south, north)
            )
            rate = turn[row * cols : (row + 1) * cols, :]
            turned = masks.turned(moved, rate, gain)
            turned_out[row, :, lanes] = turned
            if len(refs) > 1:
                edge_out[row : row + 1, lanes] = turned[0:1, :]
                edge_out[rows + row : rows + row + 1, lanes] = turned[cols - 1 :, :]
    if len(refs) > 1:
        for start in range(0, plan.spectral, 256):
            part = turned_out[:, :, start : start + 256].reshape(plan.columns, 256)
            sorted_out[:, start : start + 256] = dot(
                order[...], jnp.concatenate(split_value(part), axis=0)
            )


def swapped(plan, value):
    half = plan.depth
    zonal = lane_of(value.shape) < half
    return jnp.where(zonal, pltpu.roll(value, LANES - half, 1), pltpu.roll(value, half, 1))


def send_kernel(plan, axes, *refs):
    turned, turned_edge, turned_order, ocean_in, packed_in, permute_some, slots = refs[:7]
    turn_edge, sea, sea_order, sea_some, keep, stokes, rates, grow, refs = *refs[7:15], refs[15:]
    count = len(plan.sizes)
    near, far, sec_in, refs = refs[0], refs[1], refs[2 : 2 + count], refs[2 + count :]
    ocean_out, packed_out, coupled, extra_out, far_out, near_out = refs[:6]
    sec_out, in_order = refs[6 : 6 + count], refs[6 + count]
    section, band = lax.axis_index(axes[1]), lax.axis_index(axes[0])
    even = lax.rem(band, 2) == 0
    columns, rows, cols = plan.columns, plan.rows, plan.cols

    west_edge, east_edge = take_sections(plan, section, packed_in, sec_in, coupled)
    extra = edge_part(plan, rates, turn_edge, west_edge, east_edge)
    in_order[...] = turned_order[...]
    for number in range(2 * rows):
        slot = pl.ds(slots[number, 0], 1)
        part = jnp.concatenate([tile[number : number + 1, :] for tile in extra], axis=1)
        in_order[slot, :] = in_order[slot, :] + part
    arrived = coupled[...]
    halves = growth_halves(arrived)
    wet, wet_some = sea_order[...], twice(sea_some[...])
    rows_of = twice(halves * wet.astype(BF16))
    some_of = twice(dot(permute_some[...], halves).astype(BF16))
    wet = twice(wet)
    total = None
    some = []
    filler = jnp.zeros((plan.some - 2 * cols - 2 * rows, 256), F32)
    for number, start in enumerate(range(0, plan.spectral, 256)):
        lanes = slice(start, start + 256)
        table = growth_table(grow, number)
        from_edges = jnp.concatenate(extra[2 * number : 2 * number + 2], axis=1)
        extra_out[:, lanes] = from_edges
        grown = in_order[:, lanes] * (wet + dot(rows_of, table))
        product = stokes_product(grown, stokes[lanes, :])
        total = product if total is None else total + product
        parts = []
        for row in (0, rows - 1):
            west, east = from_edges[row : row + 1, :], from_edges[rows + row : rows + row + 1, :]
            parts += with_edges(plan, turned[row, :, lanes], west, east)
        parts += [turned_edge[:, lanes] + from_edges, filler]
        some.append(jnp.concatenate(parts, axis=0) * (wet_some + dot(some_of, table)))
    drift = pltpu.roll(arrived, LANES // 2, 1)
    new = ocean_step(
        plan, band, even, ocean_in, drift, near, far, west_edge, east_edge, keep, sea
    )
    ocean = jnp.concatenate(new, axis=0)
    ocean_out[...] = ocean
    total = total[:, :LANES] + total[:, LANES:]
    moments = total[:columns, :] + total[columns:, :]
    some = jnp.concatenate(some, axis=1)
    edges = some[2 * cols : 2 * cols + 2 * rows, :]
    fill_sections(plan, section, edges, ocean, moments, packed_out, sec_out)
    ends = (some[:cols, :], some[cols : 2 * cols, :]), (new[0], new[rows - 1])
    fill_bands(plan, even, *ends, far_out, near_out)


def grow_kernel(plan, axes, *refs):
    turned, extra, coupled, permute, sea, grow, _, waves_out = refs
    at_waves = twice(dot(permute[...], growth_halves(coupled[...])).astype(BF16))
    wet = twice(sea[...])
    for number, start in enumerate(range(0, plan.spectral, 256)):
        lanes = slice(start, start + 256)
        factor = wet + dot(at_waves, growth_table(grow, number))
        grown = grown_part(plan, turned, extra[:, lanes], factor, lanes)
        waves_out[:, :, lanes] = grown.reshape(plan.rows, plan.cols, 256)


def last_kernel(plan, axes, *refs):
    turned, ocean_in, packed_in, permute, turn_edge, sea, keep, rates, grow = refs[:9]
    count = len(plan.sizes)
    near, far, sec_in, refs = refs[9], refs[10], refs[11 : 11 + count], refs[11 + count :]
    waves_far, ocean_far, coupled, waves_out, ocean_out, done = refs
    section, band = lax.axis_index(axes[1]), lax.axis_index(axes[0])
    even = lax.rem(band, 2) == 0

    west_edge, east_edge = take_sections(plan, section, packed_in, sec_in, coupled)
    arrived = coupled[...]
    at_waves = twice(dot(permute[...], growth_halves(arrived)).astype(BF16))
    drift = pltpu.roll(arrived, LANES // 2, 1)
    extra = edge_part(plan, rates, turn_edge, west_edge, east_edge)
    new = ocean_step(
        plan, band, even, ocean_in, drift, near, far, west_edge, east_edge, keep, sea
    )
    for row, value in enumerate(new):
        ocean_out[row] = value[:, : 2 * plan.depth]
    copies = [pltpu.make_async_copy(ocean_out, ocean_far, done.at[0])]
    copies[0].start()
    wet = twice(sea[...])
    for number, start in enumerate(range(0, plan.spectral, 256)):
        lanes = slice(start, start + 256)
        factor = wet + dot(at_waves, growth_table(grow, number))
        from_edges = jnp.concatenate(extra[2 * number : 2 * number + 2], axis=1)
        grown = grown_part(plan, turned, from_edges, factor, lanes)
        waves_out[:, :, lanes] = grown.reshape(plan.rows, plan.cols, 256)
        copy = pltpu.make_async_copy(
            waves_out.at[:, :, lanes], waves_far.at[:, :, lanes], done.at[number + 1]
        )
        copy.start()
        copies.append(copy)
    for copy in copies:
        copy.wait()


def per_device(plan, axes, spectra, turning, currents, drag_rates, land_mask, ocean_target):
    stokes_once, stokes, rates, grow = (
        jnp.asarray(table) for table in build_tables(NFREQ, NDIR, drag_rates.shape[0])
    )
    columns, rows, cols, spectral = plan.columns, plan.rows, plan.cols, plan.spectral
    shape = jax.ShapeDtypeStruct
    params = pltpu.CompilerParams(vmem_limit_bytes=32 * 1024 * 1024)
    to_sections = [shape((size, LANES), F32) for size in plan.sizes]
    to_band = shape((cols, spectral // 2 + LANES), F32)
    state = shape((columns, LANES), F32)
    field = shape(spectra.shape, F32)
    at_edges = shape((2 * rows, LANES), F32)
    edge_field = shape((2 * rows, spectral), F32)
    some = plan.some
    spans = spectral // 256

    def call(kernel, outs, scratch, *args, space_in=pltpu.VMEM, space_out=pltpu.VMEM):
        return pl.pallas_call(
            functools.partial(kernel, plan, axes),
            out_shape=outs,
            in_specs=[pl.BlockSpec(memory_space=space_in)] * len(args),
            out_specs=[pl.BlockSpec(memory_space=space_out)] * len(outs),
            scratch_shapes=scratch,
            compiler_params=params,
        )(*args)

    pairs = [(i, i ^ 1) for i in range(plan.bands) if i ^ 1 < plan.bands]
    others = [(i, ((i + 1) ^ 1) - 1) for i in range(1, plan.bands)]
    others = [(i, j) for i, j in others if j < plan.bands]

    def exchange(to_far, to_near, to_sections, meanwhile):
        got = []
        if plan.relay:
            to_x, to_y, *to_sections = to_sections
            got.append(lax.ppermute(to_x, axes[1], plan.table(0, 1)))
        far_in = lax.ppermute(to_far, axes[0], others)
        near_in = lax.ppermute(to_near, axes[0], pairs)
        first = to_far
        if plan.relay:
            (first,) = call(
                relay_kernel,
                [shape((2 * plan.chunk + plan.edge, LANES), F32)],
                [],
                got[0],
                to_y,
            )
            got.append(lax.ppermute(first, axes[1], plan.table(0, 2)))
        got += [
            lax.ppermute(message, axes[1], table)
            for message, table in zip(to_sections, plan.direct)
        ]
        return meanwhile(first), [near_in, far_in, *got]

    waves, ocean, packed, order, *sent = call(
        first_kernel,
        [
            field,
            state,
            state,
            shape((columns, 2 * columns), BF16),
            *to_sections,
            to_band,
            to_band,
        ],
        [
            pltpu.VMEM(currents.shape, F32),
            pltpu.VMEM(ocean_target.shape, jnp.int32),
            pltpu.VMEM(stokes_once.shape, BF16),
            pltpu.SemaphoreType.DMA((4,)),
        ],
        *[
            pltpu.with_memory_space_constraint(array, pltpu.HBM)
            for array in (spectra, currents, ocean_target, stokes_once)
        ],
        space_in=pltpu.HBM,
    )

    def maps(first):
        return call(
            map_kernel,
            [
                shape((columns, columns), BF16),
                shape((some, columns), BF16),
                shape((2 * rows, LANES), jnp.int32),
                state,
                at_edges,
                state,
                state,
                shape((some, LANES), F32),
                shape((8, LANES), F32),
            ],
            [],
            turning,
            drag_rates,
            land_mask,
            order,
            first,
        )

    made, came = exchange(*sent[-2:], sent[:-2], maps)
    permute, permute_some, slots, turn, turn_edge, sea, sea_order, sea_some, keep = made
    for step in range(STEPS - 1):
        turned, turned_edge, turned_order = call(
            move_kernel,
            [field, edge_field, shape((columns, spectral), F32)],
            [],
            waves,
            turn,
            rates,
            *came[:2],
            order,
        )
        ocean, packed, coupled, extra, to_far, to_near, *sent = call(
            send_kernel,
            [state, state, state, edge_field, to_band, to_band] + to_sections,
            [pltpu.VMEM((columns, spectral), F32)],
            turned,
            turned_edge,
            turned_order,
            ocean,
            packed,
            permute_some,
            slots,
            turn_edge,
            sea,
            sea_order,
            sea_some,
            keep,
            stokes,
            rates,
            grow,
            *came,
        )

        def grown(first):
            (waves,) = call(
                grow_kernel, [field], [], turned, extra, coupled, permute, sea, grow, first
            )
            return waves

        waves, came = exchange(to_far, to_near, sent, grown)
    (turned,) = call(move_kernel, [field], [], waves, turn, rates, *came[:2])
    return call(
        last_kernel,
        [field, shape(currents.shape, F32)],
        [
            pltpu.VMEM((columns, LANES), F32),
            pltpu.VMEM(spectra.shape, F32),
            pltpu.VMEM(currents.shape, F32),
            pltpu.SemaphoreType.DMA((1 + spans,)),
        ],
        turned,
        ocean,
        packed,
        permute,
        turn_edge,
        sea,
        keep,
        rates,
        grow,
        *came,
        space_out=pltpu.HBM,
    )


def solution(mesh):
    sections, bands = mesh.shape["sec"], mesh.shape["lat"]

    def local(spectra, turning, currents, drag_rates, land_mask, ocean_target):
        rows, cols, spectral = spectra.shape
        plan = Plan(sections, bands, rows, cols, spectral, drag_rates.shape[0])
        return per_device(
            plan, ("lat", "sec"), spectra, turning, currents, drag_rates, land_mask, ocean_target
        )

    return jax.shard_map(
        local,
        mesh=mesh,
        in_specs=(
            P("lat", "sec", None),
            P("lat", "sec"),
            P("lat", "sec", None),
            P(),
            P("lat", "sec"),
            P("lat", "sec"),
        ),
        out_specs=(P("lat", "sec", None), P("lat", "sec", None)),
        check_vma=False,
    )
```

```python
import functools
import math

import jax
import jax.numpy as jnp
import ml_dtypes
import numpy as np
from jax import lax
from jax.experimental import pallas as pl
from jax.experimental.pallas import tpu as pltpu
from jax.sharding import PartitionSpec as P

NFREQ = 24
NDIR = 32
STEPS = 3

stokes_scale = 0.1
ocean_dt = 0.3
current_gain = 0.2

LANES = 128
F32 = jnp.float32
BF16 = jnp.bfloat16


def split_halves(table):
    high = table.astype(ml_dtypes.bfloat16)
    low = (table - high.astype(np.float64)).astype(ml_dtypes.bfloat16)
    return high, low


def build_tables(nfreq, ndir, ndepth):
    fraction = np.arange(nfreq) / (nfreq - 1)
    angles = (np.arange(ndir) + 0.5) * (2.0 * math.pi / ndir)
    east_part, north_part = np.cos(angles), np.sin(angles)
    courant = 0.1 + 0.3 * fraction
    depth_level = 0.5 + (ndepth - 2) * (1.0 - fraction)
    weights = np.maximum(1.0 - np.abs(np.arange(ndepth)[None, :] - depth_level[:, None]), 0.0)
    mean_weights = weights / weights.sum(axis=1, keepdims=True)
    x_rate = np.abs(courant[:, None] * east_part[None, :]).reshape(-1)
    y_rate = np.abs(courant[:, None] * north_part[None, :]).reshape(-1)
    turn_gain = np.repeat(1.0 - 0.5 * fraction, ndir)
    rates = np.stack([1.0 - x_rate - y_rate, x_rate, y_rate, turn_gain] * 2).astype(np.float32)
    compass = np.stack([east_part, north_part])
    stokes = (stokes_scale * weights[:, None, None, :] * compass.T[None, :, :, None]).reshape(
        nfreq * ndir, 2 * ndepth
    )
    growth = current_gain * (1.0 + fraction)
    grow = (
        growth[None, None, :, None] * mean_weights.T[None, :, :, None] * compass[:, None, None, :]
    ).reshape(2 * ndepth, nfreq * ndir)
    high, low = split_halves(stokes)
    blank = np.zeros_like(high)
    stokes_once = np.concatenate([high, low], axis=1)
    stokes_upper = np.concatenate([blank, high, blank, low], axis=1)
    high, low = split_halves(grow)
    grow = np.concatenate([high, high, low, low], axis=0)
    return (
        stokes_once,
        stokes_upper,
        rates,
        grow.reshape(2 * LANES, -1, LANES).transpose(1, 0, 2).reshape(-1, LANES),
    )


class Plan:
    def __init__(self, sections, bands, rows, cols, spectral, depth):
        self.sections, self.bands = sections, bands
        self.rows, self.cols, self.spectral, self.depth = rows, cols, spectral, depth
        self.columns = rows * cols
        self.chunk = self.columns // sections
        self.tiles = spectral // LANES
        self.some = -(-(2 * cols + 2 * rows) // 16) * 16
        self.edge = ((self.tiles // 2 + 1) * rows + 7) // 8 * 8
        self.relay = sections % 4 == 0 and bands % 2 == 0 and self.chunk <= cols
        self.quad = 4 if self.relay else 1
        self.hops = [
            (hop, flip)
            for hop in range(1, sections // self.quad)
            for flip in ((3, 1, 2, 0) if self.relay else (0,))
        ]
        self.direct = [
            [(i, self.partner(i, *hop, divmod)[0]) for i in range(sections)] for hop in self.hops
        ]
        self.edges = [any(abs(target - i) == 1 for i, target in table) for table in self.direct]
        self.sizes = [self.chunk + (self.edge if edge else 0) for edge in self.edges]
        if self.relay:
            self.sizes = [2 * (self.chunk + self.edge)] + self.sizes
        self.row_lanes = slice(spectral // 2, spectral // 2 + LANES)
        self.chunk_lanes = slice(spectral // 2 + LANES, spectral // 2 + 2 * LANES)

    def crossing(self, flip):
        bands = self.bands
        return [
            (i * bands + band, (i ^ flip) * bands + (band ^ 1))
            for i in range(self.sections)
            for band in range(bands)
        ]

    def partner(self, section, hop, flip, divide=lambda a, b: (lax.div(a, b), lax.rem(a, b))):
        groups = self.sections // self.quad
        high, low = divide(section, self.quad)
        if flip & 1:
            low = low + 1 - 2 * divide(low, 2)[1]
        if flip & 2:
            low = low + 2 - 4 * divide(low, 2)[0]
        return tuple(
            divide(high + shift, groups)[1] * self.quad + low for shift in (hop, groups - hop)
        )

    def received(self, section, messages):
        parts = []
        if self.relay:
            from_x, from_y = messages[:2]
            parts = [
                (self.partner(section, 0, 1)[1], from_x, 0, self.chunk),
                (self.partner(section, 0, 2)[1], from_y, 0, None),
                (self.partner(section, 0, 3)[1], from_y, self.chunk, 2 * self.chunk),
            ]
            messages = messages[2:]
        for message, hop, edge in zip(messages, self.hops, self.edges):
            parts.append((self.partner(section, *hop)[1], message, 0, self.chunk if edge else None))
        return parts

    def sent(self, section, messages, near):
        parts = []
        lanes = slice(0, LANES)
        if self.relay:
            to_x = messages[0]
            second = self.chunk + self.edge
            parts = [
                (self.partner(section, 0, 1)[0], to_x, 0, lanes, self.chunk),
                (self.partner(section, 0, 2)[0], near, 0, self.chunk_lanes, None),
                (self.partner(section, 0, 3)[0], to_x, second, lanes, second + self.chunk),
            ]
            messages = messages[1:]
        for message, hop, edge in zip(messages, self.hops, self.edges):
            target = self.partner(section, *hop)[0]
            parts.append((target, message, 0, lanes, self.chunk if edge else None))
        return parts


def lane_of(shape):
    return lax.broadcasted_iota(jnp.int32, shape, len(shape) - 1)


def dot(a, b):
    return jnp.dot(a, b, preferred_element_type=F32)


def split_value(value):
    high = value.astype(BF16)
    return high, (value - high.astype(F32)).astype(BF16)


def stokes_product(part, table):
    return dot(jnp.concatenate(split_value(part), axis=0), table)


def packed_half(edge, tile, half, ahead, forward):
    first = edge[:, tile * LANES : (tile + 1) * LANES]
    second = edge[:, (tile + half) * LANES : (tile + half + 1) * LANES]
    keep = jnp.where(ahead, 1, 0) == jnp.where(forward, 1, 0)
    return jnp.where(keep, first, pltpu.roll(second, NDIR // 2, 1))


def fill_band(plan, northward, edge, sea_row, out):
    half = plan.tiles // 2
    masks = Directions((plan.cols, LANES))
    for tile in range(half):
        out[:, tile * LANES : (tile + 1) * LANES] = packed_half(
            edge, tile, half, masks.northward, northward
        )
    out[:, plan.row_lanes] = sea_row


def fill_bands(plan, even, edges, sea_rows, far, near):
    for out, northward in ((far, jnp.logical_not(even)), (near, even)):
        edge = jnp.where(northward, edges[1], edges[0])
        fill_band(plan, northward, edge, jnp.where(northward, sea_rows[1], sea_rows[0]), out)


def fill_sections(plan, section, edges, ocean, ordered, packed_out, sec_out, near):
    chunk, rows, cols, half = plan.chunk, plan.rows, plan.cols, plan.tiles // 2
    lane = lane_of((plan.columns, LANES))
    packed_out[...] = jnp.where(lane < LANES // 2, ocean, ordered)
    sea_rows = ocean.reshape(rows, cols, LANES)
    masks = Directions((rows, LANES))
    for target, out, at, lanes, edge_at in plan.sent(section, sec_out, near):
        part = packed_out[pl.ds(pl.multiple_of(target * chunk, 8), chunk), :]
        out[at : at + chunk, lanes] = part
        if edge_at is None:
            continue
        eastward = target == section + 1
        edge = jnp.where(eastward, edges[rows:, :], edges[:rows, :])
        for tile in range(half):
            place = edge_at + tile * rows
            out[place : place + rows, :] = packed_half(edge, tile, half, masks.eastward, eastward)
        for row in range(rows):
            place = edge_at + half * rows + row
            out[place : place + 1, :] = jnp.where(
                eastward, sea_rows[row, cols - 1 : cols, :], sea_rows[row, 0:1, :]
            )


def take_sections(plan, section, packed_in, sec_in, coupled):
    chunk = plan.chunk
    own = pl.ds(pl.multiple_of(section * chunk, 8), chunk)
    coupled[own, :] = packed_in[own, :]
    west = east = jnp.zeros((plan.edge, LANES), F32)
    for source, message, at, edge_at in plan.received(section, sec_in):
        coupled[pl.ds(pl.multiple_of(source * chunk, 8), chunk), :] = message[at : at + chunk, :]
        if edge_at is not None:
            edge = message[edge_at : edge_at + plan.edge, :]
            west = jnp.where(source == section - 1, edge, west)
            east = jnp.where(source == section + 1, edge, east)
    return west, east


def edge_part(plan, rates, turn_edge, west_edge, east_edge):
    rows, half = plan.rows, plan.tiles // 2
    shape = (2 * rows, LANES)
    masks = Directions(shape)
    westmost = lax.broadcasted_iota(jnp.int32, shape, 0) < rows
    reached = jnp.where(masks.eastward, 1, 0) == jnp.where(westmost, 1, 0)
    parts = []
    for tile in range(plan.tiles):
        lanes = slice(tile * LANES, (tile + 1) * LANES)
        edge = slice(tile % half * rows, (tile % half + 1) * rows)
        came = jnp.concatenate([west_edge[edge, :], east_edge[edge, :]], axis=0)
        if tile >= half:
            came = pltpu.roll(came, LANES - NDIR // 2, 1)
        moved = rates[1:2, lanes] * jnp.where(reached, came, 0.0)
        parts.append(masks.turned(moved, turn_edge[...], rates[3:4, lanes]))
    return parts


def ocean_step(plan, band, even, ocean_in, stokes, near, far, west_edge, east_edge, keep, sea):
    rows, cols, half = plan.rows, plan.cols, plan.tiles // 2
    block = (cols, LANES)
    zonal = lane_of(block) < plan.depth
    place = lax.broadcasted_iota(jnp.int32, block, 0)
    at_west, at_east = place == 0, place == cols - 1
    lanes = plan.row_lanes
    south_edge = jnp.where(even, far[:, lanes], near[:, lanes])
    north_edge = jnp.where(even, near[:, lanes], far[:, lanes])
    new = []
    for row in range(rows):
        flat = slice(row * cols, (row + 1) * cols)
        edge = slice(half * rows + row, half * rows + row + 1)
        center = ocean_in[flat, :]
        west = jnp.where(at_west, west_edge[edge, :], pltpu.roll(center, 1, 0))
        east = jnp.where(at_east, east_edge[edge, :], pltpu.roll(center, cols - 1, 0))
        south = ocean_in[(row - 1) * cols : row * cols, :] if row else south_edge
        north = ocean_in[(row + 1) * cols : (row + 2) * cols, :] if row < rows - 1 else north_edge
        shear = 0.5 * jnp.where(zonal, south - north, east - west)
        y = (band * rows + row).astype(F32)
        spin = 0.2 + 0.6 * y / float(plan.bands * rows) + (shear + swapped(plan, shear))
        turn_by = ocean_dt * spin * swapped(plan, center + stokes[flat, :])
        new.append(keep[0:1, :] * (center + jnp.where(zonal, turn_by, -turn_by)) * sea[flat, :])
    return new


def twice(value, axis=1):
    return jnp.concatenate([value, value], axis=axis)


def growth_table(grow, number):
    size = 2 * LANES
    return jnp.concatenate(
        [grow[(2 * number + k) * size : (2 * number + k + 1) * size, :] for k in range(2)], axis=1
    )


def growth_halves(arrived):
    high = arrived.astype(BF16).astype(F32)
    lower = lane_of(arrived.shape) < LANES // 2
    return jnp.where(lower, high, pltpu.roll(arrived - high, LANES // 2, 1)).astype(BF16)


def with_edges(plan, turned, west, east):
    place = lax.broadcasted_iota(jnp.int32, (8, 256), 0)
    return [
        turned[0:8, :] + jnp.where(place == 0, west, 0.0),
        turned[8 : plan.cols - 8, :],
        turned[plan.cols - 8 :, :] + jnp.where(place == 7, east, 0.0),
    ]


def grown_part(plan, turned, from_edges, factor, lanes):
    rows = plan.rows
    parts = []
    for row in range(rows):
        west, east = from_edges[row : row + 1, :], from_edges[rows + row : rows + row + 1, :]
        parts += with_edges(plan, turned[row, :, lanes], west, east)
    return jnp.concatenate(parts, axis=0) * factor


def relay_kernel(plan, axes, from_x, near, to_y, to_mate):
    own = plan.chunk + plan.edge
    to_y[0 : plan.chunk, :] = near[0 : plan.chunk, plan.chunk_lanes]
    to_y[plan.chunk :, :] = from_x[own:, :]
    to_mate[...] = from_x[:own, :]


def square_places(plan):
    shape = (plan.columns, plan.columns)
    return lax.broadcasted_iota(jnp.int32, shape, 0), lax.broadcasted_iota(jnp.int32, shape, 1)


def row_of(plan, ref):
    return jnp.concatenate([ref[row : row + 1, :] for row in range(plan.rows)], axis=1)


def column_of(plan, row):
    down, across = square_places(plan)
    spread = jnp.broadcast_to(row, down.shape)
    return jnp.sum(jnp.where(down == across, spread, 0.0), axis=1, keepdims=True)


def first_kernel(plan, axes, *refs):
    waves_in, currents_in, target_in, stokes_in, refs = *refs[:4], refs[4:]
    waves, ocean_out, packed_out, order_out, refs = *refs[:4], refs[4:]
    count = len(plan.sizes)
    sec_out, lat_out, refs = refs[:count], refs[count : count + 2], refs[count + 2 :]
    currents, target, stokes, done = refs
    pairs = [(target_in, target), (waves_in, waves), (stokes_in, stokes), (currents_in, currents)]
    copies = [pltpu.make_async_copy(a, b, done.at[k]) for k, (a, b) in enumerate(pairs)]
    for copy in copies:
        copy.start()
    section, band = lax.axis_index(axes[1]), lax.axis_index(axes[0])
    even = lax.rem(band, 2) == 0
    columns, rows, cols = plan.columns, plan.rows, plan.cols
    copies[0].wait()
    down, across = square_places(plan)
    target_row = row_of(plan, target).astype(F32)
    same = column_of(plan, target_row) == target_row
    rank = jnp.sum(jnp.where(same & (down < across), 1.0, 0.0), axis=0, keepdims=True)
    slot = target_row * float(plan.chunk) + rank
    order = twice(jnp.where(slot == down.astype(F32), 1.0, 0.0)).astype(BF16)
    order_out[...] = order
    for copy in copies[1:]:
        copy.wait()
    total = None
    for start in range(0, plan.spectral, 256):
        part = waves[:, :, start : start + 256].reshape(columns, 256)
        product = stokes_product(part, stokes[start : start + 256, :])
        total = product if total is None else total + product
    moments = total[:columns] + total[columns:]
    flat = currents[...].reshape(columns, 2 * plan.depth)
    ocean = jnp.concatenate([flat, jnp.zeros((columns, LANES - 2 * plan.depth), F32)], axis=1)
    ocean_out[...] = ocean
    ordered = dot(order, jnp.concatenate(split_value(moments), axis=0))
    ordered = ordered + pltpu.roll(ordered, LANES // 2, 1)
    west = [waves[row, 0:1, :] for row in range(rows)]
    east = [waves[row, cols - 1 : cols, :] for row in range(rows)]
    edges = jnp.concatenate(west + east, axis=0)
    fill_sections(plan, section, edges, ocean, ordered, packed_out, sec_out, lat_out[1])
    sea_rows = ocean.reshape(rows, cols, LANES)
    ends = (waves[0], waves[rows - 1]), (sea_rows[0], sea_rows[rows - 1])
    fill_bands(plan, even, *ends, *lat_out)


def map_kernel(plan, axes, *refs):
    turning, drag, mask, order_twice, _, refs = *refs[:5], refs[5:]
    permute_out, permute_some_out, slots_out, turn_out, turn_edge_out = refs[:5]
    sea_out, sea_order_out, sea_some_out, keep_out = refs[5:]
    columns, rows, cols = plan.columns, plan.rows, plan.cols
    order = order_twice[:, :columns]
    sea = jnp.broadcast_to(column_of(plan, row_of(plan, mask).astype(F32)), (columns, LANES))
    turn = jnp.broadcast_to(column_of(plan, row_of(plan, turning)), (columns, LANES))
    sea_out[...] = sea
    turn_out[...] = turn
    west = [turn[row * cols : row * cols + 1, :] for row in range(rows)]
    east = [turn[(row + 1) * cols - 1 : (row + 1) * cols, :] for row in range(rows)]
    turn_edge_out[...] = jnp.concatenate(west + east, axis=0)
    sea_order_out[...] = dot(order, sea.astype(BF16))
    down, across = square_places(plan)
    same = jnp.where(down == across, 1.0, 0.0).astype(BF16)
    back = lax.dot_general(
        order, same, (((0,), (0,)), ((), ())), preferred_element_type=F32
    )
    permute = (back * sea[:, :columns]).astype(BF16)
    permute_out[...] = permute
    shape = (plan.some, columns)
    place = lax.broadcasted_iota(jnp.int32, shape, 0)
    number = place - 2 * cols
    wanted = jnp.where(
        place < 2 * cols,
        place + jnp.where(place < cols, 0, (rows - 2) * cols),
        lax.rem(number, rows) * cols + lax.div(number, rows) * (cols - 1),
    )
    wanted = jnp.where(number < 2 * rows, wanted, -1)
    chosen = jnp.where(lane_of(shape) == wanted, 1.0, 0.0).astype(BF16)
    permute_some_out[...] = dot(chosen, permute).astype(BF16)
    sea_some_out[...] = dot(chosen, sea.astype(BF16))
    slot = jnp.sum(order.astype(F32) * down.astype(F32), axis=0, keepdims=True)
    slot = jnp.broadcast_to(column_of(plan, slot), (columns, LANES)).astype(BF16)
    slots_out[...] = dot(chosen, slot)[2 * cols : 2 * cols + 2 * rows, :].astype(jnp.int32)
    keep = 1.0 - drag[...].reshape(1, plan.depth)
    blank = jnp.zeros((1, LANES - 2 * plan.depth), F32)
    keep_out[...] = jnp.broadcast_to(jnp.concatenate([keep, keep, blank], axis=1), (8, LANES))


class Directions:
    def __init__(self, shape):
        direction = lax.rem(lane_of(shape), NDIR)
        self.eastward = (direction < NDIR // 4) | (direction >= 3 * NDIR // 4)
        self.northward = direction < NDIR // 2
        self.first, self.final = direction == 0, direction == NDIR - 1

    def turned(self, moved, rate, gain):
        behind = jnp.where(
            self.first, pltpu.roll(moved, LANES - (NDIR - 1), 1), pltpu.roll(moved, 1, 1)
        )
        forward = jnp.where(
            self.final, pltpu.roll(moved, NDIR - 1, 1), pltpu.roll(moved, LANES - 1, 1)
        )
        return moved - jnp.abs(rate) * gain * (moved - jnp.where(rate > 0.0, behind, forward))


def move_kernel(plan, axes, *refs):
    waves, turn, rates, near, far, refs = *refs[:5], refs[5:]
    if len(refs) > 1:
        order, turned_out, edge_out, sorted_out = refs
    else:
        (turned_out,) = refs
    even = lax.rem(lax.axis_index(axes[0]), 2) == 0
    rows, cols, tiles = plan.rows, plan.cols, plan.tiles
    block = (cols, LANES)
    masks = Directions(block)
    place = lax.broadcasted_iota(jnp.int32, block, 0)
    outside = place == jnp.where(masks.eastward, 0, cols - 1)
    for tile in range(tiles):
        lanes = slice(tile * LANES, (tile + 1) * LANES)
        stay, along_x, along_y, gain = (rates[k : k + 1, lanes] for k in range(4))
        along_x = jnp.where(outside, 0.0, along_x)
        half = tile % (tiles // 2)
        half = slice(half * LANES, (half + 1) * LANES)
        south_edge = jnp.where(even, far[:, half], near[:, half])
        north_edge = jnp.where(even, near[:, half], far[:, half])
        if tile >= tiles // 2:
            south_edge = pltpu.roll(south_edge, LANES - NDIR // 2, 1)
            north_edge = pltpu.roll(north_edge, LANES - NDIR // 2, 1)
        for row in range(rows):
            center = waves[row, :, lanes]
            south = waves[row - 1, :, lanes] if row else south_edge
            north = waves[row + 1, :, lanes] if row < rows - 1 else north_edge
            moved = (
                stay * center
                + along_x
                * jnp.where(
                    masks.eastward, pltpu.roll(center, 1, 0), pltpu.roll(center, cols - 1, 0)
                )
                + along_y * jnp.where(masks.northward, south, north)
            )
            rate = turn[row * cols : (row + 1) * cols, :]
            turned = masks.turned(moved, rate, gain)
            turned_out[row, :, lanes] = turned
            if len(refs) > 1:
                edge_out[row : row + 1, lanes] = turned[0:1, :]
                edge_out[rows + row : rows + row + 1, lanes] = turned[cols - 1 :, :]
    if len(refs) > 1:
        for start in range(0, plan.spectral, 256):
            part = turned_out[:, :, start : start + 256].reshape(plan.columns, 256)
            sorted_out[:, start : start + 256] = dot(
                order[...], jnp.concatenate(split_value(part), axis=0)
            )


def swapped(plan, value):
    half = plan.depth
    zonal = lane_of(value.shape) < half
    return jnp.where(zonal, pltpu.roll(value, LANES - half, 1), pltpu.roll(value, half, 1))


def send_kernel(plan, axes, *refs):
    turned, turned_edge, turned_order, ocean_in, packed_in, permute_some, slots = refs[:7]
    turn_edge, sea, sea_order, sea_some, keep, stokes, rates, grow, refs = *refs[7:15], refs[15:]
    count = len(plan.sizes)
    got = count + plan.relay
    near, far, sec_in, refs = refs[0], refs[1], refs[2 : 2 + got], refs[2 + got :]
    ocean_out, packed_out, coupled, extra_out, far_out, near_out = refs[:6]
    sec_out, in_order = refs[6 : 6 + count], refs[6 + count]
    section, band = lax.axis_index(axes[1]), lax.axis_index(axes[0])
    even = lax.rem(band, 2) == 0
    columns, rows, cols = plan.columns, plan.rows, plan.cols

    west_edge, east_edge = take_sections(plan, section, packed_in, sec_in, coupled)
    extra = edge_part(plan, rates, turn_edge, west_edge, east_edge)
    in_order[...] = turned_order[...]
    for number in range(2 * rows):
        slot = pl.ds(slots[number, 0], 1)
        part = jnp.concatenate([tile[number : number + 1, :] for tile in extra], axis=1)
        in_order[slot, :] = in_order[slot, :] + part
    arrived = coupled[...]
    halves = growth_halves(arrived)
    wet, wet_some = sea_order[...], twice(sea_some[...])
    rows_of = twice(halves * wet.astype(BF16))
    some_of = twice(dot(permute_some[...], halves).astype(BF16))
    wet = twice(wet)
    total = None
    some = []
    filler = jnp.zeros((plan.some - 2 * cols - 2 * rows, 256), F32)
    for number, start in enumerate(range(0, plan.spectral, 256)):
        lanes = slice(start, start + 256)
        table = growth_table(grow, number)
        from_edges = jnp.concatenate(extra[2 * number : 2 * number + 2], axis=1)
        extra_out[:, lanes] = from_edges
        grown = in_order[:, lanes] * (wet + dot(rows_of, table))
        product = stokes_product(grown, stokes[lanes, :])
        total = product if total is None else total + product
        parts = []
        for row in (0, rows - 1):
            west, east = from_edges[row : row + 1, :], from_edges[rows + row : rows + row + 1, :]
            parts += with_edges(plan, turned[row, :, lanes], west, east)
        parts += [turned_edge[:, lanes] + from_edges, filler]
        some.append(jnp.concatenate(parts, axis=0) * (wet_some + dot(some_of, table)))
    drift = pltpu.roll(arrived, LANES // 2, 1)
    new = ocean_step(
        plan, band, even, ocean_in, drift, near, far, west_edge, east_edge, keep, sea
    )
    ocean = jnp.concatenate(new, axis=0)
    ocean_out[...] = ocean
    total = total[:, :LANES] + total[:, LANES:]
    moments = total[:columns, :] + total[columns:, :]
    some = jnp.concatenate(some, axis=1)
    edges = some[2 * cols : 2 * cols + 2 * rows, :]
    fill_sections(plan, section, edges, ocean, moments, packed_out, sec_out, near_out)
    ends = (some[:cols, :], some[cols : 2 * cols, :]), (new[0], new[rows - 1])
    fill_bands(plan, even, *ends, far_out, near_out)


def grow_kernel(plan, axes, *refs):
    turned, extra, coupled, permute, sea, grow, _, waves_out = refs
    at_waves = twice(dot(permute[...], growth_halves(coupled[...])).astype(BF16))
    wet = twice(sea[...])
    for number, start in enumerate(range(0, plan.spectral, 256)):
        lanes = slice(start, start + 256)
        factor = wet + dot(at_waves, growth_table(grow, number))
        grown = grown_part(plan, turned, extra[:, lanes], factor, lanes)
        waves_out[:, :, lanes] = grown.reshape(plan.rows, plan.cols, 256)


def last_kernel(plan, axes, *refs):
    turned, ocean_in, packed_in, permute, turn_edge, sea, keep, rates, grow = refs[:9]
    got = len(plan.sizes) + plan.relay
    near, far, sec_in, refs = refs[9], refs[10], refs[11 : 11 + got], refs[11 + got :]
    waves_far, ocean_far, coupled, waves_out, ocean_out, done = refs
    section, band = lax.axis_index(axes[1]), lax.axis_index(axes[0])
    even = lax.rem(band, 2) == 0

    west_edge, east_edge = take_sections(plan, section, packed_in, sec_in, coupled)
    arrived = coupled[...]
    at_waves = twice(dot(permute[...], growth_halves(arrived)).astype(BF16))
    drift = pltpu.roll(arrived, LANES // 2, 1)
    extra = edge_part(plan, rates, turn_edge, west_edge, east_edge)
    new = ocean_step(
        plan, band, even, ocean_in, drift, near, far, west_edge, east_edge, keep, sea
    )
    for row, value in enumerate(new):
        ocean_out[row] = value[:, : 2 * plan.depth]
    copies = [pltpu.make_async_copy(ocean_out, ocean_far, done.at[0])]
    copies[0].start()
    wet = twice(sea[...])
    for number, start in enumerate(range(0, plan.spectral, 256)):
        lanes = slice(start, start + 256)
        factor = wet + dot(at_waves, growth_table(grow, number))
        from_edges = jnp.concatenate(extra[2 * number : 2 * number + 2], axis=1)
        grown = grown_part(plan, turned, from_edges, factor, lanes)
        waves_out[:, :, lanes] = grown.reshape(plan.rows, plan.cols, 256)
        copy = pltpu.make_async_copy(
            waves_out.at[:, :, lanes], waves_far.at[:, :, lanes], done.at[number + 1]
        )
        copy.start()
        copies.append(copy)
    for copy in copies:
        copy.wait()


def per_device(plan, axes, spectra, turning, currents, drag_rates, land_mask, ocean_target):
    stokes_once, stokes, rates, grow = (
        jnp.asarray(table) for table in build_tables(NFREQ, NDIR, drag_rates.shape[0])
    )
    columns, rows, cols, spectral = plan.columns, plan.rows, plan.cols, plan.spectral
    shape = jax.ShapeDtypeStruct
    params = pltpu.CompilerParams(vmem_limit_bytes=32 * 1024 * 1024)
    to_sections = [shape((size, LANES), F32) for size in plan.sizes]
    to_far = shape((cols, plan.row_lanes.stop), F32)
    to_near = shape((cols, plan.chunk_lanes.stop), F32)
    state = shape((columns, LANES), F32)
    field = shape(spectra.shape, F32)
    at_edges = shape((2 * rows, LANES), F32)
    edge_field = shape((2 * rows, spectral), F32)
    some = plan.some
    spans = spectral // 256

    def call(kernel, outs, scratch, *args, space_in=pltpu.VMEM, space_out=pltpu.VMEM):
        return pl.pallas_call(
            functools.partial(kernel, plan, axes),
            out_shape=outs,
            in_specs=[pl.BlockSpec(memory_space=space_in)] * len(args),
            out_specs=[pl.BlockSpec(memory_space=space_out)] * len(outs),
            scratch_shapes=scratch,
            compiler_params=params,
        )(*args)

    both_axes = (axes[1], axes[0])
    pairs = [(i, i ^ 1) for i in range(plan.bands) if i ^ 1 < plan.bands]
    others = [(i, ((i + 1) ^ 1) - 1) for i in range(1, plan.bands)]
    others = [(i, j) for i, j in others if j < plan.bands]

    def exchange(to_far, to_near, to_sections, meanwhile):
        got = []
        if plan.relay:
            to_x, *to_sections = to_sections
            from_x = lax.ppermute(to_x, both_axes, plan.crossing(1))
        far_in = lax.ppermute(to_far, axes[0], others)
        near_in = lax.ppermute(to_near, axes[0], pairs)
        first = to_far
        if plan.relay:
            part = plan.chunk + plan.edge
            first, to_mate = call(
                relay_kernel,
                [shape((plan.chunk + part, LANES), F32), shape((part, LANES), F32)],
                [],
                from_x,
                near_in,
            )
            from_y = lax.ppermute(first, both_axes, plan.crossing(2))
            got = [lax.ppermute(to_mate, axes[0], pairs), from_y]
        got += [
            lax.ppermute(message, axes[1], table)
            for message, table in zip(to_sections, plan.direct)
        ]
        return meanwhile(first), [near_in, far_in, *got]

    waves, ocean, packed, order, *sent = call(
        first_kernel,
        [
            field,
            state,
            state,
            shape((columns, 2 * columns), BF16),
            *to_sections,
            to_far,
            to_near,
        ],
        [
            pltpu.VMEM(currents.shape, F32),
            pltpu.VMEM(ocean_target.shape, jnp.int32),
            pltpu.VMEM(stokes_once.shape, BF16),
            pltpu.SemaphoreType.DMA((4,)),
        ],
        *[
            pltpu.with_memory_space_constraint(array, pltpu.HBM)
            for array in (spectra, currents, ocean_target, stokes_once)
        ],
        space_in=pltpu.HBM,
    )

    def maps(first):
        return call(
            map_kernel,
            [
                shape((columns, columns), BF16),
                shape((some, columns), BF16),
                shape((2 * rows, LANES), jnp.int32),
                state,
                at_edges,
                state,
                state,
                shape((some, LANES), F32),
                shape((8, LANES), F32),
            ],
            [],
            turning,
            drag_rates,
            land_mask,
            order,
            first,
        )

    made, came = exchange(*sent[-2:], sent[:-2], maps)
    permute, permute_some, slots, turn, turn_edge, sea, sea_order, sea_some, keep = made
    for step in range(STEPS - 1):
        turned, turned_edge, turned_order = call(
            move_kernel,
            [field, edge_field, shape((columns, spectral), F32)],
            [],
            waves,
            turn,
            rates,
            *came[:2],
            order,
        )
        ocean, packed, coupled, extra, *sent = call(
            send_kernel,
            [state, state, state, edge_field, to_far, to_near] + to_sections,
            [pltpu.VMEM((columns, spectral), F32)],
            turned,
            turned_edge,
            turned_order,
            ocean,
            packed,
            permute_some,
            slots,
            turn_edge,
            sea,
            sea_order,
            sea_some,
            keep,
            stokes,
            rates,
            grow,
            *came,
        )

        def grown(first):
            (waves,) = call(
                grow_kernel, [field], [], turned, extra, coupled, permute, sea, grow, first
            )
            return waves

        waves, came = exchange(*sent[:2], sent[2:], grown)
    (turned,) = call(move_kernel, [field], [], waves, turn, rates, *came[:2])
    return call(
        last_kernel,
        [field, shape(currents.shape, F32)],
        [
            pltpu.VMEM((columns, LANES), F32),
            pltpu.VMEM(spectra.shape, F32),
            pltpu.VMEM(currents.shape, F32),
            pltpu.SemaphoreType.DMA((1 + spans,)),
        ],
        turned,
        ocean,
        packed,
        permute,
        turn_edge,
        sea,
        keep,
        rates,
        grow,
        *came,
        space_out=pltpu.HBM,
    )


def solution(mesh):
    sections, bands = mesh.shape["sec"], mesh.shape["lat"]

    def local(spectra, turning, currents, drag_rates, land_mask, ocean_target):
        rows, cols, spectral = spectra.shape
        plan = Plan(sections, bands, rows, cols, spectral, drag_rates.shape[0])
        return per_device(
            plan, ("lat", "sec"), spectra, turning, currents, drag_rates, land_mask, ocean_target
        )

    return jax.shard_map(
        local,
        mesh=mesh,
        in_specs=(
            P("lat", "sec", None),
            P("lat", "sec"),
            P("lat", "sec", None),
            P(),
            P("lat", "sec"),
            P("lat", "sec"),
        ),
        out_specs=(P("lat", "sec", None), P("lat", "sec", None)),
        check_vma=False,
    )
```

```python
import functools
import math

import jax
import jax.numpy as jnp
import ml_dtypes
import numpy as np
from jax import lax
from jax.experimental import pallas as pl
from jax.experimental.pallas import tpu as pltpu
from jax.sharding import PartitionSpec as P

NFREQ = 24
NDIR = 32
STEPS = 3

stokes_scale = 0.1
ocean_dt = 0.3
current_gain = 0.2

LANES = 128
F32 = jnp.float32
BF16 = jnp.bfloat16


def split_halves(table):
    high = table.astype(ml_dtypes.bfloat16)
    low = (table - high.astype(np.float64)).astype(ml_dtypes.bfloat16)
    return high, low


def build_tables(nfreq, ndir, ndepth):
    fraction = np.arange(nfreq) / (nfreq - 1)
    angles = (np.arange(ndir) + 0.5) * (2.0 * math.pi / ndir)
    east_part, north_part = np.cos(angles), np.sin(angles)
    courant = 0.1 + 0.3 * fraction
    depth_level = 0.5 + (ndepth - 2) * (1.0 - fraction)
    weights = np.maximum(1.0 - np.abs(np.arange(ndepth)[None, :] - depth_level[:, None]), 0.0)
    mean_weights = weights / weights.sum(axis=1, keepdims=True)
    x_rate = np.abs(courant[:, None] * east_part[None, :]).reshape(-1)
    y_rate = np.abs(courant[:, None] * north_part[None, :]).reshape(-1)
    turn_gain = np.repeat(1.0 - 0.5 * fraction, ndir)
    rates = np.stack([1.0 - x_rate - y_rate, x_rate, y_rate, turn_gain] * 2).astype(np.float32)
    compass = np.stack([east_part, north_part])
    stokes = (stokes_scale * weights[:, None, None, :] * compass.T[None, :, :, None]).reshape(
        nfreq * ndir, 2 * ndepth
    )
    growth = current_gain * (1.0 + fraction)
    grow = (
        growth[None, None, :, None] * mean_weights.T[None, :, :, None] * compass[:, None, None, :]
    ).reshape(2 * ndepth, nfreq * ndir)
    pairs = stokes.reshape(-1, 2, LANES // ndir, ndir, 2 * ndepth)
    stokes = np.concatenate([pairs[:, 0, :, : ndir // 2], pairs[:, 1, :, ndir // 2 :]], axis=2)
    high, low = split_halves(stokes.reshape(nfreq * ndir // 2, 2 * ndepth))
    blank = np.zeros_like(high)
    stokes_once = np.concatenate([high, low], axis=1)
    stokes_upper = np.concatenate([blank, high, blank, low], axis=1)
    high, low = split_halves(grow)
    grow = np.concatenate([high, high, low, low], axis=0)
    return (
        stokes_once,
        stokes_upper,
        rates,
        grow.reshape(2 * LANES, -1, LANES).transpose(1, 0, 2).reshape(-1, LANES),
    )


class Plan:
    def __init__(self, sections, bands, rows, cols, spectral, depth):
        self.sections, self.bands = sections, bands
        self.rows, self.cols, self.spectral, self.depth = rows, cols, spectral, depth
        self.columns = rows * cols
        self.chunk = self.columns // sections
        self.tiles = spectral // LANES
        self.some = -(-(2 * cols + 2 * rows) // 16) * 16
        self.edge = ((self.tiles // 2 + 1) * rows + 7) // 8 * 8
        self.relay = sections % 4 == 0 and bands % 2 == 0 and self.chunk <= cols
        self.quad = 4 if self.relay else 1
        self.hops = [
            (hop, flip)
            for hop in range(1, sections // self.quad)
            for flip in ((3, 1, 2, 0) if self.relay else (0,))
        ]
        self.direct = [
            [(i, self.partner(i, *hop, divmod)[0]) for i in range(sections)] for hop in self.hops
        ]
        self.edges = [any(abs(target - i) == 1 for i, target in table) for table in self.direct]
        self.sizes = [self.chunk + (self.edge if edge else 0) for edge in self.edges]
        if self.relay:
            self.sizes = [2 * (self.chunk + self.edge)] + self.sizes
        self.row_lanes = slice(spectral // 2, spectral // 2 + LANES)
        self.chunk_lanes = slice(spectral // 2 + LANES, spectral // 2 + 2 * LANES)

    def crossing(self, flip):
        bands = self.bands
        return [
            (i * bands + band, (i ^ flip) * bands + (band ^ 1))
            for i in range(self.sections)
            for band in range(bands)
        ]

    def partner(self, section, hop, flip, divide=lambda a, b: (lax.div(a, b), lax.rem(a, b))):
        groups = self.sections // self.quad
        high, low = divide(section, self.quad)
        if flip & 1:
            low = low + 1 - 2 * divide(low, 2)[1]
        if flip & 2:
            low = low + 2 - 4 * divide(low, 2)[0]
        return tuple(
            divide(high + shift, groups)[1] * self.quad + low for shift in (hop, groups - hop)
        )

    def received(self, section, messages):
        parts = []
        if self.relay:
            from_x, from_y = messages[:2]
            parts = [
                (self.partner(section, 0, 1)[1], from_x, 0, self.chunk),
                (self.partner(section, 0, 2)[1], from_y, 0, None),
                (self.partner(section, 0, 3)[1], from_y, self.chunk, 2 * self.chunk),
            ]
            messages = messages[2:]
        for message, hop, edge in zip(messages, self.hops, self.edges):
            parts.append((self.partner(section, *hop)[1], message, 0, self.chunk if edge else None))
        return parts

    def sent(self, section, messages, near):
        parts = []
        lanes = slice(0, LANES)
        if self.relay:
            to_x = messages[0]
            second = self.chunk + self.edge
            parts = [
                (self.partner(section, 0, 1)[0], to_x, 0, lanes, self.chunk),
                (self.partner(section, 0, 2)[0], near, 0, self.chunk_lanes, None),
                (self.partner(section, 0, 3)[0], to_x, second, lanes, second + self.chunk),
            ]
            messages = messages[1:]
        for message, hop, edge in zip(messages, self.hops, self.edges):
            target = self.partner(section, *hop)[0]
            parts.append((target, message, 0, lanes, self.chunk if edge else None))
        return parts


def lane_of(shape):
    return lax.broadcasted_iota(jnp.int32, shape, len(shape) - 1)


def dot(a, b):
    return jnp.dot(a, b, preferred_element_type=F32)


def split_value(value):
    high = value.astype(BF16)
    return high, (value - high.astype(F32)).astype(BF16)


def opposed(part):
    first, second = part[:, :LANES], part[:, LANES:]
    lower = lax.rem(lane_of(first.shape), NDIR) < NDIR // 2
    shift = NDIR // 2
    return jnp.where(lower, first, second) - jnp.where(
        lower, pltpu.roll(first, LANES - shift, 1), pltpu.roll(second, shift, 1)
    )


def stokes_product(part, table):
    return dot(jnp.concatenate(split_value(opposed(part)), axis=1), twice(table, 0))


def packed_half(edge, tile, half, ahead, forward):
    first = edge[:, tile * LANES : (tile + 1) * LANES]
    second = edge[:, (tile + half) * LANES : (tile + half + 1) * LANES]
    keep = jnp.where(ahead, 1, 0) == jnp.where(forward, 1, 0)
    return jnp.where(keep, first, pltpu.roll(second, NDIR // 2, 1))


def fill_band(plan, northward, edge, sea_row, out):
    half = plan.tiles // 2
    masks = Directions((plan.cols, LANES))
    for tile in range(half):
        out[:, tile * LANES : (tile + 1) * LANES] = packed_half(
            edge, tile, half, masks.northward, northward
        )
    out[:, plan.row_lanes] = sea_row


def fill_bands(plan, even, edges, sea_rows, far, near):
    for out, northward in ((far, jnp.logical_not(even)), (near, even)):
        edge = jnp.where(northward, edges[1], edges[0])
        fill_band(plan, northward, edge, jnp.where(northward, sea_rows[1], sea_rows[0]), out)


def fill_sections(plan, section, edges, ocean, ordered, packed_out, sec_out, near):
    chunk, rows, cols, half = plan.chunk, plan.rows, plan.cols, plan.tiles // 2
    lane = lane_of((plan.columns, LANES))
    packed_out[...] = jnp.where(lane < LANES // 2, ocean, ordered)
    sea_rows = ocean.reshape(rows, cols, LANES)
    masks = Directions((rows, LANES))
    for target, out, at, lanes, edge_at in plan.sent(section, sec_out, near):
        part = packed_out[pl.ds(pl.multiple_of(target * chunk, 8), chunk), :]
        out[at : at + chunk, lanes] = part
        if edge_at is None:
            continue
        eastward = target == section + 1
        edge = jnp.where(eastward, edges[rows:, :], edges[:rows, :])
        for tile in range(half):
            place = edge_at + tile * rows
            out[place : place + rows, :] = packed_half(edge, tile, half, masks.eastward, eastward)
        for row in range(rows):
            place = edge_at + half * rows + row
            out[place : place + 1, :] = jnp.where(
                eastward, sea_rows[row, cols - 1 : cols, :], sea_rows[row, 0:1, :]
            )


def take_sections(plan, section, packed_in, sec_in, coupled):
    chunk = plan.chunk
    own = pl.ds(pl.multiple_of(section * chunk, 8), chunk)
    coupled[own, :] = packed_in[own, :]
    west = east = jnp.zeros((plan.edge, LANES), F32)
    for source, message, at, edge_at in plan.received(section, sec_in):
        coupled[pl.ds(pl.multiple_of(source * chunk, 8), chunk), :] = message[at : at + chunk, :]
        if edge_at is not None:
            edge = message[edge_at : edge_at + plan.edge, :]
            west = jnp.where(source == section - 1, edge, west)
            east = jnp.where(source == section + 1, edge, east)
    return west, east


def edge_part(plan, rates, turn_edge, west_edge, east_edge):
    rows, half = plan.rows, plan.tiles // 2
    shape = (2 * rows, LANES)
    masks = Directions(shape)
    westmost = lax.broadcasted_iota(jnp.int32, shape, 0) < rows
    reached = jnp.where(masks.eastward, 1, 0) == jnp.where(westmost, 1, 0)
    parts = []
    for tile in range(plan.tiles):
        lanes = slice(tile * LANES, (tile + 1) * LANES)
        edge = slice(tile % half * rows, (tile % half + 1) * rows)
        came = jnp.concatenate([west_edge[edge, :], east_edge[edge, :]], axis=0)
        if tile >= half:
            came = pltpu.roll(came, LANES - NDIR // 2, 1)
        moved = rates[1:2, lanes] * jnp.where(reached, came, 0.0)
        parts.append(masks.turned(moved, turn_edge[...], rates[3:4, lanes]))
    return parts


def ocean_step(plan, band, even, ocean_in, stokes, near, far, west_edge, east_edge, keep, sea):
    rows, cols, half = plan.rows, plan.cols, plan.tiles // 2
    block = (cols, LANES)
    zonal = lane_of(block) < plan.depth
    place = lax.broadcasted_iota(jnp.int32, block, 0)
    at_west, at_east = place == 0, place == cols - 1
    lanes = plan.row_lanes
    south_edge = jnp.where(even, far[:, lanes], near[:, lanes])
    north_edge = jnp.where(even, near[:, lanes], far[:, lanes])
    new = []
    for row in range(rows):
        flat = slice(row * cols, (row + 1) * cols)
        edge = slice(half * rows + row, half * rows + row + 1)
        center = ocean_in[flat, :]
        west = jnp.where(at_west, west_edge[edge, :], pltpu.roll(center, 1, 0))
        east = jnp.where(at_east, east_edge[edge, :], pltpu.roll(center, cols - 1, 0))
        south = ocean_in[(row - 1) * cols : row * cols, :] if row else south_edge
        north = ocean_in[(row + 1) * cols : (row + 2) * cols, :] if row < rows - 1 else north_edge
        shear = 0.5 * jnp.where(zonal, south - north, east - west)
        y = (band * rows + row).astype(F32)
        spin = 0.2 + 0.6 * y / float(plan.bands * rows) + (shear + swapped(plan, shear))
        turn_by = ocean_dt * spin * swapped(plan, center + stokes[flat, :])
        new.append(keep[0:1, :] * (center + jnp.where(zonal, turn_by, -turn_by)) * sea[flat, :])
    return new


def twice(value, axis=1):
    return jnp.concatenate([value, value], axis=axis)


def growth_table(grow, number):
    size = 2 * LANES
    return jnp.concatenate(
        [grow[(2 * number + k) * size : (2 * number + k + 1) * size, :] for k in range(2)], axis=1
    )


def growth_halves(arrived):
    high = arrived.astype(BF16).astype(F32)
    lower = lane_of(arrived.shape) < LANES // 2
    return jnp.where(lower, high, pltpu.roll(arrived - high, LANES // 2, 1)).astype(BF16)


def with_edges(plan, turned, west, east):
    place = lax.broadcasted_iota(jnp.int32, (8, 256), 0)
    return [
        turned[0:8, :] + jnp.where(place == 0, west, 0.0),
        turned[8 : plan.cols - 8, :],
        turned[plan.cols - 8 :, :] + jnp.where(place == 7, east, 0.0),
    ]


def grown_part(plan, turned, from_edges, factor, lanes):
    rows = plan.rows
    parts = []
    for row in range(rows):
        west, east = from_edges[row : row + 1, :], from_edges[rows + row : rows + row + 1, :]
        parts += with_edges(plan, turned[row, :, lanes], west, east)
    return jnp.concatenate(parts, axis=0) * factor


def relay_kernel(plan, axes, from_x, near, to_y, to_mate):
    own = plan.chunk + plan.edge
    to_y[0 : plan.chunk, :] = near[0 : plan.chunk, plan.chunk_lanes]
    to_y[plan.chunk :, :] = from_x[own:, :]
    to_mate[...] = from_x[:own, :]


def square_places(plan):
    shape = (plan.columns, plan.columns)
    return lax.broadcasted_iota(jnp.int32, shape, 0), lax.broadcasted_iota(jnp.int32, shape, 1)


def row_of(plan, ref):
    return jnp.concatenate([ref[row : row + 1, :] for row in range(plan.rows)], axis=1)


def column_of(plan, row):
    down, across = square_places(plan)
    spread = jnp.broadcast_to(row, down.shape)
    return jnp.sum(jnp.where(down == across, spread, 0.0), axis=1, keepdims=True)


def first_kernel(plan, axes, *refs):
    waves_in, currents_in, target_in, stokes_in, refs = *refs[:4], refs[4:]
    waves, ocean_out, packed_out, order_out, refs = *refs[:4], refs[4:]
    count = len(plan.sizes)
    sec_out, lat_out, refs = refs[:count], refs[count : count + 2], refs[count + 2 :]
    currents, target, stokes, done = refs
    pairs = [(target_in, target), (waves_in, waves), (stokes_in, stokes), (currents_in, currents)]
    copies = [pltpu.make_async_copy(a, b, done.at[k]) for k, (a, b) in enumerate(pairs)]
    for copy in copies:
        copy.start()
    section, band = lax.axis_index(axes[1]), lax.axis_index(axes[0])
    even = lax.rem(band, 2) == 0
    columns, rows, cols = plan.columns, plan.rows, plan.cols
    copies[0].wait()
    down, across = square_places(plan)
    target_row = row_of(plan, target).astype(F32)
    same = column_of(plan, target_row) == target_row
    rank = jnp.sum(jnp.where(same & (down < across), 1.0, 0.0), axis=0, keepdims=True)
    slot = target_row * float(plan.chunk) + rank
    order = twice(jnp.where(slot == down.astype(F32), 1.0, 0.0)).astype(BF16)
    order_out[...] = order
    for copy in copies[1:]:
        copy.wait()
    total = None
    for start in range(0, plan.spectral, 256):
        part = waves[:, :, start : start + 256].reshape(columns, 256)
        product = stokes_product(part, stokes[start // 2 : start // 2 + LANES, :])
        total = product if total is None else total + product
    moments = total
    flat = currents[...].reshape(columns, 2 * plan.depth)
    ocean = jnp.concatenate([flat, jnp.zeros((columns, LANES - 2 * plan.depth), F32)], axis=1)
    ocean_out[...] = ocean
    ordered = dot(order, jnp.concatenate(split_value(moments), axis=0))
    ordered = ordered + pltpu.roll(ordered, LANES // 2, 1)
    west = [waves[row, 0:1, :] for row in range(rows)]
    east = [waves[row, cols - 1 : cols, :] for row in range(rows)]
    edges = jnp.concatenate(west + east, axis=0)
    fill_sections(plan, section, edges, ocean, ordered, packed_out, sec_out, lat_out[1])
    sea_rows = ocean.reshape(rows, cols, LANES)
    ends = (waves[0], waves[rows - 1]), (sea_rows[0], sea_rows[rows - 1])
    fill_bands(plan, even, *ends, *lat_out)


def map_kernel(plan, axes, *refs):
    turning, drag, mask, order_twice, _, refs = *refs[:5], refs[5:]
    permute_out, permute_some_out, slots_out, turn_out, turn_edge_out = refs[:5]
    sea_out, sea_order_out, sea_some_out, keep_out = refs[5:]
    columns, rows, cols = plan.columns, plan.rows, plan.cols
    order = order_twice[:, :columns]
    sea = jnp.broadcast_to(column_of(plan, row_of(plan, mask).astype(F32)), (columns, LANES))
    turn = jnp.broadcast_to(column_of(plan, row_of(plan, turning)), (columns, LANES))
    sea_out[...] = sea
    turn_out[...] = turn
    west = [turn[row * cols : row * cols + 1, :] for row in range(rows)]
    east = [turn[(row + 1) * cols - 1 : (row + 1) * cols, :] for row in range(rows)]
    turn_edge_out[...] = jnp.concatenate(west + east, axis=0)
    sea_order_out[...] = dot(order, sea.astype(BF16))
    down, across = square_places(plan)
    same = jnp.where(down == across, 1.0, 0.0).astype(BF16)
    back = lax.dot_general(
        order, same, (((0,), (0,)), ((), ())), preferred_element_type=F32
    )
    permute = (back * sea[:, :columns]).astype(BF16)
    permute_out[...] = permute
    shape = (plan.some, columns)
    place = lax.broadcasted_iota(jnp.int32, shape, 0)
    number = place - 2 * cols
    wanted = jnp.where(
        place < 2 * cols,
        place + jnp.where(place < cols, 0, (rows - 2) * cols),
        lax.rem(number, rows) * cols + lax.div(number, rows) * (cols - 1),
    )
    wanted = jnp.where(number < 2 * rows, wanted, -1)
    chosen = jnp.where(lane_of(shape) == wanted, 1.0, 0.0).astype(BF16)
    permute_some_out[...] = dot(chosen, permute).astype(BF16)
    sea_some_out[...] = dot(chosen, sea.astype(BF16))
    slot = jnp.sum(order.astype(F32) * down.astype(F32), axis=0, keepdims=True)
    slot = jnp.broadcast_to(column_of(plan, slot), (columns, LANES)).astype(BF16)
    slots_out[...] = dot(chosen, slot)[2 * cols : 2 * cols + 2 * rows, :].astype(jnp.int32)
    keep = 1.0 - drag[...].reshape(1, plan.depth)
    blank = jnp.zeros((1, LANES - 2 * plan.depth), F32)
    keep_out[...] = jnp.broadcast_to(jnp.concatenate([keep, keep, blank], axis=1), (8, LANES))


class Directions:
    def __init__(self, shape):
        direction = lax.rem(lane_of(shape), NDIR)
        self.eastward = (direction < NDIR // 4) | (direction >= 3 * NDIR // 4)
        self.northward = direction < NDIR // 2
        self.first, self.final = direction == 0, direction == NDIR - 1

    def turned(self, moved, rate, gain):
        behind = jnp.where(
            self.first, pltpu.roll(moved, LANES - (NDIR - 1), 1), pltpu.roll(moved, 1, 1)
        )
        forward = jnp.where(
            self.final, pltpu.roll(moved, NDIR - 1, 1), pltpu.roll(moved, LANES - 1, 1)
        )
        return moved - jnp.abs(rate) * gain * (moved - jnp.where(rate > 0.0, behind, forward))


def move_kernel(plan, axes, *refs):
    waves, turn, rates, near, far, refs = *refs[:5], refs[5:]
    if len(refs) > 1:
        order, turned_out, edge_out, sorted_out = refs
    else:
        (turned_out,) = refs
    even = lax.rem(lax.axis_index(axes[0]), 2) == 0
    rows, cols, tiles = plan.rows, plan.cols, plan.tiles
    block = (cols, LANES)
    masks = Directions(block)
    place = lax.broadcasted_iota(jnp.int32, block, 0)
    outside = place == jnp.where(masks.eastward, 0, cols - 1)
    for tile in range(tiles):
        lanes = slice(tile * LANES, (tile + 1) * LANES)
        stay, along_x, along_y, gain = (rates[k : k + 1, lanes] for k in range(4))
        along_x = jnp.where(outside, 0.0, along_x)
        half = tile % (tiles // 2)
        half = slice(half * LANES, (half + 1) * LANES)
        south_edge = jnp.where(even, far[:, half], near[:, half])
        north_edge = jnp.where(even, near[:, half], far[:, half])
        if tile >= tiles // 2:
            south_edge = pltpu.roll(south_edge, LANES - NDIR // 2, 1)
            north_edge = pltpu.roll(north_edge, LANES - NDIR // 2, 1)
        for row in range(rows):
            center = waves[row, :, lanes]
            south = waves[row - 1, :, lanes] if row else south_edge
            north = waves[row + 1, :, lanes] if row < rows - 1 else north_edge
            moved = (
                stay * center
                + along_x
                * jnp.where(
                    masks.eastward, pltpu.roll(center, 1, 0), pltpu.roll(center, cols - 1, 0)
                )
                + along_y * jnp.where(masks.northward, south, north)
            )
            rate = turn[row * cols : (row + 1) * cols, :]
            turned = masks.turned(moved, rate, gain)
            turned_out[row, :, lanes] = turned
            if len(refs) > 1:
                edge_out[row : row + 1, lanes] = turned[0:1, :]
                edge_out[rows + row : rows + row + 1, lanes] = turned[cols - 1 :, :]
    if len(refs) > 1:
        for start in range(0, plan.spectral, 256):
            part = turned_out[:, :, start : start + 256].reshape(plan.columns, 256)
            sorted_out[:, start : start + 256] = dot(
                order[...], jnp.concatenate(split_value(part), axis=0)
            )


def swapped(plan, value):
    half = plan.depth
    zonal = lane_of(value.shape) < half
    return jnp.where(zonal, pltpu.roll(value, LANES - half, 1), pltpu.roll(value, half, 1))


def send_kernel(plan, axes, *refs):
    turned, turned_edge, turned_order, ocean_in, packed_in, permute_some, slots = refs[:7]
    turn_edge, sea, sea_order, sea_some, keep, stokes, rates, grow, refs = *refs[7:15], refs[15:]
    count = len(plan.sizes)
    got = count + plan.relay
    near, far, sec_in, refs = refs[0], refs[1], refs[2 : 2 + got], refs[2 + got :]
    ocean_out, packed_out, coupled, extra_out, far_out, near_out = refs[:6]
    sec_out, in_order = refs[6 : 6 + count], refs[6 + count]
    section, band = lax.axis_index(axes[1]), lax.axis_index(axes[0])
    even = lax.rem(band, 2) == 0
    columns, rows, cols = plan.columns, plan.rows, plan.cols

    west_edge, east_edge = take_sections(plan, section, packed_in, sec_in, coupled)
    extra = edge_part(plan, rates, turn_edge, west_edge, east_edge)
    in_order[...] = turned_order[...]
    for number in range(2 * rows):
        slot = pl.ds(slots[number, 0], 1)
        part = jnp.concatenate([tile[number : number + 1, :] for tile in extra], axis=1)
        in_order[slot, :] = in_order[slot, :] + part
    arrived = coupled[...]
    halves = growth_halves(arrived)
    wet, wet_some = sea_order[...], twice(sea_some[...])
    rows_of = twice(halves * wet.astype(BF16))
    some_of = twice(dot(permute_some[...], halves).astype(BF16))
    wet = twice(wet)
    total = None
    some, grown = [], []
    filler = jnp.zeros((plan.some - 2 * cols - 2 * rows, 256), F32)
    for number, start in enumerate(range(0, plan.spectral, 256)):
        lanes = slice(start, start + 256)
        table = growth_table(grow, number)
        from_edges = jnp.concatenate(extra[2 * number : 2 * number + 2], axis=1)
        extra_out[:, lanes] = from_edges
        grown.append(in_order[:, lanes] * (wet + dot(rows_of, table)))
        parts = []
        for row in (0, rows - 1):
            west, east = from_edges[row : row + 1, :], from_edges[rows + row : rows + row + 1, :]
            parts += with_edges(plan, turned[row, :, lanes], west, east)
        parts += [turned_edge[:, lanes] + from_edges, filler]
        some.append(jnp.concatenate(parts, axis=0) * (wet_some + dot(some_of, table)))
    for number, start in enumerate(range(0, plan.spectral, 256)):
        lanes = slice(start, start + 256)
        product = stokes_product(grown[number], stokes[start // 2 : start // 2 + LANES, :])
        total = product if total is None else total + product
    drift = pltpu.roll(arrived, LANES // 2, 1)
    new = ocean_step(
        plan, band, even, ocean_in, drift, near, far, west_edge, east_edge, keep, sea
    )
    ocean = jnp.concatenate(new, axis=0)
    ocean_out[...] = ocean
    moments = total[:, :LANES] + total[:, LANES:]
    some = jnp.concatenate(some, axis=1)
    edges = some[2 * cols : 2 * cols + 2 * rows, :]
    fill_sections(plan, section, edges, ocean, moments, packed_out, sec_out, near_out)
    ends = (some[:cols, :], some[cols : 2 * cols, :]), (new[0], new[rows - 1])
    fill_bands(plan, even, *ends, far_out, near_out)


def grow_kernel(plan, axes, *refs):
    turned, extra, coupled, permute, sea, grow, _, waves_out = refs
    at_waves = twice(dot(permute[...], growth_halves(coupled[...])).astype(BF16))
    wet = twice(sea[...])
    for number, start in enumerate(range(0, plan.spectral, 256)):
        lanes = slice(start, start + 256)
        factor = wet + dot(at_waves, growth_table(grow, number))
        grown = grown_part(plan, turned, extra[:, lanes], factor, lanes)
        waves_out[:, :, lanes] = grown.reshape(plan.rows, plan.cols, 256)


def last_kernel(plan, axes, *refs):
    turned, ocean_in, packed_in, permute, turn_edge, sea, keep, rates, grow = refs[:9]
    got = len(plan.sizes) + plan.relay
    near, far, sec_in, refs = refs[9], refs[10], refs[11 : 11 + got], refs[11 + got :]
    waves_far, ocean_far, coupled, waves_out, ocean_out, done = refs
    section, band = lax.axis_index(axes[1]), lax.axis_index(axes[0])
    even = lax.rem(band, 2) == 0

    west_edge, east_edge = take_sections(plan, section, packed_in, sec_in, coupled)
    arrived = coupled[...]
    at_waves = twice(dot(permute[...], growth_halves(arrived)).astype(BF16))
    drift = pltpu.roll(arrived, LANES // 2, 1)
    extra = edge_part(plan, rates, turn_edge, west_edge, east_edge)
    new = ocean_step(
        plan, band, even, ocean_in, drift, near, far, west_edge, east_edge, keep, sea
    )
    for row, value in enumerate(new):
        ocean_out[row] = value[:, : 2 * plan.depth]
    copies = [pltpu.make_async_copy(ocean_out, ocean_far, done.at[0])]
    copies[0].start()
    wet = twice(sea[...])
    for number, start in enumerate(range(0, plan.spectral, 256)):
        lanes = slice(start, start + 256)
        factor = wet + dot(at_waves, growth_table(grow, number))
        from_edges = jnp.concatenate(extra[2 * number : 2 * number + 2], axis=1)
        grown = grown_part(plan, turned, from_edges, factor, lanes)
        waves_out[:, :, lanes] = grown.reshape(plan.rows, plan.cols, 256)
        copy = pltpu.make_async_copy(
            waves_out.at[:, :, lanes], waves_far.at[:, :, lanes], done.at[number + 1]
        )
        copy.start()
        copies.append(copy)
    for copy in copies:
        copy.wait()


def per_device(plan, axes, spectra, turning, currents, drag_rates, land_mask, ocean_target):
    stokes_once, stokes, rates, grow = (
        jnp.asarray(table) for table in build_tables(NFREQ, NDIR, drag_rates.shape[0])
    )
    columns, rows, cols, spectral = plan.columns, plan.rows, plan.cols, plan.spectral
    shape = jax.ShapeDtypeStruct
    params = pltpu.CompilerParams(vmem_limit_bytes=32 * 1024 * 1024)
    to_sections = [shape((size, LANES), F32) for size in plan.sizes]
    to_far = shape((cols, plan.row_lanes.stop), F32)
    to_near = shape((cols, plan.chunk_lanes.stop), F32)
    state = shape((columns, LANES), F32)
    field = shape(spectra.shape, F32)
    at_edges = shape((2 * rows, LANES), F32)
    edge_field = shape((2 * rows, spectral), F32)
    some = plan.some
    spans = spectral // 256

    def call(kernel, outs, scratch, *args, space_in=pltpu.VMEM, space_out=pltpu.VMEM):
        return pl.pallas_call(
            functools.partial(kernel, plan, axes),
            out_shape=outs,
            in_specs=[pl.BlockSpec(memory_space=space_in)] * len(args),
            out_specs=[pl.BlockSpec(memory_space=space_out)] * len(outs),
            scratch_shapes=scratch,
            compiler_params=params,
        )(*args)

    both_axes = (axes[1], axes[0])
    pairs = [(i, i ^ 1) for i in range(plan.bands) if i ^ 1 < plan.bands]
    others = [(i, ((i + 1) ^ 1) - 1) for i in range(1, plan.bands)]
    others = [(i, j) for i, j in others if j < plan.bands]

    def exchange(to_far, to_near, to_sections, meanwhile):
        got = []
        if plan.relay:
            to_x, *to_sections = to_sections
            from_x = lax.ppermute(to_x, both_axes, plan.crossing(1))
        far_in = lax.ppermute(to_far, axes[0], others)
        near_in = lax.ppermute(to_near, axes[0], pairs)
        first = to_far
        if plan.relay:
            part = plan.chunk + plan.edge
            first, to_mate = call(
                relay_kernel,
                [shape((plan.chunk + part, LANES), F32), shape((part, LANES), F32)],
                [],
                from_x,
                near_in,
            )
            from_y = lax.ppermute(first, both_axes, plan.crossing(2))
            got = [lax.ppermute(to_mate, axes[0], pairs), from_y]
        got += [
            lax.ppermute(message, axes[1], table)
            for message, table in zip(to_sections, plan.direct)
        ]
        return meanwhile(first), [near_in, far_in, *got]

    waves, ocean, packed, order, *sent = call(
        first_kernel,
        [
            field,
            state,
            state,
            shape((columns, 2 * columns), BF16),
            *to_sections,
            to_far,
            to_near,
        ],
        [
            pltpu.VMEM(currents.shape, F32),
            pltpu.VMEM(ocean_target.shape, jnp.int32),
            pltpu.VMEM(stokes_once.shape, BF16),
            pltpu.SemaphoreType.DMA((4,)),
        ],
        *[
            pltpu.with_memory_space_constraint(array, pltpu.HBM)
            for array in (spectra, currents, ocean_target, stokes_once)
        ],
        space_in=pltpu.HBM,
    )

    def maps(first):
        return call(
            map_kernel,
            [
                shape((columns, columns), BF16),
                shape((some, columns), BF16),
                shape((2 * rows, LANES), jnp.int32),
                state,
                at_edges,
                state,
                state,
                shape((some, LANES), F32),
                shape((8, LANES), F32),
            ],
            [],
            turning,
            drag_rates,
            land_mask,
            order,
            first,
        )

    made, came = exchange(*sent[-2:], sent[:-2], maps)
    permute, permute_some, slots, turn, turn_edge, sea, sea_order, sea_some, keep = made
    for step in range(STEPS - 1):
        turned, turned_edge, turned_order = call(
            move_kernel,
            [field, edge_field, shape((columns, spectral), F32)],
            [],
            waves,
            turn,
            rates,
            *came[:2],
            order,
        )
        ocean, packed, coupled, extra, *sent = call(
            send_kernel,
            [state, state, state, edge_field, to_far, to_near] + to_sections,
            [pltpu.VMEM((columns, spectral), F32)],
            turned,
            turned_edge,
            turned_order,
            ocean,
            packed,
            permute_some,
            slots,
            turn_edge,
            sea,
            sea_order,
            sea_some,
            keep,
            stokes,
            rates,
            grow,
            *came,
        )

        def grown(first):
            (waves,) = call(
                grow_kernel, [field], [], turned, extra, coupled, permute, sea, grow, first
            )
            return waves

        waves, came = exchange(*sent[:2], sent[2:], grown)
    (turned,) = call(move_kernel, [field], [], waves, turn, rates, *came[:2])
    return call(
        last_kernel,
        [field, shape(currents.shape, F32)],
        [
            pltpu.VMEM((columns, LANES), F32),
            pltpu.VMEM(spectra.shape, F32),
            pltpu.VMEM(currents.shape, F32),
            pltpu.SemaphoreType.DMA((1 + spans,)),
        ],
        turned,
        ocean,
        packed,
        permute,
        turn_edge,
        sea,
        keep,
        rates,
        grow,
        *came,
        space_out=pltpu.HBM,
    )


def solution(mesh):
    sections, bands = mesh.shape["sec"], mesh.shape["lat"]

    def local(spectra, turning, currents, drag_rates, land_mask, ocean_target):
        rows, cols, spectral = spectra.shape
        plan = Plan(sections, bands, rows, cols, spectral, drag_rates.shape[0])
        return per_device(
            plan, ("lat", "sec"), spectra, turning, currents, drag_rates, land_mask, ocean_target
        )

    return jax.shard_map(
        local,
        mesh=mesh,
        in_specs=(
            P("lat", "sec", None),
            P("lat", "sec"),
            P("lat", "sec", None),
            P(),
            P("lat", "sec"),
            P("lat", "sec"),
        ),
        out_specs=(P("lat", "sec", None), P("lat", "sec", None)),
        check_vma=False,
    )
```

```python
import functools
import math

import jax
import jax.numpy as jnp
import ml_dtypes
import numpy as np
from jax import lax
from jax.experimental import pallas as pl
from jax.experimental.pallas import tpu as pltpu
from jax.sharding import PartitionSpec as P

NFREQ = 24
NDIR = 32
STEPS = 3

stokes_scale = 0.1
ocean_dt = 0.3
current_gain = 0.2

LANES = 128
F32 = jnp.float32
BF16 = jnp.bfloat16


def split_halves(table):
    high = table.astype(ml_dtypes.bfloat16)
    low = (table - high.astype(np.float64)).astype(ml_dtypes.bfloat16)
    return high, low


def build_tables(nfreq, ndir, ndepth):
    fraction = np.arange(nfreq) / (nfreq - 1)
    angles = (np.arange(ndir) + 0.5) * (2.0 * math.pi / ndir)
    east_part, north_part = np.cos(angles), np.sin(angles)
    courant = 0.1 + 0.3 * fraction
    depth_level = 0.5 + (ndepth - 2) * (1.0 - fraction)
    weights = np.maximum(1.0 - np.abs(np.arange(ndepth)[None, :] - depth_level[:, None]), 0.0)
    mean_weights = weights / weights.sum(axis=1, keepdims=True)
    x_rate = np.abs(courant[:, None] * east_part[None, :]).reshape(-1)
    y_rate = np.abs(courant[:, None] * north_part[None, :]).reshape(-1)
    turn_gain = np.repeat(1.0 - 0.5 * fraction, ndir)
    rates = np.stack([1.0 - x_rate - y_rate, x_rate, y_rate, turn_gain] * 2).astype(np.float32)
    compass = np.stack([east_part, north_part])
    stokes = (stokes_scale * weights[:, None, None, :] * compass.T[None, :, :, None]).reshape(
        nfreq * ndir, 2 * ndepth
    )
    growth = current_gain * (1.0 + fraction)
    grow = (
        growth[None, None, :, None] * mean_weights.T[None, :, :, None] * compass[:, None, None, :]
    ).reshape(2 * ndepth, nfreq * ndir)
    pairs = stokes.reshape(-1, 2, LANES // ndir, ndir, 2 * ndepth)
    stokes = np.concatenate([pairs[:, 0, :, : ndir // 2], pairs[:, 1, :, ndir // 2 :]], axis=2)
    high, low = split_halves(stokes.reshape(nfreq * ndir // 2, 2 * ndepth))
    blank = np.zeros_like(high)
    stokes_once = np.concatenate([high, low], axis=1)
    stokes_upper = np.concatenate([blank, high, blank, low], axis=1)
    high, low = split_halves(grow)
    grow = np.concatenate([high, high, low, low], axis=0)
    return (
        stokes_once,
        stokes_upper,
        rates,
        grow.reshape(2 * LANES, -1, LANES).transpose(1, 0, 2).reshape(-1, LANES),
    )


class Plan:
    def __init__(self, sections, bands, rows, cols, spectral, depth):
        self.sections, self.bands = sections, bands
        self.rows, self.cols, self.spectral, self.depth = rows, cols, spectral, depth
        self.columns = rows * cols
        self.chunk = self.columns // sections
        self.tiles = spectral // LANES
        self.some = -(-(2 * cols + 2 * rows) // 16) * 16
        self.edge = ((self.tiles // 2 + 1) * rows + 7) // 8 * 8
        self.relay = sections % 4 == 0 and bands % 2 == 0 and self.chunk <= cols
        self.quad = 4 if self.relay else 1
        self.hops = [
            (hop, flip)
            for hop in range(1, sections // self.quad)
            for flip in ((3, 1, 2, 0) if self.relay else (0,))
        ]
        self.direct = [
            [(i, self.partner(i, *hop, divmod)[0]) for i in range(sections)] for hop in self.hops
        ]
        self.edges = [any(abs(target - i) == 1 for i, target in table) for table in self.direct]
        self.sizes = [self.chunk + (self.edge if edge else 0) for edge in self.edges]
        near_rows = cols * (spectral // 2 + LANES + depth) // LANES
        self.x_rows = max(2 * (self.chunk + self.edge), (near_rows + 8) // 8 * 8)
        if self.relay:
            self.sizes = [self.x_rows] + self.sizes
        start = spectral // 2
        self.far_lanes = slice(start, start + depth)
        self.chunk_lanes = slice(start, start + LANES)
        self.near_lanes = slice(start + LANES, start + LANES + depth)

    def crossing(self, flip):
        bands = self.bands
        return [
            (i * bands + band, (i ^ flip) * bands + (band ^ 1))
            for i in range(self.sections)
            for band in range(bands)
        ]

    def partner(self, section, hop, flip, divide=lambda a, b: (lax.div(a, b), lax.rem(a, b))):
        groups = self.sections // self.quad
        high, low = divide(section, self.quad)
        if flip & 1:
            low = low + 1 - 2 * divide(low, 2)[1]
        if flip & 2:
            low = low + 2 - 4 * divide(low, 2)[0]
        return tuple(
            divide(high + shift, groups)[1] * self.quad + low for shift in (hop, groups - hop)
        )

    def received(self, section, messages):
        parts = []
        if self.relay:
            from_x, from_y = messages[:2]
            parts = [
                (self.partner(section, 0, 1)[1], from_x, 0, self.chunk),
                (self.partner(section, 0, 2)[1], from_y, 0, None),
                (self.partner(section, 0, 3)[1], from_y, self.chunk, 2 * self.chunk),
            ]
            messages = messages[2:]
        for message, hop, edge in zip(messages, self.hops, self.edges):
            parts.append((self.partner(section, *hop)[1], message, 0, self.chunk if edge else None))
        return parts

    def sent(self, section, messages, near):
        parts = []
        lanes = slice(0, LANES)
        if self.relay:
            to_x = messages[0]
            second = self.chunk + self.edge
            parts = [
                (self.partner(section, 0, 1)[0], to_x, 0, lanes, self.chunk),
                (self.partner(section, 0, 2)[0], near, 0, self.chunk_lanes, None),
                (self.partner(section, 0, 3)[0], to_x, second, lanes, second + self.chunk),
            ]
            messages = messages[1:]
        for message, hop, edge in zip(messages, self.hops, self.edges):
            target = self.partner(section, *hop)[0]
            parts.append((target, message, 0, lanes, self.chunk if edge else None))
        return parts


def lane_of(shape):
    return lax.broadcasted_iota(jnp.int32, shape, len(shape) - 1)


def dot(a, b):
    return jnp.dot(a, b, preferred_element_type=F32)


def split_value(value):
    high = value.astype(BF16)
    return high, (value - high.astype(F32)).astype(BF16)


def opposed(part):
    first, second = part[:, :LANES], part[:, LANES:]
    lower = lax.rem(lane_of(first.shape), NDIR) < NDIR // 2
    shift = NDIR // 2
    return jnp.where(lower, first, second) - jnp.where(
        lower, pltpu.roll(first, LANES - shift, 1), pltpu.roll(second, shift, 1)
    )


def stokes_product(part, table):
    return dot(jnp.concatenate(split_value(opposed(part)), axis=1), twice(table, 0))


def packed_half(edge, tile, half, ahead, forward):
    first = edge[:, tile * LANES : (tile + 1) * LANES]
    second = edge[:, (tile + half) * LANES : (tile + half + 1) * LANES]
    keep = jnp.where(ahead, 1, 0) == jnp.where(forward, 1, 0)
    return jnp.where(keep, first, pltpu.roll(second, NDIR // 2, 1))


def fill_band(plan, northward, edge, sea_row, out, lanes):
    half = plan.tiles // 2
    masks = Directions((plan.cols, LANES))
    for tile in range(half):
        out[:, tile * LANES : (tile + 1) * LANES] = packed_half(
            edge, tile, half, masks.northward, northward
        )
    out[:, lanes] = sea_row[:, : plan.depth]


def fill_bands(plan, even, edges, sea_rows, far, near):
    for out, northward, lanes in (
        (far, jnp.logical_not(even), plan.far_lanes),
        (near, even, plan.near_lanes),
    ):
        edge = jnp.where(northward, edges[1], edges[0])
        sea_row = jnp.where(northward, sea_rows[1], sea_rows[0])
        fill_band(plan, northward, edge, sea_row, out, lanes)


def fill_sections(plan, section, edges, ocean, ordered, packed_out, sec_out, near):
    chunk, rows, cols, half = plan.chunk, plan.rows, plan.cols, plan.tiles // 2
    lane = lane_of((plan.columns, LANES))
    packed_out[...] = jnp.where(lane < LANES // 2, ocean, ordered)
    sea_rows = ocean.reshape(rows, cols, LANES)
    masks = Directions((rows, LANES))
    if plan.relay:
        used = 2 * (chunk + plan.edge)
        sec_out[0][used:, :] = jnp.zeros((plan.x_rows - used, LANES), F32)
    for target, out, at, lanes, edge_at in plan.sent(section, sec_out, near):
        part = packed_out[pl.ds(pl.multiple_of(target * chunk, 8), chunk), :]
        out[at : at + chunk, lanes] = part
        if edge_at is None:
            continue
        eastward = target == section + 1
        edge = jnp.where(eastward, edges[rows:, :], edges[:rows, :])
        for tile in range(half):
            place = edge_at + tile * rows
            out[place : place + rows, :] = packed_half(edge, tile, half, masks.eastward, eastward)
        for row in range(rows):
            place = edge_at + half * rows + row
            out[place : place + 1, :] = jnp.where(
                eastward, sea_rows[row, cols - 1 : cols, :], sea_rows[row, 0:1, :]
            )


def take_sections(plan, section, packed_in, sec_in, coupled):
    chunk = plan.chunk
    own = pl.ds(pl.multiple_of(section * chunk, 8), chunk)
    coupled[own, :] = packed_in[own, :]
    west = east = jnp.zeros((plan.edge, LANES), F32)
    for source, message, at, edge_at in plan.received(section, sec_in):
        coupled[pl.ds(pl.multiple_of(source * chunk, 8), chunk), :] = message[at : at + chunk, :]
        if edge_at is not None:
            edge = message[edge_at : edge_at + plan.edge, :]
            west = jnp.where(source == section - 1, edge, west)
            east = jnp.where(source == section + 1, edge, east)
    return west, east


def edge_part(plan, rates, turn_edge, west_edge, east_edge):
    rows, half = plan.rows, plan.tiles // 2
    shape = (2 * rows, LANES)
    masks = Directions(shape)
    westmost = lax.broadcasted_iota(jnp.int32, shape, 0) < rows
    reached = jnp.where(masks.eastward, 1, 0) == jnp.where(westmost, 1, 0)
    parts = []
    for tile in range(plan.tiles):
        lanes = slice(tile * LANES, (tile + 1) * LANES)
        edge = slice(tile % half * rows, (tile % half + 1) * rows)
        came = jnp.concatenate([west_edge[edge, :], east_edge[edge, :]], axis=0)
        if tile >= half:
            came = pltpu.roll(came, LANES - NDIR // 2, 1)
        moved = rates[1:2, lanes] * jnp.where(reached, came, 0.0)
        parts.append(masks.turned(moved, turn_edge[...], rates[3:4, lanes]))
    return parts


def ocean_step(plan, band, even, ocean_in, stokes, near, far, west_edge, east_edge, keep, sea):
    rows, cols, half = plan.rows, plan.cols, plan.tiles // 2
    block = (cols, LANES)
    zonal = lane_of(block) < plan.depth
    place = lax.broadcasted_iota(jnp.int32, block, 0)
    at_west, at_east = place == 0, place == cols - 1
    blank = jnp.zeros((cols, LANES - plan.depth), F32)
    far = jnp.concatenate([far[:, plan.far_lanes], blank], axis=1)
    near = jnp.concatenate([near[:, plan.near_lanes], blank], axis=1)
    south_edge, north_edge = jnp.where(even, far, near), jnp.where(even, near, far)
    new = []
    for row in range(rows):
        flat = slice(row * cols, (row + 1) * cols)
        edge = slice(half * rows + row, half * rows + row + 1)
        center = ocean_in[flat, :]
        west = jnp.where(at_west, west_edge[edge, :], pltpu.roll(center, 1, 0))
        east = jnp.where(at_east, east_edge[edge, :], pltpu.roll(center, cols - 1, 0))
        south = ocean_in[(row - 1) * cols : row * cols, :] if row else south_edge
        north = ocean_in[(row + 1) * cols : (row + 2) * cols, :] if row < rows - 1 else north_edge
        shear = 0.5 * jnp.where(zonal, south - north, east - west)
        y = (band * rows + row).astype(F32)
        spin = 0.2 + 0.6 * y / float(plan.bands * rows) + (shear + swapped(plan, shear))
        turn_by = ocean_dt * spin * swapped(plan, center + stokes[flat, :])
        new.append(keep[0:1, :] * (center + jnp.where(zonal, turn_by, -turn_by)) * sea[flat, :])
    return new


def twice(value, axis=1):
    return jnp.concatenate([value, value], axis=axis)


def growth_table(grow, number):
    size = 2 * LANES
    return jnp.concatenate(
        [grow[(2 * number + k) * size : (2 * number + k + 1) * size, :] for k in range(2)], axis=1
    )


def growth_halves(arrived):
    high = arrived.astype(BF16).astype(F32)
    lower = lane_of(arrived.shape) < LANES // 2
    return jnp.where(lower, high, pltpu.roll(arrived - high, LANES // 2, 1)).astype(BF16)


def with_edges(plan, turned, west, east):
    place = lax.broadcasted_iota(jnp.int32, (8, 256), 0)
    return [
        turned[0:8, :] + jnp.where(place == 0, west, 0.0),
        turned[8 : plan.cols - 8, :],
        turned[plan.cols - 8 :, :] + jnp.where(place == 7, east, 0.0),
    ]


def grown_part(plan, turned, from_edges, factor, lanes):
    rows = plan.rows
    parts = []
    for row in range(rows):
        west, east = from_edges[row : row + 1, :], from_edges[rows + row : rows + row + 1, :]
        parts += with_edges(plan, turned[row, :, lanes], west, east)
    return jnp.concatenate(parts, axis=0) * factor


def relay_kernel(plan, axes, from_x, near, to_y, to_mate):
    own = plan.chunk + plan.edge
    to_y[0 : plan.chunk, :] = near[0 : plan.chunk, plan.chunk_lanes]
    to_y[plan.chunk :, :] = from_x[own : 2 * own, :]
    to_mate[...] = from_x[:own, :]


def square_places(plan):
    shape = (plan.columns, plan.columns)
    return lax.broadcasted_iota(jnp.int32, shape, 0), lax.broadcasted_iota(jnp.int32, shape, 1)


def row_of(plan, ref):
    return jnp.concatenate([ref[row : row + 1, :] for row in range(plan.rows)], axis=1)


def column_of(plan, row):
    down, across = square_places(plan)
    spread = jnp.broadcast_to(row, down.shape)
    return jnp.sum(jnp.where(down == across, spread, 0.0), axis=1, keepdims=True)


def first_kernel(plan, axes, *refs):
    waves_in, currents_in, target_in, stokes_in, refs = *refs[:4], refs[4:]
    waves, ocean_out, packed_out, order_out, refs = *refs[:4], refs[4:]
    count = len(plan.sizes)
    sec_out, lat_out, refs = refs[:count], refs[count : count + 2], refs[count + 2 :]
    currents, target, stokes, done = refs
    pairs = [(target_in, target), (waves_in, waves), (stokes_in, stokes), (currents_in, currents)]
    copies = [pltpu.make_async_copy(a, b, done.at[k]) for k, (a, b) in enumerate(pairs)]
    for copy in copies:
        copy.start()
    section, band = lax.axis_index(axes[1]), lax.axis_index(axes[0])
    even = lax.rem(band, 2) == 0
    columns, rows, cols = plan.columns, plan.rows, plan.cols
    copies[0].wait()
    down, across = square_places(plan)
    target_row = row_of(plan, target).astype(F32)
    same = column_of(plan, target_row) == target_row
    rank = jnp.sum(jnp.where(same & (down < across), 1.0, 0.0), axis=0, keepdims=True)
    slot = target_row * float(plan.chunk) + rank
    order = twice(jnp.where(slot == down.astype(F32), 1.0, 0.0)).astype(BF16)
    order_out[...] = order
    for copy in copies[1:]:
        copy.wait()
    total = None
    for start in range(0, plan.spectral, 256):
        part = waves[:, :, start : start + 256].reshape(columns, 256)
        product = stokes_product(part, stokes[start // 2 : start // 2 + LANES, :])
        total = product if total is None else total + product
    moments = total
    flat = currents[...].reshape(columns, 2 * plan.depth)
    ocean = jnp.concatenate([flat, jnp.zeros((columns, LANES - 2 * plan.depth), F32)], axis=1)
    ocean_out[...] = ocean
    ordered = dot(order, jnp.concatenate(split_value(moments), axis=0))
    ordered = ordered + pltpu.roll(ordered, LANES // 2, 1)
    west = [waves[row, 0:1, :] for row in range(rows)]
    east = [waves[row, cols - 1 : cols, :] for row in range(rows)]
    edges = jnp.concatenate(west + east, axis=0)
    fill_sections(plan, section, edges, ocean, ordered, packed_out, sec_out, lat_out[1])
    sea_rows = ocean.reshape(rows, cols, LANES)
    ends = (waves[0], waves[rows - 1]), (sea_rows[0], sea_rows[rows - 1])
    fill_bands(plan, even, *ends, *lat_out)


def map_kernel(plan, axes, *refs):
    turning, drag, mask, order_twice, _, refs = *refs[:5], refs[5:]
    permute_out, permute_some_out, slots_out, turn_out, turn_edge_out = refs[:5]
    sea_out, sea_order_out, sea_some_out, keep_out = refs[5:]
    columns, rows, cols = plan.columns, plan.rows, plan.cols
    order = order_twice[:, :columns]
    sea = jnp.broadcast_to(column_of(plan, row_of(plan, mask).astype(F32)), (columns, LANES))
    turn = jnp.broadcast_to(column_of(plan, row_of(plan, turning)), (columns, LANES))
    sea_out[...] = sea
    turn_out[...] = turn
    west = [turn[row * cols : row * cols + 1, :] for row in range(rows)]
    east = [turn[(row + 1) * cols - 1 : (row + 1) * cols, :] for row in range(rows)]
    turn_edge_out[...] = jnp.concatenate(west + east, axis=0)
    sea_order_out[...] = dot(order, sea.astype(BF16))
    down, across = square_places(plan)
    same = jnp.where(down == across, 1.0, 0.0).astype(BF16)
    back = lax.dot_general(
        order, same, (((0,), (0,)), ((), ())), preferred_element_type=F32
    )
    permute = (back * sea[:, :columns]).astype(BF16)
    permute_out[...] = permute
    shape = (plan.some, columns)
    place = lax.broadcasted_iota(jnp.int32, shape, 0)
    number = place - 2 * cols
    wanted = jnp.where(
        place < 2 * cols,
        place + jnp.where(place < cols, 0, (rows - 2) * cols),
        lax.rem(number, rows) * cols + lax.div(number, rows) * (cols - 1),
    )
    wanted = jnp.where(number < 2 * rows, wanted, -1)
    chosen = jnp.where(lane_of(shape) == wanted, 1.0, 0.0).astype(BF16)
    permute_some_out[...] = dot(chosen, permute).astype(BF16)
    sea_some_out[...] = dot(chosen, sea.astype(BF16))
    slot = jnp.sum(order.astype(F32) * down.astype(F32), axis=0, keepdims=True)
    slot = jnp.broadcast_to(column_of(plan, slot), (columns, LANES)).astype(BF16)
    slots_out[...] = dot(chosen, slot)[2 * cols : 2 * cols + 2 * rows, :].astype(jnp.int32)
    keep = 1.0 - drag[...].reshape(1, plan.depth)
    blank = jnp.zeros((1, LANES - 2 * plan.depth), F32)
    keep_out[...] = jnp.broadcast_to(jnp.concatenate([keep, keep, blank], axis=1), (8, LANES))


class Directions:
    def __init__(self, shape):
        direction = lax.rem(lane_of(shape), NDIR)
        self.eastward = (direction < NDIR // 4) | (direction >= 3 * NDIR // 4)
        self.northward = direction < NDIR // 2
        self.first, self.final = direction == 0, direction == NDIR - 1

    def turned(self, moved, rate, gain):
        behind = jnp.where(
            self.first, pltpu.roll(moved, LANES - (NDIR - 1), 1), pltpu.roll(moved, 1, 1)
        )
        forward = jnp.where(
            self.final, pltpu.roll(moved, NDIR - 1, 1), pltpu.roll(moved, LANES - 1, 1)
        )
        return moved - jnp.abs(rate) * gain * (moved - jnp.where(rate > 0.0, behind, forward))


def move_kernel(plan, axes, *refs):
    waves, turn, rates, near, far, refs = *refs[:5], refs[5:]
    if len(refs) > 1:
        order, turned_out, edge_out, sorted_out = refs
    else:
        (turned_out,) = refs
    even = lax.rem(lax.axis_index(axes[0]), 2) == 0
    rows, cols, tiles = plan.rows, plan.cols, plan.tiles
    block = (cols, LANES)
    masks = Directions(block)
    place = lax.broadcasted_iota(jnp.int32, block, 0)
    outside = place == jnp.where(masks.eastward, 0, cols - 1)
    for tile in range(tiles):
        lanes = slice(tile * LANES, (tile + 1) * LANES)
        stay, along_x, along_y, gain = (rates[k : k + 1, lanes] for k in range(4))
        along_x = jnp.where(outside, 0.0, along_x)
        half = tile % (tiles // 2)
        half = slice(half * LANES, (half + 1) * LANES)
        south_edge = jnp.where(even, far[:, half], near[:, half])
        north_edge = jnp.where(even, near[:, half], far[:, half])
        if tile >= tiles // 2:
            south_edge = pltpu.roll(south_edge, LANES - NDIR // 2, 1)
            north_edge = pltpu.roll(north_edge, LANES - NDIR // 2, 1)
        for row in range(rows):
            center = waves[row, :, lanes]
            south = waves[row - 1, :, lanes] if row else south_edge
            north = waves[row + 1, :, lanes] if row < rows - 1 else north_edge
            moved = (
                stay * center
                + along_x
                * jnp.where(
                    masks.eastward, pltpu.roll(center, 1, 0), pltpu.roll(center, cols - 1, 0)
                )
                + along_y * jnp.where(masks.northward, south, north)
            )
            rate = turn[row * cols : (row + 1) * cols, :]
            turned = masks.turned(moved, rate, gain)
            turned_out[row, :, lanes] = turned
            if len(refs) > 1:
                edge_out[row : row + 1, lanes] = turned[0:1, :]
                edge_out[rows + row : rows + row + 1, lanes] = turned[cols - 1 :, :]
    if len(refs) > 1:
        for start in range(0, plan.spectral, 256):
            part = turned_out[:, :, start : start + 256].reshape(plan.columns, 256)
            sorted_out[:, start : start + 256] = dot(
                order[...], jnp.concatenate(split_value(part), axis=0)
            )


def swapped(plan, value):
    half = plan.depth
    zonal = lane_of(value.shape) < half
    return jnp.where(zonal, pltpu.roll(value, LANES - half, 1), pltpu.roll(value, half, 1))


def send_kernel(plan, axes, *refs):
    turned, turned_edge, turned_order, ocean_in, packed_in, permute_some, slots = refs[:7]
    turn_edge, sea, sea_order, sea_some, keep, stokes, rates, grow, refs = *refs[7:15], refs[15:]
    count = len(plan.sizes)
    got = count + plan.relay
    near, far, sec_in, refs = refs[0], refs[1], refs[2 : 2 + got], refs[2 + got :]
    ocean_out, packed_out, coupled, extra_out, far_out, near_out = refs[:6]
    sec_out, in_order = refs[6 : 6 + count], refs[6 + count]
    section, band = lax.axis_index(axes[1]), lax.axis_index(axes[0])
    even = lax.rem(band, 2) == 0
    columns, rows, cols = plan.columns, plan.rows, plan.cols

    west_edge, east_edge = take_sections(plan, section, packed_in, sec_in, coupled)
    extra = edge_part(plan, rates, turn_edge, west_edge, east_edge)
    in_order[...] = turned_order[...]
    for number in range(2 * rows):
        slot = pl.ds(slots[number, 0], 1)
        part = jnp.concatenate([tile[number : number + 1, :] for tile in extra], axis=1)
        in_order[slot, :] = in_order[slot, :] + part
    arrived = coupled[...]
    halves = growth_halves(arrived)
    wet, wet_some = sea_order[...], twice(sea_some[...])
    rows_of = twice(halves * wet.astype(BF16))
    some_of = twice(dot(permute_some[...], halves).astype(BF16))
    wet = twice(wet)
    total = None
    some, grown = [], []
    filler = jnp.zeros((plan.some - 2 * cols - 2 * rows, 256), F32)
    for number, start in enumerate(range(0, plan.spectral, 256)):
        lanes = slice(start, start + 256)
        table = growth_table(grow, number)
        from_edges = jnp.concatenate(extra[2 * number : 2 * number + 2], axis=1)
        extra_out[:, lanes] = from_edges
        grown.append(in_order[:, lanes] * (wet + dot(rows_of, table)))
        parts = []
        for row in (0, rows - 1):
            west, east = from_edges[row : row + 1, :], from_edges[rows + row : rows + row + 1, :]
            parts += with_edges(plan, turned[row, :, lanes], west, east)
        parts += [turned_edge[:, lanes] + from_edges, filler]
        some.append(jnp.concatenate(parts, axis=0) * (wet_some + dot(some_of, table)))
    for number, start in enumerate(range(0, plan.spectral, 256)):
        lanes = slice(start, start + 256)
        product = stokes_product(grown[number], stokes[start // 2 : start // 2 + LANES, :])
        total = product if total is None else total + product
    drift = pltpu.roll(arrived, LANES // 2, 1)
    new = ocean_step(
        plan, band, even, ocean_in, drift, near, far, west_edge, east_edge, keep, sea
    )
    ocean = jnp.concatenate(new, axis=0)
    ocean_out[...] = ocean
    moments = total[:, :LANES] + total[:, LANES:]
    some = jnp.concatenate(some, axis=1)
    edges = some[2 * cols : 2 * cols + 2 * rows, :]
    fill_sections(plan, section, edges, ocean, moments, packed_out, sec_out, near_out)
    ends = (some[:cols, :], some[cols : 2 * cols, :]), (new[0], new[rows - 1])
    fill_bands(plan, even, *ends, far_out, near_out)


def grow_kernel(plan, axes, *refs):
    turned, extra, coupled, permute, sea, grow, _, waves_out = refs
    at_waves = twice(dot(permute[...], growth_halves(coupled[...])).astype(BF16))
    wet = twice(sea[...])
    for number, start in enumerate(range(0, plan.spectral, 256)):
        lanes = slice(start, start + 256)
        factor = wet + dot(at_waves, growth_table(grow, number))
        grown = grown_part(plan, turned, extra[:, lanes], factor, lanes)
        waves_out[:, :, lanes] = grown.reshape(plan.rows, plan.cols, 256)


def last_kernel(plan, axes, *refs):
    turned, ocean_in, packed_in, permute, turn_edge, sea, keep, rates, grow = refs[:9]
    got = len(plan.sizes) + plan.relay
    near, far, sec_in, refs = refs[9], refs[10], refs[11 : 11 + got], refs[11 + got :]
    waves_far, ocean_far, coupled, waves_out, ocean_out, done = refs
    section, band = lax.axis_index(axes[1]), lax.axis_index(axes[0])
    even = lax.rem(band, 2) == 0

    west_edge, east_edge = take_sections(plan, section, packed_in, sec_in, coupled)
    arrived = coupled[...]
    at_waves = twice(dot(permute[...], growth_halves(arrived)).astype(BF16))
    drift = pltpu.roll(arrived, LANES // 2, 1)
    extra = edge_part(plan, rates, turn_edge, west_edge, east_edge)
    new = ocean_step(
        plan, band, even, ocean_in, drift, near, far, west_edge, east_edge, keep, sea
    )
    for row, value in enumerate(new):
        ocean_out[row] = value[:, : 2 * plan.depth]
    copies = [pltpu.make_async_copy(ocean_out, ocean_far, done.at[0])]
    copies[0].start()
    wet = twice(sea[...])
    for number, start in enumerate(range(0, plan.spectral, 256)):
        lanes = slice(start, start + 256)
        factor = wet + dot(at_waves, growth_table(grow, number))
        from_edges = jnp.concatenate(extra[2 * number : 2 * number + 2], axis=1)
        grown = grown_part(plan, turned, from_edges, factor, lanes)
        waves_out[:, :, lanes] = grown.reshape(plan.rows, plan.cols, 256)
        copy = pltpu.make_async_copy(
            waves_out.at[:, :, lanes], waves_far.at[:, :, lanes], done.at[number + 1]
        )
        copy.start()
        copies.append(copy)
    for copy in copies:
        copy.wait()


def per_device(plan, axes, spectra, turning, currents, drag_rates, land_mask, ocean_target):
    stokes_once, stokes, rates, grow = (
        jnp.asarray(table) for table in build_tables(NFREQ, NDIR, drag_rates.shape[0])
    )
    columns, rows, cols, spectral = plan.columns, plan.rows, plan.cols, plan.spectral
    shape = jax.ShapeDtypeStruct
    params = pltpu.CompilerParams(vmem_limit_bytes=32 * 1024 * 1024)
    to_sections = [shape((size, LANES), F32) for size in plan.sizes]
    to_far = shape((cols, plan.far_lanes.stop), F32)
    to_near = shape((cols, plan.near_lanes.stop), F32)
    state = shape((columns, LANES), F32)
    field = shape(spectra.shape, F32)
    at_edges = shape((2 * rows, LANES), F32)
    edge_field = shape((2 * rows, spectral), F32)
    some = plan.some
    spans = spectral // 256

    def call(kernel, outs, scratch, *args, space_in=pltpu.VMEM, space_out=pltpu.VMEM):
        return pl.pallas_call(
            functools.partial(kernel, plan, axes),
            out_shape=outs,
            in_specs=[pl.BlockSpec(memory_space=space_in)] * len(args),
            out_specs=[pl.BlockSpec(memory_space=space_out)] * len(outs),
            scratch_shapes=scratch,
            compiler_params=params,
        )(*args)

    both_axes = (axes[1], axes[0])
    pairs = [(i, i ^ 1) for i in range(plan.bands) if i ^ 1 < plan.bands]
    others = [(i, ((i + 1) ^ 1) - 1) for i in range(1, plan.bands)]
    others = [(i, j) for i, j in others if j < plan.bands]

    def exchange(to_far, to_near, to_sections, meanwhile):
        got = []
        if plan.relay:
            to_x, *to_sections = to_sections
            from_x = lax.ppermute(to_x, both_axes, plan.crossing(1))
        far_in = lax.ppermute(to_far, axes[0], others)
        near_in = lax.ppermute(to_near, axes[0], pairs)
        first = to_far
        if plan.relay:
            part = plan.chunk + plan.edge
            first, to_mate = call(
                relay_kernel,
                [shape((plan.chunk + part, LANES), F32), shape((part, LANES), F32)],
                [],
                from_x,
                near_in,
            )
            from_y = lax.ppermute(first, both_axes, plan.crossing(2))
            got = [lax.ppermute(to_mate, axes[0], pairs), from_y]
        got += [
            lax.ppermute(message, axes[1], table)
            for message, table in zip(to_sections, plan.direct)
        ]
        return meanwhile(first), [near_in, far_in, *got]

    waves, ocean, packed, order, *sent = call(
        first_kernel,
        [
            field,
            state,
            state,
            shape((columns, 2 * columns), BF16),
            *to_sections,
            to_far,
            to_near,
        ],
        [
            pltpu.VMEM(currents.shape, F32),
            pltpu.VMEM(ocean_target.shape, jnp.int32),
            pltpu.VMEM(stokes_once.shape, BF16),
            pltpu.SemaphoreType.DMA((4,)),
        ],
        *[
            pltpu.with_memory_space_constraint(array, pltpu.HBM)
            for array in (spectra, currents, ocean_target, stokes_once)
        ],
        space_in=pltpu.HBM,
    )

    def maps(first):
        return call(
            map_kernel,
            [
                shape((columns, columns), BF16),
                shape((some, columns), BF16),
                shape((2 * rows, LANES), jnp.int32),
                state,
                at_edges,
                state,
                state,
                shape((some, LANES), F32),
                shape((8, LANES), F32),
            ],
            [],
            turning,
            drag_rates,
            land_mask,
            order,
            first,
        )

    made, came = exchange(*sent[-2:], sent[:-2], maps)
    permute, permute_some, slots, turn, turn_edge, sea, sea_order, sea_some, keep = made
    for step in range(STEPS - 1):
        turned, turned_edge, turned_order = call(
            move_kernel,
            [field, edge_field, shape((columns, spectral), F32)],
            [],
            waves,
            turn,
            rates,
            *came[:2],
            order,
        )
        ocean, packed, coupled, extra, *sent = call(
            send_kernel,
            [state, state, state, edge_field, to_far, to_near] + to_sections,
            [pltpu.VMEM((columns, spectral), F32)],
            turned,
            turned_edge,
            turned_order,
            ocean,
            packed,
            permute_some,
            slots,
            turn_edge,
            sea,
            sea_order,
            sea_some,
            keep,
            stokes,
            rates,
            grow,
            *came,
        )

        def grown(first):
            (waves,) = call(
                grow_kernel, [field], [], turned, extra, coupled, permute, sea, grow, first
            )
            return waves

        waves, came = exchange(*sent[:2], sent[2:], grown)
    (turned,) = call(move_kernel, [field], [], waves, turn, rates, *came[:2])
    return call(
        last_kernel,
        [field, shape(currents.shape, F32)],
        [
            pltpu.VMEM((columns, LANES), F32),
            pltpu.VMEM(spectra.shape, F32),
            pltpu.VMEM(currents.shape, F32),
            pltpu.SemaphoreType.DMA((1 + spans,)),
        ],
        turned,
        ocean,
        packed,
        permute,
        turn_edge,
        sea,
        keep,
        rates,
        grow,
        *came,
        space_out=pltpu.HBM,
    )


def solution(mesh):
    sections, bands = mesh.shape["sec"], mesh.shape["lat"]

    def local(spectra, turning, currents, drag_rates, land_mask, ocean_target):
        rows, cols, spectral = spectra.shape
        plan = Plan(sections, bands, rows, cols, spectral, drag_rates.shape[0])
        return per_device(
            plan, ("lat", "sec"), spectra, turning, currents, drag_rates, land_mask, ocean_target
        )

    return jax.shard_map(
        local,
        mesh=mesh,
        in_specs=(
            P("lat", "sec", None),
            P("lat", "sec"),
            P("lat", "sec", None),
            P(),
            P("lat", "sec"),
            P("lat", "sec"),
        ),
        out_specs=(P("lat", "sec", None), P("lat", "sec", None)),
        check_vma=False,
    )
```

```python
import functools
import math

import jax
import jax.numpy as jnp
import ml_dtypes
import numpy as np
from jax import lax
from jax.experimental import pallas as pl
from jax.experimental.pallas import tpu as pltpu
from jax.sharding import PartitionSpec as P

NFREQ = 24
NDIR = 32
STEPS = 3

stokes_scale = 0.1
ocean_dt = 0.3
current_gain = 0.2

LANES = 128
F32 = jnp.float32
BF16 = jnp.bfloat16


def split_halves(table):
    high = table.astype(ml_dtypes.bfloat16)
    low = (table - high.astype(np.float64)).astype(ml_dtypes.bfloat16)
    return high, low


def build_tables(nfreq, ndir, ndepth):
    fraction = np.arange(nfreq) / (nfreq - 1)
    angles = (np.arange(ndir) + 0.5) * (2.0 * math.pi / ndir)
    east_part, north_part = np.cos(angles), np.sin(angles)
    courant = 0.1 + 0.3 * fraction
    depth_level = 0.5 + (ndepth - 2) * (1.0 - fraction)
    weights = np.maximum(1.0 - np.abs(np.arange(ndepth)[None, :] - depth_level[:, None]), 0.0)
    mean_weights = weights / weights.sum(axis=1, keepdims=True)
    x_rate = np.abs(courant[:, None] * east_part[None, :]).reshape(-1)
    y_rate = np.abs(courant[:, None] * north_part[None, :]).reshape(-1)
    turn_gain = np.repeat(1.0 - 0.5 * fraction, ndir)
    rates = np.stack([1.0 - x_rate - y_rate, x_rate, y_rate, turn_gain] * 2).astype(np.float32)
    compass = np.stack([east_part, north_part])
    stokes = (stokes_scale * weights[:, None, None, :] * compass.T[None, :, :, None]).reshape(
        nfreq * ndir, 2 * ndepth
    )
    growth = current_gain * (1.0 + fraction)
    grow = (
        growth[None, None, :, None] * mean_weights.T[None, :, :, None] * compass[:, None, None, :]
    ).reshape(2 * ndepth, nfreq * ndir)
    pairs = stokes.reshape(-1, 2, LANES // ndir, ndir, 2 * ndepth)
    stokes = np.concatenate([pairs[:, 0, :, : ndir // 2], pairs[:, 1, :, ndir // 2 :]], axis=2)
    high, low = split_halves(stokes.reshape(nfreq * ndir // 2, 2 * ndepth))
    blank = np.zeros_like(high)
    stokes_once = np.concatenate([high, low], axis=1)
    stokes_upper = np.concatenate([blank, high, blank, low], axis=1)
    high, low = split_halves(grow)
    grow = np.concatenate([high, high, low, low], axis=0)
    return (
        stokes_once,
        stokes_upper,
        rates,
        grow.reshape(2 * LANES, -1, LANES).transpose(1, 0, 2).reshape(-1, LANES),
    )


class Plan:
    def __init__(self, sections, bands, rows, cols, spectral, depth):
        self.sections, self.bands = sections, bands
        self.rows, self.cols, self.spectral, self.depth = rows, cols, spectral, depth
        self.columns = rows * cols
        self.chunk = self.columns // sections
        self.tiles = spectral // LANES
        self.some = -(-(2 * cols + 2 * rows) // 16) * 16
        self.edge = ((self.tiles // 2 + 1) * rows + 7) // 8 * 8
        self.relay = sections % 4 == 0 and bands % 2 == 0 and self.chunk <= cols
        self.quad = 4 if self.relay else 1
        self.hops = [
            (hop, flip)
            for hop in range(1, sections // self.quad)
            for flip in ((3, 1, 2, 0) if self.relay else (0,))
        ]
        self.direct = [
            [(i, self.partner(i, *hop, divmod)[0]) for i in range(sections)] for hop in self.hops
        ]
        self.edges = [any(abs(target - i) == 1 for i, target in table) for table in self.direct]
        self.sizes = [self.chunk + (self.edge if edge else 0) for edge in self.edges]
        near_rows = cols * (spectral // 2 + LANES + depth) // LANES
        self.x_rows = max(2 * (self.chunk + self.edge), (near_rows + 8) // 8 * 8)
        if self.relay:
            self.sizes = [self.x_rows] + self.sizes
        start = spectral // 2
        self.far_lanes = slice(start, start + depth)
        self.chunk_lanes = slice(start, start + LANES)
        self.near_lanes = slice(start + LANES, start + LANES + depth)

    def crossing(self, flip):
        bands = self.bands
        return [
            (i * bands + band, (i ^ flip) * bands + (band ^ 1))
            for i in range(self.sections)
            for band in range(bands)
        ]

    def partner(self, section, hop, flip, divide=lambda a, b: (lax.div(a, b), lax.rem(a, b))):
        groups = self.sections // self.quad
        high, low = divide(section, self.quad)
        if flip & 1:
            low = low + 1 - 2 * divide(low, 2)[1]
        if flip & 2:
            low = low + 2 - 4 * divide(low, 2)[0]
        return tuple(
            divide(high + shift, groups)[1] * self.quad + low for shift in (hop, groups - hop)
        )

    def received(self, section, messages):
        parts = []
        if self.relay:
            from_x, from_y = messages[:2]
            parts = [
                (self.partner(section, 0, 1)[1], from_x, 0, self.chunk),
                (self.partner(section, 0, 2)[1], from_y, 0, None),
                (self.partner(section, 0, 3)[1], from_y, self.chunk, 2 * self.chunk),
            ]
            messages = messages[2:]
        for message, hop, edge in zip(messages, self.hops, self.edges):
            parts.append((self.partner(section, *hop)[1], message, 0, self.chunk if edge else None))
        return parts

    def sent(self, section, messages, near):
        parts = []
        lanes = slice(0, LANES)
        if self.relay:
            to_x = messages[0]
            second = self.chunk + self.edge
            parts = [
                (self.partner(section, 0, 1)[0], to_x, 0, lanes, self.chunk),
                (self.partner(section, 0, 2)[0], near, 0, self.chunk_lanes, None),
                (self.partner(section, 0, 3)[0], to_x, second, lanes, second + self.chunk),
            ]
            messages = messages[1:]
        for message, hop, edge in zip(messages, self.hops, self.edges):
            target = self.partner(section, *hop)[0]
            parts.append((target, message, 0, lanes, self.chunk if edge else None))
        return parts


def lane_of(shape):
    return lax.broadcasted_iota(jnp.int32, shape, len(shape) - 1)


def dot(a, b):
    return jnp.dot(a, b, preferred_element_type=F32)


def split_value(value):
    high = value.astype(BF16)
    return high, (value - high.astype(F32)).astype(BF16)


def opposed(part):
    first, second = part[:, :LANES], part[:, LANES:]
    lower = lax.rem(lane_of(first.shape), NDIR) < NDIR // 2
    shift = NDIR // 2
    return jnp.where(lower, first, second) - jnp.where(
        lower, pltpu.roll(first, LANES - shift, 1), pltpu.roll(second, shift, 1)
    )


def stokes_product(part, table):
    return dot(jnp.concatenate(split_value(opposed(part)), axis=1), twice(table, 0))


def packed_half(edge, tile, half, ahead, forward):
    first = edge[:, tile * LANES : (tile + 1) * LANES]
    second = edge[:, (tile + half) * LANES : (tile + half + 1) * LANES]
    keep = jnp.where(ahead, 1, 0) == jnp.where(forward, 1, 0)
    return jnp.where(keep, first, pltpu.roll(second, NDIR // 2, 1))


def fill_band(plan, northward, edge, sea_row, out, lanes):
    half = plan.tiles // 2
    masks = Directions((plan.cols, LANES))
    for tile in range(half):
        out[:, tile * LANES : (tile + 1) * LANES] = packed_half(
            edge, tile, half, masks.northward, northward
        )
    out[:, lanes] = sea_row[:, : plan.depth]


def fill_bands(plan, even, edges, sea_rows, far, near):
    for out, northward, lanes in (
        (far, jnp.logical_not(even), plan.far_lanes),
        (near, even, plan.near_lanes),
    ):
        edge = jnp.where(northward, edges[1], edges[0])
        sea_row = jnp.where(northward, sea_rows[1], sea_rows[0])
        fill_band(plan, northward, edge, sea_row, out, lanes)


def fill_sections(plan, section, edges, ocean, ordered, packed_out, sec_out, near):
    chunk, rows, cols, half = plan.chunk, plan.rows, plan.cols, plan.tiles // 2
    lane = lane_of((plan.columns, LANES))
    packed_out[...] = jnp.where(lane < LANES // 2, ocean, ordered)
    sea_rows = ocean.reshape(rows, cols, LANES)
    masks = Directions((rows, LANES))
    if plan.relay:
        used = 2 * (chunk + plan.edge)
        sec_out[0][used:, :] = jnp.zeros((plan.x_rows - used, LANES), F32)
    for target, out, at, lanes, edge_at in plan.sent(section, sec_out, near):
        part = packed_out[pl.ds(pl.multiple_of(target * chunk, 8), chunk), :]
        out[at : at + chunk, lanes] = part
        if edge_at is None:
            continue
        eastward = target == section + 1
        edge = jnp.where(eastward, edges[rows:, :], edges[:rows, :])
        for tile in range(half):
            place = edge_at + tile * rows
            out[place : place + rows, :] = packed_half(edge, tile, half, masks.eastward, eastward)
        for row in range(rows):
            place = edge_at + half * rows + row
            out[place : place + 1, :] = jnp.where(
                eastward, sea_rows[row, cols - 1 : cols, :], sea_rows[row, 0:1, :]
            )


def take_sections(plan, section, packed_in, sec_in, coupled):
    chunk = plan.chunk
    own = pl.ds(pl.multiple_of(section * chunk, 8), chunk)
    coupled[own, :] = packed_in[own, :]
    west = east = jnp.zeros((plan.edge, LANES), F32)
    for source, message, at, edge_at in plan.received(section, sec_in):
        coupled[pl.ds(pl.multiple_of(source * chunk, 8), chunk), :] = message[at : at + chunk, :]
        if edge_at is not None:
            edge = message[edge_at : edge_at + plan.edge, :]
            west = jnp.where(source == section - 1, edge, west)
            east = jnp.where(source == section + 1, edge, east)
    return west, east


def edge_part(plan, rates, turn_edge, west_edge, east_edge):
    rows, half = plan.rows, plan.tiles // 2
    shape = (2 * rows, LANES)
    masks = Directions(shape)
    westmost = lax.broadcasted_iota(jnp.int32, shape, 0) < rows
    reached = jnp.where(masks.eastward, 1, 0) == jnp.where(westmost, 1, 0)
    parts = []
    for tile in range(plan.tiles):
        lanes = slice(tile * LANES, (tile + 1) * LANES)
        edge = slice(tile % half * rows, (tile % half + 1) * rows)
        came = jnp.concatenate([west_edge[edge, :], east_edge[edge, :]], axis=0)
        if tile >= half:
            came = pltpu.roll(came, LANES - NDIR // 2, 1)
        moved = rates[1:2, lanes] * jnp.where(reached, came, 0.0)
        parts.append(masks.turned(moved, turn_edge[...], rates[3:4, lanes]))
    return parts


def ocean_step(plan, band, even, ocean_in, stokes, near, far, west_edge, east_edge, keep, sea):
    rows, cols, half = plan.rows, plan.cols, plan.tiles // 2
    block = (cols, LANES)
    zonal = lane_of(block) < plan.depth
    place = lax.broadcasted_iota(jnp.int32, block, 0)
    at_west, at_east = place == 0, place == cols - 1
    blank = jnp.zeros((cols, LANES - plan.depth), F32)
    far = jnp.concatenate([far[:, plan.far_lanes], blank], axis=1)
    near = jnp.concatenate([near[:, plan.near_lanes], blank], axis=1)
    south_edge, north_edge = jnp.where(even, far, near), jnp.where(even, near, far)
    new = []
    for row in range(rows):
        flat = slice(row * cols, (row + 1) * cols)
        edge = slice(half * rows + row, half * rows + row + 1)
        center = ocean_in[flat, :]
        west = jnp.where(at_west, west_edge[edge, :], pltpu.roll(center, 1, 0))
        east = jnp.where(at_east, east_edge[edge, :], pltpu.roll(center, cols - 1, 0))
        south = ocean_in[(row - 1) * cols : row * cols, :] if row else south_edge
        north = ocean_in[(row + 1) * cols : (row + 2) * cols, :] if row < rows - 1 else north_edge
        shear = 0.5 * jnp.where(zonal, south - north, east - west)
        y = (band * rows + row).astype(F32)
        spin = 0.2 + 0.6 * y / float(plan.bands * rows) + (shear + swapped(plan, shear))
        turn_by = ocean_dt * spin * swapped(plan, center + stokes[flat, :])
        new.append(keep[0:1, :] * (center + jnp.where(zonal, turn_by, -turn_by)) * sea[flat, :])
    return new


def twice(value, axis=1):
    return jnp.concatenate([value, value], axis=axis)


def growth_table(grow, number):
    size = 2 * LANES
    return jnp.concatenate(
        [grow[(2 * number + k) * size : (2 * number + k + 1) * size, :] for k in range(2)], axis=1
    )


def growth_halves(arrived):
    high = arrived.astype(BF16).astype(F32)
    lower = lane_of(arrived.shape) < LANES // 2
    return jnp.where(lower, high, pltpu.roll(arrived - high, LANES // 2, 1)).astype(BF16)


def with_edges(plan, turned, west, east):
    place = lax.broadcasted_iota(jnp.int32, (8, 256), 0)
    return [
        turned[0:8, :] + jnp.where(place == 0, west, 0.0),
        turned[8 : plan.cols - 8, :],
        turned[plan.cols - 8 :, :] + jnp.where(place == 7, east, 0.0),
    ]


def grown_part(plan, turned, from_edges, factor, lanes):
    rows = plan.rows
    parts = []
    for row in range(rows):
        west, east = from_edges[row : row + 1, :], from_edges[rows + row : rows + row + 1, :]
        parts += with_edges(plan, turned[row, :, lanes], west, east)
    return jnp.concatenate(parts, axis=0) * factor


def relay_kernel(plan, axes, from_x, near, to_y, to_mate):
    own = plan.chunk + plan.edge
    to_y[0 : plan.chunk, :] = near[0 : plan.chunk, plan.chunk_lanes]
    to_y[plan.chunk :, :] = from_x[own : 2 * own, :]
    to_mate[...] = from_x[:own, :]


def square_places(plan):
    shape = (plan.columns, plan.columns)
    return lax.broadcasted_iota(jnp.int32, shape, 0), lax.broadcasted_iota(jnp.int32, shape, 1)


def row_of(plan, ref):
    return jnp.concatenate([ref[row : row + 1, :] for row in range(plan.rows)], axis=1)


def column_of(plan, row):
    down, across = square_places(plan)
    spread = jnp.broadcast_to(row, down.shape)
    return jnp.sum(jnp.where(down == across, spread, 0.0), axis=1, keepdims=True)


def first_kernel(plan, axes, *refs):
    waves_in, currents_in, target_in, stokes_in, refs = *refs[:4], refs[4:]
    waves, ocean_out, packed_out, order_out, refs = *refs[:4], refs[4:]
    count = len(plan.sizes)
    sec_out, lat_out, refs = refs[:count], refs[count : count + 2], refs[count + 2 :]
    currents, target, stokes, done = refs
    pairs = [(target_in, target), (waves_in, waves), (stokes_in, stokes), (currents_in, currents)]
    copies = [pltpu.make_async_copy(a, b, done.at[k]) for k, (a, b) in enumerate(pairs)]
    for copy in copies:
        copy.start()
    section, band = lax.axis_index(axes[1]), lax.axis_index(axes[0])
    even = lax.rem(band, 2) == 0
    columns, rows, cols = plan.columns, plan.rows, plan.cols
    copies[0].wait()
    down, across = square_places(plan)
    target_row = row_of(plan, target).astype(F32)
    same = column_of(plan, target_row) == target_row
    rank = jnp.sum(jnp.where(same & (down < across), 1.0, 0.0), axis=0, keepdims=True)
    slot = target_row * float(plan.chunk) + rank
    order = twice(jnp.where(slot == down.astype(F32), 1.0, 0.0)).astype(BF16)
    order_out[...] = order
    for copy in copies[1:]:
        copy.wait()
    total = None
    for start in range(0, plan.spectral, 256):
        part = waves[:, :, start : start + 256].reshape(columns, 256)
        product = stokes_product(part, stokes[start // 2 : start // 2 + LANES, :])
        total = product if total is None else total + product
    moments = total
    flat = currents[...].reshape(columns, 2 * plan.depth)
    ocean = jnp.concatenate([flat, jnp.zeros((columns, LANES - 2 * plan.depth), F32)], axis=1)
    ocean_out[...] = ocean
    ordered = dot(order, jnp.concatenate(split_value(moments), axis=0))
    ordered = ordered + pltpu.roll(ordered, LANES // 2, 1)
    west = [waves[row, 0:1, :] for row in range(rows)]
    east = [waves[row, cols - 1 : cols, :] for row in range(rows)]
    edges = jnp.concatenate(west + east, axis=0)
    fill_sections(plan, section, edges, ocean, ordered, packed_out, sec_out, lat_out[1])
    sea_rows = ocean.reshape(rows, cols, LANES)
    ends = (waves[0], waves[rows - 1]), (sea_rows[0], sea_rows[rows - 1])
    fill_bands(plan, even, *ends, *lat_out)


def map_kernel(plan, axes, *refs):
    inputs, (order_twice, _), refs = refs[:6], refs[6:8], refs[8:]
    tables, (turning, drag, mask, done) = refs[9:12], refs[12:]
    targets = (turning, drag, mask, *tables)
    copies = [pltpu.make_async_copy(*pair, done.at[k]) for k, pair in enumerate(zip(inputs, targets))]
    for copy in copies:
        copy.start()
    permute_out, permute_some_out, slots_out, turn_out, turn_edge_out = refs[:5]
    sea_out, sea_order_out, sea_some_out, keep_out = refs[5:9]
    columns, rows, cols = plan.columns, plan.rows, plan.cols
    order = order_twice[:, :columns]
    for copy in copies[:3]:
        copy.wait()
    sea = jnp.broadcast_to(column_of(plan, row_of(plan, mask).astype(F32)), (columns, LANES))
    turn = jnp.broadcast_to(column_of(plan, row_of(plan, turning)), (columns, LANES))
    sea_out[...] = sea
    turn_out[...] = turn
    west = [turn[row * cols : row * cols + 1, :] for row in range(rows)]
    east = [turn[(row + 1) * cols - 1 : (row + 1) * cols, :] for row in range(rows)]
    turn_edge_out[...] = jnp.concatenate(west + east, axis=0)
    sea_order_out[...] = dot(order, sea.astype(BF16))
    down, across = square_places(plan)
    same = jnp.where(down == across, 1.0, 0.0).astype(BF16)
    back = lax.dot_general(
        order, same, (((0,), (0,)), ((), ())), preferred_element_type=F32
    )
    permute = (back * sea[:, :columns]).astype(BF16)
    permute_out[...] = permute
    shape = (plan.some, columns)
    place = lax.broadcasted_iota(jnp.int32, shape, 0)
    number = place - 2 * cols
    wanted = jnp.where(
        place < 2 * cols,
        place + jnp.where(place < cols, 0, (rows - 2) * cols),
        lax.rem(number, rows) * cols + lax.div(number, rows) * (cols - 1),
    )
    wanted = jnp.where(number < 2 * rows, wanted, -1)
    chosen = jnp.where(lane_of(shape) == wanted, 1.0, 0.0).astype(BF16)
    permute_some_out[...] = dot(chosen, permute).astype(BF16)
    sea_some_out[...] = dot(chosen, sea.astype(BF16))
    slot = jnp.sum(order.astype(F32) * down.astype(F32), axis=0, keepdims=True)
    slot = jnp.broadcast_to(column_of(plan, slot), (columns, LANES)).astype(BF16)
    slots_out[...] = dot(chosen, slot)[2 * cols : 2 * cols + 2 * rows, :].astype(jnp.int32)
    keep = 1.0 - drag[...].reshape(1, plan.depth)
    blank = jnp.zeros((1, LANES - 2 * plan.depth), F32)
    keep_out[...] = jnp.broadcast_to(jnp.concatenate([keep, keep, blank], axis=1), (8, LANES))
    for copy in copies[3:]:
        copy.wait()


class Directions:
    def __init__(self, shape):
        direction = lax.rem(lane_of(shape), NDIR)
        self.eastward = (direction < NDIR // 4) | (direction >= 3 * NDIR // 4)
        self.northward = direction < NDIR // 2
        self.first, self.final = direction == 0, direction == NDIR - 1

    def turned(self, moved, rate, gain):
        behind = jnp.where(
            self.first, pltpu.roll(moved, LANES - (NDIR - 1), 1), pltpu.roll(moved, 1, 1)
        )
        forward = jnp.where(
            self.final, pltpu.roll(moved, NDIR - 1, 1), pltpu.roll(moved, LANES - 1, 1)
        )
        return moved - jnp.abs(rate) * gain * (moved - jnp.where(rate > 0.0, behind, forward))


def move_kernel(plan, axes, *refs):
    waves, turn, rates, near, far, refs = *refs[:5], refs[5:]
    if len(refs) > 1:
        order, turned_out, edge_out, sorted_out = refs
    else:
        (turned_out,) = refs
    even = lax.rem(lax.axis_index(axes[0]), 2) == 0
    rows, cols, tiles = plan.rows, plan.cols, plan.tiles
    block = (cols, LANES)
    masks = Directions(block)
    place = lax.broadcasted_iota(jnp.int32, block, 0)
    outside = place == jnp.where(masks.eastward, 0, cols - 1)
    for tile in range(tiles):
        lanes = slice(tile * LANES, (tile + 1) * LANES)
        stay, along_x, along_y, gain = (rates[k : k + 1, lanes] for k in range(4))
        along_x = jnp.where(outside, 0.0, along_x)
        half = tile % (tiles // 2)
        half = slice(half * LANES, (half + 1) * LANES)
        south_edge = jnp.where(even, far[:, half], near[:, half])
        north_edge = jnp.where(even, near[:, half], far[:, half])
        if tile >= tiles // 2:
            south_edge = pltpu.roll(south_edge, LANES - NDIR // 2, 1)
            north_edge = pltpu.roll(north_edge, LANES - NDIR // 2, 1)
        for row in range(rows):
            center = waves[row, :, lanes]
            south = waves[row - 1, :, lanes] if row else south_edge
            north = waves[row + 1, :, lanes] if row < rows - 1 else north_edge
            moved = (
                stay * center
                + along_x
                * jnp.where(
                    masks.eastward, pltpu.roll(center, 1, 0), pltpu.roll(center, cols - 1, 0)
                )
                + along_y * jnp.where(masks.northward, south, north)
            )
            rate = turn[row * cols : (row + 1) * cols, :]
            turned = masks.turned(moved, rate, gain)
            turned_out[row, :, lanes] = turned
            if len(refs) > 1:
                edge_out[row : row + 1, lanes] = turned[0:1, :]
                edge_out[rows + row : rows + row + 1, lanes] = turned[cols - 1 :, :]
    if len(refs) > 1:
        for start in range(0, plan.spectral, 256):
            part = turned_out[:, :, start : start + 256].reshape(plan.columns, 256)
            sorted_out[:, start : start + 256] = dot(
                order[...], jnp.concatenate(split_value(part), axis=0)
            )


def swapped(plan, value):
    half = plan.depth
    zonal = lane_of(value.shape) < half
    return jnp.where(zonal, pltpu.roll(value, LANES - half, 1), pltpu.roll(value, half, 1))


def send_kernel(plan, axes, *refs):
    turned, turned_edge, turned_order, ocean_in, packed_in, permute_some, slots = refs[:7]
    turn_edge, sea, sea_order, sea_some, keep, stokes, rates, grow, refs = *refs[7:15], refs[15:]
    count = len(plan.sizes)
    got = count + plan.relay
    near, far, sec_in, refs = refs[0], refs[1], refs[2 : 2 + got], refs[2 + got :]
    ocean_out, packed_out, coupled, extra_out, far_out, near_out = refs[:6]
    sec_out, in_order = refs[6 : 6 + count], refs[6 + count]
    section, band = lax.axis_index(axes[1]), lax.axis_index(axes[0])
    even = lax.rem(band, 2) == 0
    columns, rows, cols = plan.columns, plan.rows, plan.cols

    west_edge, east_edge = take_sections(plan, section, packed_in, sec_in, coupled)
    extra = edge_part(plan, rates, turn_edge, west_edge, east_edge)
    in_order[...] = turned_order[...]
    for number in range(2 * rows):
        slot = pl.ds(slots[number, 0], 1)
        part = jnp.concatenate([tile[number : number + 1, :] for tile in extra], axis=1)
        in_order[slot, :] = in_order[slot, :] + part
    arrived = coupled[...]
    halves = growth_halves(arrived)
    wet, wet_some = sea_order[...], twice(sea_some[...])
    rows_of = twice(halves * wet.astype(BF16))
    some_of = twice(dot(permute_some[...], halves).astype(BF16))
    wet = twice(wet)
    total = None
    some, grown = [], []
    filler = jnp.zeros((plan.some - 2 * cols - 2 * rows, 256), F32)
    for number, start in enumerate(range(0, plan.spectral, 256)):
        lanes = slice(start, start + 256)
        table = growth_table(grow, number)
        from_edges = jnp.concatenate(extra[2 * number : 2 * number + 2], axis=1)
        extra_out[:, lanes] = from_edges
        grown.append(in_order[:, lanes] * (wet + dot(rows_of, table)))
        parts = []
        for row in (0, rows - 1):
            west, east = from_edges[row : row + 1, :], from_edges[rows + row : rows + row + 1, :]
            parts += with_edges(plan, turned[row, :, lanes], west, east)
        parts += [turned_edge[:, lanes] + from_edges, filler]
        some.append(jnp.concatenate(parts, axis=0) * (wet_some + dot(some_of, table)))
    for number, start in enumerate(range(0, plan.spectral, 256)):
        lanes = slice(start, start + 256)
        product = stokes_product(grown[number], stokes[start // 2 : start // 2 + LANES, :])
        total = product if total is None else total + product
    drift = pltpu.roll(arrived, LANES // 2, 1)
    new = ocean_step(
        plan, band, even, ocean_in, drift, near, far, west_edge, east_edge, keep, sea
    )
    ocean = jnp.concatenate(new, axis=0)
    ocean_out[...] = ocean
    moments = total[:, :LANES] + total[:, LANES:]
    some = jnp.concatenate(some, axis=1)
    edges = some[2 * cols : 2 * cols + 2 * rows, :]
    fill_sections(plan, section, edges, ocean, moments, packed_out, sec_out, near_out)
    ends = (some[:cols, :], some[cols : 2 * cols, :]), (new[0], new[rows - 1])
    fill_bands(plan, even, *ends, far_out, near_out)


def grow_kernel(plan, axes, *refs):
    turned, extra, coupled, permute, sea, grow, _, waves_out = refs
    at_waves = twice(dot(permute[...], growth_halves(coupled[...])).astype(BF16))
    wet = twice(sea[...])
    for number, start in enumerate(range(0, plan.spectral, 256)):
        lanes = slice(start, start + 256)
        factor = wet + dot(at_waves, growth_table(grow, number))
        grown = grown_part(plan, turned, extra[:, lanes], factor, lanes)
        waves_out[:, :, lanes] = grown.reshape(plan.rows, plan.cols, 256)


def last_kernel(plan, axes, *refs):
    turned, ocean_in, packed_in, permute, turn_edge, sea, keep, rates, grow = refs[:9]
    got = len(plan.sizes) + plan.relay
    near, far, sec_in, refs = refs[9], refs[10], refs[11 : 11 + got], refs[11 + got :]
    waves_far, ocean_far, coupled, waves_out, ocean_out, done = refs
    section, band = lax.axis_index(axes[1]), lax.axis_index(axes[0])
    even = lax.rem(band, 2) == 0

    west_edge, east_edge = take_sections(plan, section, packed_in, sec_in, coupled)
    arrived = coupled[...]
    at_waves = twice(dot(permute[...], growth_halves(arrived)).astype(BF16))
    drift = pltpu.roll(arrived, LANES // 2, 1)
    extra = edge_part(plan, rates, turn_edge, west_edge, east_edge)
    new = ocean_step(
        plan, band, even, ocean_in, drift, near, far, west_edge, east_edge, keep, sea
    )
    for row, value in enumerate(new):
        ocean_out[row] = value[:, : 2 * plan.depth]
    copies = [pltpu.make_async_copy(ocean_out, ocean_far, done.at[0])]
    copies[0].start()
    wet = twice(sea[...])
    for number, start in enumerate(range(0, plan.spectral, 256)):
        lanes = slice(start, start + 256)
        factor = wet + dot(at_waves, growth_table(grow, number))
        from_edges = jnp.concatenate(extra[2 * number : 2 * number + 2], axis=1)
        grown = grown_part(plan, turned, from_edges, factor, lanes)
        waves_out[:, :, lanes] = grown.reshape(plan.rows, plan.cols, 256)
        copy = pltpu.make_async_copy(
            waves_out.at[:, :, lanes], waves_far.at[:, :, lanes], done.at[number + 1]
        )
        copy.start()
        copies.append(copy)
    for copy in copies:
        copy.wait()


def per_device(plan, axes, spectra, turning, currents, drag_rates, land_mask, ocean_target):
    stokes_once, *tables = (
        jnp.asarray(table) for table in build_tables(NFREQ, NDIR, drag_rates.shape[0])
    )
    columns, rows, cols, spectral = plan.columns, plan.rows, plan.cols, plan.spectral
    shape = jax.ShapeDtypeStruct
    params = pltpu.CompilerParams(vmem_limit_bytes=32 * 1024 * 1024)
    to_sections = [shape((size, LANES), F32) for size in plan.sizes]
    to_far = shape((cols, plan.far_lanes.stop), F32)
    to_near = shape((cols, plan.near_lanes.stop), F32)
    state = shape((columns, LANES), F32)
    field = shape(spectra.shape, F32)
    at_edges = shape((2 * rows, LANES), F32)
    edge_field = shape((2 * rows, spectral), F32)
    some = plan.some
    spans = spectral // 256

    def call(kernel, outs, scratch, *args, space_in=pltpu.VMEM, space_out=pltpu.VMEM):
        spaces = space_in if isinstance(space_in, list) else [space_in] * len(args)
        return pl.pallas_call(
            functools.partial(kernel, plan, axes),
            out_shape=outs,
            in_specs=[pl.BlockSpec(memory_space=space) for space in spaces],
            out_specs=[pl.BlockSpec(memory_space=space_out)] * len(outs),
            scratch_shapes=scratch,
            compiler_params=params,
        )(*args)

    both_axes = (axes[1], axes[0])
    pairs = [(i, i ^ 1) for i in range(plan.bands) if i ^ 1 < plan.bands]
    others = [(i, ((i + 1) ^ 1) - 1) for i in range(1, plan.bands)]
    others = [(i, j) for i, j in others if j < plan.bands]

    def exchange(to_far, to_near, to_sections, meanwhile):
        got = []
        if plan.relay:
            to_x, *to_sections = to_sections
            from_x = lax.ppermute(to_x, both_axes, plan.crossing(1))
        far_in = lax.ppermute(to_far, axes[0], others)
        near_in = lax.ppermute(to_near, axes[0], pairs)
        first = to_far
        if plan.relay:
            part = plan.chunk + plan.edge
            first, to_mate = call(
                relay_kernel,
                [shape((plan.chunk + part, LANES), F32), shape((part, LANES), F32)],
                [],
                from_x,
                near_in,
            )
            from_y = lax.ppermute(first, both_axes, plan.crossing(2))
            got = [lax.ppermute(to_mate, axes[0], pairs), from_y]
        got += [
            lax.ppermute(message, axes[1], table)
            for message, table in zip(to_sections, plan.direct)
        ]
        return meanwhile(first), [near_in, far_in, *got]

    waves, ocean, packed, order, *sent = call(
        first_kernel,
        [
            field,
            state,
            state,
            shape((columns, 2 * columns), BF16),
            *to_sections,
            to_far,
            to_near,
        ],
        [
            pltpu.VMEM(currents.shape, F32),
            pltpu.VMEM(ocean_target.shape, jnp.int32),
            pltpu.VMEM(stokes_once.shape, BF16),
            pltpu.SemaphoreType.DMA((4,)),
        ],
        *[
            pltpu.with_memory_space_constraint(array, pltpu.HBM)
            for array in (spectra, currents, ocean_target, stokes_once)
        ],
        space_in=pltpu.HBM,
    )

    def maps(first):
        return call(
            map_kernel,
            [
                shape((columns, columns), BF16),
                shape((some, columns), BF16),
                shape((2 * rows, LANES), jnp.int32),
                state,
                at_edges,
                state,
                state,
                shape((some, LANES), F32),
                shape((8, LANES), F32),
                *[shape(table.shape, table.dtype) for table in tables],
            ],
            [
                pltpu.VMEM(turning.shape, F32),
                pltpu.VMEM(drag_rates.shape, F32),
                pltpu.VMEM(land_mask.shape, jnp.int32),
                pltpu.SemaphoreType.DMA((6,)),
            ],
            *[
                pltpu.with_memory_space_constraint(array, pltpu.HBM)
                for array in (turning, drag_rates, land_mask, *tables)
            ],
            order,
            first,
            space_in=[pltpu.HBM] * 6 + [pltpu.VMEM] * 2,
        )

    made, came = exchange(*sent[-2:], sent[:-2], maps)
    permute, permute_some, slots, turn, turn_edge, sea, sea_order, sea_some, keep, stokes, rates, grow = made
    for step in range(STEPS - 1):
        turned, turned_edge, turned_order = call(
            move_kernel,
            [field, edge_field, shape((columns, spectral), F32)],
            [],
            waves,
            turn,
            rates,
            *came[:2],
            order,
        )
        ocean, packed, coupled, extra, *sent = call(
            send_kernel,
            [state, state, state, edge_field, to_far, to_near] + to_sections,
            [pltpu.VMEM((columns, spectral), F32)],
            turned,
            turned_edge,
            turned_order,
            ocean,
            packed,
            permute_some,
            slots,
            turn_edge,
            sea,
            sea_order,
            sea_some,
            keep,
            stokes,
            rates,
            grow,
            *came,
        )

        def grown(first):
            (waves,) = call(
                grow_kernel, [field], [], turned, extra, coupled, permute, sea, grow, first
            )
            return waves

        waves, came = exchange(*sent[:2], sent[2:], grown)
    (turned,) = call(move_kernel, [field], [], waves, turn, rates, *came[:2])
    return call(
        last_kernel,
        [field, shape(currents.shape, F32)],
        [
            pltpu.VMEM((columns, LANES), F32),
            pltpu.VMEM(spectra.shape, F32),
            pltpu.VMEM(currents.shape, F32),
            pltpu.SemaphoreType.DMA((1 + spans,)),
        ],
        turned,
        ocean,
        packed,
        permute,
        turn_edge,
        sea,
        keep,
        rates,
        grow,
        *came,
        space_out=pltpu.HBM,
    )


def solution(mesh):
    sections, bands = mesh.shape["sec"], mesh.shape["lat"]

    def local(spectra, turning, currents, drag_rates, land_mask, ocean_target):
        rows, cols, spectral = spectra.shape
        plan = Plan(sections, bands, rows, cols, spectral, drag_rates.shape[0])
        return per_device(
            plan, ("lat", "sec"), spectra, turning, currents, drag_rates, land_mask, ocean_target
        )

    return jax.shard_map(
        local,
        mesh=mesh,
        in_specs=(
            P("lat", "sec", None),
            P("lat", "sec"),
            P("lat", "sec", None),
            P(),
            P("lat", "sec"),
            P("lat", "sec"),
        ),
        out_specs=(P("lat", "sec", None), P("lat", "sec", None)),
        check_vma=False,
    )
```

```python
import functools
import math

import jax
import jax.numpy as jnp
import ml_dtypes
import numpy as np
from jax import lax
from jax.experimental import pallas as pl
from jax.experimental.pallas import tpu as pltpu
from jax.sharding import PartitionSpec as P

NFREQ = 24
NDIR = 32
STEPS = 3

stokes_scale = 0.1
ocean_dt = 0.3
current_gain = 0.2

LANES = 128
F32 = jnp.float32
BF16 = jnp.bfloat16


def split_halves(table):
    high = table.astype(ml_dtypes.bfloat16)
    low = (table - high.astype(np.float64)).astype(ml_dtypes.bfloat16)
    return high, low


def build_tables(nfreq, ndir, ndepth):
    fraction = np.arange(nfreq) / (nfreq - 1)
    angles = (np.arange(ndir) + 0.5) * (2.0 * math.pi / ndir)
    east_part, north_part = np.cos(angles), np.sin(angles)
    courant = 0.1 + 0.3 * fraction
    depth_level = 0.5 + (ndepth - 2) * (1.0 - fraction)
    weights = np.maximum(1.0 - np.abs(np.arange(ndepth)[None, :] - depth_level[:, None]), 0.0)
    mean_weights = weights / weights.sum(axis=1, keepdims=True)
    x_rate = np.abs(courant[:, None] * east_part[None, :]).reshape(-1)
    y_rate = np.abs(courant[:, None] * north_part[None, :]).reshape(-1)
    turn_gain = np.repeat(1.0 - 0.5 * fraction, ndir)
    rates = np.stack([1.0 - x_rate - y_rate, x_rate, y_rate, turn_gain] * 2).astype(np.float32)
    compass = np.stack([east_part, north_part])
    stokes = (stokes_scale * weights[:, None, None, :] * compass.T[None, :, :, None]).reshape(
        nfreq * ndir, 2 * ndepth
    )
    growth = current_gain * (1.0 + fraction)
    grow = (
        growth[None, None, :, None] * mean_weights.T[None, :, :, None] * compass[:, None, None, :]
    ).reshape(2 * ndepth, nfreq * ndir)
    pairs = stokes.reshape(-1, 2, LANES // ndir, ndir, 2 * ndepth)
    stokes = np.concatenate([pairs[:, 0, :, : ndir // 2], pairs[:, 1, :, ndir // 2 :]], axis=2)
    high, low = split_halves(stokes.reshape(nfreq * ndir // 2, 2 * ndepth))
    blank = np.zeros_like(high)
    stokes_once = np.concatenate([high, low], axis=1)
    stokes_upper = np.concatenate([blank, high, blank, low], axis=1)
    high, low = split_halves(grow)
    grow = np.concatenate([high, high, low, low], axis=0)
    return (
        stokes_once,
        stokes_upper,
        rates,
        grow.reshape(2 * LANES, -1, LANES).transpose(1, 0, 2).reshape(-1, LANES),
    )


class Plan:
    def __init__(self, sections, bands, rows, cols, spectral, depth):
        self.sections, self.bands = sections, bands
        self.rows, self.cols, self.spectral, self.depth = rows, cols, spectral, depth
        self.columns = rows * cols
        self.chunk = self.columns // sections
        self.tiles = spectral // LANES
        self.some = -(-(2 * cols + 2 * rows) // 16) * 16
        self.edge = ((self.tiles // 2 + 1) * rows + 7) // 8 * 8
        self.relay = sections % 4 == 0 and bands % 2 == 0 and self.chunk <= cols
        self.quad = 4 if self.relay else 1
        self.hops = [
            (hop, flip)
            for hop in range(1, sections // self.quad)
            for flip in ((3, 1, 2, 0) if self.relay else (0,))
        ]
        self.direct = [
            [(i, self.partner(i, *hop, divmod)[0]) for i in range(sections)] for hop in self.hops
        ]
        self.edges = [any(abs(target - i) == 1 for i, target in table) for table in self.direct]
        self.sizes = [self.chunk + (self.edge if edge else 0) for edge in self.edges]
        near_rows = cols * (spectral // 2 + LANES + depth) // LANES
        self.x_rows = max(2 * (self.chunk + self.edge), (near_rows + 8) // 8 * 8)
        if self.relay:
            self.sizes = [self.x_rows] + self.sizes
        start = spectral // 2
        self.far_lanes = slice(start, start + depth)
        self.chunk_lanes = slice(start, start + LANES)
        self.near_lanes = slice(start + LANES, start + LANES + depth)

    def crossing(self, flip):
        bands = self.bands
        return [
            (i * bands + band, (i ^ flip) * bands + (band ^ 1))
            for i in range(self.sections)
            for band in range(bands)
        ]

    def partner(self, section, hop, flip, divide=lambda a, b: (lax.div(a, b), lax.rem(a, b))):
        groups = self.sections // self.quad
        high, low = divide(section, self.quad)
        if flip & 1:
            low = low + 1 - 2 * divide(low, 2)[1]
        if flip & 2:
            low = low + 2 - 4 * divide(low, 2)[0]
        return tuple(
            divide(high + shift, groups)[1] * self.quad + low for shift in (hop, groups - hop)
        )

    def received(self, section, messages):
        parts = []
        if self.relay:
            from_x, from_y = messages[:2]
            parts = [
                (self.partner(section, 0, 1)[1], from_x, 0, self.chunk),
                (self.partner(section, 0, 2)[1], from_y, 0, None),
                (self.partner(section, 0, 3)[1], from_y, self.chunk, 2 * self.chunk),
            ]
            messages = messages[2:]
        for message, hop, edge in zip(messages, self.hops, self.edges):
            parts.append((self.partner(section, *hop)[1], message, 0, self.chunk if edge else None))
        return parts

    def sent(self, section, messages, near):
        parts = []
        lanes = slice(0, LANES)
        if self.relay:
            to_x = messages[0]
            second = self.chunk + self.edge
            parts = [
                (self.partner(section, 0, 1)[0], to_x, 0, lanes, self.chunk),
                (self.partner(section, 0, 2)[0], near, 0, self.chunk_lanes, None),
                (self.partner(section, 0, 3)[0], to_x, second, lanes, second + self.chunk),
            ]
            messages = messages[1:]
        for message, hop, edge in zip(messages, self.hops, self.edges):
            target = self.partner(section, *hop)[0]
            parts.append((target, message, 0, lanes, self.chunk if edge else None))
        return parts


def lane_of(shape):
    return lax.broadcasted_iota(jnp.int32, shape, len(shape) - 1)


def dot(a, b):
    return jnp.dot(a, b, preferred_element_type=F32)


def split_value(value):
    high = value.astype(BF16)
    return high, (value - high.astype(F32)).astype(BF16)


def opposed(part):
    first, second = part[:, :LANES], part[:, LANES:]
    lower = lax.rem(lane_of(first.shape), NDIR) < NDIR // 2
    shift = NDIR // 2
    return jnp.where(lower, first, second) - jnp.where(
        lower, pltpu.roll(first, LANES - shift, 1), pltpu.roll(second, shift, 1)
    )


def stokes_product(part, table):
    return dot(jnp.concatenate(split_value(opposed(part)), axis=1), twice(table, 0))


def packed_half(edge, tile, half, ahead, forward):
    first = edge[:, tile * LANES : (tile + 1) * LANES]
    second = edge[:, (tile + half) * LANES : (tile + half + 1) * LANES]
    keep = jnp.where(ahead, 1, 0) == jnp.where(forward, 1, 0)
    return jnp.where(keep, first, pltpu.roll(second, NDIR // 2, 1))


def fill_band(plan, northward, edge, sea_row, out, lanes):
    half = plan.tiles // 2
    masks = Directions((plan.cols, LANES))
    for tile in range(half):
        out[:, tile * LANES : (tile + 1) * LANES] = packed_half(
            edge, tile, half, masks.northward, northward
        )
    out[:, lanes] = sea_row[:, : plan.depth]


def fill_bands(plan, even, edges, sea_rows, far, near):
    for out, northward, lanes in (
        (far, jnp.logical_not(even), plan.far_lanes),
        (near, even, plan.near_lanes),
    ):
        edge = jnp.where(northward, edges[1], edges[0])
        sea_row = jnp.where(northward, sea_rows[1], sea_rows[0])
        fill_band(plan, northward, edge, sea_row, out, lanes)


def fill_sections(plan, section, edges, ocean, ordered, packed_out, sec_out, near):
    chunk, rows, cols, half = plan.chunk, plan.rows, plan.cols, plan.tiles // 2
    lane = lane_of((plan.columns, LANES))
    packed_out[...] = jnp.where(lane < LANES // 2, ocean, ordered)
    sea_rows = ocean.reshape(rows, cols, LANES)
    masks = Directions((rows, LANES))
    if plan.relay:
        used = 2 * (chunk + plan.edge)
        sec_out[0][used:, :] = jnp.zeros((plan.x_rows - used, LANES), F32)
    for target, out, at, lanes, edge_at in plan.sent(section, sec_out, near):
        part = packed_out[pl.ds(pl.multiple_of(target * chunk, 8), chunk), :]
        out[at : at + chunk, lanes] = part
        if edge_at is None:
            continue
        eastward = target == section + 1
        edge = jnp.where(eastward, edges[rows:, :], edges[:rows, :])
        for tile in range(half):
            place = edge_at + tile * rows
            out[place : place + rows, :] = packed_half(edge, tile, half, masks.eastward, eastward)
        for row in range(rows):
            place = edge_at + half * rows + row
            out[place : place + 1, :] = jnp.where(
                eastward, sea_rows[row, cols - 1 : cols, :], sea_rows[row, 0:1, :]
            )


def take_sections(plan, section, packed_in, sec_in, coupled):
    chunk = plan.chunk
    own = pl.ds(pl.multiple_of(section * chunk, 8), chunk)
    coupled[own, :] = packed_in[own, :]
    west = east = jnp.zeros((plan.edge, LANES), F32)
    for source, message, at, edge_at in plan.received(section, sec_in):
        coupled[pl.ds(pl.multiple_of(source * chunk, 8), chunk), :] = message[at : at + chunk, :]
        if edge_at is not None:
            edge = message[edge_at : edge_at + plan.edge, :]
            west = jnp.where(source == section - 1, edge, west)
            east = jnp.where(source == section + 1, edge, east)
    return west, east


def edge_part(plan, rates, turn_edge, west_edge, east_edge):
    rows, half = plan.rows, plan.tiles // 2
    shape = (2 * rows, LANES)
    masks = Directions(shape)
    westmost = lax.broadcasted_iota(jnp.int32, shape, 0) < rows
    reached = jnp.where(masks.eastward, 1, 0) == jnp.where(westmost, 1, 0)
    parts = []
    for tile in range(plan.tiles):
        lanes = slice(tile * LANES, (tile + 1) * LANES)
        edge = slice(tile % half * rows, (tile % half + 1) * rows)
        came = jnp.concatenate([west_edge[edge, :], east_edge[edge, :]], axis=0)
        if tile >= half:
            came = pltpu.roll(came, LANES - NDIR // 2, 1)
        moved = rates[1:2, lanes] * jnp.where(reached, came, 0.0)
        parts.append(masks.turned(moved, turn_edge[...], rates[3:4, lanes]))
    return parts


def ocean_step(plan, band, even, ocean_in, stokes, near, far, west_edge, east_edge, keep, sea):
    rows, cols, half = plan.rows, plan.cols, plan.tiles // 2
    block = (cols, LANES)
    zonal = lane_of(block) < plan.depth
    place = lax.broadcasted_iota(jnp.int32, block, 0)
    at_west, at_east = place == 0, place == cols - 1
    blank = jnp.zeros((cols, LANES - plan.depth), F32)
    far = jnp.concatenate([far[:, plan.far_lanes], blank], axis=1)
    near = jnp.concatenate([near[:, plan.near_lanes], blank], axis=1)
    south_edge, north_edge = jnp.where(even, far, near), jnp.where(even, near, far)
    new = []
    for row in range(rows):
        flat = slice(row * cols, (row + 1) * cols)
        edge = slice(half * rows + row, half * rows + row + 1)
        center = ocean_in[flat, :]
        west = jnp.where(at_west, west_edge[edge, :], pltpu.roll(center, 1, 0))
        east = jnp.where(at_east, east_edge[edge, :], pltpu.roll(center, cols - 1, 0))
        south = ocean_in[(row - 1) * cols : row * cols, :] if row else south_edge
        north = ocean_in[(row + 1) * cols : (row + 2) * cols, :] if row < rows - 1 else north_edge
        shear = 0.5 * jnp.where(zonal, south - north, east - west)
        y = (band * rows + row).astype(F32)
        spin = 0.2 + 0.6 * y / float(plan.bands * rows) + (shear + swapped(plan, shear))
        turn_by = ocean_dt * spin * swapped(plan, center + stokes[flat, :])
        new.append(keep[0:1, :] * (center + jnp.where(zonal, turn_by, -turn_by)) * sea[flat, :])
    return new


def twice(value, axis=1):
    return jnp.concatenate([value, value], axis=axis)


def growth_table(grow, number):
    size = 2 * LANES
    return jnp.concatenate(
        [grow[(2 * number + k) * size : (2 * number + k + 1) * size, :] for k in range(2)], axis=1
    )


def growth_halves(arrived):
    high = arrived.astype(BF16).astype(F32)
    lower = lane_of(arrived.shape) < LANES // 2
    return jnp.where(lower, high, pltpu.roll(arrived - high, LANES // 2, 1)).astype(BF16)


def with_edges(plan, turned, west, east):
    place = lax.broadcasted_iota(jnp.int32, (8, 256), 0)
    return [
        turned[0:8, :] + jnp.where(place == 0, west, 0.0),
        turned[8 : plan.cols - 8, :],
        turned[plan.cols - 8 :, :] + jnp.where(place == 7, east, 0.0),
    ]


def grown_part(plan, turned, from_edges, factor, lanes):
    rows = plan.rows
    parts = []
    for row in range(rows):
        west, east = from_edges[row : row + 1, :], from_edges[rows + row : rows + row + 1, :]
        parts += with_edges(plan, turned[row, :, lanes], west, east)
    return jnp.concatenate(parts, axis=0) * factor


def relay_kernel(plan, axes, from_x, near, to_y, to_mate):
    own = plan.chunk + plan.edge
    to_y[0 : plan.chunk, :] = near[0 : plan.chunk, plan.chunk_lanes]
    to_y[plan.chunk :, :] = from_x[own : 2 * own, :]
    to_mate[...] = from_x[:own, :]


def square_places(plan):
    shape = (plan.columns, plan.columns)
    return lax.broadcasted_iota(jnp.int32, shape, 0), lax.broadcasted_iota(jnp.int32, shape, 1)


def row_of(plan, ref):
    return jnp.concatenate([ref[row : row + 1, :] for row in range(plan.rows)], axis=1)


def column_of(plan, row):
    down, across = square_places(plan)
    spread = jnp.broadcast_to(row, down.shape)
    return jnp.sum(jnp.where(down == across, spread, 0.0), axis=1, keepdims=True)


def first_kernel(plan, axes, *refs):
    waves_in, currents_in, target_in, stokes_in, refs = *refs[:4], refs[4:]
    waves, ocean_out, packed_out, order_out, refs = *refs[:4], refs[4:]
    count = len(plan.sizes)
    sec_out, lat_out, refs = refs[:count], refs[count : count + 2], refs[count + 2 :]
    currents, target, stokes, done = refs
    pairs = [(target_in, target), (waves_in, waves), (stokes_in, stokes), (currents_in, currents)]
    copies = [pltpu.make_async_copy(a, b, done.at[k]) for k, (a, b) in enumerate(pairs)]
    for copy in copies:
        copy.start()
    section, band = lax.axis_index(axes[1]), lax.axis_index(axes[0])
    even = lax.rem(band, 2) == 0
    columns, rows, cols = plan.columns, plan.rows, plan.cols
    copies[0].wait()
    down, across = square_places(plan)
    target_row = row_of(plan, target).astype(F32)
    same = column_of(plan, target_row) == target_row
    rank = jnp.sum(jnp.where(same & (down < across), 1.0, 0.0), axis=0, keepdims=True)
    slot = target_row * float(plan.chunk) + rank
    order = twice(jnp.where(slot == down.astype(F32), 1.0, 0.0)).astype(BF16)
    order_out[...] = order
    for copy in copies[1:]:
        copy.wait()
    total = None
    for start in range(0, plan.spectral, 256):
        part = waves[:, :, start : start + 256].reshape(columns, 256)
        product = stokes_product(part, stokes[start // 2 : start // 2 + LANES, :])
        total = product if total is None else total + product
    moments = total
    flat = currents[...].reshape(columns, 2 * plan.depth)
    ocean = jnp.concatenate([flat, jnp.zeros((columns, LANES - 2 * plan.depth), F32)], axis=1)
    ocean_out[...] = ocean
    ordered = dot(order, jnp.concatenate(split_value(moments), axis=0))
    ordered = ordered + pltpu.roll(ordered, LANES // 2, 1)
    west = [waves[row, 0:1, :] for row in range(rows)]
    east = [waves[row, cols - 1 : cols, :] for row in range(rows)]
    edges = jnp.concatenate(west + east, axis=0)
    fill_sections(plan, section, edges, ocean, ordered, packed_out, sec_out, lat_out[1])
    sea_rows = ocean.reshape(rows, cols, LANES)
    ends = (waves[0], waves[rows - 1]), (sea_rows[0], sea_rows[rows - 1])
    fill_bands(plan, even, *ends, *lat_out)


def map_kernel(plan, axes, *refs):
    turning, drag, mask, order_twice, _, refs = *refs[:5], refs[5:]
    permute_out, permute_some_out, slots_out, turn_out, turn_edge_out = refs[:5]
    sea_out, sea_order_out, sea_some_out, keep_out = refs[5:]
    columns, rows, cols = plan.columns, plan.rows, plan.cols
    order = order_twice[:, :columns]
    sea = jnp.broadcast_to(column_of(plan, row_of(plan, mask).astype(F32)), (columns, LANES))
    turn = jnp.broadcast_to(column_of(plan, row_of(plan, turning)), (columns, LANES))
    sea_out[...] = sea
    turn_out[...] = turn
    west = [turn[row * cols : row * cols + 1, :] for row in range(rows)]
    east = [turn[(row + 1) * cols - 1 : (row + 1) * cols, :] for row in range(rows)]
    turn_edge_out[...] = jnp.concatenate(west + east, axis=0)
    sea_order_out[...] = dot(order, sea.astype(BF16))
    down, across = square_places(plan)
    same = jnp.where(down == across, 1.0, 0.0).astype(BF16)
    back = lax.dot_general(
        order, same, (((0,), (0,)), ((), ())), preferred_element_type=F32
    )
    permute = (back * sea[:, :columns]).astype(BF16)
    permute_out[...] = permute
    shape = (plan.some, columns)
    place = lax.broadcasted_iota(jnp.int32, shape, 0)
    number = place - 2 * cols
    wanted = jnp.where(
        place < 2 * cols,
        place + jnp.where(place < cols, 0, (rows - 2) * cols),
        lax.rem(number, rows) * cols + lax.div(number, rows) * (cols - 1),
    )
    wanted = jnp.where(number < 2 * rows, wanted, -1)
    chosen = jnp.where(lane_of(shape) == wanted, 1.0, 0.0).astype(BF16)
    permute_some_out[...] = dot(chosen, permute).astype(BF16)
    sea_some_out[...] = dot(chosen, sea.astype(BF16))
    slot = jnp.sum(order.astype(F32) * down.astype(F32), axis=0, keepdims=True)
    slot = jnp.broadcast_to(column_of(plan, slot), (columns, LANES)).astype(BF16)
    slots_out[...] = dot(chosen, slot)[2 * cols : 2 * cols + 2 * rows, :].astype(jnp.int32)
    keep = 1.0 - drag[...].reshape(1, plan.depth)
    blank = jnp.zeros((1, LANES - 2 * plan.depth), F32)
    keep_out[...] = jnp.broadcast_to(jnp.concatenate([keep, keep, blank], axis=1), (8, LANES))


class Directions:
    def __init__(self, shape):
        direction = lax.rem(lane_of(shape), NDIR)
        self.eastward = (direction < NDIR // 4) | (direction >= 3 * NDIR // 4)
        self.northward = direction < NDIR // 2
        self.first, self.final = direction == 0, direction == NDIR - 1

    def turned(self, moved, rate, gain):
        behind = jnp.where(
            self.first, pltpu.roll(moved, LANES - (NDIR - 1), 1), pltpu.roll(moved, 1, 1)
        )
        forward = jnp.where(
            self.final, pltpu.roll(moved, NDIR - 1, 1), pltpu.roll(moved, LANES - 1, 1)
        )
        return moved - jnp.abs(rate) * gain * (moved - jnp.where(rate > 0.0, behind, forward))


def move_kernel(plan, axes, *refs):
    waves, turn, rates, near, far, refs = *refs[:5], refs[5:]
    if len(refs) > 1:
        order, turned_out, edge_out, sorted_out = refs
    else:
        (turned_out,) = refs
    even = lax.rem(lax.axis_index(axes[0]), 2) == 0
    rows, cols, tiles = plan.rows, plan.cols, plan.tiles
    block = (cols, LANES)
    masks = Directions(block)
    place = lax.broadcasted_iota(jnp.int32, block, 0)
    outside = place == jnp.where(masks.eastward, 0, cols - 1)

    def edge_tile(first, second, tile):
        half = tile % (tiles // 2)
        half = slice(half * LANES, (half + 1) * LANES)
        came = jnp.where(even, first[:, half], second[:, half])
        return came if tile < tiles // 2 else pltpu.roll(came, LANES - NDIR // 2, 1)

    def fill(row, tile):
        lanes = slice(tile * LANES, (tile + 1) * LANES)
        rate = turn[row * cols : (row + 1) * cols, :]
        stay, along_x, along_y, gain = (rates[k : k + 1, lanes] for k in range(4))
        center = waves[row, :, lanes]
        south = waves[row - 1, :, lanes] if row else edge_tile(far, near, tile)
        north = waves[row + 1, :, lanes] if row < rows - 1 else edge_tile(near, far, tile)
        moved = (
            stay * center
            + jnp.where(outside, 0.0, along_x)
            * jnp.where(
                masks.eastward, pltpu.roll(center, 1, 0), pltpu.roll(center, cols - 1, 0)
            )
            + along_y * jnp.where(masks.northward, south, north)
        )
        turned_out[row, :, lanes] = masks.turned(moved, rate, gain)

    if len(refs) == 1:
        for row in range(rows):
            for tile in range(tiles):
                fill(row, tile)
        return
    for tile in range(tiles):
        lanes = slice(tile * LANES, (tile + 1) * LANES)
        stay, along_x, along_y, gain = (rates[k : k + 1, lanes] for k in range(4))
        along_x = jnp.where(outside, 0.0, along_x)
        half = tile % (tiles // 2)
        half = slice(half * LANES, (half + 1) * LANES)
        south_edge = jnp.where(even, far[:, half], near[:, half])
        north_edge = jnp.where(even, near[:, half], far[:, half])
        if tile >= tiles // 2:
            south_edge = pltpu.roll(south_edge, LANES - NDIR // 2, 1)
            north_edge = pltpu.roll(north_edge, LANES - NDIR // 2, 1)
        for row in range(rows):
            center = waves[row, :, lanes]
            south = waves[row - 1, :, lanes] if row else south_edge
            north = waves[row + 1, :, lanes] if row < rows - 1 else north_edge
            moved = (
                stay * center
                + along_x
                * jnp.where(
                    masks.eastward, pltpu.roll(center, 1, 0), pltpu.roll(center, cols - 1, 0)
                )
                + along_y * jnp.where(masks.northward, south, north)
            )
            rate = turn[row * cols : (row + 1) * cols, :]
            turned = masks.turned(moved, rate, gain)
            turned_out[row, :, lanes] = turned
            if len(refs) > 1:
                edge_out[row : row + 1, lanes] = turned[0:1, :]
                edge_out[rows + row : rows + row + 1, lanes] = turned[cols - 1 :, :]
    if len(refs) > 1:
        for start in range(0, plan.spectral, 256):
            part = turned_out[:, :, start : start + 256].reshape(plan.columns, 256)
            sorted_out[:, start : start + 256] = dot(
                order[...], jnp.concatenate(split_value(part), axis=0)
            )


def swapped(plan, value):
    half = plan.depth
    zonal = lane_of(value.shape) < half
    return jnp.where(zonal, pltpu.roll(value, LANES - half, 1), pltpu.roll(value, half, 1))


def send_kernel(plan, axes, *refs):
    turned, turned_edge, turned_order, ocean_in, packed_in, permute_some, slots = refs[:7]
    turn_edge, sea, sea_order, sea_some, keep, stokes, rates, grow, refs = *refs[7:15], refs[15:]
    count = len(plan.sizes)
    got = count + plan.relay
    near, far, sec_in, refs = refs[0], refs[1], refs[2 : 2 + got], refs[2 + got :]
    ocean_out, packed_out, coupled, extra_out, far_out, near_out = refs[:6]
    sec_out, in_order = refs[6 : 6 + count], refs[6 + count]
    section, band = lax.axis_index(axes[1]), lax.axis_index(axes[0])
    even = lax.rem(band, 2) == 0
    columns, rows, cols = plan.columns, plan.rows, plan.cols

    west_edge, east_edge = take_sections(plan, section, packed_in, sec_in, coupled)
    extra = edge_part(plan, rates, turn_edge, west_edge, east_edge)
    in_order[...] = turned_order[...]
    for number in range(2 * rows):
        slot = pl.ds(slots[number, 0], 1)
        part = jnp.concatenate([tile[number : number + 1, :] for tile in extra], axis=1)
        in_order[slot, :] = in_order[slot, :] + part
    arrived = coupled[...]
    halves = growth_halves(arrived)
    wet, wet_some = sea_order[...], twice(sea_some[...])
    rows_of = twice(halves * wet.astype(BF16))
    some_of = twice(dot(permute_some[...], halves).astype(BF16))
    wet = twice(wet)
    total = None
    some, grown = [], []
    filler = jnp.zeros((plan.some - 2 * cols - 2 * rows, 256), F32)
    for number, start in enumerate(range(0, plan.spectral, 256)):
        lanes = slice(start, start + 256)
        table = growth_table(grow, number)
        from_edges = jnp.concatenate(extra[2 * number : 2 * number + 2], axis=1)
        extra_out[:, lanes] = from_edges
        grown.append(in_order[:, lanes] * (wet + dot(rows_of, table)))
        parts = []
        for row in (0, rows - 1):
            west, east = from_edges[row : row + 1, :], from_edges[rows + row : rows + row + 1, :]
            parts += with_edges(plan, turned[row, :, lanes], west, east)
        parts += [turned_edge[:, lanes] + from_edges, filler]
        some.append(jnp.concatenate(parts, axis=0) * (wet_some + dot(some_of, table)))
    for number, start in enumerate(range(0, plan.spectral, 256)):
        lanes = slice(start, start + 256)
        product = stokes_product(grown[number], stokes[start // 2 : start // 2 + LANES, :])
        total = product if total is None else total + product
    drift = pltpu.roll(arrived, LANES // 2, 1)
    new = ocean_step(
        plan, band, even, ocean_in, drift, near, far, west_edge, east_edge, keep, sea
    )
    ocean = jnp.concatenate(new, axis=0)
    ocean_out[...] = ocean
    moments = total[:, :LANES] + total[:, LANES:]
    some = jnp.concatenate(some, axis=1)
    edges = some[2 * cols : 2 * cols + 2 * rows, :]
    fill_sections(plan, section, edges, ocean, moments, packed_out, sec_out, near_out)
    ends = (some[:cols, :], some[cols : 2 * cols, :]), (new[0], new[rows - 1])
    fill_bands(plan, even, *ends, far_out, near_out)


def grow_kernel(plan, axes, *refs):
    turned, extra, coupled, permute, sea, grow, _, waves_out = refs
    at_waves = twice(dot(permute[...], growth_halves(coupled[...])).astype(BF16))
    wet = twice(sea[...])
    for number, start in enumerate(range(0, plan.spectral, 256)):
        lanes = slice(start, start + 256)
        factor = wet + dot(at_waves, growth_table(grow, number))
        grown = grown_part(plan, turned, extra[:, lanes], factor, lanes)
        waves_out[:, :, lanes] = grown.reshape(plan.rows, plan.cols, 256)


def last_kernel(plan, axes, *refs):
    turned, ocean_in, packed_in, permute, turn_edge, sea, keep, rates, grow = refs[:9]
    got = len(plan.sizes) + plan.relay
    near, far, sec_in, refs = refs[9], refs[10], refs[11 : 11 + got], refs[11 + got :]
    waves_far, ocean_far, coupled, waves_out, ocean_out, done = refs
    section, band = lax.axis_index(axes[1]), lax.axis_index(axes[0])
    even = lax.rem(band, 2) == 0

    west_edge, east_edge = take_sections(plan, section, packed_in, sec_in, coupled)
    arrived = coupled[...]
    at_waves = twice(dot(permute[...], growth_halves(arrived)).astype(BF16))
    drift = pltpu.roll(arrived, LANES // 2, 1)
    extra = edge_part(plan, rates, turn_edge, west_edge, east_edge)
    new = ocean_step(
        plan, band, even, ocean_in, drift, near, far, west_edge, east_edge, keep, sea
    )
    for row, value in enumerate(new):
        ocean_out[row] = value[:, : 2 * plan.depth]
    copies = [pltpu.make_async_copy(ocean_out, ocean_far, done.at[0])]
    copies[0].start()
    wet = twice(sea[...])
    for number, start in enumerate(range(0, plan.spectral, 256)):
        lanes = slice(start, start + 256)
        factor = wet + dot(at_waves, growth_table(grow, number))
        from_edges = jnp.concatenate(extra[2 * number : 2 * number + 2], axis=1)
        grown = grown_part(plan, turned, from_edges, factor, lanes)
        waves_out[:, :, lanes] = grown.reshape(plan.rows, plan.cols, 256)
        copy = pltpu.make_async_copy(
            waves_out.at[:, :, lanes], waves_far.at[:, :, lanes], done.at[number + 1]
        )
        copy.start()
        copies.append(copy)
    for copy in copies:
        copy.wait()


def per_device(plan, axes, spectra, turning, currents, drag_rates, land_mask, ocean_target):
    stokes_once, stokes, rates, grow = (
        jnp.asarray(table) for table in build_tables(NFREQ, NDIR, drag_rates.shape[0])
    )
    columns, rows, cols, spectral = plan.columns, plan.rows, plan.cols, plan.spectral
    shape = jax.ShapeDtypeStruct
    params = pltpu.CompilerParams(vmem_limit_bytes=32 * 1024 * 1024)
    to_sections = [shape((size, LANES), F32) for size in plan.sizes]
    to_far = shape((cols, plan.far_lanes.stop), F32)
    to_near = shape((cols, plan.near_lanes.stop), F32)
    state = shape((columns, LANES), F32)
    field = shape(spectra.shape, F32)
    at_edges = shape((2 * rows, LANES), F32)
    edge_field = shape((2 * rows, spectral), F32)
    some = plan.some
    spans = spectral // 256

    def call(kernel, outs, scratch, *args, space_in=pltpu.VMEM, space_out=pltpu.VMEM):
        return pl.pallas_call(
            functools.partial(kernel, plan, axes),
            out_shape=outs,
            in_specs=[pl.BlockSpec(memory_space=space_in)] * len(args),
            out_specs=[pl.BlockSpec(memory_space=space_out)] * len(outs),
            scratch_shapes=scratch,
            compiler_params=params,
        )(*args)

    both_axes = (axes[1], axes[0])
    pairs = [(i, i ^ 1) for i in range(plan.bands) if i ^ 1 < plan.bands]
    others = [(i, ((i + 1) ^ 1) - 1) for i in range(1, plan.bands)]
    others = [(i, j) for i, j in others if j < plan.bands]

    def exchange(to_far, to_near, to_sections, meanwhile):
        got = []
        if plan.relay:
            to_x, *to_sections = to_sections
            from_x = lax.ppermute(to_x, both_axes, plan.crossing(1))
        far_in = lax.ppermute(to_far, axes[0], others)
        near_in = lax.ppermute(to_near, axes[0], pairs)
        first = to_far
        if plan.relay:
            part = plan.chunk + plan.edge
            first, to_mate = call(
                relay_kernel,
                [shape((plan.chunk + part, LANES), F32), shape((part, LANES), F32)],
                [],
                from_x,
                near_in,
            )
            from_y = lax.ppermute(first, both_axes, plan.crossing(2))
            got = [lax.ppermute(to_mate, axes[0], pairs), from_y]
        got += [
            lax.ppermute(message, axes[1], table)
            for message, table in zip(to_sections, plan.direct)
        ]
        return meanwhile(first), [near_in, far_in, *got]

    waves, ocean, packed, order, *sent = call(
        first_kernel,
        [
            field,
            state,
            state,
            shape((columns, 2 * columns), BF16),
            *to_sections,
            to_far,
            to_near,
        ],
        [
            pltpu.VMEM(currents.shape, F32),
            pltpu.VMEM(ocean_target.shape, jnp.int32),
            pltpu.VMEM(stokes_once.shape, BF16),
            pltpu.SemaphoreType.DMA((4,)),
        ],
        *[
            pltpu.with_memory_space_constraint(array, pltpu.HBM)
            for array in (spectra, currents, ocean_target, stokes_once)
        ],
        space_in=pltpu.HBM,
    )

    def maps(first):
        return call(
            map_kernel,
            [
                shape((columns, columns), BF16),
                shape((some, columns), BF16),
                shape((2 * rows, LANES), jnp.int32),
                state,
                at_edges,
                state,
                state,
                shape((some, LANES), F32),
                shape((8, LANES), F32),
            ],
            [],
            turning,
            drag_rates,
            land_mask,
            order,
            first,
        )

    made, came = exchange(*sent[-2:], sent[:-2], maps)
    permute, permute_some, slots, turn, turn_edge, sea, sea_order, sea_some, keep = made
    for step in range(STEPS - 1):
        turned, turned_edge, turned_order = call(
            move_kernel,
            [field, edge_field, shape((columns, spectral), F32)],
            [],
            waves,
            turn,
            rates,
            *came[:2],
            order,
        )
        ocean, packed, coupled, extra, *sent = call(
            send_kernel,
            [state, state, state, edge_field, to_far, to_near] + to_sections,
            [pltpu.VMEM((columns, spectral), F32)],
            turned,
            turned_edge,
            turned_order,
            ocean,
            packed,
            permute_some,
            slots,
            turn_edge,
            sea,
            sea_order,
            sea_some,
            keep,
            stokes,
            rates,
            grow,
            *came,
        )

        def grown(first):
            (waves,) = call(
                grow_kernel, [field], [], turned, extra, coupled, permute, sea, grow, first
            )
            return waves

        waves, came = exchange(*sent[:2], sent[2:], grown)
    (turned,) = call(move_kernel, [field], [], waves, turn, rates, *came[:2])
    return call(
        last_kernel,
        [field, shape(currents.shape, F32)],
        [
            pltpu.VMEM((columns, LANES), F32),
            pltpu.VMEM(spectra.shape, F32),
            pltpu.VMEM(currents.shape, F32),
            pltpu.SemaphoreType.DMA((1 + spans,)),
        ],
        turned,
        ocean,
        packed,
        permute,
        turn_edge,
        sea,
        keep,
        rates,
        grow,
        *came,
        space_out=pltpu.HBM,
    )


def solution(mesh):
    sections, bands = mesh.shape["sec"], mesh.shape["lat"]

    def local(spectra, turning, currents, drag_rates, land_mask, ocean_target):
        rows, cols, spectral = spectra.shape
        plan = Plan(sections, bands, rows, cols, spectral, drag_rates.shape[0])
        return per_device(
            plan, ("lat", "sec"), spectra, turning, currents, drag_rates, land_mask, ocean_target
        )

    return jax.shard_map(
        local,
        mesh=mesh,
        in_specs=(
            P("lat", "sec", None),
            P("lat", "sec"),
            P("lat", "sec", None),
            P(),
            P("lat", "sec"),
            P("lat", "sec"),
        ),
        out_specs=(P("lat", "sec", None), P("lat", "sec", None)),
        check_vma=False,
    )
```

```python
import functools
import math

import jax
import jax.numpy as jnp
import ml_dtypes
import numpy as np
from jax import lax
from jax.experimental import pallas as pl
from jax.experimental.pallas import tpu as pltpu
from jax.sharding import PartitionSpec as P

NFREQ = 24
NDIR = 32
STEPS = 3

stokes_scale = 0.1
ocean_dt = 0.3
current_gain = 0.2

LANES = 128
F32 = jnp.float32
BF16 = jnp.bfloat16


def split_halves(table):
    high = table.astype(ml_dtypes.bfloat16)
    low = (table - high.astype(np.float64)).astype(ml_dtypes.bfloat16)
    return high, low


def build_tables(nfreq, ndir, ndepth):
    fraction = np.arange(nfreq) / (nfreq - 1)
    angles = (np.arange(ndir) + 0.5) * (2.0 * math.pi / ndir)
    east_part, north_part = np.cos(angles), np.sin(angles)
    courant = 0.1 + 0.3 * fraction
    depth_level = 0.5 + (ndepth - 2) * (1.0 - fraction)
    weights = np.maximum(1.0 - np.abs(np.arange(ndepth)[None, :] - depth_level[:, None]), 0.0)
    mean_weights = weights / weights.sum(axis=1, keepdims=True)
    x_rate = np.abs(courant[:, None] * east_part[None, :]).reshape(-1)
    y_rate = np.abs(courant[:, None] * north_part[None, :]).reshape(-1)
    turn_gain = np.repeat(1.0 - 0.5 * fraction, ndir)
    rates = np.stack([1.0 - x_rate - y_rate, x_rate, y_rate, turn_gain] * 2).astype(np.float32)
    compass = np.stack([east_part, north_part])
    stokes = (stokes_scale * weights[:, None, None, :] * compass.T[None, :, :, None]).reshape(
        nfreq * ndir, 2 * ndepth
    )
    growth = current_gain * (1.0 + fraction)
    grow = (
        growth[None, None, :, None] * mean_weights.T[None, :, :, None] * compass[:, None, None, :]
    ).reshape(2 * ndepth, nfreq * ndir)
    pairs = stokes.reshape(-1, 2, LANES // ndir, ndir, 2 * ndepth)
    stokes = np.concatenate([pairs[:, 0, :, : ndir // 2], pairs[:, 1, :, ndir // 2 :]], axis=2)
    high, low = split_halves(stokes.reshape(nfreq * ndir // 2, 2 * ndepth))
    blank = np.zeros_like(high)
    stokes_once = np.concatenate([high, low], axis=1)
    stokes_upper = np.concatenate([blank, high, blank, low], axis=1)
    high, low = split_halves(grow)
    grow = np.concatenate([high, high, low, low], axis=0)
    return (
        stokes_once,
        stokes_upper,
        rates,
        grow.reshape(2 * LANES, -1, LANES).transpose(1, 0, 2).reshape(-1, LANES),
    )


class Plan:
    def __init__(self, sections, bands, rows, cols, spectral, depth):
        self.sections, self.bands = sections, bands
        self.rows, self.cols, self.spectral, self.depth = rows, cols, spectral, depth
        self.columns = rows * cols
        self.chunk = self.columns // sections
        self.tiles = spectral // LANES
        self.some = -(-(2 * cols + 2 * rows) // 16) * 16
        self.edge = ((self.tiles // 2 + 1) * rows + 7) // 8 * 8
        self.relay = sections % 4 == 0 and bands % 2 == 0 and self.chunk <= cols
        self.quad = 4 if self.relay else 1
        self.hops = [
            (hop, flip)
            for hop in range(1, sections // self.quad)
            for flip in ((3, 1, 2, 0) if self.relay else (0,))
        ]
        self.direct = [
            [(i, self.partner(i, *hop, divmod)[0]) for i in range(sections)] for hop in self.hops
        ]
        self.edges = [any(abs(target - i) == 1 for i, target in table) for table in self.direct]
        self.sizes = [self.chunk + (self.edge if edge else 0) for edge in self.edges]
        near_rows = cols * (spectral // 2 + LANES + depth) // LANES
        self.x_rows = max(2 * (self.chunk + self.edge), (near_rows + 8) // 8 * 8)
        if self.relay:
            self.sizes = [self.x_rows] + self.sizes
        start = spectral // 2
        self.far_lanes = slice(start, start + depth)
        self.chunk_lanes = slice(start, start + LANES)
        self.near_lanes = slice(start + LANES, start + LANES + depth)

    def crossing(self, flip):
        bands = self.bands
        return [
            (i * bands + band, (i ^ flip) * bands + (band ^ 1))
            for i in range(self.sections)
            for band in range(bands)
        ]

    def partner(self, section, hop, flip, divide=lambda a, b: (lax.div(a, b), lax.rem(a, b))):
        groups = self.sections // self.quad
        high, low = divide(section, self.quad)
        if flip & 1:
            low = low + 1 - 2 * divide(low, 2)[1]
        if flip & 2:
            low = low + 2 - 4 * divide(low, 2)[0]
        return tuple(
            divide(high + shift, groups)[1] * self.quad + low for shift in (hop, groups - hop)
        )

    def received(self, section, messages):
        parts = []
        if self.relay:
            from_x, from_y = messages[:2]
            parts = [
                (self.partner(section, 0, 1)[1], from_x, 0, self.chunk),
                (self.partner(section, 0, 2)[1], from_y, 0, None),
                (self.partner(section, 0, 3)[1], from_y, self.chunk, 2 * self.chunk),
            ]
            messages = messages[2:]
        for message, hop, edge in zip(messages, self.hops, self.edges):
            parts.append((self.partner(section, *hop)[1], message, 0, self.chunk if edge else None))
        return parts

    def sent(self, section, messages, near):
        parts = []
        lanes = slice(0, LANES)
        if self.relay:
            to_x = messages[0]
            second = self.chunk + self.edge
            parts = [
                (self.partner(section, 0, 1)[0], to_x, 0, lanes, self.chunk),
                (self.partner(section, 0, 2)[0], near, 0, self.chunk_lanes, None),
                (self.partner(section, 0, 3)[0], to_x, second, lanes, second + self.chunk),
            ]
            messages = messages[1:]
        for message, hop, edge in zip(messages, self.hops, self.edges):
            target = self.partner(section, *hop)[0]
            parts.append((target, message, 0, lanes, self.chunk if edge else None))
        return parts


def lane_of(shape):
    return lax.broadcasted_iota(jnp.int32, shape, len(shape) - 1)


def dot(a, b):
    return jnp.dot(a, b, preferred_element_type=F32)


def split_value(value):
    high = value.astype(BF16)
    return high, (value - high.astype(F32)).astype(BF16)


def opposed(part):
    first, second = part[:, :LANES], part[:, LANES:]
    lower = lax.rem(lane_of(first.shape), NDIR) < NDIR // 2
    shift = NDIR // 2
    return jnp.where(lower, first, second) - jnp.where(
        lower, pltpu.roll(first, LANES - shift, 1), pltpu.roll(second, shift, 1)
    )


def stokes_product(part, table):
    return dot(jnp.concatenate(split_value(opposed(part)), axis=1), twice(table, 0))


def packed_half(edge, tile, half, ahead, forward):
    first = edge[:, tile * LANES : (tile + 1) * LANES]
    second = edge[:, (tile + half) * LANES : (tile + half + 1) * LANES]
    keep = jnp.where(ahead, 1, 0) == jnp.where(forward, 1, 0)
    return jnp.where(keep, first, pltpu.roll(second, NDIR // 2, 1))


def fill_band(plan, northward, edge, sea_row, out, lanes):
    half = plan.tiles // 2
    masks = Directions((plan.cols, LANES))
    for tile in range(half):
        out[:, tile * LANES : (tile + 1) * LANES] = packed_half(
            edge, tile, half, masks.northward, northward
        )
    out[:, lanes] = sea_row[:, : plan.depth]


def fill_bands(plan, even, edges, sea_rows, far, near):
    for out, northward, lanes in (
        (far, jnp.logical_not(even), plan.far_lanes),
        (near, even, plan.near_lanes),
    ):
        edge = jnp.where(northward, edges[1], edges[0])
        sea_row = jnp.where(northward, sea_rows[1], sea_rows[0])
        fill_band(plan, northward, edge, sea_row, out, lanes)


def fill_sections(plan, section, edges, ocean, ordered, packed_out, sec_out, near):
    chunk, rows, cols, half = plan.chunk, plan.rows, plan.cols, plan.tiles // 2
    lane = lane_of((plan.columns, LANES))
    packed_out[...] = jnp.where(lane < LANES // 2, ocean, ordered)
    sea_rows = ocean.reshape(rows, cols, LANES)
    masks = Directions((rows, LANES))
    if plan.relay:
        used = 2 * (chunk + plan.edge)
        sec_out[0][used:, :] = jnp.zeros((plan.x_rows - used, LANES), F32)
    for target, out, at, lanes, edge_at in plan.sent(section, sec_out, near):
        part = packed_out[pl.ds(pl.multiple_of(target * chunk, 8), chunk), :]
        out[at : at + chunk, lanes] = part
        if edge_at is None:
            continue
        eastward = target == section + 1
        edge = jnp.where(eastward, edges[rows:, :], edges[:rows, :])
        for tile in range(half):
            place = edge_at + tile * rows
            out[place : place + rows, :] = packed_half(edge, tile, half, masks.eastward, eastward)
        for row in range(rows):
            place = edge_at + half * rows + row
            out[place : place + 1, :] = jnp.where(
                eastward, sea_rows[row, cols - 1 : cols, :], sea_rows[row, 0:1, :]
            )


def take_sections(plan, section, packed_in, sec_in, coupled):
    chunk = plan.chunk
    own = pl.ds(pl.multiple_of(section * chunk, 8), chunk)
    coupled[own, :] = packed_in[own, :]
    west = east = jnp.zeros((plan.edge, LANES), F32)
    for source, message, at, edge_at in plan.received(section, sec_in):
        coupled[pl.ds(pl.multiple_of(source * chunk, 8), chunk), :] = message[at : at + chunk, :]
        if edge_at is not None:
            edge = message[edge_at : edge_at + plan.edge, :]
            west = jnp.where(source == section - 1, edge, west)
            east = jnp.where(source == section + 1, edge, east)
    return west, east


def edge_part(plan, rates, turn_edge, west_edge, east_edge):
    rows, half = plan.rows, plan.tiles // 2
    shape = (2 * rows, LANES)
    masks = Directions(shape)
    westmost = lax.broadcasted_iota(jnp.int32, shape, 0) < rows
    reached = jnp.where(masks.eastward, 1, 0) == jnp.where(westmost, 1, 0)
    parts = []
    for tile in range(plan.tiles):
        lanes = slice(tile * LANES, (tile + 1) * LANES)
        edge = slice(tile % half * rows, (tile % half + 1) * rows)
        came = jnp.concatenate([west_edge[edge, :], east_edge[edge, :]], axis=0)
        if tile >= half:
            came = pltpu.roll(came, LANES - NDIR // 2, 1)
        moved = rates[1:2, lanes] * jnp.where(reached, came, 0.0)
        parts.append(masks.turned(moved, turn_edge[...], rates[3:4, lanes]))
    return parts


def ocean_step(plan, band, even, ocean_in, stokes, near, far, west_edge, east_edge, keep, sea):
    rows, cols, half = plan.rows, plan.cols, plan.tiles // 2
    block = (cols, LANES)
    zonal = lane_of(block) < plan.depth
    place = lax.broadcasted_iota(jnp.int32, block, 0)
    at_west, at_east = place == 0, place == cols - 1
    blank = jnp.zeros((cols, LANES - plan.depth), F32)
    far = jnp.concatenate([far[:, plan.far_lanes], blank], axis=1)
    near = jnp.concatenate([near[:, plan.near_lanes], blank], axis=1)
    south_edge, north_edge = jnp.where(even, far, near), jnp.where(even, near, far)
    new = []
    for row in range(rows):
        flat = slice(row * cols, (row + 1) * cols)
        edge = slice(half * rows + row, half * rows + row + 1)
        center = ocean_in[flat, :]
        west = jnp.where(at_west, west_edge[edge, :], pltpu.roll(center, 1, 0))
        east = jnp.where(at_east, east_edge[edge, :], pltpu.roll(center, cols - 1, 0))
        south = ocean_in[(row - 1) * cols : row * cols, :] if row else south_edge
        north = ocean_in[(row + 1) * cols : (row + 2) * cols, :] if row < rows - 1 else north_edge
        shear = 0.5 * jnp.where(zonal, south - north, east - west)
        y = (band * rows + row).astype(F32)
        spin = 0.2 + 0.6 * y / float(plan.bands * rows) + (shear + swapped(plan, shear))
        turn_by = ocean_dt * spin * swapped(plan, center + stokes[flat, :])
        new.append(keep[0:1, :] * (center + jnp.where(zonal, turn_by, -turn_by)) * sea[flat, :])
    return new


def twice(value, axis=1):
    return jnp.concatenate([value, value], axis=axis)


def growth_table(grow, number):
    size = 2 * LANES
    return jnp.concatenate(
        [grow[(2 * number + k) * size : (2 * number + k + 1) * size, :] for k in range(2)], axis=1
    )


def growth_halves(arrived):
    high = arrived.astype(BF16).astype(F32)
    lower = lane_of(arrived.shape) < LANES // 2
    return jnp.where(lower, high, pltpu.roll(arrived - high, LANES // 2, 1)).astype(BF16)


def with_edges(plan, turned, west, east):
    place = lax.broadcasted_iota(jnp.int32, (8, 256), 0)
    return [
        turned[0:8, :] + jnp.where(place == 0, west, 0.0),
        turned[8 : plan.cols - 8, :],
        turned[plan.cols - 8 :, :] + jnp.where(place == 7, east, 0.0),
    ]


def grown_part(plan, turned, from_edges, factor, lanes):
    rows = plan.rows
    parts = []
    for row in range(rows):
        west, east = from_edges[row : row + 1, :], from_edges[rows + row : rows + row + 1, :]
        parts += with_edges(plan, turned[row, :, lanes], west, east)
    return jnp.concatenate(parts, axis=0) * factor


def relay_kernel(plan, axes, from_x, near, to_y, to_mate):
    own = plan.chunk + plan.edge
    to_y[0 : plan.chunk, :] = near[0 : plan.chunk, plan.chunk_lanes]
    to_y[plan.chunk :, :] = from_x[own : 2 * own, :]
    to_mate[...] = from_x[:own, :]


def square_places(plan):
    shape = (plan.columns, plan.columns)
    return lax.broadcasted_iota(jnp.int32, shape, 0), lax.broadcasted_iota(jnp.int32, shape, 1)


def row_of(plan, ref):
    return jnp.concatenate([ref[row : row + 1, :] for row in range(plan.rows)], axis=1)


def column_of(plan, row):
    down, across = square_places(plan)
    spread = jnp.broadcast_to(row, down.shape)
    return jnp.sum(jnp.where(down == across, spread, 0.0), axis=1, keepdims=True)


def first_kernel(plan, axes, *refs):
    waves_in, currents_in, target_in, stokes_in, refs = *refs[:4], refs[4:]
    waves, ocean_out, packed_out, order_out, refs = *refs[:4], refs[4:]
    count = len(plan.sizes)
    sec_out, lat_out, refs = refs[:count], refs[count : count + 2], refs[count + 2 :]
    currents, target, stokes, done = refs
    pairs = [(target_in, target), (waves_in, waves), (stokes_in, stokes), (currents_in, currents)]
    copies = [pltpu.make_async_copy(a, b, done.at[k]) for k, (a, b) in enumerate(pairs)]
    for copy in copies:
        copy.start()
    section, band = lax.axis_index(axes[1]), lax.axis_index(axes[0])
    even = lax.rem(band, 2) == 0
    columns, rows, cols = plan.columns, plan.rows, plan.cols
    copies[0].wait()
    down, across = square_places(plan)
    target_row = row_of(plan, target).astype(F32)
    same = column_of(plan, target_row) == target_row
    rank = jnp.sum(jnp.where(same & (down < across), 1.0, 0.0), axis=0, keepdims=True)
    slot = target_row * float(plan.chunk) + rank
    order = twice(jnp.where(slot == down.astype(F32), 1.0, 0.0)).astype(BF16)
    order_out[...] = order
    for copy in copies[1:]:
        copy.wait()
    total = None
    for start in range(0, plan.spectral, 256):
        part = waves[:, :, start : start + 256].reshape(columns, 256)
        product = stokes_product(part, stokes[start // 2 : start // 2 + LANES, :])
        total = product if total is None else total + product
    moments = total
    flat = currents[...].reshape(columns, 2 * plan.depth)
    ocean = jnp.concatenate([flat, jnp.zeros((columns, LANES - 2 * plan.depth), F32)], axis=1)
    ocean_out[...] = ocean
    ordered = dot(order, jnp.concatenate(split_value(moments), axis=0))
    ordered = ordered + pltpu.roll(ordered, LANES // 2, 1)
    west = [waves[row, 0:1, :] for row in range(rows)]
    east = [waves[row, cols - 1 : cols, :] for row in range(rows)]
    edges = jnp.concatenate(west + east, axis=0)
    fill_sections(plan, section, edges, ocean, ordered, packed_out, sec_out, lat_out[1])
    sea_rows = ocean.reshape(rows, cols, LANES)
    ends = (waves[0], waves[rows - 1]), (sea_rows[0], sea_rows[rows - 1])
    fill_bands(plan, even, *ends, *lat_out)


def map_kernel(plan, axes, *refs):
    inputs, (order_twice, _), refs = refs[:6], refs[6:8], refs[8:]
    tables, (turning, drag, mask, done) = refs[9:12], refs[12:]
    targets = (turning, drag, mask, *tables)
    copies = [pltpu.make_async_copy(*pair, done.at[k]) for k, pair in enumerate(zip(inputs, targets))]
    for copy in copies:
        copy.start()
    permute_out, permute_some_out, slots_out, turn_out, turn_edge_out = refs[:5]
    sea_out, sea_order_out, sea_some_out, keep_out = refs[5:9]
    columns, rows, cols = plan.columns, plan.rows, plan.cols
    order = order_twice[:, :columns]
    for copy in copies[:3]:
        copy.wait()
    sea = jnp.broadcast_to(column_of(plan, row_of(plan, mask).astype(F32)), (columns, LANES))
    turn = jnp.broadcast_to(column_of(plan, row_of(plan, turning)), (columns, LANES))
    sea_out[...] = sea
    turn_out[...] = turn
    west = [turn[row * cols : row * cols + 1, :] for row in range(rows)]
    east = [turn[(row + 1) * cols - 1 : (row + 1) * cols, :] for row in range(rows)]
    turn_edge_out[...] = jnp.concatenate(west + east, axis=0)
    sea_order_out[...] = dot(order, sea.astype(BF16))
    down, across = square_places(plan)
    same = jnp.where(down == across, 1.0, 0.0).astype(BF16)
    back = lax.dot_general(
        order, same, (((0,), (0,)), ((), ())), preferred_element_type=F32
    )
    permute = (back * sea[:, :columns]).astype(BF16)
    permute_out[...] = permute
    shape = (plan.some, columns)
    place = lax.broadcasted_iota(jnp.int32, shape, 0)
    number = place - 2 * cols
    wanted = jnp.where(
        place < 2 * cols,
        place + jnp.where(place < cols, 0, (rows - 2) * cols),
        lax.rem(number, rows) * cols + lax.div(number, rows) * (cols - 1),
    )
    wanted = jnp.where(number < 2 * rows, wanted, -1)
    chosen = jnp.where(lane_of(shape) == wanted, 1.0, 0.0).astype(BF16)
    permute_some_out[...] = dot(chosen, permute).astype(BF16)
    sea_some_out[...] = dot(chosen, sea.astype(BF16))
    slot = jnp.sum(order.astype(F32) * down.astype(F32), axis=0, keepdims=True)
    slot = jnp.broadcast_to(column_of(plan, slot), (columns, LANES)).astype(BF16)
    slots_out[...] = dot(chosen, slot)[2 * cols : 2 * cols + 2 * rows, :].astype(jnp.int32)
    keep = 1.0 - drag[...].reshape(1, plan.depth)
    blank = jnp.zeros((1, LANES - 2 * plan.depth), F32)
    keep_out[...] = jnp.broadcast_to(jnp.concatenate([keep, keep, blank], axis=1), (8, LANES))
    for copy in copies[3:]:
        copy.wait()


class Directions:
    def __init__(self, shape):
        direction = lax.rem(lane_of(shape), NDIR)
        self.eastward = (direction < NDIR // 4) | (direction >= 3 * NDIR // 4)
        self.northward = direction < NDIR // 2
        self.first, self.final = direction == 0, direction == NDIR - 1

    def turned(self, moved, rate, gain):
        behind = jnp.where(
            self.first, pltpu.roll(moved, LANES - (NDIR - 1), 1), pltpu.roll(moved, 1, 1)
        )
        forward = jnp.where(
            self.final, pltpu.roll(moved, NDIR - 1, 1), pltpu.roll(moved, LANES - 1, 1)
        )
        return moved - jnp.abs(rate) * gain * (moved - jnp.where(rate > 0.0, behind, forward))


def move_kernel(plan, axes, *refs):
    waves, turn, rates, near, far, refs = *refs[:5], refs[5:]
    if len(refs) > 1:
        order, turned_out, edge_out, sorted_out = refs
    else:
        (turned_out,) = refs
    even = lax.rem(lax.axis_index(axes[0]), 2) == 0
    rows, cols, tiles = plan.rows, plan.cols, plan.tiles
    block = (cols, LANES)
    masks = Directions(block)
    place = lax.broadcasted_iota(jnp.int32, block, 0)
    outside = place == jnp.where(masks.eastward, 0, cols - 1)

    def edge_tile(first, second, tile):
        half = tile % (tiles // 2)
        half = slice(half * LANES, (half + 1) * LANES)
        came = jnp.where(even, first[:, half], second[:, half])
        return came if tile < tiles // 2 else pltpu.roll(came, LANES - NDIR // 2, 1)

    def fill(row, tile):
        lanes = slice(tile * LANES, (tile + 1) * LANES)
        rate = turn[row * cols : (row + 1) * cols, :]
        stay, along_x, along_y, gain = (rates[k : k + 1, lanes] for k in range(4))
        center = waves[row, :, lanes]
        south = waves[row - 1, :, lanes] if row else edge_tile(far, near, tile)
        north = waves[row + 1, :, lanes] if row < rows - 1 else edge_tile(near, far, tile)
        moved = (
            stay * center
            + jnp.where(outside, 0.0, along_x)
            * jnp.where(
                masks.eastward, pltpu.roll(center, 1, 0), pltpu.roll(center, cols - 1, 0)
            )
            + along_y * jnp.where(masks.northward, south, north)
        )
        turned_out[row, :, lanes] = masks.turned(moved, rate, gain)

    if len(refs) == 1:
        for row in range(rows):
            for tile in range(tiles):
                fill(row, tile)
        return
    for tile in range(tiles):
        lanes = slice(tile * LANES, (tile + 1) * LANES)
        stay, along_x, along_y, gain = (rates[k : k + 1, lanes] for k in range(4))
        along_x = jnp.where(outside, 0.0, along_x)
        half = tile % (tiles // 2)
        half = slice(half * LANES, (half + 1) * LANES)
        south_edge = jnp.where(even, far[:, half], near[:, half])
        north_edge = jnp.where(even, near[:, half], far[:, half])
        if tile >= tiles // 2:
            south_edge = pltpu.roll(south_edge, LANES - NDIR // 2, 1)
            north_edge = pltpu.roll(north_edge, LANES - NDIR // 2, 1)
        for row in range(rows):
            center = waves[row, :, lanes]
            south = waves[row - 1, :, lanes] if row else south_edge
            north = waves[row + 1, :, lanes] if row < rows - 1 else north_edge
            moved = (
                stay * center
                + along_x
                * jnp.where(
                    masks.eastward, pltpu.roll(center, 1, 0), pltpu.roll(center, cols - 1, 0)
                )
                + along_y * jnp.where(masks.northward, south, north)
            )
            rate = turn[row * cols : (row + 1) * cols, :]
            turned = masks.turned(moved, rate, gain)
            turned_out[row, :, lanes] = turned
            if len(refs) > 1:
                edge_out[row : row + 1, lanes] = turned[0:1, :]
                edge_out[rows + row : rows + row + 1, lanes] = turned[cols - 1 :, :]
    if len(refs) > 1:
        for start in range(0, plan.spectral, 256):
            part = turned_out[:, :, start : start + 256].reshape(plan.columns, 256)
            sorted_out[:, start : start + 256] = dot(
                order[...], jnp.concatenate(split_value(part), axis=0)
            )


def swapped(plan, value):
    half = plan.depth
    zonal = lane_of(value.shape) < half
    return jnp.where(zonal, pltpu.roll(value, LANES - half, 1), pltpu.roll(value, half, 1))


def send_kernel(plan, axes, *refs):
    turned, turned_edge, turned_order, ocean_in, packed_in, permute_some, slots = refs[:7]
    turn_edge, sea, sea_order, sea_some, keep, stokes, rates, grow, refs = *refs[7:15], refs[15:]
    count = len(plan.sizes)
    got = count + plan.relay
    near, far, sec_in, refs = refs[0], refs[1], refs[2 : 2 + got], refs[2 + got :]
    ocean_out, packed_out, coupled, extra_out, far_out, near_out = refs[:6]
    sec_out, in_order = refs[6 : 6 + count], refs[6 + count]
    section, band = lax.axis_index(axes[1]), lax.axis_index(axes[0])
    even = lax.rem(band, 2) == 0
    columns, rows, cols = plan.columns, plan.rows, plan.cols

    west_edge, east_edge = take_sections(plan, section, packed_in, sec_in, coupled)
    extra = edge_part(plan, rates, turn_edge, west_edge, east_edge)
    in_order[...] = turned_order[...]
    for number in range(2 * rows):
        slot = pl.ds(slots[number, 0], 1)
        part = jnp.concatenate([tile[number : number + 1, :] for tile in extra], axis=1)
        in_order[slot, :] = in_order[slot, :] + part
    arrived = coupled[...]
    halves = growth_halves(arrived)
    wet, wet_some = sea_order[...], twice(sea_some[...])
    rows_of = twice(halves * wet.astype(BF16))
    some_of = twice(dot(permute_some[...], halves).astype(BF16))
    wet = twice(wet)
    total = None
    some, grown = [], []
    filler = jnp.zeros((plan.some - 2 * cols - 2 * rows, 256), F32)
    for number, start in enumerate(range(0, plan.spectral, 256)):
        lanes = slice(start, start + 256)
        table = growth_table(grow, number)
        from_edges = jnp.concatenate(extra[2 * number : 2 * number + 2], axis=1)
        extra_out[:, lanes] = from_edges
        grown.append(in_order[:, lanes] * (wet + dot(rows_of, table)))
        parts = []
        for row in (0, rows - 1):
            west, east = from_edges[row : row + 1, :], from_edges[rows + row : rows + row + 1, :]
            parts += with_edges(plan, turned[row, :, lanes], west, east)
        parts += [turned_edge[:, lanes] + from_edges, filler]
        some.append(jnp.concatenate(parts, axis=0) * (wet_some + dot(some_of, table)))
    for number, start in enumerate(range(0, plan.spectral, 256)):
        lanes = slice(start, start + 256)
        product = stokes_product(grown[number], stokes[start // 2 : start // 2 + LANES, :])
        total = product if total is None else total + product
    drift = pltpu.roll(arrived, LANES // 2, 1)
    new = ocean_step(
        plan, band, even, ocean_in, drift, near, far, west_edge, east_edge, keep, sea
    )
    ocean = jnp.concatenate(new, axis=0)
    ocean_out[...] = ocean
    moments = total[:, :LANES] + total[:, LANES:]
    some = jnp.concatenate(some, axis=1)
    edges = some[2 * cols : 2 * cols + 2 * rows, :]
    fill_sections(plan, section, edges, ocean, moments, packed_out, sec_out, near_out)
    ends = (some[:cols, :], some[cols : 2 * cols, :]), (new[0], new[rows - 1])
    fill_bands(plan, even, *ends, far_out, near_out)


def grow_kernel(plan, axes, *refs):
    turned, extra, coupled, permute, sea, grow, _, waves_out = refs
    at_waves = twice(dot(permute[...], growth_halves(coupled[...])).astype(BF16))
    wet = twice(sea[...])
    for number, start in enumerate(range(0, plan.spectral, 256)):
        lanes = slice(start, start + 256)
        factor = wet + dot(at_waves, growth_table(grow, number))
        grown = grown_part(plan, turned, extra[:, lanes], factor, lanes)
        waves_out[:, :, lanes] = grown.reshape(plan.rows, plan.cols, 256)


def last_kernel(plan, axes, *refs):
    turned, ocean_in, packed_in, permute, turn_edge, sea, keep, rates, grow = refs[:9]
    got = len(plan.sizes) + plan.relay
    near, far, sec_in, refs = refs[9], refs[10], refs[11 : 11 + got], refs[11 + got :]
    waves_far, ocean_far, coupled, waves_out, ocean_out, done = refs
    section, band = lax.axis_index(axes[1]), lax.axis_index(axes[0])
    even = lax.rem(band, 2) == 0

    west_edge, east_edge = take_sections(plan, section, packed_in, sec_in, coupled)
    arrived = coupled[...]
    at_waves = twice(dot(permute[...], growth_halves(arrived)).astype(BF16))
    drift = pltpu.roll(arrived, LANES // 2, 1)
    extra = edge_part(plan, rates, turn_edge, west_edge, east_edge)
    new = ocean_step(
        plan, band, even, ocean_in, drift, near, far, west_edge, east_edge, keep, sea
    )
    for row, value in enumerate(new):
        ocean_out[row] = value[:, : 2 * plan.depth]
    copies = [pltpu.make_async_copy(ocean_out, ocean_far, done.at[0])]
    copies[0].start()
    wet = twice(sea[...])
    for number, start in enumerate(range(0, plan.spectral, 256)):
        lanes = slice(start, start + 256)
        factor = wet + dot(at_waves, growth_table(grow, number))
        from_edges = jnp.concatenate(extra[2 * number : 2 * number + 2], axis=1)
        grown = grown_part(plan, turned, from_edges, factor, lanes)
        waves_out[:, :, lanes] = grown.reshape(plan.rows, plan.cols, 256)
        copy = pltpu.make_async_copy(
            waves_out.at[:, :, lanes], waves_far.at[:, :, lanes], done.at[number + 1]
        )
        copy.start()
        copies.append(copy)
    for copy in copies:
        copy.wait()


def per_device(plan, axes, spectra, turning, currents, drag_rates, land_mask, ocean_target):
    stokes_once, *tables = (
        jnp.asarray(table) for table in build_tables(NFREQ, NDIR, drag_rates.shape[0])
    )
    columns, rows, cols, spectral = plan.columns, plan.rows, plan.cols, plan.spectral
    shape = jax.ShapeDtypeStruct
    params = pltpu.CompilerParams(vmem_limit_bytes=32 * 1024 * 1024)
    to_sections = [shape((size, LANES), F32) for size in plan.sizes]
    to_far = shape((cols, plan.far_lanes.stop), F32)
    to_near = shape((cols, plan.near_lanes.stop), F32)
    state = shape((columns, LANES), F32)
    field = shape(spectra.shape, F32)
    at_edges = shape((2 * rows, LANES), F32)
    edge_field = shape((2 * rows, spectral), F32)
    some = plan.some
    spans = spectral // 256

    def call(kernel, outs, scratch, *args, space_in=pltpu.VMEM, space_out=pltpu.VMEM):
        spaces = space_in if isinstance(space_in, list) else [space_in] * len(args)
        return pl.pallas_call(
            functools.partial(kernel, plan, axes),
            out_shape=outs,
            in_specs=[pl.BlockSpec(memory_space=space) for space in spaces],
            out_specs=[pl.BlockSpec(memory_space=space_out)] * len(outs),
            scratch_shapes=scratch,
            compiler_params=params,
        )(*args)

    both_axes = (axes[1], axes[0])
    pairs = [(i, i ^ 1) for i in range(plan.bands) if i ^ 1 < plan.bands]
    others = [(i, ((i + 1) ^ 1) - 1) for i in range(1, plan.bands)]
    others = [(i, j) for i, j in others if j < plan.bands]

    def exchange(to_far, to_near, to_sections, meanwhile):
        got = []
        if plan.relay:
            to_x, *to_sections = to_sections
            from_x = lax.ppermute(to_x, both_axes, plan.crossing(1))
        far_in = lax.ppermute(to_far, axes[0], others)
        near_in = lax.ppermute(to_near, axes[0], pairs)
        first = to_far
        if plan.relay:
            part = plan.chunk + plan.edge
            first, to_mate = call(
                relay_kernel,
                [shape((plan.chunk + part, LANES), F32), shape((part, LANES), F32)],
                [],
                from_x,
                near_in,
            )
            from_y = lax.ppermute(first, both_axes, plan.crossing(2))
            got = [lax.ppermute(to_mate, axes[0], pairs), from_y]
        got += [
            lax.ppermute(message, axes[1], table)
            for message, table in zip(to_sections, plan.direct)
        ]
        return meanwhile(first), [near_in, far_in, *got]

    waves, ocean, packed, order, *sent = call(
        first_kernel,
        [
            field,
            state,
            state,
            shape((columns, 2 * columns), BF16),
            *to_sections,
            to_far,
            to_near,
        ],
        [
            pltpu.VMEM(currents.shape, F32),
            pltpu.VMEM(ocean_target.shape, jnp.int32),
            pltpu.VMEM(stokes_once.shape, BF16),
            pltpu.SemaphoreType.DMA((4,)),
        ],
        *[
            pltpu.with_memory_space_constraint(array, pltpu.HBM)
            for array in (spectra, currents, ocean_target, stokes_once)
        ],
        space_in=pltpu.HBM,
    )

    def maps(first):
        return call(
            map_kernel,
            [
                shape((columns, columns), BF16),
                shape((some, columns), BF16),
                shape((2 * rows, LANES), jnp.int32),
                state,
                at_edges,
                state,
                state,
                shape((some, LANES), F32),
                shape((8, LANES), F32),
                *[shape(table.shape, table.dtype) for table in tables],
            ],
            [
                pltpu.VMEM(turning.shape, F32),
                pltpu.VMEM(drag_rates.shape, F32),
                pltpu.VMEM(land_mask.shape, jnp.int32),
                pltpu.SemaphoreType.DMA((6,)),
            ],
            *[
                pltpu.with_memory_space_constraint(array, pltpu.HBM)
                for array in (turning, drag_rates, land_mask, *tables)
            ],
            order,
            first,
            space_in=[pltpu.HBM] * 6 + [pltpu.VMEM] * 2,
        )

    made, came = exchange(*sent[-2:], sent[:-2], maps)
    permute, permute_some, slots, turn, turn_edge, sea, sea_order, sea_some, keep, stokes, rates, grow = made
    for step in range(STEPS - 1):
        turned, turned_edge, turned_order = call(
            move_kernel,
            [field, edge_field, shape((columns, spectral), F32)],
            [],
            waves,
            turn,
            rates,
            *came[:2],
            order,
        )
        ocean, packed, coupled, extra, *sent = call(
            send_kernel,
            [state, state, state, edge_field, to_far, to_near] + to_sections,
            [pltpu.VMEM((columns, spectral), F32)],
            turned,
            turned_edge,
            turned_order,
            ocean,
            packed,
            permute_some,
            slots,
            turn_edge,
            sea,
            sea_order,
            sea_some,
            keep,
            stokes,
            rates,
            grow,
            *came,
        )

        def grown(first):
            (waves,) = call(
                grow_kernel, [field], [], turned, extra, coupled, permute, sea, grow, first
            )
            return waves

        waves, came = exchange(*sent[:2], sent[2:], grown)
    (turned,) = call(move_kernel, [field], [], waves, turn, rates, *came[:2])
    return call(
        last_kernel,
        [field, shape(currents.shape, F32)],
        [
            pltpu.VMEM((columns, LANES), F32),
            pltpu.VMEM(spectra.shape, F32),
            pltpu.VMEM(currents.shape, F32),
            pltpu.SemaphoreType.DMA((1 + spans,)),
        ],
        turned,
        ocean,
        packed,
        permute,
        turn_edge,
        sea,
        keep,
        rates,
        grow,
        *came,
        space_out=pltpu.HBM,
    )


def solution(mesh):
    sections, bands = mesh.shape["sec"], mesh.shape["lat"]

    def local(spectra, turning, currents, drag_rates, land_mask, ocean_target):
        rows, cols, spectral = spectra.shape
        plan = Plan(sections, bands, rows, cols, spectral, drag_rates.shape[0])
        return per_device(
            plan, ("lat", "sec"), spectra, turning, currents, drag_rates, land_mask, ocean_target
        )

    return jax.shard_map(
        local,
        mesh=mesh,
        in_specs=(
            P("lat", "sec", None),
            P("lat", "sec"),
            P("lat", "sec", None),
            P(),
            P("lat", "sec"),
            P("lat", "sec"),
        ),
        out_specs=(P("lat", "sec", None), P("lat", "sec", None)),
        check_vma=False,
    )
```
